32 devices in a mesh: chan: 8 (over z, core), tm: 4 (over y, x).
Axes of the slice: x: 2, y: 2, z: 4, core: 2. Of those that a mesh axis runs over, the one named last changes fastest.
Arguments:
- samples: bfloat16 [512, 32, 512], P('chan', 'tm'), may hold values from -6 to 6
- valid: int32 [512, 32], P('chan', 'tm'), may hold values 0 or 1
- offsets: int32 [8], replicated, may hold values from 0 to 31
Outputs:
- correlations: bfloat16 [4, 8, 512, 512], P('tm', None, 'chan')
The draws below stay inside these ranges and needn't reach their ends.
All inputs are finite; a program needn't handle non-finite values. No bound on the sum of `valid` on one device may be relied on, other than what follows from the above.
Results may differ from the reference program's by a relative error of at most 0.0045.
Values may be sent and summed in bfloat16 or wider, within the bound.
No kernel may reach another device: no remote copies, remote signals or barrier semaphores. Data moves between devices by JAX's collectives and lax.ppermute only.
A program may use at most 64 MiB of HBM per device.

```python
import math
import jax
import jax.numpy as jnp
from jax import lax

CH_DEV = 64
WIN_DEV = 8
SAMPLES = 512
PAIRS = 8
OFFSET_SPAN = 32
BINS = 256
CHANNELS = 512
WINDOWS = 32
N_TM = 4


def set_ends(values, own_key, smallest, largest):
    shape = values.shape
    index_at = [jax.random.randint(jax.random.fold_in(own_key, axis), (), 0, shape[axis]) for axis in range(len(shape))]
    values = values.at[tuple(index_at)].set(smallest)
    longest = shape.index(max(shape))
    index_at[longest] = (index_at[longest] + 1) % shape[longest]
    return values.at[tuple(index_at)].set(largest)


def shard_levels(key, extent, shards, low, top_value):
    def one(axis_at, parts):
        steps = jax.random.uniform(jax.random.fold_in(jax.random.fold_in(key, 6), axis_at), (parts,), jnp.float32, low / len(shards), top_value / len(shards))
        return jnp.repeat(jnp.exp(steps), extent[axis_at] // parts).reshape((-1,) + (1,) * (len(extent) - axis_at - 1))

    level = one(*shards[0])
    for cut in shards[1:]:
        level = level * one(*cut)
    return level


def centred(stream_key, dims, scale, bound, cuts=(), kind=jnp.bfloat16):
    entries = jax.random.normal(stream_key, dims, jnp.float32) * scale
    if len(cuts) > 0:
        entries = shard_levels(stream_key, dims, cuts, -0.22, 0.18) * entries
    return jnp.clip(entries, min=-bound, max=bound).astype(kind)


def setup_inputs(seed: int = 0) -> dict:
    streams_of = jax.random.split(jax.random.key(seed), 4)
    samples = centred(streams_of[0], (CHANNELS, WINDOWS, SAMPLES), 1.0, 6.0, ((0, 8), (1, 4)))
    valid = set_ends((jax.random.randint(streams_of[1], (CHANNELS, WINDOWS), 0, 8) < 7).astype(jnp.int32), jax.random.fold_in(streams_of[1], 1), 0, 1)
    offsets = set_ends(jax.random.randint(streams_of[2], (PAIRS,), 0, OFFSET_SPAN), jax.random.fold_in(streams_of[2], 1), 0, OFFSET_SPAN - 1).astype(jnp.int32)
    return dict(samples=samples, valid=valid, offsets=offsets)


def forward_table(length):
    bins = length // 2
    rows = jnp.arange(length).astype(jnp.int32)
    freqs = (jnp.arange(bins) + 1).astype(jnp.int32)
    angle = jnp.mod(rows[:, None] * freqs[None, :], length).astype(jnp.float32) * (2.0 * math.pi / length)
    return jnp.concatenate([jnp.cos(angle), -jnp.sin(angle)], axis=1).astype(jnp.bfloat16)

def inverse_table(length):
    bins = length // 2
    freqs = (jnp.arange(bins) + 1).astype(jnp.int32)
    lags = jnp.arange(length).astype(jnp.int32)
    angle = jnp.mod(freqs[:, None] * lags[None, :], length).astype(jnp.float32) * (2.0 * math.pi / length)
    return jnp.concatenate([jnp.cos(angle), -jnp.sin(angle)], axis=0)

def whiten(samples, valid, forward):
    chans, wins, length = samples.shape
    bins = length // 2
    raw = jnp.dot(samples.reshape(chans * wins, length), forward, preferred_element_type=jnp.float32)
    raw = raw.reshape(chans, wins, 2 * bins)
    real_part = raw[..., :bins]
    imag_part = raw[..., bins:]
    power = real_part * real_part + imag_part * imag_part
    level = lax.optimization_barrier(jnp.mean(power, axis=-1, keepdims=True))
    scale = valid[..., None].astype(jnp.float32) * lax.rsqrt(power + 0.01 * level + 1e-06)
    return (real_part * scale, imag_part * scale)

def reference(samples, valid, offsets):
    forward = forward_table(SAMPLES)
    inverse = inverse_table(SAMPLES)
    blocks = CHANNELS // CH_DEV
    white_re, white_im = lax.map(lambda pair: whiten(pair[0], pair[1], forward), (samples.reshape(blocks, CH_DEV, WINDOWS, SAMPLES), valid.reshape(blocks, CH_DEV, WINDOWS)))
    white_re = white_re.reshape(CHANNELS, WINDOWS, BINS)
    white_im = white_im.reshape(CHANNELS, WINDOWS, BINS)
    padding = jnp.zeros((OFFSET_SPAN, WINDOWS, BINS), jnp.float32)
    padded_re = jnp.concatenate([white_re, padding], axis=0)
    padded_im = jnp.concatenate([white_im, padding], axis=0)
    position = jnp.arange(WINDOWS).astype(jnp.int32)
    ends = ((jnp.arange(N_TM) + 1) * WIN_DEV).astype(jnp.int32)
    delay = ends[:, None] - 1 - position[None, :]
    weights = jnp.where(delay >= 0, jnp.power(jnp.float32(0.99), jnp.maximum(delay, 0).astype(jnp.float32)), jnp.float32(0.0))

    def block(index):
        start = (index * CH_DEV).astype(jnp.int32)
        ext_re = lax.dynamic_slice_in_dim(padded_re, start, CH_DEV + OFFSET_SPAN, 0)
        ext_im = lax.dynamic_slice_in_dim(padded_im, start, CH_DEV + OFFSET_SPAN, 0)
        own_re = ext_re[:CH_DEV]
        own_im = ext_im[:CH_DEV]

        def one_pair(offset):
            part_re = lax.dynamic_slice_in_dim(ext_re, offset.astype(jnp.int32), CH_DEV, 0)
            part_im = lax.dynamic_slice_in_dim(ext_im, offset.astype(jnp.int32), CH_DEV, 0)
            cross_re = own_re * part_re + own_im * part_im
            cross_im = own_im * part_re - own_re * part_im
            stack_re = jnp.einsum('gw,cwf->gcf', weights, cross_re, precision=lax.Precision.HIGHEST)
            stack_im = jnp.einsum('gw,cwf->gcf', weights, cross_im, precision=lax.Precision.HIGHEST)
            return (stack_re, stack_im)
        stack_re, stack_im = jax.vmap(one_pair)(offsets)
        joined = jnp.concatenate([stack_re, stack_im], axis=-1).reshape(-1, 2 * BINS)
        corr = jnp.dot(joined, inverse, precision=lax.Precision.HIGHEST, preferred_element_type=jnp.float32)
        corr = corr * BINS ** (-0.5)
        corr = corr.reshape(PAIRS, N_TM, CH_DEV, SAMPLES).astype(jnp.bfloat16)
        return jnp.transpose(corr, (1, 0, 2, 3))
    result = lax.map(block, jnp.arange(blocks).astype(jnp.int32))
    return jnp.transpose(result, (1, 2, 0, 3, 4)).reshape(N_TM, PAIRS, CHANNELS, SAMPLES)
```

```python
import functools

import jax
import jax.numpy as jnp
import numpy as np
from jax import lax
from jax.experimental import pallas as pl
from jax.experimental.pallas import tpu as pltpu
from jax.sharding import PartitionSpec as P

OFFSET_SPAN = 32
LANES = 128
DECAY = 0.99
VMEM = 48 * 1024 * 1024


def dft_table(length):
    bins = length // 2
    rows = np.arange(length)
    freqs = np.arange(bins) + 1
    angle = np.mod(rows[:, None] * freqs[None, :], length) * (2.0 * np.pi / length)
    return np.concatenate([np.cos(angle), -np.sin(angle)], axis=1).astype(np.float32)


def whiten_kernel(chans, wins, span, x_ref, valid_ref, table_ref, white_ref, edge_ref, raw_ref):
    length = x_ref.shape[1]
    bins = length // 2
    tiles = bins // LANES
    raw = jnp.dot(x_ref[...], table_ref[...], preferred_element_type=jnp.float32)
    for t in range(2 * tiles):
        raw_ref[t] = raw[:, t * LANES : (t + 1) * LANES]
    owner = lax.broadcasted_iota(jnp.int32, (wins, wins * LANES), 0)
    column = lax.broadcasted_iota(jnp.int32, (wins, wins * LANES), 1) // LANES
    spread = (owner == column).astype(jnp.bfloat16)
    keep = lax.dot_general(
        valid_ref[...].astype(jnp.float32).astype(jnp.bfloat16),
        spread,
        (((0,), (0,)), ((), ())),
        preferred_element_type=jnp.float32,
    )
    for w in range(wins):
        part = [raw_ref[t, pl.ds(w, chans, stride=wins), :] for t in range(2 * tiles)]
        power = [part[t] * part[t] + part[tiles + t] * part[tiles + t] for t in range(tiles)]
        total = power[0]
        for t in range(1, tiles):
            total = total + power[t]
        level = jnp.sum(total, axis=-1, keepdims=True) * (0.01 / bins) + 1e-06
        alive = keep[:, w * LANES : (w + 1) * LANES]
        for t in range(tiles):
            scale = alive * lax.rsqrt(power[t] + level)
            for s in (t, tiles + t):
                value = part[s] * scale
                white_ref[w, s] = value
                edge_ref[w, s] = value[:span].astype(jnp.bfloat16)


def cross_kernel(first, rows, wins, span, offsets_ref, white_ref, edge_ref, *rest):
    out_ref, ext_ref = rest[-2:]
    chans = white_ref.shape[2]
    pairs = out_ref.shape[0]
    tiles = white_ref.shape[1] // 2
    if first + rows + span > chans:
        source, base = ext_ref, first
        own = chans - first
        ext_ref[:, :, :own, :] = white_ref[:, :, first:, :]
        ext_ref[:, :, own:, :] = edge_ref[...].astype(jnp.float32)
    else:
        source, base = white_ref, 0
    block = 16
    decay = [float(np.float32(DECAY) ** np.float32(wins - 1 - w)) for w in range(wins)]
    for c in range(0, rows, block):
        at = first - base + c
        for t in range(tiles):
            head_re = [source[w, t, at : at + block, :] * decay[w] for w in range(wins)]
            head_im = [source[w, tiles + t, at : at + block, :] * decay[w] for w in range(wins)]

            def one_pair(k, carry):
                start = offsets_ref[k] + at
                total_re = total_im = None
                for w in range(wins):
                    part_re = source[w, t, pl.ds(start, block), :]
                    part_im = source[w, tiles + t, pl.ds(start, block), :]
                    cross_re = head_re[w] * part_re + head_im[w] * part_im
                    cross_im = head_im[w] * part_re - head_re[w] * part_im
                    total_re = cross_re if w == 0 else total_re + cross_re
                    total_im = cross_im if w == 0 else total_im + cross_im
                where = pl.ds(first + c, block)
                out_ref[k, where, t * LANES : (t + 1) * LANES] = total_re.astype(out_ref.dtype)
                s = tiles + t
                out_ref[k, where, s * LANES : (s + 1) * LANES] = total_im.astype(out_ref.dtype)
                return carry

            lax.fori_loop(0, pairs, one_pair, 0)


def prefix_kernel(factor, got_ref, out_ref):
    groups = got_ref.shape[0]
    running = jnp.zeros(got_ref.shape[1:], jnp.float32)
    for g in range(groups):
        out_ref[g] = running.astype(out_ref.dtype)
        running = (running + got_ref[g].astype(jnp.float32)) * factor


def lag_kernel(scale, own_ref, before_ref, table_ref, out_ref):
    stack = own_ref[...].astype(jnp.float32) + before_ref[...].astype(jnp.float32)
    high = stack.astype(jnp.bfloat16)
    low = (stack - high.astype(jnp.float32)).astype(jnp.bfloat16)
    dims = (((1,), (1,)), ((), ()))
    table = table_ref[...]
    lagged = lax.dot_general(high, table, dims, preferred_element_type=jnp.float32)
    lagged = lagged + lax.dot_general(low, table, dims, preferred_element_type=jnp.float32)
    out_ref[...] = (lagged * scale).astype(out_ref.dtype)


def whole(memory=pltpu.VMEM):
    return pl.BlockSpec(memory_space=memory)


def per_device(samples, valid, offsets):
    chans, wins, length = samples.shape
    bins = length // 2
    span = OFFSET_SPAN
    pairs = offsets.shape[0]
    tiles = bins // LANES
    groups = lax.axis_size("tm")
    share = pairs * chans // groups
    factor = float(np.float32(DECAY) ** np.float32(wins))
    table = jnp.asarray(dft_table(length).astype(jnp.bfloat16))
    params = pltpu.CompilerParams(vmem_limit_bytes=VMEM)

    white, edge = pl.pallas_call(
        functools.partial(whiten_kernel, chans, wins, span),
        out_shape=(
            jax.ShapeDtypeStruct((wins, 2 * tiles, chans, LANES), jnp.float32),
            jax.ShapeDtypeStruct((wins, 2 * tiles, span, LANES), jnp.bfloat16),
        ),
        in_specs=[whole()] * 3,
        out_specs=(whole(), whole()),
        scratch_shapes=[pltpu.VMEM((2 * tiles, chans * wins, LANES), jnp.float32)],
        compiler_params=params,
        name="whiten",
    )(samples.reshape(chans * wins, length), valid.T, table)

    length_c = lax.axis_size("chan")
    edge = lax.ppermute(edge, "chan", [(i, i - 1) for i in range(1, length_c)])

    def cross(first, rows, *more):
        ext = chans - first + span
        return pl.pallas_call(
            functools.partial(cross_kernel, first, rows, wins, span),
            out_shape=jax.ShapeDtypeStruct((pairs, chans, length), jnp.bfloat16),
            in_specs=[whole(pltpu.SMEM)] + [whole()] * (1 + len(more)),
            out_specs=whole(),
            scratch_shapes=[pltpu.VMEM((wins, 2 * tiles, ext, LANES), jnp.float32)],
            compiler_params=params,
            name="cross",
        )(offsets, white, *more)

    local = cross(0, chans, edge)
    got = lax.all_to_all(
        local.reshape(groups, share, length), "tm", split_axis=0, concat_axis=0, tiled=True
    )
    before = pl.pallas_call(
        functools.partial(prefix_kernel, factor),
        out_shape=jax.ShapeDtypeStruct((groups, share, length), jnp.bfloat16),
        in_specs=[whole()],
        out_specs=whole(),
        compiler_params=params,
        name="prefix",
    )(got)
    before = lax.all_to_all(before, "tm", split_axis=0, concat_axis=0, tiled=True)
    result = pl.pallas_call(
        functools.partial(lag_kernel, bins**-0.5),
        out_shape=jax.ShapeDtypeStruct((pairs * chans, length), jnp.bfloat16),
        in_specs=[whole()] * 3,
        out_specs=whole(),
        compiler_params=params,
        name="lags",
    )(local.reshape(pairs * chans, length), before.reshape(pairs * chans, length), table)
    return result.reshape(1, pairs, chans, length)


def solution(mesh):
    in_specs = (P("chan", "tm", None), P("chan", "tm"), P())
    out_specs = P("tm", None, "chan", None)
    return jax.shard_map(
        per_device, mesh=mesh, in_specs=in_specs, out_specs=out_specs, check_vma=False
    )
```

```python
import functools

import jax
import jax.numpy as jnp
import numpy as np
from jax import lax
from jax.experimental import pallas as pl
from jax.experimental.pallas import tpu as pltpu
from jax.sharding import PartitionSpec as P

OFFSET_SPAN = 32
LANES = 128
DECAY = 0.99
VMEM = 48 * 1024 * 1024


def dft_table(length):
    bins = length // 2
    rows = np.arange(length)
    freqs = np.arange(bins) + 1
    angle = np.mod(rows[:, None] * freqs[None, :], length) * (2.0 * np.pi / length)
    return np.concatenate([np.cos(angle), -np.sin(angle)], axis=1).astype(np.float32)


def whiten_kernel(
    chans, wins, span, x_hbm, valid_hbm, table_hbm, white_ref, edge_ref, x_ref, valid_ref, table_ref, raw_ref, sems
):
    copies = [
        pltpu.make_async_copy(table_hbm, table_ref, sems.at[0]),
        pltpu.make_async_copy(x_hbm, x_ref, sems.at[1]),
        pltpu.make_async_copy(valid_hbm, valid_ref, sems.at[2]),
    ]
    for copy in copies:
        copy.start()
    for copy in copies:
        copy.wait()
    length = x_ref.shape[1]
    bins = length // 2
    tiles = bins // LANES
    raw = jnp.dot(x_ref[...], table_ref[...], preferred_element_type=jnp.float32)
    for t in range(2 * tiles):
        raw_ref[t] = raw[:, t * LANES : (t + 1) * LANES]
    owner = lax.broadcasted_iota(jnp.int32, (wins, wins * LANES), 0)
    column = lax.broadcasted_iota(jnp.int32, (wins, wins * LANES), 1) // LANES
    spread = (owner == column).astype(jnp.bfloat16)
    keep = lax.dot_general(
        valid_ref[...].astype(jnp.float32).astype(jnp.bfloat16),
        spread,
        (((0,), (0,)), ((), ())),
        preferred_element_type=jnp.float32,
    )
    for w in range(wins):
        part = [raw_ref[t, pl.ds(w, chans, stride=wins), :] for t in range(2 * tiles)]
        power = [part[t] * part[t] + part[tiles + t] * part[tiles + t] for t in range(tiles)]
        total = power[0]
        for t in range(1, tiles):
            total = total + power[t]
        level = jnp.sum(total, axis=-1, keepdims=True) * (0.01 / bins) + 1e-06
        alive = keep[:, w * LANES : (w + 1) * LANES]
        for t in range(tiles):
            scale = alive * lax.rsqrt(power[t] + level)
            for s in (t, tiles + t):
                value = part[s] * scale
                white_ref[w, s] = value
                edge_ref[w, s] = value[:span].astype(jnp.bfloat16)


def cross_kernel(first, rows, wins, span, offsets_ref, white_ref, *rest):
    out_ref = rest[-1] if len(rest) == 1 else rest[1]
    chans = white_ref.shape[2]
    pairs = out_ref.shape[0]
    tiles = white_ref.shape[1] // 2
    if first + rows + span > chans:
        edge_ref, _, ext_ref = rest
        source, base = ext_ref, first
        own = chans - first
        ext_ref[:, :, :own, :] = white_ref[:, :, first:, :]
        ext_ref[:, :, own:, :] = edge_ref[...].astype(jnp.float32)
    else:
        source, base = white_ref, 0
    block = 16
    decay = [float(np.float32(DECAY) ** np.float32(wins - 1 - w)) for w in range(wins)]
    for c in range(0, rows, block):
        at = first - base + c
        for t in range(tiles):
            head_re = [source[w, t, at : at + block, :] * decay[w] for w in range(wins)]
            head_im = [source[w, tiles + t, at : at + block, :] * decay[w] for w in range(wins)]

            def one_pair(k, carry):
                start = offsets_ref[k] + at
                total_re = total_im = None
                for w in range(wins):
                    part_re = source[w, t, pl.ds(start, block), :]
                    part_im = source[w, tiles + t, pl.ds(start, block), :]
                    cross_re = head_re[w] * part_re + head_im[w] * part_im
                    cross_im = head_im[w] * part_re - head_re[w] * part_im
                    total_re = cross_re if w == 0 else total_re + cross_re
                    total_im = cross_im if w == 0 else total_im + cross_im
                where = pl.ds(c, block)
                out_ref[k, where, t * LANES : (t + 1) * LANES] = total_re.astype(out_ref.dtype)
                s = tiles + t
                out_ref[k, where, s * LANES : (s + 1) * LANES] = total_im.astype(out_ref.dtype)
                return carry

            lax.fori_loop(0, pairs, one_pair, 0)


def prefix_kernel(factor, got_ref, out_ref):
    groups = got_ref.shape[0]
    running = jnp.zeros(got_ref.shape[1:], jnp.float32)
    for g in range(groups):
        out_ref[g] = running.astype(out_ref.dtype)
        running = (running + got_ref[g].astype(jnp.float32)) * factor


def lag_kernel(scale, own_ref, before_ref, table_ref, *rest):
    out_ref = rest[-1]
    pairs, rows, length = own_ref.shape
    stack = own_ref[...].astype(jnp.float32) + before_ref[...].astype(jnp.float32)
    stack = stack.reshape(pairs * rows, length)
    high = stack.astype(jnp.bfloat16)
    low = (stack - high.astype(jnp.float32)).astype(jnp.bfloat16)
    dims = (((1,), (1,)), ((), ()))
    table = table_ref[...]
    lagged = lax.dot_general(high, table, dims, preferred_element_type=jnp.float32)
    lagged = lagged + lax.dot_general(low, table, dims, preferred_element_type=jnp.float32)
    out_ref[...] = (lagged * scale).astype(out_ref.dtype).reshape(pairs, rows, length)


def cost(flops, moved):
    return pl.CostEstimate(flops=flops, bytes_accessed=moved, transcendentals=0)


def whole(memory=pltpu.VMEM):
    return pl.BlockSpec(memory_space=memory)


def per_device(samples, valid, offsets):
    chans, wins, length = samples.shape
    bins = length // 2
    span = OFFSET_SPAN
    pairs = offsets.shape[0]
    tiles = bins // LANES
    groups = lax.axis_size("tm")
    share = pairs * chans // groups
    factor = float(np.float32(DECAY) ** np.float32(wins))
    table = jnp.asarray(dft_table(length).astype(jnp.bfloat16))
    params = pltpu.CompilerParams(vmem_limit_bytes=VMEM)

    white, edge = pl.pallas_call(
        functools.partial(whiten_kernel, chans, wins, span),
        out_shape=(
            jax.ShapeDtypeStruct((wins, 2 * tiles, chans, LANES), jnp.float32),
            jax.ShapeDtypeStruct((wins, 2 * tiles, span, LANES), jnp.bfloat16),
        ),
        in_specs=[whole(pl.ANY)] * 3,
        out_specs=(whole(), whole()),
        scratch_shapes=[
            pltpu.VMEM((chans * wins, length), jnp.bfloat16),
            pltpu.VMEM((wins, chans), jnp.int32),
            pltpu.VMEM((length, 2 * bins), jnp.bfloat16),
            pltpu.VMEM((2 * tiles, chans * wins, LANES), jnp.float32),
            pltpu.SemaphoreType.DMA((3,)),
        ],
        cost_estimate=cost(chans * wins * length * length * 2, 2 * 1024 * 1024),
        compiler_params=params,
        name="whiten",
    )(samples.reshape(chans * wins, length), valid.T, table)

    length_c = lax.axis_size("chan")
    edge = lax.ppermute(edge, "chan", [(i, i - 1) for i in range(1, length_c)])

    def cross(first, rows, *more):
        shape = (wins, 2 * tiles, chans - first + span, LANES)
        return pl.pallas_call(
            functools.partial(cross_kernel, first, rows, wins, span),
            out_shape=jax.ShapeDtypeStruct((pairs, rows, length), jnp.bfloat16),
            in_specs=[whole(pltpu.SMEM)] + [whole()] * (1 + len(more)),
            out_specs=whole(),
            scratch_shapes=[pltpu.VMEM(shape, jnp.float32)] * len(more),
            compiler_params=params,
            cost_estimate=cost(pairs * rows * wins * bins * 8, 4 * 1024 * 1024),
            name="cross",
        )(offsets, white, *more)

    def prefix(got):
        return pl.pallas_call(
            functools.partial(prefix_kernel, factor),
            out_shape=jax.ShapeDtypeStruct(got.shape, jnp.bfloat16),
            in_specs=[whole()],
            out_specs=whole(),
            compiler_params=params,
            cost_estimate=cost(got.size * 4, 1024 * 1024),
            name="prefix",
        )(got)

    def lags(at, rows, local, before, *so_far):
        spec = pl.BlockSpec((pairs, rows, length), lambda i: (0, at // rows, 0))
        return pl.pallas_call(
            functools.partial(lag_kernel, bins**-0.5),
            grid=(1,),
            out_shape=jax.ShapeDtypeStruct((pairs, chans, length), jnp.bfloat16),
            in_specs=[whole()] * 3 + [whole(pl.ANY)] * len(so_far),
            out_specs=spec,
            input_output_aliases={3: 0} if so_far else {},
            compiler_params=params,
            cost_estimate=cost(local.size * length * 4, 2 * 1024 * 1024),
            name="lags",
        )(local, before, table, *so_far)

    def exchange(value):
        parts = value.reshape(groups, -1, length)
        parts = lax.all_to_all(parts, "tm", split_axis=0, concat_axis=0, tiled=True)
        return parts

    half = chans - span
    local_a = cross(0, half)
    got_a = exchange(local_a)
    local_b = cross(half, chans - half, edge)
    got_b = exchange(local_b)
    before_a = exchange(prefix(got_a))
    before_b = exchange(prefix(got_b))
    result = lags(0, half, local_a, before_a.reshape(local_a.shape))
    result = lags(half, chans - half, local_b, before_b.reshape(local_b.shape), result)
    return result.reshape(1, pairs, chans, length)


def solution(mesh):
    in_specs = (P("chan", "tm", None), P("chan", "tm"), P())
    out_specs = P("tm", None, "chan", None)
    return jax.shard_map(
        per_device, mesh=mesh, in_specs=in_specs, out_specs=out_specs, check_vma=False
    )
```

```python
import functools

import jax
import jax.numpy as jnp
import numpy as np
from jax import lax
from jax.experimental import pallas as pl
from jax.experimental.pallas import tpu as pltpu
from jax.sharding import PartitionSpec as P

OFFSET_SPAN = 32
LANES = 128
DECAY = 0.99
VMEM = 24 * 1024 * 1024


def dft_table(length):
    bins = length // 2
    rows = np.arange(length)
    freqs = np.arange(bins) + 1
    angle = np.mod(rows[:, None] * freqs[None, :], length) * (2.0 * np.pi / length)
    return np.concatenate([np.cos(angle), -np.sin(angle)], axis=1).astype(np.float32)


def whiten_kernel(
    chans, wins, span, x_hbm, valid_hbm, table_hbm, white_ref, edge_ref, x_ref, valid_ref, table_ref, raw_ref, sems
):
    copies = [
        pltpu.make_async_copy(table_hbm, table_ref, sems.at[0]),
        pltpu.make_async_copy(x_hbm, x_ref, sems.at[1]),
        pltpu.make_async_copy(valid_hbm, valid_ref, sems.at[2]),
    ]
    for copy in copies:
        copy.start()
    for copy in copies:
        copy.wait()
    length = x_ref.shape[1]
    bins = length // 2
    tiles = bins // LANES
    raw = jnp.dot(x_ref[...], table_ref[...], preferred_element_type=jnp.float32)
    for t in range(2 * tiles):
        raw_ref[t] = raw[:, t * LANES : (t + 1) * LANES]
    owner = lax.broadcasted_iota(jnp.int32, (wins, wins * LANES), 0)
    column = lax.broadcasted_iota(jnp.int32, (wins, wins * LANES), 1) // LANES
    spread = (owner == column).astype(jnp.bfloat16)
    keep = lax.dot_general(
        valid_ref[...].astype(jnp.float32).astype(jnp.bfloat16),
        spread,
        (((0,), (0,)), ((), ())),
        preferred_element_type=jnp.float32,
    )
    for w in range(wins):
        part = [raw_ref[t, pl.ds(w, chans, stride=wins), :] for t in range(2 * tiles)]
        power = [part[t] * part[t] + part[tiles + t] * part[tiles + t] for t in range(tiles)]
        total = power[0]
        for t in range(1, tiles):
            total = total + power[t]
        level = jnp.sum(total, axis=-1, keepdims=True) * (0.01 / bins) + 1e-06
        alive = keep[:, w * LANES : (w + 1) * LANES]
        for t in range(tiles):
            scale = alive * lax.rsqrt(power[t] + level)
            for s in (t, tiles + t):
                value = part[s] * scale
                white_ref[w, s] = value
                edge_ref[w, s] = value[:span].astype(jnp.bfloat16)


def cross_kernel(first, rows, wins, span, offsets_ref, white_ref, *rest):
    out_ref = rest[-1] if len(rest) == 1 else rest[1]
    chans = white_ref.shape[2]
    pairs = out_ref.shape[0]
    tiles = white_ref.shape[1] // 2
    if first + rows + span > chans:
        edge_ref, _, ext_ref = rest
        source, base = ext_ref, first
        own = chans - first
        ext_ref[:, :, :own, :] = white_ref[:, :, first:, :]
        ext_ref[:, :, own:, :] = edge_ref[...].astype(jnp.float32)
    else:
        source, base = white_ref, 0
    block = 16
    decay = [float(np.float32(DECAY) ** np.float32(wins - 1 - w)) for w in range(wins)]
    for c in range(0, rows, block):
        at = first - base + c
        for t in range(tiles):
            head_re = [source[w, t, at : at + block, :] * decay[w] for w in range(wins)]
            head_im = [source[w, tiles + t, at : at + block, :] * decay[w] for w in range(wins)]

            def one_pair(k, carry):
                start = offsets_ref[k] + at
                total_re = total_im = None
                for w in range(wins):
                    part_re = source[w, t, pl.ds(start, block), :]
                    part_im = source[w, tiles + t, pl.ds(start, block), :]
                    cross_re = head_re[w] * part_re + head_im[w] * part_im
                    cross_im = head_im[w] * part_re - head_re[w] * part_im
                    total_re = cross_re if w == 0 else total_re + cross_re
                    total_im = cross_im if w == 0 else total_im + cross_im
                where = pl.ds(c, block)
                out_ref[k, where, t * LANES : (t + 1) * LANES] = total_re.astype(out_ref.dtype)
                s = tiles + t
                out_ref[k, where, s * LANES : (s + 1) * LANES] = total_im.astype(out_ref.dtype)
                return carry

            lax.fori_loop(0, pairs, one_pair, 0)


def lag_kernel(scale, factor, got_ref, table_ref, *rest):
    out_ref = rest[-1]
    groups, pairs, rows, length = got_ref.shape
    mine = lax.axis_index("tm")
    stack = None
    for h in range(groups):
        weight = jnp.float32(0.0)
        for lag in range(groups - h):
            weight = jnp.where(mine - h == lag, jnp.float32(factor**lag), weight)
        term = got_ref[h].astype(jnp.float32) * weight
        stack = term if h == 0 else stack + term
    stack = stack.reshape(pairs * rows, length)
    high = stack.astype(jnp.bfloat16)
    low = (stack - high.astype(jnp.float32)).astype(jnp.bfloat16)
    dims = (((1,), (1,)), ((), ()))
    table = table_ref[...]
    lagged = lax.dot_general(high, table, dims, preferred_element_type=jnp.float32)
    lagged = lagged + lax.dot_general(low, table, dims, preferred_element_type=jnp.float32)
    out_ref[...] = (lagged * scale).astype(out_ref.dtype).reshape(pairs, rows, length)


def cost(flops, moved):
    return pl.CostEstimate(flops=flops, bytes_accessed=moved, transcendentals=0)


def whole(memory=pltpu.VMEM):
    return pl.BlockSpec(memory_space=memory)


def per_device(samples, valid, offsets):
    chans, wins, length = samples.shape
    bins = length // 2
    span = OFFSET_SPAN
    pairs = offsets.shape[0]
    tiles = bins // LANES
    groups = lax.axis_size("tm")
    factor = float(np.float32(DECAY) ** np.float32(wins))
    table = jnp.asarray(dft_table(length).astype(jnp.bfloat16))
    params = pltpu.CompilerParams(vmem_limit_bytes=VMEM)

    white, edge = pl.pallas_call(
        functools.partial(whiten_kernel, chans, wins, span),
        out_shape=(
            jax.ShapeDtypeStruct((wins, 2 * tiles, chans, LANES), jnp.float32),
            jax.ShapeDtypeStruct((wins, 2 * tiles, span, LANES), jnp.bfloat16),
        ),
        in_specs=[whole(pltpu.HBM)] * 3,
        out_specs=(whole(), whole()),
        scratch_shapes=[
            pltpu.VMEM((chans * wins, length), jnp.bfloat16),
            pltpu.VMEM((wins, chans), jnp.int32),
            pltpu.VMEM((length, 2 * bins), jnp.bfloat16),
            pltpu.VMEM((2 * tiles, chans * wins, LANES), jnp.float32),
            pltpu.SemaphoreType.DMA((3,)),
        ],
        cost_estimate=cost(chans * wins * length * length * 2, 2 * 1024 * 1024),
        compiler_params=params,
        name="whiten",
    )(samples.reshape(chans * wins, length), valid.T, table)

    length_c = lax.axis_size("chan")
    edge = lax.ppermute(edge, "chan", [(i, i - 1) for i in range(1, length_c)])

    def cross(first, rows, *more):
        shape = (wins, 2 * tiles, chans - first + span, LANES)
        return pl.pallas_call(
            functools.partial(cross_kernel, first, rows, wins, span),
            out_shape=jax.ShapeDtypeStruct((pairs, rows, length), jnp.bfloat16),
            in_specs=[whole(pltpu.SMEM)] + [whole()] * (1 + len(more)),
            out_specs=whole(),
            scratch_shapes=[pltpu.VMEM(shape, jnp.float32)] * len(more),
            compiler_params=params,
            cost_estimate=cost(pairs * rows * wins * bins * 8, 4 * 1024 * 1024),
            name="cross",
        )(offsets, white, *more)

    def lags(at, rows, got, *so_far):
        step = 4
        return pl.pallas_call(
            functools.partial(lag_kernel, bins**-0.5, factor),
            grid=(pairs // step,),
            out_shape=jax.ShapeDtypeStruct((pairs, chans, length), jnp.bfloat16),
            in_specs=[
                pl.BlockSpec((groups, step, rows, length), lambda i: (0, i, 0, 0)),
                whole(),
            ]
            + [whole(pl.ANY)] * len(so_far),
            out_specs=pl.BlockSpec((step, rows, length), lambda i: (i, at // rows, 0)),
            input_output_aliases={2: 0} if so_far else {},
            compiler_params=params,
            cost_estimate=cost(pairs * rows * length * length * 4, 3 * 1024 * 1024),
            name="lags",
        )(got, table, *so_far)

    half = chans - span
    got_a = lax.all_gather(cross(0, half), "tm")
    got_b = lax.all_gather(cross(half, chans - half, edge), "tm")
    result = lags(0, half, got_a)
    result = lags(half, chans - half, got_b, result)
    return result.reshape(1, pairs, chans, length)


def solution(mesh):
    in_specs = (P("chan", "tm", None), P("chan", "tm"), P())
    out_specs = P("tm", None, "chan", None)
    return jax.shard_map(
        per_device, mesh=mesh, in_specs=in_specs, out_specs=out_specs, check_vma=False
    )
```

```python
import functools

import jax
import jax.numpy as jnp
import numpy as np
from jax import lax
from jax.experimental import pallas as pl
from jax.experimental.pallas import tpu as pltpu
from jax.sharding import PartitionSpec as P

OFFSET_SPAN = 32
LANES = 128
DECAY = 0.99
VMEM = 16 * 1024 * 1024


def dft_table(length):
    bins = length // 2
    rows = np.arange(length)
    freqs = np.arange(bins) + 1
    angle = np.mod(rows[:, None] * freqs[None, :], length) * (2.0 * np.pi / length)
    return np.concatenate([np.cos(angle), -np.sin(angle)], axis=1).astype(np.float32)


def whiten_kernel(
    chans, wins, span, x_hbm, valid_hbm, table_hbm, white_ref, edge_ref, x_ref, valid_ref, table_ref, raw_ref, sems
):
    copies = [
        pltpu.make_async_copy(table_hbm, table_ref, sems.at[0]),
        pltpu.make_async_copy(x_hbm, x_ref, sems.at[1]),
        pltpu.make_async_copy(valid_hbm, valid_ref, sems.at[2]),
    ]
    for copy in copies:
        copy.start()
    for copy in copies:
        copy.wait()
    length = x_ref.shape[1]
    bins = length // 2
    tiles = bins // LANES
    raw = jnp.dot(x_ref[...], table_ref[...], preferred_element_type=jnp.float32)
    for t in range(2 * tiles):
        raw_ref[t] = raw[:, t * LANES : (t + 1) * LANES]
    owner = lax.broadcasted_iota(jnp.int32, (wins, wins * LANES), 0)
    column = lax.broadcasted_iota(jnp.int32, (wins, wins * LANES), 1) // LANES
    spread = (owner == column).astype(jnp.bfloat16)
    keep = lax.dot_general(
        valid_ref[...].astype(jnp.float32).astype(jnp.bfloat16),
        spread,
        (((0,), (0,)), ((), ())),
        preferred_element_type=jnp.float32,
    )
    for w in range(wins):
        part = [raw_ref[t, pl.ds(w, chans, stride=wins), :] for t in range(2 * tiles)]
        power = [part[t] * part[t] + part[tiles + t] * part[tiles + t] for t in range(tiles)]
        total = power[0]
        for t in range(1, tiles):
            total = total + power[t]
        level = jnp.sum(total, axis=-1, keepdims=True) * (0.01 / bins) + 1e-06
        alive = keep[:, w * LANES : (w + 1) * LANES]
        for t in range(tiles):
            scale = alive * lax.rsqrt(power[t] + level)
            for s in (t, tiles + t):
                value = part[s] * scale
                white_ref[w, s] = value
                edge_ref[w, s] = value[:span].astype(jnp.bfloat16)


def cross_kernel(first, rows, wins, span, offsets_ref, white_ref, *rest):
    out_ref = rest[-1] if len(rest) == 1 else rest[1]
    chans = white_ref.shape[2]
    pairs = out_ref.shape[0]
    tiles = white_ref.shape[1] // 2
    if first + rows + span > chans:
        edge_ref, _, ext_ref = rest
        source, base = ext_ref, first
        own = chans - first
        ext_ref[:, :, :own, :] = white_ref[:, :, first:, :]
        ext_ref[:, :, own:, :] = edge_ref[...].astype(jnp.float32)
    else:
        source, base = white_ref, 0
    block = 16
    decay = [float(np.float32(DECAY) ** np.float32(wins - 1 - w)) for w in range(wins)]
    for c in range(0, rows, block):
        at = first - base + c
        for t in range(tiles):
            head_re = [source[w, t, at : at + block, :] * decay[w] for w in range(wins)]
            head_im = [source[w, tiles + t, at : at + block, :] * decay[w] for w in range(wins)]

            def one_pair(k, carry):
                start = offsets_ref[k] + at
                total_re = total_im = None
                for w in range(wins):
                    part_re = source[w, t, pl.ds(start, block), :]
                    part_im = source[w, tiles + t, pl.ds(start, block), :]
                    cross_re = head_re[w] * part_re + head_im[w] * part_im
                    cross_im = head_im[w] * part_re - head_re[w] * part_im
                    total_re = cross_re if w == 0 else total_re + cross_re
                    total_im = cross_im if w == 0 else total_im + cross_im
                where = pl.ds(c, block)
                out_ref[k, where, t * LANES : (t + 1) * LANES] = total_re.astype(out_ref.dtype)
                s = tiles + t
                out_ref[k, where, s * LANES : (s + 1) * LANES] = total_im.astype(out_ref.dtype)
                return carry

            lax.fori_loop(0, pairs, one_pair, 0)


def lag_kernel(scale, weights, aliased, table_ref, *rest):
    terms = rest[: len(weights)]
    out_ref = rest[-1]
    pairs, rows, length = out_ref.shape
    stack = terms[0][...].astype(jnp.float32)
    for weight, term in zip(weights[1:], terms[1:]):
        stack = stack + term[...].astype(jnp.float32) * weight
    stack = stack.reshape(pairs * rows, length)
    high = stack.astype(jnp.bfloat16)
    low = (stack - high.astype(jnp.float32)).astype(jnp.bfloat16)
    dims = (((1,), (1,)), ((), ()))
    table = table_ref[...]
    lagged = lax.dot_general(high, table, dims, preferred_element_type=jnp.float32)
    lagged = lagged + lax.dot_general(low, table, dims, preferred_element_type=jnp.float32)
    out_ref[...] = (lagged * scale).astype(out_ref.dtype).reshape(pairs, rows, length)


def cost(flops, moved):
    return pl.CostEstimate(flops=flops, bytes_accessed=moved, transcendentals=0)


def whole(memory=pltpu.VMEM):
    return pl.BlockSpec(memory_space=memory)


def per_device(samples, valid, offsets):
    chans, wins, length = samples.shape
    bins = length // 2
    span = OFFSET_SPAN
    pairs = offsets.shape[0]
    tiles = bins // LANES
    groups = lax.axis_size("tm")
    factor = float(np.float32(DECAY) ** np.float32(wins))
    table = jnp.asarray(dft_table(length).astype(jnp.bfloat16))
    params = pltpu.CompilerParams(vmem_limit_bytes=VMEM)

    white, edge = pl.pallas_call(
        functools.partial(whiten_kernel, chans, wins, span),
        out_shape=(
            jax.ShapeDtypeStruct((wins, 2 * tiles, chans, LANES), jnp.float32),
            jax.ShapeDtypeStruct((wins, 2 * tiles, span, LANES), jnp.bfloat16),
        ),
        in_specs=[whole(pltpu.HBM)] * 3,
        out_specs=(whole(), whole()),
        scratch_shapes=[
            pltpu.VMEM((chans * wins, length), jnp.bfloat16),
            pltpu.VMEM((wins, chans), jnp.int32),
            pltpu.VMEM((length, 2 * bins), jnp.bfloat16),
            pltpu.VMEM((2 * tiles, chans * wins, LANES), jnp.float32),
            pltpu.SemaphoreType.DMA((3,)),
        ],
        cost_estimate=cost(chans * wins * length * length * 2, 2 * 1024 * 1024),
        compiler_params=params,
        name="whiten",
    )(samples.reshape(chans * wins, length), valid.T, table)

    length_c = lax.axis_size("chan")
    edge = lax.ppermute(edge, "chan", [(i, i - 1) for i in range(1, length_c)])

    def cross(first, rows, *more):
        shape = (wins, 2 * tiles, chans - first + span, LANES)
        return pl.pallas_call(
            functools.partial(cross_kernel, first, rows, wins, span),
            out_shape=jax.ShapeDtypeStruct((pairs, rows, length), jnp.bfloat16),
            in_specs=[whole(pltpu.SMEM)] + [whole()] * (1 + len(more)),
            out_specs=whole(),
            scratch_shapes=[pltpu.VMEM(shape, jnp.float32)] * len(more),
            compiler_params=params,
            cost_estimate=cost(pairs * rows * wins * bins * 8, 4 * 1024 * 1024),
            name="cross",
        )(offsets, white, *more)

    def lags(at, terms, *so_far):
        rows = terms[0].shape[1]
        step = 4
        return pl.pallas_call(
            functools.partial(lag_kernel, bins**-0.5, weights, bool(so_far)),
            grid=(pairs // step,),
            out_shape=jax.ShapeDtypeStruct((pairs, chans, length), jnp.bfloat16),
            in_specs=[whole()]
            + [pl.BlockSpec((step, rows, length), lambda i: (i, 0, 0))] * groups
            + [whole(pl.ANY)] * len(so_far),
            out_specs=pl.BlockSpec((step, rows, length), lambda i: (i, at // rows, 0)),
            input_output_aliases={1 + groups: 0} if so_far else {},
            compiler_params=params,
            cost_estimate=cost(pairs * rows * length * length * 4, 3 * 1024 * 1024),
            name="lags",
        )(table, *terms, *so_far)

    weights = [float(np.float32(factor) ** np.float32(d)) for d in range(groups)]

    def earlier(local):
        shifted = [
            lax.ppermute(local, "tm", [(h, h + d) for h in range(groups - d)])
            for d in range(1, groups)
        ]
        return [local] + shifted

    half = chans - span
    terms_a = earlier(cross(0, half))
    terms_b = earlier(cross(half, chans - half, edge))
    result = lags(0, terms_a)
    result = lags(half, terms_b, result)
    return result.reshape(1, pairs, chans, length)


def solution(mesh):
    in_specs = (P("chan", "tm", None), P("chan", "tm"), P())
    out_specs = P("tm", None, "chan", None)
    return jax.shard_map(
        per_device, mesh=mesh, in_specs=in_specs, out_specs=out_specs, check_vma=False
    )
```

```python
import functools
import math

import jax
import jax.numpy as jnp
import numpy as np
from jax import lax
from jax.experimental import pallas as pl
from jax.experimental.pallas import tpu as pltpu
from jax.sharding import PartitionSpec as P

OFFSET_SPAN = 32
LANES = 128
DECAY = 0.99
VMEM = 16 * 1024 * 1024


def turns(number, length):
    part = (number - length * jnp.floor(number / length + 0.5)) * (1.0 / length)
    square = part * part
    cosine, sine = jnp.float32(0.0), jnp.float32(0.0)
    for k in range(10, -1, -1):
        cosine = cosine * square + (-1) ** k * (2 * math.pi) ** (2 * k) / math.factorial(2 * k)
        sine = sine * square + (-1) ** k * (2 * math.pi) ** (2 * k + 1) / math.factorial(2 * k + 1)
    return cosine, sine * part


def table_kernel(coarse_step, table_ref):
    length = table_ref.shape[0]
    bins = length // 2

    def small(rows, step):
        row = lax.broadcasted_iota(jnp.int32, (rows, bins), 0)
        freq = lax.broadcasted_iota(jnp.int32, (rows, bins), 1) + 1
        return turns((row * (step * freq)).astype(jnp.float32), length)

    coarse_cos, coarse_sin = small(length // coarse_step, coarse_step)
    fine_cos, fine_sin = small(coarse_step, 1)
    for i in range(length // coarse_step):
        rows = slice(i * coarse_step, (i + 1) * coarse_step)
        cos_i, sin_i = coarse_cos[i : i + 1], coarse_sin[i : i + 1]
        table_ref[rows, :bins] = (cos_i * fine_cos - sin_i * fine_sin).astype(jnp.bfloat16)
        table_ref[rows, bins:] = -(sin_i * fine_cos + cos_i * fine_sin).astype(jnp.bfloat16)


def whiten_kernel(chans, wins, span, x_ref, valid_ref, table_ref, white_ref, edge_ref, raw_ref):
    length = x_ref.shape[1]
    bins = length // 2
    tiles = bins // LANES
    raw = jnp.dot(x_ref[...], table_ref[...], preferred_element_type=jnp.float32)
    for t in range(2 * tiles):
        raw_ref[t] = raw[:, t * LANES : (t + 1) * LANES]
    owner = lax.broadcasted_iota(jnp.int32, (wins, wins * LANES), 0)
    column = lax.broadcasted_iota(jnp.int32, (wins, wins * LANES), 1) // LANES
    spread = (owner == column).astype(jnp.bfloat16)
    keep = lax.dot_general(
        valid_ref[...].astype(jnp.float32).astype(jnp.bfloat16),
        spread,
        (((0,), (0,)), ((), ())),
        preferred_element_type=jnp.float32,
    )
    for w in range(wins):
        part = [raw_ref[t, pl.ds(w, chans, stride=wins), :] for t in range(2 * tiles)]
        power = [part[t] * part[t] + part[tiles + t] * part[tiles + t] for t in range(tiles)]
        total = power[0]
        for t in range(1, tiles):
            total = total + power[t]
        level = jnp.sum(total, axis=-1, keepdims=True) * (0.01 / bins) + 1e-06
        alive = keep[:, w * LANES : (w + 1) * LANES]
        for t in range(tiles):
            scale = alive * lax.rsqrt(power[t] + level)
            for s in (t, tiles + t):
                value = part[s] * scale
                white_ref[w, s] = value
                edge_ref[w, s] = value[:span].astype(jnp.bfloat16)


def cross_kernel(first, rows, counts, wins, offsets_ref, white_ref, *rest):
    chans = white_ref.shape[2]
    tiles = white_ref.shape[1] // 2
    if len(rest) > len(counts):
        edge_ref, ext_ref = rest[0], rest[-1]
        outs = rest[1:-1]
        source, at_first = ext_ref, 0
        own = chans - first
        ext_ref[:, :, :own, :] = white_ref[:, :, first:, :]
        ext_ref[:, :, own:, :] = edge_ref[...].astype(jnp.float32)
    else:
        outs = rest
        source, at_first = white_ref, first
    block = 16
    decay = [float(np.float32(DECAY) ** np.float32(wins - 1 - w)) for w in range(wins)]
    for c in range(0, rows, block):
        at = at_first + c
        for t in range(tiles):
            head_re = [source[w, t, at : at + block, :] * decay[w] for w in range(wins)]
            head_im = [source[w, tiles + t, at : at + block, :] * decay[w] for w in range(wins)]
            past = 0
            for out_ref, count in zip(outs, counts):

                def one_pair(k, carry, out_ref=out_ref, past=past):
                    start = offsets_ref[past + k] + at
                    total_re = total_im = None
                    for w in range(wins):
                        part_re = source[w, t, pl.ds(start, block), :]
                        part_im = source[w, tiles + t, pl.ds(start, block), :]
                        cross_re = head_re[w] * part_re + head_im[w] * part_im
                        cross_im = head_im[w] * part_re - head_re[w] * part_im
                        total_re = cross_re if w == 0 else total_re + cross_re
                        total_im = cross_im if w == 0 else total_im + cross_im
                    for s, total in ((t, total_re), (tiles + t, total_im)):
                        lanes = slice(s * LANES, (s + 1) * LANES)
                        out_ref[k, c : c + block, lanes] = total.astype(out_ref.dtype)
                    return carry

                lax.fori_loop(0, count, one_pair, 0)
                past += count


def chosen(options, place):
    value = jnp.float32(options[0])
    for i, option in enumerate(options[1:]):
        value = jnp.where(place == i + 1, jnp.float32(option), value)
    return value


def weighted(terms, weights, place):
    total = None
    for term, options in zip(terms, weights):
        value = term[...].astype(jnp.float32)
        if set(options) != {1.0}:
            value = value * (options[0] if len(set(options)) == 1 else chosen(options, place))
        total = value if total is None else total + value
    return total


def mix_kernel(columns, weights, *refs):
    place = lax.rem(lax.axis_index("tm"), columns)
    count = len(weights[0])
    for out_ref, own in zip(refs[-len(weights) :], weights):
        out_ref[...] = weighted(refs[:count], own, place).astype(out_ref.dtype)


def lag_kernel(scale, columns, place_at, counts, weights, table_ref, *rest):
    first_pair, first = place_at
    terms = sum(counts)
    stage_ref, sems, out_hbm = rest[-2], rest[-1], rest[-3]
    place = lax.rem(lax.axis_index("tm"), columns)
    dims = (((1,), (1,)), ((), ()))
    table = table_ref[...]
    copies = []
    at = 0
    pair = 0
    for group, (count, own) in enumerate(zip(counts, weights)):
        refs = rest[at : at + count]
        pairs, rows, length = refs[0].shape
        stack = weighted(refs, own, place).reshape(pairs * rows, length)
        high = stack.astype(jnp.bfloat16)
        low = (stack - high.astype(jnp.float32)).astype(jnp.bfloat16)
        lagged = lax.dot_general(high, table, dims, preferred_element_type=jnp.float32)
        lagged = lagged + lax.dot_general(low, table, dims, preferred_element_type=jnp.float32)
        here = stage_ref.at[pl.ds(pair, pairs)]
        here[...] = (lagged * scale).astype(stage_ref.dtype).reshape(pairs, rows, length)
        there = out_hbm.at[pl.ds(first_pair + pair, pairs), pl.ds(first, rows)]
        copies.append(pltpu.make_async_copy(here, there, sems.at[group]))
        copies[-1].start()
        at += count
        pair += pairs
    for copy in copies:
        copy.wait()


def cost(flops, moved):
    return pl.CostEstimate(flops=flops, bytes_accessed=moved, transcendentals=0)


def whole(memory=pltpu.VMEM):
    return pl.BlockSpec(memory_space=memory)


def per_device(samples, valid, offsets):
    chans, wins, length = samples.shape
    bins = length // 2
    span = OFFSET_SPAN
    pairs = offsets.shape[0]
    tiles = bins // LANES
    groups = lax.axis_size("tm")
    factor = float(np.float32(DECAY) ** np.float32(wins))
    params = pltpu.CompilerParams(vmem_limit_bytes=VMEM)

    table = pl.pallas_call(
        functools.partial(table_kernel, 16),
        out_shape=jax.ShapeDtypeStruct((length, 2 * bins), jnp.bfloat16),
        out_specs=whole(),
        compiler_params=params,
        cost_estimate=cost(length * bins * 32, 512 * 1024),
        name="table",
    )()

    white, edge = pl.pallas_call(
        functools.partial(whiten_kernel, chans, wins, span),
        out_shape=(
            jax.ShapeDtypeStruct((wins, 2 * tiles, chans, LANES), jnp.float32),
            jax.ShapeDtypeStruct((wins, 2 * tiles, span, LANES), jnp.bfloat16),
        ),
        in_specs=[whole()] * 3,
        out_specs=(whole(), whole()),
        scratch_shapes=[pltpu.VMEM((2 * tiles, chans * wins, LANES), jnp.float32)],
        compiler_params=params,
        cost_estimate=cost(chans * wins * length * length * 2, 2 * 1024 * 1024),
        name="whiten",
    )(samples.reshape(chans * wins, length), valid.T, table)

    ring = lax.axis_size("chan")
    edge = lax.ppermute(edge, "chan", [(i, i - 1) for i in range(1, ring)])

    def cross(first, rows, counts, *more):
        shape = (wins, 2 * tiles, chans - first + span, LANES)
        return pl.pallas_call(
            functools.partial(cross_kernel, first, rows, counts, wins),
            out_shape=[jax.ShapeDtypeStruct((n, rows, length), jnp.bfloat16) for n in counts],
            in_specs=[whole(pltpu.SMEM)] + [whole()] * (1 + len(more)),
            out_specs=[whole()] * len(counts),
            scratch_shapes=[pltpu.VMEM(shape, jnp.float32)] * len(more),
            compiler_params=params,
            cost_estimate=cost(sum(counts) * rows * wins * bins * 8, 4 * 1024 * 1024),
            name="cross",
        )(offsets, white, *more)

    columns = min(d for d in range(1, groups + 1) if groups % d == 0 and d * d >= groups)
    lines = groups // columns
    power = [float(np.float32(factor) ** np.float32(d)) for d in range(groups + columns)]

    def down(value, by):
        pairs_of = [(h, h + by * columns) for h in range(groups - by * columns)]
        return lax.ppermute(value, "tm", pairs_of)

    def across(value, by, needed):
        pairs_of = [
            (h, h - h % columns + (h % columns + by) % columns)
            for h in range(groups)
            if h % columns + by < columns or needed(h // columns)
        ]
        return lax.ppermute(value, "tm", pairs_of)

    def same(value):
        return [value] * columns

    def mix(terms, weights, after):
        return pl.pallas_call(
            functools.partial(mix_kernel, columns, weights),
            out_shape=[jax.ShapeDtypeStruct(terms[0].shape, jnp.bfloat16)] * len(weights),
            in_specs=[whole()] * len(terms) + [whole(pl.ANY)] * len(after),
            out_specs=[whole()] * len(weights),
            compiler_params=params,
            cost_estimate=cost(len(terms) * terms[0].size * 4, 1024 * 1024),
            name="mix",
        )(*terms, *after)

    def lines_first(local, *after):
        got = [down(local, d) for d in range(1, lines)]
        weights = [same(1.0)] + [same(power[d * columns]) for d in range(1, lines)]
        onward = []
        for r in range(1, columns):
            onward.append(
                [[1.0 if lo + r < columns else 0.0 for lo in range(columns)]]
                + [
                    [power[d * columns] if lo + r < columns else power[(d - 1) * columns] for lo in range(columns)]
                    for d in range(1, lines)
                ]
            )
        sent = mix([local] + got, onward, after) if onward else []
        more = [across(v, r + 1, lambda line: line > 0) for r, v in enumerate(sent)]
        return [local] + got + more, weights + [same(power[r]) for r in range(1, columns)]

    def columns_first(local, *after):
        got = [across(local, r, lambda line: line < lines - 1) for r in range(1, columns)]
        weights = [same(1.0)] + [
            [power[r] if lo >= r else 0.0 for lo in range(columns)] for r in range(1, columns)
        ]
        onward = [
            [power[columns - 1 - (lo - r) % columns] for lo in range(columns)]
            for r in range(columns)
        ]
        if lines == 1:
            return [local] + got, weights
        (sent,) = mix([local] + got, [onward], after)
        more = [down(sent, d) for d in range(1, lines)]
        weights += [
            [power[lo + 1 + (d - 1) * columns] for lo in range(columns)] for d in range(1, lines)
        ]
        return [local] + got + more, weights

    def lags(first_pair, first, pieces, *so_far):
        terms = [term for piece in pieces for term in piece[0]]
        counts = [len(piece[0]) for piece in pieces]
        weights = [piece[1] for piece in pieces]
        rows = terms[0].shape[1]
        size = sum(piece[0][0].shape[0] for piece in pieces)
        return pl.pallas_call(
            functools.partial(lag_kernel, bins**-0.5, columns, (first_pair, first), counts, weights),
            out_shape=jax.ShapeDtypeStruct((pairs, chans, length), jnp.bfloat16),
            in_specs=[whole()] * (1 + len(terms)) + [whole(pl.ANY)] * len(so_far),
            out_specs=whole(pl.ANY),
            scratch_shapes=[
                pltpu.VMEM((size, rows, length), jnp.bfloat16),
                pltpu.SemaphoreType.DMA((len(pieces),)),
            ],
            input_output_aliases={1 + len(terms): 0} if so_far else {},
            compiler_params=params,
            cost_estimate=cost(size * rows * length * length * 4, 1024 * 1024),
            name="lags",
        )(table, *terms, *so_far)

    half = chans - span
    (local_a,) = cross(0, half, [pairs])
    local_b, local_c = cross(half, chans - half, [pairs // 2, pairs - pairs // 2], edge)
    piece_a = lines_first(local_a, local_c)
    piece_b = lines_first(local_b)
    piece_c = columns_first(local_c)
    result = lags(0, 0, [piece_a])
    result = lags(0, half, [piece_b], result)
    result = lags(pairs // 2, half, [piece_c], result)
    return result.reshape(1, pairs, chans, length)


def solution(mesh):
    in_specs = (P("chan", "tm", None), P("chan", "tm"), P())
    out_specs = P("tm", None, "chan", None)
    return jax.shard_map(
        per_device, mesh=mesh, in_specs=in_specs, out_specs=out_specs, check_vma=False
    )
```

```python
import functools
import math

import jax
import jax.numpy as jnp
import numpy as np
from jax import lax
from jax.experimental import pallas as pl
from jax.experimental.pallas import tpu as pltpu
from jax.sharding import PartitionSpec as P

OFFSET_SPAN = 32
LANES = 128
DECAY = 0.99
VMEM = 24 * 1024 * 1024


def turns(number, length):
    part = (number - length * jnp.floor(number / length + 0.5)) * (1.0 / length)
    square = part * part
    cosine, sine = jnp.float32(0.0), jnp.float32(0.0)
    for k in range(10, -1, -1):
        cosine = cosine * square + (-1) ** k * (2 * math.pi) ** (2 * k) / math.factorial(2 * k)
        sine = sine * square + (-1) ** k * (2 * math.pi) ** (2 * k + 1) / math.factorial(2 * k + 1)
    return cosine, sine * part


def fill_table(table_ref, step):
    length = table_ref.shape[0]
    bins = length // 2

    def small(rows, by):
        row = lax.broadcasted_iota(jnp.int32, (rows, bins), 0)
        freq = lax.broadcasted_iota(jnp.int32, (rows, bins), 1) + 1
        return turns((row * (by * freq)).astype(jnp.float32), length)

    coarse_cos, coarse_sin = small(length // step, step)
    fine_cos, fine_sin = small(step, 1)
    for i in range(length // step):
        rows = slice(i * step, (i + 1) * step)
        cos_i, sin_i = coarse_cos[i : i + 1], coarse_sin[i : i + 1]
        table_ref[rows, :bins] = (cos_i * fine_cos - sin_i * fine_sin).astype(jnp.bfloat16)
        table_ref[rows, bins:] = -(sin_i * fine_cos + cos_i * fine_sin).astype(jnp.bfloat16)


def whiten_kernel(
    span,
    x_hbm,
    valid_hbm,
    offsets_hbm,
    white_ref,
    short_ref,
    edge_ref,
    table_ref,
    pick_ref,
    x_ref,
    valid_ref,
    offsets_ref,
    raw_ref,
    sems,
):
    wins, chans, length = white_ref.shape
    bins = length // 2
    tiles = bins // LANES
    pairs = offsets_ref.shape[0]
    copies = [
        pltpu.make_async_copy(valid_hbm, valid_ref, sems.at[0]),
        pltpu.make_async_copy(offsets_hbm, offsets_ref, sems.at[1]),
    ]
    starts = list(range(0, chans, span))
    for i, c in enumerate(starts):
        part = pl.ds(c * wins, span * wins)
        copies.append(pltpu.make_async_copy(x_hbm.at[part], x_ref.at[part], sems.at[2 + i]))
    for copy in copies:
        copy.start()
    fill_table(table_ref, 16)
    copies[0].wait()
    copies[1].wait()
    ahead = lax.broadcasted_iota(jnp.int32, (span, 2 * span), 1) - lax.broadcasted_iota(
        jnp.int32, (span, 2 * span), 0
    )
    for k in range(pairs):
        chosen_row = jnp.where(ahead == offsets_ref[k], jnp.float32(1.0), jnp.float32(0.0))
        pick_ref[k] = chosen_row.astype(jnp.bfloat16)
    owner = lax.broadcasted_iota(jnp.int32, (wins, wins * LANES), 0)
    column = lax.broadcasted_iota(jnp.int32, (wins, wins * LANES), 1) // LANES
    keep = lax.dot_general(
        valid_ref[...].astype(jnp.float32).astype(jnp.bfloat16),
        (owner == column).astype(jnp.float32).astype(jnp.bfloat16),
        (((0,), (0,)), ((), ())),
        preferred_element_type=jnp.float32,
    )
    for i, c in enumerate(starts):
        copies[2 + i].wait()
        raw = jnp.dot(
            x_ref[c * wins : (c + span) * wins, :],
            table_ref[...],
            preferred_element_type=jnp.float32,
        )
        for t in range(2 * tiles):
            raw_ref[i, t] = raw[:, t * LANES : (t + 1) * LANES]
        for w in range(wins):
            part = [raw_ref[i, t, pl.ds(w, span, stride=wins), :] for t in range(2 * tiles)]
            power = [part[t] * part[t] + part[tiles + t] * part[tiles + t] for t in range(tiles)]
            total = power[0]
            for t in range(1, tiles):
                total = total + power[t]
            level = jnp.sum(total, axis=-1, keepdims=True) * (0.01 / bins) + 1e-06
            alive = keep[c : c + span, w * LANES : (w + 1) * LANES]
            for t in range(tiles):
                scale = alive * lax.rsqrt(power[t] + level)
                for s in (t, tiles + t):
                    value = part[s] * scale
                    here = pl.ds(w * length + s * LANES, LANES)
                    white_ref[w, c : c + span, s * LANES : (s + 1) * LANES] = value
                    short_ref[c : c + span, here] = value.astype(jnp.bfloat16)
                    if c == 0:
                        edge_ref[:, here] = value.astype(jnp.bfloat16)


def cross_kernel(first, pick_ref, white_ref, short_ref, *rest):
    out_ref, parts_ref = rest[-2:] if len(rest) == 2 else (rest[1], rest[2])
    wins, chans, length = white_ref.shape
    pairs, rows, reach = pick_ref.shape
    bins = length // 2
    if len(rest) == 2:
        near = short_ref[first : first + reach, :]
    else:
        ext_ref = rest[3]
        ext_ref[: chans - first] = short_ref[first:, :]
        ext_ref[chans - first :] = rest[0][...]
        near = ext_ref[...]
    pick = pick_ref[...].reshape(pairs * rows, reach)
    decay = [float(np.float32(DECAY) ** np.float32(wins - 1 - w)) for w in range(wins)]
    for w in range(wins):
        parts_ref[w] = jnp.dot(
            pick, near[:, w * length : (w + 1) * length], preferred_element_type=jnp.float32
        )
    for c in range(0, rows, 16):
        for t in range(bins // LANES):
            re = slice(t * LANES, (t + 1) * LANES)
            im = slice(bins + t * LANES, bins + (t + 1) * LANES)
            head = slice(first + c, first + c + 16)
            head_re = [white_ref[w, head, re] * decay[w] for w in range(wins)]
            head_im = [white_ref[w, head, im] * decay[w] for w in range(wins)]
            for k in range(pairs):
                here = slice(k * rows + c, k * rows + c + 16)
                total_re = total_im = None
                for w in range(wins):
                    part_re, part_im = parts_ref[w, here, re], parts_ref[w, here, im]
                    cross_re = head_re[w] * part_re + head_im[w] * part_im
                    cross_im = head_im[w] * part_re - head_re[w] * part_im
                    total_re = cross_re if w == 0 else total_re + cross_re
                    total_im = cross_im if w == 0 else total_im + cross_im
                out_ref[k, c : c + 16, re] = total_re.astype(out_ref.dtype)
                out_ref[k, c : c + 16, im] = total_im.astype(out_ref.dtype)


def prefix_kernel(factor, got_ref, out_ref):
    running = jnp.zeros(got_ref.shape[1:], jnp.float32)
    for g in range(got_ref.shape[0]):
        out_ref[g] = running.astype(out_ref.dtype)
        running = (running + got_ref[g].astype(jnp.float32)) * factor


def chosen(options, place):
    value = jnp.float32(options[0])
    for i, option in enumerate(options[1:]):
        value = jnp.where(place == i + 1, jnp.float32(option), value)
    return value


def weighted(terms, weights, place):
    total = None
    for term, options in zip(terms, weights):
        value = term[...].astype(jnp.float32)
        if set(options) != {1.0}:
            value = value * (options[0] if len(set(options)) == 1 else chosen(options, place))
        total = value if total is None else total + value
    return total


def mix_kernel(columns, weights, *refs):
    place = lax.rem(lax.axis_index("tm"), columns)
    count = len(weights[0])
    for out_ref, own in zip(refs[-len(weights) :], weights):
        out_ref[...] = weighted(refs[:count], own, place).astype(out_ref.dtype)


def lag_kernel(scale, columns, place_at, counts, weights, table_ref, *rest):
    first_pair, first = place_at
    terms = sum(counts)
    stage_ref, sems, out_hbm = rest[-2], rest[-1], rest[-3]
    place = lax.rem(lax.axis_index("tm"), columns)
    dims = (((1,), (1,)), ((), ()))
    table = table_ref[...]
    copies = []
    at = 0
    pair = 0
    for group, (count, own) in enumerate(zip(counts, weights)):
        refs = rest[at : at + count]
        pairs, rows, length = refs[0].shape
        stack = weighted(refs, own, place).reshape(pairs * rows, length)
        high = stack.astype(jnp.bfloat16)
        low = (stack - high.astype(jnp.float32)).astype(jnp.bfloat16)
        lagged = lax.dot_general(high, table, dims, preferred_element_type=jnp.float32)
        lagged = lagged + lax.dot_general(low, table, dims, preferred_element_type=jnp.float32)
        here = stage_ref.at[pl.ds(pair, pairs)]
        here[...] = (lagged * scale).astype(stage_ref.dtype).reshape(pairs, rows, length)
        there = out_hbm.at[pl.ds(first_pair + pair, pairs), pl.ds(first, rows)]
        copies.append(pltpu.make_async_copy(here, there, sems.at[group]))
        copies[-1].start()
        at += count
        pair += pairs
    for copy in copies:
        copy.wait()


def cost(flops, moved):
    return pl.CostEstimate(flops=flops, bytes_accessed=moved, transcendentals=0)


def whole(memory=pltpu.VMEM):
    return pl.BlockSpec(memory_space=memory)


def per_device(samples, valid, offsets):
    chans, wins, length = samples.shape
    bins = length // 2
    span = OFFSET_SPAN
    pairs = offsets.shape[0]
    tiles = bins // LANES
    groups = lax.axis_size("tm")
    factor = float(np.float32(DECAY) ** np.float32(wins))
    params = pltpu.CompilerParams(vmem_limit_bytes=VMEM)

    def in_hbm(value):
        return pltpu.with_memory_space_constraint(value, pltpu.HBM)

    half = chans - span
    white, short, edge, table, pick = pl.pallas_call(
        functools.partial(whiten_kernel, span),
        out_shape=(
            jax.ShapeDtypeStruct((wins, chans, length), jnp.float32),
            jax.ShapeDtypeStruct((chans, wins * length), jnp.bfloat16),
            jax.ShapeDtypeStruct((span, wins * length), jnp.bfloat16),
            jax.ShapeDtypeStruct((length, length), jnp.bfloat16),
            jax.ShapeDtypeStruct((pairs, span, 2 * span), jnp.bfloat16),
        ),
        in_specs=[whole(pltpu.HBM)] * 3,
        out_specs=(whole(),) * 5,
        scratch_shapes=[
            pltpu.VMEM((chans * wins, length), jnp.bfloat16),
            pltpu.VMEM((wins, chans), jnp.int32),
            pltpu.SMEM((pairs,), jnp.int32),
            pltpu.VMEM((chans // span, 2 * tiles, span * wins, LANES), jnp.float32),
            pltpu.SemaphoreType.DMA((2 + chans // span,)),
        ],
        compiler_params=params,
        cost_estimate=cost(chans * wins * length * length * 2, 2 * 1024 * 1024),
        name="whiten",
    )(in_hbm(samples.reshape(chans * wins, length)), in_hbm(valid.T), in_hbm(offsets))

    ring = lax.axis_size("chan")
    edge = lax.ppermute(edge, "chan", [(i, i - 1) for i in range(1, ring)])

    def cross(first, *more):
        return pl.pallas_call(
            functools.partial(cross_kernel, first),
            out_shape=jax.ShapeDtypeStruct((pairs, span, length), jnp.bfloat16),
            in_specs=[whole()] * (3 + len(more)),
            out_specs=whole(),
            scratch_shapes=[pltpu.VMEM((wins, pairs * span, length), jnp.float32)]
            + [pltpu.VMEM((2 * span, wins * length), jnp.bfloat16)] * len(more),
            compiler_params=params,
            cost_estimate=cost(pairs * span * wins * bins * 8, 4 * 1024 * 1024),
            name="cross",
        )(pick, white, short, *more)

    columns = min(d for d in range(1, groups + 1) if groups % d == 0 and d * d >= groups)
    lines = groups // columns
    power = [float(np.float32(factor) ** np.float32(d)) for d in range(groups + columns)]

    def down(value, by):
        pairs_of = [(h, h + by * columns) for h in range(groups - by * columns)]
        return lax.ppermute(value, "tm", pairs_of)

    def across(value, by, needed):
        pairs_of = [
            (h, h - h % columns + (h % columns + by) % columns)
            for h in range(groups)
            if h % columns + by < columns or needed(h // columns)
        ]
        return lax.ppermute(value, "tm", pairs_of)

    def same(value):
        return [value] * columns

    def mix(terms, weights, after):
        return pl.pallas_call(
            functools.partial(mix_kernel, columns, weights),
            out_shape=[jax.ShapeDtypeStruct(terms[0].shape, jnp.bfloat16)] * len(weights),
            in_specs=[whole()] * len(terms) + [whole(pl.ANY)] * len(after),
            out_specs=[whole()] * len(weights),
            compiler_params=params,
            cost_estimate=cost(len(terms) * terms[0].size * 4, 1024 * 1024),
            name="mix",
        )(*terms, *after)

    def lines_first(local, *after):
        got = [down(local, d) for d in range(1, lines)]
        weights = [same(1.0)] + [same(power[d * columns]) for d in range(1, lines)]
        onward = []
        for r in range(1, columns):
            onward.append(
                [[1.0 if lo + r < columns else 0.0 for lo in range(columns)]]
                + [
                    [power[d * columns] if lo + r < columns else power[(d - 1) * columns] for lo in range(columns)]
                    for d in range(1, lines)
                ]
            )
        sent = mix([local] + got, onward, after) if onward else []
        more = [across(v, r + 1, lambda line: line > 0) for r, v in enumerate(sent)]
        return [local] + got + more, weights + [same(power[r]) for r in range(1, columns)]

    def columns_first(local, *after):
        got = [across(local, r, lambda line: line < lines - 1) for r in range(1, columns)]
        weights = [same(1.0)] + [
            [power[r] if lo >= r else 0.0 for lo in range(columns)] for r in range(1, columns)
        ]
        onward = [
            [power[columns - 1 - (lo - r) % columns] for lo in range(columns)]
            for r in range(columns)
        ]
        if lines == 1:
            return [local] + got, weights
        (sent,) = mix([local] + got, [onward], after)
        more = [down(sent, d) for d in range(1, lines)]
        weights += [
            [power[lo + 1 + (d - 1) * columns] for lo in range(columns)] for d in range(1, lines)
        ]
        return [local] + got + more, weights

    def lags(first_pair, first, pieces, *so_far):
        terms = [term for piece in pieces for term in piece[0]]
        counts = [len(piece[0]) for piece in pieces]
        weights = [piece[1] for piece in pieces]
        rows = terms[0].shape[1]
        size = sum(piece[0][0].shape[0] for piece in pieces)
        return pl.pallas_call(
            functools.partial(lag_kernel, bins**-0.5, columns, (first_pair, first), counts, weights),
            out_shape=jax.ShapeDtypeStruct((pairs, chans, length), jnp.bfloat16),
            in_specs=[whole()] * (1 + len(terms)) + [whole(pl.ANY)] * len(so_far),
            out_specs=whole(pl.ANY),
            scratch_shapes=[
                pltpu.VMEM((size, rows, length), jnp.bfloat16),
                pltpu.SemaphoreType.DMA((len(pieces),)),
            ],
            input_output_aliases={1 + len(terms): 0} if so_far else {},
            compiler_params=params,
            cost_estimate=cost(size * rows * length * length * 4, 1024 * 1024),
            name="lags",
        )(table, *terms, *so_far)

    def exchange(value):
        return lax.all_to_all(value, "tm", split_axis=0, concat_axis=0, tiled=True)

    local_a = cross(0)
    local_b = cross(half, edge)
    piece_a = lines_first(local_a, local_b)
    got = exchange(local_b.reshape(groups, -1, length))
    before = pl.pallas_call(
        functools.partial(prefix_kernel, factor),
        out_shape=jax.ShapeDtypeStruct(got.shape, jnp.bfloat16),
        in_specs=[whole()],
        out_specs=whole(),
        compiler_params=params,
        cost_estimate=cost(got.size * 4, 1024 * 1024),
        name="prefix",
    )(got)
    before = exchange(before).reshape(local_b.shape)
    piece_b = ([local_b, before], [same(1.0), same(1.0)])
    result = lags(0, 0, [piece_a])
    result = lags(0, half, [piece_b], result)
    return result.reshape(1, pairs, chans, length)


def solution(mesh):
    in_specs = (P("chan", "tm", None), P("chan", "tm"), P())
    out_specs = P("tm", None, "chan", None)
    return jax.shard_map(
        per_device, mesh=mesh, in_specs=in_specs, out_specs=out_specs, check_vma=False
    )
```

```python
import functools
import math

import jax
import jax.numpy as jnp
import numpy as np
from jax import lax
from jax.experimental import pallas as pl
from jax.experimental.pallas import tpu as pltpu
from jax.sharding import PartitionSpec as P

OFFSET_SPAN = 32
LANES = 128
DECAY = 0.99
VMEM = 24 * 1024 * 1024


def turns(number, length):
    part = (number - length * jnp.floor(number / length + 0.5)) * (1.0 / length)
    square = part * part
    cosine, sine = jnp.float32(0.0), jnp.float32(0.0)
    for k in range(10, -1, -1):
        cosine = cosine * square + (-1) ** k * (2 * math.pi) ** (2 * k) / math.factorial(2 * k)
        sine = sine * square + (-1) ** k * (2 * math.pi) ** (2 * k + 1) / math.factorial(2 * k + 1)
    return cosine, sine * part


def fill_table(table_ref, step):
    length = table_ref.shape[0]
    bins = length // 2

    def small(rows, by):
        row = lax.broadcasted_iota(jnp.int32, (rows, bins), 0)
        freq = lax.broadcasted_iota(jnp.int32, (rows, bins), 1) + 1
        return turns((row * (by * freq)).astype(jnp.float32), length)

    coarse_cos, coarse_sin = small(length // step, step)
    fine_cos, fine_sin = small(step, 1)
    for i in range(length // step):
        rows = slice(i * step, (i + 1) * step)
        cos_i, sin_i = coarse_cos[i : i + 1], coarse_sin[i : i + 1]
        table_ref[rows, :bins] = (cos_i * fine_cos - sin_i * fine_sin).astype(jnp.bfloat16)
        table_ref[rows, bins:] = -(sin_i * fine_cos + cos_i * fine_sin).astype(jnp.bfloat16)


def whiten_block(x, table, keep, raw_ref, white_ref, short_ref):
    wins, span, length = white_ref.shape
    bins = length // 2
    tiles = bins // LANES
    raw = jnp.dot(x, table, preferred_element_type=jnp.float32)
    for t in range(2 * tiles):
        raw_ref[t] = raw[:, t * LANES : (t + 1) * LANES]
    for w in range(wins):
        part = [raw_ref[t, pl.ds(w, span, stride=wins), :] for t in range(2 * tiles)]
        power = [part[t] * part[t] + part[tiles + t] * part[tiles + t] for t in range(tiles)]
        total = power[0]
        for t in range(1, tiles):
            total = total + power[t]
        level = jnp.sum(total, axis=-1, keepdims=True) * (0.01 / bins) + 1e-06
        alive = keep[:, w * LANES : (w + 1) * LANES]
        for t in range(tiles):
            scale = alive * lax.rsqrt(power[t] + level)
            for s in (t, tiles + t):
                value = part[s] * scale
                here = pl.ds(w * length + s * LANES, LANES)
                white_ref[w, :, s * LANES : (s + 1) * LANES] = value
                short_ref[:, here] = value.astype(jnp.bfloat16)


def head_kernel(
    x_hbm,
    valid_hbm,
    offsets_hbm,
    white_ref,
    short_ref,
    table_ref,
    pick_ref,
    keep_ref,
    x_ref,
    valid_ref,
    offsets_ref,
    raw_ref,
    sems,
):
    wins, span, length = white_ref.shape
    pairs = offsets_ref.shape[0]
    copies = [
        pltpu.make_async_copy(valid_hbm, valid_ref, sems.at[0]),
        pltpu.make_async_copy(offsets_hbm, offsets_ref, sems.at[1]),
        pltpu.make_async_copy(x_hbm.at[pl.ds(0, span * wins)], x_ref, sems.at[2]),
    ]
    for copy in copies:
        copy.start()
    fill_table(table_ref, 16)
    copies[0].wait()
    copies[1].wait()
    ahead = lax.broadcasted_iota(jnp.int32, (span, 2 * span), 1) - lax.broadcasted_iota(
        jnp.int32, (span, 2 * span), 0
    )
    for k in range(pairs):
        chosen_row = jnp.where(ahead == offsets_ref[k], jnp.float32(1.0), jnp.float32(0.0))
        pick_ref[k] = chosen_row.astype(jnp.bfloat16)
    owner = lax.broadcasted_iota(jnp.int32, (wins, wins * LANES), 0)
    column = lax.broadcasted_iota(jnp.int32, (wins, wins * LANES), 1) // LANES
    keep_ref[...] = lax.dot_general(
        valid_ref[...].astype(jnp.float32).astype(jnp.bfloat16),
        (owner == column).astype(jnp.float32).astype(jnp.bfloat16),
        (((0,), (0,)), ((), ())),
        preferred_element_type=jnp.float32,
    )
    copies[2].wait()
    whiten_block(x_ref[...], table_ref[...], keep_ref[:span], raw_ref, white_ref, short_ref)


def stack_pairs(pick_ref, white_ref, near_ref, parts_ref, out_refs):
    wins, _, length = white_ref.shape
    pairs, rows, reach = pick_ref.shape
    bins = length // 2
    pick = pick_ref[...].reshape(pairs * rows, reach)
    decay = [float(np.float32(DECAY) ** np.float32(wins - 1 - w)) for w in range(wins)]
    for w in range(wins):
        parts_ref[w] = jnp.dot(
            pick, near_ref[:, w * length : (w + 1) * length], preferred_element_type=jnp.float32
        )
    for c in range(0, rows, 16):
        for t in range(bins // LANES):
            re = slice(t * LANES, (t + 1) * LANES)
            im = slice(bins + t * LANES, bins + (t + 1) * LANES)
            head_re = [white_ref[w, c : c + 16, re] * decay[w] for w in range(wins)]
            head_im = [white_ref[w, c : c + 16, im] * decay[w] for w in range(wins)]
            for k in range(pairs):
                here = slice(k * rows + c, k * rows + c + 16)
                total_re = total_im = None
                for w in range(wins):
                    part_re, part_im = parts_ref[w, here, re], parts_ref[w, here, im]
                    cross_re = head_re[w] * part_re + head_im[w] * part_im
                    cross_im = head_im[w] * part_re - head_re[w] * part_im
                    total_re = cross_re if w == 0 else total_re + cross_re
                    total_im = cross_im if w == 0 else total_im + cross_im
                for out_ref in out_refs:
                    out_ref[k, c : c + 16, re] = total_re.astype(out_ref.dtype)
                    out_ref[k, c : c + 16, im] = total_im.astype(out_ref.dtype)


def tail_kernel(
    x_ref, table_ref, keep_ref, pick_ref, head_ref, edge_ref, white_ref, short_ref, out_ref, raw_ref, near_ref, parts_ref
):
    wins, span, length = white_ref.shape
    rows = slice(span * wins, 2 * span * wins)
    whiten_block(x_ref[rows, :], table_ref[...], keep_ref[span:], raw_ref, white_ref, short_ref)
    near_ref[:span] = edge_ref[...]
    near_ref[span:] = short_ref[...]
    stack_pairs(pick_ref, head_ref, near_ref, parts_ref, [out_ref])


def cross_kernel(pick_ref, white_ref, short_ref, edge_ref, send_ref, keep_ref, near_ref, parts_ref):
    span = short_ref.shape[0]
    near_ref[:span] = short_ref[...]
    near_ref[span:] = edge_ref[...]
    stack_pairs(pick_ref, white_ref, near_ref, parts_ref, [send_ref, keep_ref])


def prefix_kernel(factor, got_ref, out_ref):
    running = jnp.zeros(got_ref.shape[1:], jnp.float32)
    for g in range(got_ref.shape[0]):
        out_ref[g] = running.astype(out_ref.dtype)
        running = (running + got_ref[g].astype(jnp.float32)) * factor


def chosen(options, place):
    value = jnp.float32(options[0])
    for i, option in enumerate(options[1:]):
        value = jnp.where(place == i + 1, jnp.float32(option), value)
    return value


def weighted(terms, weights, place):
    total = None
    for term, options in zip(terms, weights):
        value = term[...].astype(jnp.float32)
        if set(options) != {1.0}:
            value = value * (options[0] if len(set(options)) == 1 else chosen(options, place))
        total = value if total is None else total + value
    return total


def mix_kernel(columns, weights, *refs):
    place = lax.rem(lax.axis_index("tm"), columns)
    count = len(weights[0])
    for out_ref, own in zip(refs[-len(weights) :], weights):
        out_ref[...] = weighted(refs[:count], own, place).astype(out_ref.dtype)


def lag_kernel(scale, columns, firsts, weights, table_ref, *rest):
    out_hbm, stage_ref, sems = rest[-3:]
    place = lax.rem(lax.axis_index("tm"), columns)
    dims = (((1,), (1,)), ((), ()))
    table = table_ref[...]
    copies = []
    at = 0
    for piece, (first, own) in enumerate(zip(firsts, weights)):
        refs = rest[at : at + len(own)]
        pairs, rows, length = refs[0].shape
        stack = weighted(refs, own, place).reshape(pairs * rows, length)
        high = stack.astype(jnp.bfloat16)
        low = (stack - high.astype(jnp.float32)).astype(jnp.bfloat16)
        lagged = lax.dot_general(high, table, dims, preferred_element_type=jnp.float32)
        lagged = lagged + lax.dot_general(low, table, dims, preferred_element_type=jnp.float32)
        stage_ref[piece] = (lagged * scale).astype(stage_ref.dtype).reshape(pairs, rows, length)
        there = out_hbm.at[:, pl.ds(first, rows)]
        copies.append(pltpu.make_async_copy(stage_ref.at[piece], there, sems.at[piece]))
        copies[-1].start()
        at += len(own)
    for copy in copies:
        copy.wait()


def cost(flops, moved):
    return pl.CostEstimate(flops=flops, bytes_accessed=moved, transcendentals=0)


def whole(memory=pltpu.VMEM):
    return pl.BlockSpec(memory_space=memory)


def per_device(samples, valid, offsets):
    chans, wins, length = samples.shape
    bins = length // 2
    span = OFFSET_SPAN
    pairs = offsets.shape[0]
    tiles = bins // LANES
    groups = lax.axis_size("tm")
    factor = float(np.float32(DECAY) ** np.float32(wins))
    params = pltpu.CompilerParams(vmem_limit_bytes=VMEM)

    def in_hbm(value):
        return pltpu.with_memory_space_constraint(value, pltpu.HBM)

    half = chans - span
    flat = samples.reshape(chans * wins, length)
    white_type = jax.ShapeDtypeStruct((wins, span, length), jnp.float32)
    short_type = jax.ShapeDtypeStruct((span, wins * length), jnp.bfloat16)
    local_type = jax.ShapeDtypeStruct((pairs, span, length), jnp.bfloat16)
    raw_scratch = pltpu.VMEM((2 * tiles, span * wins, LANES), jnp.float32)
    near_scratch = pltpu.VMEM((2 * span, wins * length), jnp.bfloat16)
    parts_scratch = pltpu.VMEM((wins, pairs * span, length), jnp.float32)

    white_a, short_a, table, pick, keep = pl.pallas_call(
        head_kernel,
        out_shape=(
            white_type,
            short_type,
            jax.ShapeDtypeStruct((length, length), jnp.bfloat16),
            jax.ShapeDtypeStruct((pairs, span, 2 * span), jnp.bfloat16),
            jax.ShapeDtypeStruct((chans, wins * LANES), jnp.float32),
        ),
        in_specs=[whole(pltpu.HBM)] * 3,
        out_specs=(whole(),) * 5,
        scratch_shapes=[
            pltpu.VMEM((span * wins, length), jnp.bfloat16),
            pltpu.VMEM((wins, chans), jnp.int32),
            pltpu.SMEM((pairs,), jnp.int32),
            raw_scratch,
            pltpu.SemaphoreType.DMA((3,)),
        ],
        compiler_params=params,
        cost_estimate=cost(span * wins * length * length * 2, 2 * 1024 * 1024),
        name="head",
    )(in_hbm(flat), in_hbm(valid.T), in_hbm(offsets))

    ring = lax.axis_size("chan")
    edge = lax.ppermute(short_a, "chan", [(i, i - 1) for i in range(1, ring)])

    white_b, short_b, local_a = pl.pallas_call(
        tail_kernel,
        out_shape=(white_type, short_type, local_type),
        in_specs=[whole()] * 6,
        out_specs=(whole(),) * 3,
        scratch_shapes=[raw_scratch, near_scratch, parts_scratch],
        compiler_params=params,
        cost_estimate=cost(span * wins * length * length * 4, 4 * 1024 * 1024),
        name="tail",
    )(flat, table, keep, pick, white_a, short_a)

    local_b, kept_b = pl.pallas_call(
        cross_kernel,
        out_shape=(local_type, local_type),
        in_specs=[whole()] * 4,
        out_specs=(whole(),) * 2,
        scratch_shapes=[near_scratch, parts_scratch],
        compiler_params=params,
        cost_estimate=cost(pairs * span * wins * bins * 8, 4 * 1024 * 1024),
        name="cross",
    )(pick, white_b, short_b, edge)

    columns = min(d for d in range(1, groups + 1) if groups % d == 0 and d * d >= groups)
    lines = groups // columns
    power = [float(np.float32(factor) ** np.float32(d)) for d in range(groups + columns)]

    def down(value, by):
        pairs_of = [(h, h + by * columns) for h in range(groups - by * columns)]
        return lax.ppermute(value, "tm", pairs_of)

    def across(value, by, needed):
        pairs_of = [
            (h, h - h % columns + (h % columns + by) % columns)
            for h in range(groups)
            if h % columns + by < columns or needed(h // columns)
        ]
        return lax.ppermute(value, "tm", pairs_of)

    def same(value):
        return [value] * columns

    def mix(terms, weights, after):
        return pl.pallas_call(
            functools.partial(mix_kernel, columns, weights),
            out_shape=[jax.ShapeDtypeStruct(terms[0].shape, jnp.bfloat16)] * len(weights),
            in_specs=[whole()] * len(terms) + [whole(pl.ANY)] * len(after),
            out_specs=[whole()] * len(weights),
            compiler_params=params,
            cost_estimate=cost(len(terms) * terms[0].size * 4, 1024 * 1024),
            name="mix",
        )(*terms, *after)

    def lines_first(local, *after):
        got = [down(local, d) for d in range(1, lines)]
        weights = [same(1.0)] + [same(power[d * columns]) for d in range(1, lines)]
        onward = []
        for r in range(1, columns):
            onward.append(
                [[1.0 if lo + r < columns else 0.0 for lo in range(columns)]]
                + [
                    [power[d * columns] if lo + r < columns else power[(d - 1) * columns] for lo in range(columns)]
                    for d in range(1, lines)
                ]
            )
        sent = mix([local] + got, onward, after) if onward else []
        more = [across(v, r + 1, lambda line: line > 0) for r, v in enumerate(sent)]
        return [local] + got + more, weights + [same(power[r]) for r in range(1, columns)]

    def columns_first(local, *after):
        got = [across(local, r, lambda line: line < lines - 1) for r in range(1, columns)]
        weights = [same(1.0)] + [
            [power[r] if lo >= r else 0.0 for lo in range(columns)] for r in range(1, columns)
        ]
        onward = [
            [power[columns - 1 - (lo - r) % columns] for lo in range(columns)]
            for r in range(columns)
        ]
        if lines == 1:
            return [local] + got, weights
        (sent,) = mix([local] + got, [onward], after)
        more = [down(sent, d) for d in range(1, lines)]
        weights += [
            [power[lo + 1 + (d - 1) * columns] for lo in range(columns)] for d in range(1, lines)
        ]
        return [local] + got + more, weights

    def lags(pieces):
        terms = [term for _, values, _ in pieces for term in values]
        firsts = [first for first, _, _ in pieces]
        weights = [own for _, _, own in pieces]
        return pl.pallas_call(
            functools.partial(lag_kernel, bins**-0.5, columns, firsts, weights),
            out_shape=jax.ShapeDtypeStruct((pairs, chans, length), jnp.bfloat16),
            in_specs=[whole()] * (1 + len(terms)),
            out_specs=whole(pl.ANY),
            scratch_shapes=[
                pltpu.VMEM((len(pieces), pairs, span, length), jnp.bfloat16),
                pltpu.SemaphoreType.DMA((len(pieces),)),
            ],
            compiler_params=params,
            cost_estimate=cost(pairs * chans * length * length * 4, 1024 * 1024),
            name="lags",
        )(table, *terms)

    def exchange(value):
        return lax.all_to_all(value, "tm", split_axis=0, concat_axis=0, tiled=True)

    piece_a = lines_first(local_a, local_b)
    got = exchange(local_b.reshape(groups, -1, length))
    before = pl.pallas_call(
        functools.partial(prefix_kernel, factor),
        out_shape=jax.ShapeDtypeStruct(got.shape, jnp.bfloat16),
        in_specs=[whole()],
        out_specs=whole(),
        compiler_params=params,
        cost_estimate=cost(got.size * 4, 1024 * 1024),
        name="prefix",
    )(got)
    before = exchange(before).reshape(local_b.shape)
    result = lags([(0,) + piece_a, (half, [kept_b, before], [same(1.0), same(1.0)])])
    return result.reshape(1, pairs, chans, length)


def solution(mesh):
    in_specs = (P("chan", "tm", None), P("chan", "tm"), P())
    out_specs = P("tm", None, "chan", None)
    return jax.shard_map(
        per_device, mesh=mesh, in_specs=in_specs, out_specs=out_specs, check_vma=False
    )
```

```python
import functools
import math

import jax
import jax.numpy as jnp
import numpy as np
from jax import lax
from jax.experimental import pallas as pl
from jax.experimental.pallas import tpu as pltpu
from jax.sharding import PartitionSpec as P

OFFSET_SPAN = 32
LANES = 128
DECAY = 0.99
VMEM = 24 * 1024 * 1024


def turns(number, length):
    part = (number - length * jnp.floor(number / length + 0.5)) * (1.0 / length)
    square = part * part
    cosine, sine = jnp.float32(0.0), jnp.float32(0.0)
    for k in range(10, -1, -1):
        cosine = cosine * square + (-1) ** k * (2 * math.pi) ** (2 * k) / math.factorial(2 * k)
        sine = sine * square + (-1) ** k * (2 * math.pi) ** (2 * k + 1) / math.factorial(2 * k + 1)
    return cosine, sine * part


def fill_table(table_ref, step):
    length = table_ref.shape[0]
    bins = length // 2

    def small(rows, by):
        row = lax.broadcasted_iota(jnp.int32, (rows, bins), 0)
        freq = lax.broadcasted_iota(jnp.int32, (rows, bins), 1) + 1
        return turns((row * (by * freq)).astype(jnp.float32), length)

    coarse_cos, coarse_sin = small(length // step, step)
    fine_cos, fine_sin = small(step, 1)
    for i in range(length // step):
        rows = slice(i * step, (i + 1) * step)
        cos_i, sin_i = coarse_cos[i : i + 1], coarse_sin[i : i + 1]
        table_ref[rows, :bins] = (cos_i * fine_cos - sin_i * fine_sin).astype(jnp.bfloat16)
        table_ref[rows, bins:] = -(sin_i * fine_cos + cos_i * fine_sin).astype(jnp.bfloat16)


def whiten_block(x, table, keep, raw_ref, white_ref, short_ref):
    wins, span, length = white_ref.shape
    bins = length // 2
    tiles = bins // LANES
    raw = jnp.dot(x, table, preferred_element_type=jnp.float32)
    for t in range(2 * tiles):
        raw_ref[t] = raw[:, t * LANES : (t + 1) * LANES]
    for w in range(wins):
        part = [raw_ref[t, pl.ds(w, span, stride=wins), :] for t in range(2 * tiles)]
        power = [part[t] * part[t] + part[tiles + t] * part[tiles + t] for t in range(tiles)]
        total = power[0]
        for t in range(1, tiles):
            total = total + power[t]
        level = jnp.sum(total, axis=-1, keepdims=True) * (0.01 / bins) + 1e-06
        alive = keep[:, w * LANES : (w + 1) * LANES]
        for t in range(tiles):
            scale = alive * lax.rsqrt(power[t] + level)
            for s in (t, tiles + t):
                value = part[s] * scale
                here = pl.ds(w * length + s * LANES, LANES)
                white_ref[w, :, s * LANES : (s + 1) * LANES] = value
                short_ref[:, here] = value.astype(jnp.bfloat16)


def head_kernel(
    x_hbm,
    valid_hbm,
    offsets_hbm,
    white_ref,
    short_ref,
    table_ref,
    pick_ref,
    keep_ref,
    x_ref,
    valid_ref,
    offsets_ref,
    raw_ref,
    sems,
):
    wins, span, length = white_ref.shape
    pairs = offsets_ref.shape[0]
    copies = [
        pltpu.make_async_copy(valid_hbm, valid_ref, sems.at[0]),
        pltpu.make_async_copy(offsets_hbm, offsets_ref, sems.at[1]),
        pltpu.make_async_copy(x_hbm.at[pl.ds(0, span * wins)], x_ref, sems.at[2]),
    ]
    for copy in copies:
        copy.start()
    fill_table(table_ref, 16)
    copies[0].wait()
    copies[1].wait()
    ahead = lax.broadcasted_iota(jnp.int32, (span, 2 * span), 1) - lax.broadcasted_iota(
        jnp.int32, (span, 2 * span), 0
    )
    for k in range(pairs):
        chosen_row = jnp.where(ahead == offsets_ref[k], jnp.float32(1.0), jnp.float32(0.0))
        pick_ref[k] = chosen_row.astype(jnp.bfloat16)
    owner = lax.broadcasted_iota(jnp.int32, (wins, wins * LANES), 0)
    column = lax.broadcasted_iota(jnp.int32, (wins, wins * LANES), 1) // LANES
    keep_ref[...] = lax.dot_general(
        valid_ref[...].astype(jnp.float32).astype(jnp.bfloat16),
        (owner == column).astype(jnp.float32).astype(jnp.bfloat16),
        (((0,), (0,)), ((), ())),
        preferred_element_type=jnp.float32,
    )
    copies[2].wait()
    whiten_block(x_ref[...], table_ref[...], keep_ref[:span], raw_ref, white_ref, short_ref)


def stack_pairs(pick_ref, white_ref, near_ref, parts_ref, out_ref):
    wins, _, length = white_ref.shape
    pairs, rows, reach = pick_ref.shape
    bins = length // 2
    pick = pick_ref[...].reshape(pairs * rows, reach)
    decay = [float(np.float32(DECAY) ** np.float32(wins - 1 - w)) for w in range(wins)]
    for w in range(wins):
        parts_ref[w] = jnp.dot(
            pick, near_ref[:, w * length : (w + 1) * length], preferred_element_type=jnp.float32
        )
    for c in range(0, rows, 16):
        for t in range(bins // LANES):
            re = slice(t * LANES, (t + 1) * LANES)
            im = slice(bins + t * LANES, bins + (t + 1) * LANES)
            head_re = [white_ref[w, c : c + 16, re] * decay[w] for w in range(wins)]
            head_im = [white_ref[w, c : c + 16, im] * decay[w] for w in range(wins)]
            for k in range(pairs):
                here = slice(k * rows + c, k * rows + c + 16)
                total_re = total_im = None
                for w in range(wins):
                    part_re, part_im = parts_ref[w, here, re], parts_ref[w, here, im]
                    cross_re = head_re[w] * part_re + head_im[w] * part_im
                    cross_im = head_im[w] * part_re - head_re[w] * part_im
                    total_re = cross_re if w == 0 else total_re + cross_re
                    total_im = cross_im if w == 0 else total_im + cross_im
                out_ref[k, c : c + 16, re] = total_re.astype(out_ref.dtype)
                out_ref[k, c : c + 16, im] = total_im.astype(out_ref.dtype)


def tail_kernel(
    x_ref, table_ref, keep_ref, pick_ref, head_ref, edge_ref, white_ref, short_ref, out_ref, raw_ref, near_ref, parts_ref
):
    wins, span, length = white_ref.shape
    rows = slice(span * wins, 2 * span * wins)
    whiten_block(x_ref[rows, :], table_ref[...], keep_ref[span:], raw_ref, white_ref, short_ref)
    near_ref[:span] = edge_ref[...]
    near_ref[span:] = short_ref[...]
    stack_pairs(pick_ref, head_ref, near_ref, parts_ref, out_ref)


def cross_kernel(pick_ref, white_ref, short_ref, edge_ref, out_ref, near_ref, parts_ref):
    span = short_ref.shape[0]
    near_ref[:span] = short_ref[...]
    near_ref[span:] = edge_ref[...]
    stack_pairs(pick_ref, white_ref, near_ref, parts_ref, out_ref)


def chosen(options, place):
    value = jnp.float32(options[0])
    for i, option in enumerate(options[1:]):
        value = jnp.where(place == i + 1, jnp.float32(option), value)
    return value


def weighted(terms, weights, place):
    total = None
    for term, options in zip(terms, weights):
        value = term[...].astype(jnp.float32)
        if set(options) != {1.0}:
            value = value * (options[0] if len(set(options)) == 1 else chosen(options, place))
        total = value if total is None else total + value
    return total


def mix_kernel(weights, *refs):
    place = lax.axis_index("tm")
    total = weighted(refs[: len(weights)], weights, place)
    refs[-1][...] = total.astype(refs[-1].dtype)


def lag_kernel(scale, first, weights, table_ref, *rest):
    out_hbm, stage_ref, sems = rest[-3:]
    place = lax.axis_index("tm")
    dims = (((1,), (1,)), ((), ()))
    pairs, rows, length = stage_ref.shape
    refs = rest[: len(weights)]
    stack = weighted(refs, weights, place).reshape(pairs * rows, length)
    high = stack.astype(jnp.bfloat16)
    low = (stack - high.astype(jnp.float32)).astype(jnp.bfloat16)
    table = table_ref[...]
    lagged = lax.dot_general(high, table, dims, preferred_element_type=jnp.float32)
    lagged = lagged + lax.dot_general(low, table, dims, preferred_element_type=jnp.float32)
    stage_ref[...] = (lagged * scale).astype(stage_ref.dtype).reshape(pairs, rows, length)
    copy = pltpu.make_async_copy(stage_ref, out_hbm.at[:, pl.ds(first, rows)], sems.at[0])
    copy.start()
    copy.wait()


def cost(flops, moved):
    return pl.CostEstimate(flops=flops, bytes_accessed=moved, transcendentals=0)


def whole(memory=pltpu.VMEM):
    return pl.BlockSpec(memory_space=memory)


def per_device(samples, valid, offsets):
    chans, wins, length = samples.shape
    bins = length // 2
    span = OFFSET_SPAN
    pairs = offsets.shape[0]
    tiles = bins // LANES
    groups = lax.axis_size("tm")
    factor = float(np.float32(DECAY) ** np.float32(wins))
    params = pltpu.CompilerParams(vmem_limit_bytes=VMEM)

    def in_hbm(value):
        return pltpu.with_memory_space_constraint(value, pltpu.HBM)

    half = chans - span
    flat = samples.reshape(chans * wins, length)
    white_type = jax.ShapeDtypeStruct((wins, span, length), jnp.float32)
    short_type = jax.ShapeDtypeStruct((span, wins * length), jnp.bfloat16)
    local_type = jax.ShapeDtypeStruct((pairs, span, length), jnp.bfloat16)
    raw_scratch = pltpu.VMEM((2 * tiles, span * wins, LANES), jnp.float32)
    near_scratch = pltpu.VMEM((2 * span, wins * length), jnp.bfloat16)
    parts_scratch = pltpu.VMEM((wins, pairs * span, length), jnp.float32)

    white_a, short_a, table, pick, keep = pl.pallas_call(
        head_kernel,
        out_shape=(
            white_type,
            short_type,
            jax.ShapeDtypeStruct((length, length), jnp.bfloat16),
            jax.ShapeDtypeStruct((pairs, span, 2 * span), jnp.bfloat16),
            jax.ShapeDtypeStruct((chans, wins * LANES), jnp.float32),
        ),
        in_specs=[whole(pltpu.HBM)] * 3,
        out_specs=(whole(),) * 5,
        scratch_shapes=[
            pltpu.VMEM((span * wins, length), jnp.bfloat16),
            pltpu.VMEM((wins, chans), jnp.int32),
            pltpu.SMEM((pairs,), jnp.int32),
            raw_scratch,
            pltpu.SemaphoreType.DMA((3,)),
        ],
        compiler_params=params,
        cost_estimate=cost(span * wins * length * length * 2, 2 * 1024 * 1024),
        name="head",
    )(in_hbm(flat), in_hbm(valid.T), in_hbm(offsets))

    ring = lax.axis_size("chan")
    edge = lax.ppermute(short_a, "chan", [(i, i - 1) for i in range(1, ring)])

    white_b, short_b, local_a = pl.pallas_call(
        tail_kernel,
        out_shape=(white_type, short_type, local_type),
        in_specs=[whole()] * 6,
        out_specs=(whole(),) * 3,
        scratch_shapes=[raw_scratch, near_scratch, parts_scratch],
        compiler_params=params,
        cost_estimate=cost(span * wins * length * length * 4, 4 * 1024 * 1024),
        name="tail",
    )(flat, table, keep, pick, white_a, short_a)

    local_b = pl.pallas_call(
        cross_kernel,
        out_shape=local_type,
        in_specs=[whole()] * 4,
        out_specs=whole(),
        scratch_shapes=[near_scratch, parts_scratch],
        compiler_params=params,
        cost_estimate=cost(pairs * span * wins * bins * 8, 4 * 1024 * 1024),
        name="cross",
    )(pick, white_b, short_b, edge)

    power = [float(np.float32(factor) ** np.float32(d)) for d in range(groups)]
    columns = min(d for d in range(1, groups + 1) if groups % d == 0 and d * d >= groups)
    square = columns == 2 and groups == columns * columns

    def sent(value, moves):
        return lax.ppermute(value, "tm", moves)

    def faded(moves):
        origin = {there: here for here, there in moves}
        return [power[h - origin[h]] if h in origin else 0.0 for h in range(groups)]

    if square:
        low, high = [(0, 1), (1, 3)], [(0, 2), (2, 3)]
        straight = [[(0, 3), (1, 2)], low, high]
    else:
        straight = [[(h, h + d) for h in range(groups - d)] for d in range(1, groups)]

    def mix(terms, weights, after):
        return pl.pallas_call(
            functools.partial(mix_kernel, weights),
            out_shape=local_type,
            in_specs=[whole()] * len(terms) + [whole(pl.ANY)],
            out_specs=whole(),
            compiler_params=params,
            cost_estimate=cost(len(terms) * terms[0].size * 4, 1024 * 1024),
            name="mix",
        )(*terms, after)

    def lags(first, terms, weights, *so_far):
        return pl.pallas_call(
            functools.partial(lag_kernel, bins**-0.5, first, weights),
            out_shape=jax.ShapeDtypeStruct((pairs, chans, length), jnp.bfloat16),
            in_specs=[whole()] * (1 + len(terms)) + [whole(pl.ANY)] * len(so_far),
            out_specs=whole(pl.ANY),
            scratch_shapes=[
                pltpu.VMEM((pairs, span, length), jnp.bfloat16),
                pltpu.SemaphoreType.DMA((1,)),
            ],
            input_output_aliases={1 + len(terms): 0} if so_far else {},
            compiler_params=params,
            cost_estimate=cost(pairs * span * length * length * 4, 1024 * 1024),
            name="lags",
        )(table, *terms, *so_far)

    unit = [1.0] * groups
    terms_b = [local_b] + [sent(local_b, moves) for moves in straight]
    weights_b = [unit] + [faded(moves) for moves in straight]
    if square:
        got_low, got_high = sent(local_a, low), sent(local_a, high)
        onward = mix([got_low, got_high], [[0.0, 0.0, 0.0, 1.0], [0.0, 0.0, 1.0, 0.0]], local_b)
        terms_a = [local_a, got_low, got_high, sent(onward, [(2, 3), (3, 2)])]
        weights_a = [unit, faded(low), faded(high), [0.0, 0.0, power[1], power[3]]]
    else:
        terms_a = [local_a] + [sent(local_a, moves) for moves in straight]
        weights_a = weights_b
    result = lags(half, terms_b, weights_b)
    result = lags(0, terms_a, weights_a, result)
    return result.reshape(1, pairs, chans, length)


def solution(mesh):
    in_specs = (P("chan", "tm", None), P("chan", "tm"), P())
    out_specs = P("tm", None, "chan", None)
    return jax.shard_map(
        per_device, mesh=mesh, in_specs=in_specs, out_specs=out_specs, check_vma=False
    )
```

```python
import functools
import math

import jax
import jax.numpy as jnp
import numpy as np
from jax import lax
from jax.experimental import pallas as pl
from jax.experimental.pallas import tpu as pltpu
from jax.sharding import PartitionSpec as P

OFFSET_SPAN = 32
LANES = 128
DECAY = 0.99
VMEM = 24 * 1024 * 1024


def turns(number, length):
    part = (number - length * jnp.floor(number / length + 0.5)) * (1.0 / length)
    square = part * part
    cosine, sine = jnp.float32(0.0), jnp.float32(0.0)
    for k in range(10, -1, -1):
        cosine = cosine * square + (-1) ** k * (2 * math.pi) ** (2 * k) / math.factorial(2 * k)
        sine = sine * square + (-1) ** k * (2 * math.pi) ** (2 * k + 1) / math.factorial(2 * k + 1)
    return cosine, sine * part


def fill_table(table_ref, step):
    length = table_ref.shape[0]
    bins = length // 2

    def small(rows, by):
        row = lax.broadcasted_iota(jnp.int32, (rows, bins), 0)
        freq = lax.broadcasted_iota(jnp.int32, (rows, bins), 1) + 1
        return turns((row * (by * freq)).astype(jnp.float32), length)

    coarse_cos, coarse_sin = small(length // step, step)
    fine_cos, fine_sin = small(step, 1)
    for i in range(length // step):
        rows = slice(i * step, (i + 1) * step)
        cos_i, sin_i = coarse_cos[i : i + 1], coarse_sin[i : i + 1]
        table_ref[rows, :bins] = (cos_i * fine_cos - sin_i * fine_sin).astype(jnp.bfloat16)
        table_ref[rows, bins:] = -(sin_i * fine_cos + cos_i * fine_sin).astype(jnp.bfloat16)


def whiten_block(x, table, keep, raw_ref, white_ref, short_ref):
    wins, span, length = white_ref.shape
    bins = length // 2
    tiles = bins // LANES
    raw = jnp.dot(x, table, preferred_element_type=jnp.float32)
    for t in range(2 * tiles):
        raw_ref[t] = raw[:, t * LANES : (t + 1) * LANES]
    for w in range(wins):
        part = [raw_ref[t, pl.ds(w, span, stride=wins), :] for t in range(2 * tiles)]
        power = [part[t] * part[t] + part[tiles + t] * part[tiles + t] for t in range(tiles)]
        total = power[0]
        for t in range(1, tiles):
            total = total + power[t]
        level = jnp.sum(total, axis=-1, keepdims=True) * (0.01 / bins) + 1e-06
        alive = keep[:, w * LANES : (w + 1) * LANES]
        for t in range(tiles):
            scale = alive * lax.rsqrt(power[t] + level)
            for s in (t, tiles + t):
                value = part[s] * scale
                here = pl.ds(w * length + s * LANES, LANES)
                white_ref[w, :, s * LANES : (s + 1) * LANES] = value
                short_ref[:, here] = value.astype(jnp.bfloat16)


def head_kernel(
    x_hbm,
    valid_hbm,
    offsets_hbm,
    white_ref,
    short_ref,
    table_ref,
    pick_ref,
    keep_ref,
    x_ref,
    valid_ref,
    offsets_ref,
    raw_ref,
    sems,
):
    wins, span, length = white_ref.shape
    pairs = offsets_ref.shape[0]
    copies = [
        pltpu.make_async_copy(valid_hbm, valid_ref, sems.at[0]),
        pltpu.make_async_copy(offsets_hbm, offsets_ref, sems.at[1]),
        pltpu.make_async_copy(x_hbm.at[pl.ds(0, span * wins)], x_ref, sems.at[2]),
    ]
    for copy in copies:
        copy.start()
    fill_table(table_ref, 16)
    copies[0].wait()
    copies[1].wait()
    ahead = lax.broadcasted_iota(jnp.int32, (span, 2 * span), 1) - lax.broadcasted_iota(
        jnp.int32, (span, 2 * span), 0
    )
    for k in range(pairs):
        chosen_row = jnp.where(ahead == offsets_ref[k], jnp.float32(1.0), jnp.float32(0.0))
        pick_ref[k] = chosen_row.astype(jnp.bfloat16)
    owner = lax.broadcasted_iota(jnp.int32, (wins, wins * LANES), 0)
    column = lax.broadcasted_iota(jnp.int32, (wins, wins * LANES), 1) // LANES
    keep_ref[...] = lax.dot_general(
        valid_ref[...].astype(jnp.float32).astype(jnp.bfloat16),
        (owner == column).astype(jnp.float32).astype(jnp.bfloat16),
        (((0,), (0,)), ((), ())),
        preferred_element_type=jnp.float32,
    )
    copies[2].wait()
    whiten_block(x_ref[...], table_ref[...], keep_ref[:span], raw_ref, white_ref, short_ref)


def stack_pairs(pick_ref, white_ref, near_ref, parts_ref, out_ref):
    wins, _, length = white_ref.shape
    pairs, rows, reach = pick_ref.shape
    bins = length // 2
    pick = pick_ref[...].reshape(pairs * rows, reach)
    decay = [float(np.float32(DECAY) ** np.float32(wins - 1 - w)) for w in range(wins)]
    for w in range(wins):
        parts_ref[w] = jnp.dot(
            pick, near_ref[:, w * length : (w + 1) * length], preferred_element_type=jnp.float32
        )
    for c in range(0, rows, 16):
        for t in range(bins // LANES):
            re = slice(t * LANES, (t + 1) * LANES)
            im = slice(bins + t * LANES, bins + (t + 1) * LANES)
            head_re = [white_ref[w, c : c + 16, re] * decay[w] for w in range(wins)]
            head_im = [white_ref[w, c : c + 16, im] * decay[w] for w in range(wins)]
            for k in range(pairs):
                here = slice(k * rows + c, k * rows + c + 16)
                total_re = total_im = None
                for w in range(wins):
                    part_re, part_im = parts_ref[w, here, re], parts_ref[w, here, im]
                    cross_re = head_re[w] * part_re + head_im[w] * part_im
                    cross_im = head_im[w] * part_re - head_re[w] * part_im
                    total_re = cross_re if w == 0 else total_re + cross_re
                    total_im = cross_im if w == 0 else total_im + cross_im
                out_ref[k, c : c + 16, re] = total_re.astype(out_ref.dtype)
                out_ref[k, c : c + 16, im] = total_im.astype(out_ref.dtype)


def tail_kernel(
    x_ref, table_ref, keep_ref, pick_ref, head_ref, edge_ref, white_ref, short_ref, out_ref, raw_ref, near_ref, parts_ref
):
    wins, span, length = white_ref.shape
    rows = slice(span * wins, 2 * span * wins)
    whiten_block(x_ref[rows, :], table_ref[...], keep_ref[span:], raw_ref, white_ref, short_ref)
    near_ref[:span] = edge_ref[...]
    near_ref[span:] = short_ref[...]
    stack_pairs(pick_ref, head_ref, near_ref, parts_ref, out_ref)


def cross_kernel(pick_ref, white_ref, short_ref, edge_ref, out_ref, near_ref, parts_ref):
    span = short_ref.shape[0]
    near_ref[:span] = short_ref[...]
    near_ref[span:] = edge_ref[...]
    stack_pairs(pick_ref, white_ref, near_ref, parts_ref, out_ref)


def chosen(options, place):
    value = jnp.float32(options[0])
    for i, option in enumerate(options[1:]):
        value = jnp.where(place == i + 1, jnp.float32(option), value)
    return value


def weighted(terms, weights, place):
    total = None
    for term, options in zip(terms, weights):
        value = term[...].astype(jnp.float32)
        if set(options) != {1.0}:
            value = value * (options[0] if len(set(options)) == 1 else chosen(options, place))
        total = value if total is None else total + value
    return total


def whereabouts(groups):
    return lax.rem(lax.axis_index("chan"), 2) * groups + lax.axis_index("tm")


def mix_kernel(weights, *refs):
    place = whereabouts(len(weights[0]) // 2)
    total = weighted(refs[: len(weights)], weights, place)
    refs[-1][...] = total.astype(refs[-1].dtype)


def lag_kernel(scale, first, weights, table_ref, *rest):
    out_hbm, stage_ref, sems = rest[-3:]
    place = whereabouts(len(weights[0]) // 2)
    dims = (((1,), (1,)), ((), ()))
    pairs, rows, length = stage_ref.shape
    refs = rest[: len(weights)]
    stack = weighted(refs, weights, place).reshape(pairs * rows, length)
    high = stack.astype(jnp.bfloat16)
    low = (stack - high.astype(jnp.float32)).astype(jnp.bfloat16)
    table = table_ref[...]
    lagged = lax.dot_general(high, table, dims, preferred_element_type=jnp.float32)
    lagged = lagged + lax.dot_general(low, table, dims, preferred_element_type=jnp.float32)
    stage_ref[...] = (lagged * scale).astype(stage_ref.dtype).reshape(pairs, rows, length)
    copy = pltpu.make_async_copy(stage_ref, out_hbm.at[:, pl.ds(first, rows)], sems.at[0])
    copy.start()
    copy.wait()


def cost(flops, moved):
    return pl.CostEstimate(flops=flops, bytes_accessed=moved, transcendentals=0)


def whole(memory=pltpu.VMEM):
    return pl.BlockSpec(memory_space=memory)


def per_device(samples, valid, offsets):
    chans, wins, length = samples.shape
    bins = length // 2
    span = OFFSET_SPAN
    pairs = offsets.shape[0]
    tiles = bins // LANES
    groups = lax.axis_size("tm")
    factor = float(np.float32(DECAY) ** np.float32(wins))
    params = pltpu.CompilerParams(vmem_limit_bytes=VMEM)

    def in_hbm(value):
        return pltpu.with_memory_space_constraint(value, pltpu.HBM)

    half = chans - span
    flat = samples.reshape(chans * wins, length)
    white_type = jax.ShapeDtypeStruct((wins, span, length), jnp.float32)
    short_type = jax.ShapeDtypeStruct((span, wins * length), jnp.bfloat16)
    local_type = jax.ShapeDtypeStruct((pairs, span, length), jnp.bfloat16)
    raw_scratch = pltpu.VMEM((2 * tiles, span * wins, LANES), jnp.float32)
    near_scratch = pltpu.VMEM((2 * span, wins * length), jnp.bfloat16)
    parts_scratch = pltpu.VMEM((wins, pairs * span, length), jnp.float32)

    white_a, short_a, table, pick, keep = pl.pallas_call(
        head_kernel,
        out_shape=(
            white_type,
            short_type,
            jax.ShapeDtypeStruct((length, length), jnp.bfloat16),
            jax.ShapeDtypeStruct((pairs, span, 2 * span), jnp.bfloat16),
            jax.ShapeDtypeStruct((chans, wins * LANES), jnp.float32),
        ),
        in_specs=[whole(pltpu.HBM)] * 3,
        out_specs=(whole(),) * 5,
        scratch_shapes=[
            pltpu.VMEM((span * wins, length), jnp.bfloat16),
            pltpu.VMEM((wins, chans), jnp.int32),
            pltpu.SMEM((pairs,), jnp.int32),
            raw_scratch,
            pltpu.SemaphoreType.DMA((3,)),
        ],
        compiler_params=params,
        cost_estimate=cost(span * wins * length * length * 2, 2 * 1024 * 1024),
        name="head",
    )(in_hbm(flat), in_hbm(valid.T), in_hbm(offsets))

    ring = lax.axis_size("chan")
    edge = lax.ppermute(short_a, "chan", [(i, i - 1) for i in range(1, ring)])

    white_b, short_b, local_a = pl.pallas_call(
        tail_kernel,
        out_shape=(white_type, short_type, local_type),
        in_specs=[whole()] * 6,
        out_specs=(whole(),) * 3,
        scratch_shapes=[raw_scratch, near_scratch, parts_scratch],
        compiler_params=params,
        cost_estimate=cost(span * wins * length * length * 4, 4 * 1024 * 1024),
        name="tail",
    )(flat, table, keep, pick, white_a, short_a)

    local_b = pl.pallas_call(
        cross_kernel,
        out_shape=local_type,
        in_specs=[whole()] * 4,
        out_specs=whole(),
        scratch_shapes=[near_scratch, parts_scratch],
        compiler_params=params,
        cost_estimate=cost(pairs * span * wins * bins * 8, 4 * 1024 * 1024),
        name="cross",
    )(pick, white_b, short_b, edge)

    power = [float(np.float32(factor) ** np.float32(d)) for d in range(groups)]
    columns = min(d for d in range(1, groups + 1) if groups % d == 0 and d * d >= groups)
    square = columns == 2 and groups == columns * columns

    def sent(value, even, odd):
        moves = [
            (c * groups + here, c * groups + there)
            for c in range(ring)
            for here, there in (odd if c % 2 else even)
        ]
        return lax.ppermute(value, ("chan", "tm"), moves)

    def mix(terms, weights, after):
        return pl.pallas_call(
            functools.partial(mix_kernel, weights),
            out_shape=local_type,
            in_specs=[whole()] * len(terms) + [whole(pl.ANY)],
            out_specs=whole(),
            compiler_params=params,
            cost_estimate=cost(len(terms) * terms[0].size * 4, 1024 * 1024),
            name="mix",
        )(*terms, after)

    def lags(first, terms, weights, *so_far):
        return pl.pallas_call(
            functools.partial(lag_kernel, bins**-0.5, first, weights),
            out_shape=jax.ShapeDtypeStruct((pairs, chans, length), jnp.bfloat16),
            in_specs=[whole()] * (1 + len(terms)) + [whole(pl.ANY)] * len(so_far),
            out_specs=whole(pl.ANY),
            scratch_shapes=[
                pltpu.VMEM((pairs, span, length), jnp.bfloat16),
                pltpu.SemaphoreType.DMA((1,)),
            ],
            input_output_aliases={1 + len(terms): 0} if so_far else {},
            compiler_params=params,
            cost_estimate=cost(pairs * span * length * length * 4, 1024 * 1024),
            name="lags",
        )(table, *terms, *so_far)

    unit = [1.0] * (2 * groups)

    def two_hops(local, after):
        f, ff = power[1], power[2]
        got = sent(local, [(0, 2), (1, 3)], [(0, 1), (1, 0), (2, 3)])
        total = mix(
            [local, got],
            [[1.0, 1.0, 1.0, 0.0, f, 1.0, 0.0, 0.0], [ff, ff, ff, 1.0, 1.0, f, 0.0, 0.0]],
            after,
        )
        more = sent(total, [(0, 1), (2, 3), (3, 2)], [(0, 2), (1, 3)])
        weights = [
            unit,
            [ff, ff, ff, ff, 0.0, f, 0.0, f],
            [f, f, f, f, 0.0, 0.0, f, ff],
        ]
        return [local, got, more], weights

    def one_hop(local, after):
        terms, weights = [local], [unit]
        for d in range(1, groups):
            moves = [(h, h + d) for h in range(groups - d)]
            terms.append(sent(local, moves, moves))
            weights.append([power[d]] * (2 * groups))
        return terms, weights

    spread = two_hops if square else one_hop
    result = lags(0, *spread(local_a, local_b))
    result = lags(half, *spread(local_b, local_b), result)
    return result.reshape(1, pairs, chans, length)


def solution(mesh):
    in_specs = (P("chan", "tm", None), P("chan", "tm"), P())
    out_specs = P("tm", None, "chan", None)
    return jax.shard_map(
        per_device, mesh=mesh, in_specs=in_specs, out_specs=out_specs, check_vma=False
    )
```

```python
import functools
import math

import jax
import jax.numpy as jnp
import numpy as np
from jax import lax
from jax.experimental import pallas as pl
from jax.experimental.pallas import tpu as pltpu
from jax.sharding import PartitionSpec as P

OFFSET_SPAN = 32
LANES = 128
DECAY = 0.99
VMEM = 24 * 1024 * 1024


def turns(number, length):
    part = (number - length * jnp.floor(number / length + 0.5)) * (1.0 / length)
    square = part * part
    cosine, sine = jnp.float32(0.0), jnp.float32(0.0)
    for k in range(10, -1, -1):
        cosine = cosine * square + (-1) ** k * (2 * math.pi) ** (2 * k) / math.factorial(2 * k)
        sine = sine * square + (-1) ** k * (2 * math.pi) ** (2 * k + 1) / math.factorial(2 * k + 1)
    return cosine, sine * part


def fill_table(table_ref, step):
    length = table_ref.shape[0]
    bins = length // 2

    def small(rows, by):
        row = lax.broadcasted_iota(jnp.int32, (rows, bins), 0)
        freq = lax.broadcasted_iota(jnp.int32, (rows, bins), 1) + 1
        return turns((row * (by * freq)).astype(jnp.float32), length)

    coarse_cos, coarse_sin = small(length // step, step)
    fine_cos, fine_sin = small(step, 1)
    for i in range(length // step):
        rows = slice(i * step, (i + 1) * step)
        cos_i, sin_i = coarse_cos[i : i + 1], coarse_sin[i : i + 1]
        table_ref[rows, :bins] = (cos_i * fine_cos - sin_i * fine_sin).astype(jnp.bfloat16)
        table_ref[rows, bins:] = -(sin_i * fine_cos + cos_i * fine_sin).astype(jnp.bfloat16)


def whiten_rows(first, rows, x, table, keep, raw_ref, white_ref, short_ref):
    wins, _, length = white_ref.shape
    bins = length // 2
    tiles = bins // LANES
    raw = jnp.dot(x, table, preferred_element_type=jnp.float32)
    for t in range(2 * tiles):
        raw_ref[t, first * wins : (first + rows) * wins] = raw[:, t * LANES : (t + 1) * LANES]
    here = slice(first, first + rows)
    for w in range(wins):
        part = [raw_ref[t, pl.ds(first * wins + w, rows, stride=wins), :] for t in range(2 * tiles)]
        power = [part[t] * part[t] + part[tiles + t] * part[tiles + t] for t in range(tiles)]
        total = power[0]
        for t in range(1, tiles):
            total = total + power[t]
        level = jnp.sum(total, axis=-1, keepdims=True) * (0.01 / bins) + 1e-06
        alive = keep[:, w * LANES : (w + 1) * LANES]
        for t in range(tiles):
            scale = alive * lax.rsqrt(power[t] + level)
            for s in (t, tiles + t):
                value = part[s] * scale
                lanes = slice(w * length + s * LANES, w * length + (s + 1) * LANES)
                white_ref[w, here, s * LANES : (s + 1) * LANES] = value
                short_ref[here, lanes] = value.astype(jnp.bfloat16)


def head_kernel(
    x_hbm,
    valid_hbm,
    offsets_hbm,
    white_ref,
    short_ref,
    table_ref,
    pick_ref,
    keep_ref,
    x_ref,
    valid_ref,
    offsets_ref,
    raw_ref,
    sems,
):
    wins, span, length = white_ref.shape
    pairs = offsets_ref.shape[0]
    rows = 16
    pieces = [pl.ds(c * wins, rows * wins) for c in range(0, span, rows)]
    copies = [
        pltpu.make_async_copy(x_hbm.at[piece], x_ref.at[piece], sems.at[2 + i])
        for i, piece in enumerate(pieces)
    ]
    valid_copy = pltpu.make_async_copy(valid_hbm, valid_ref, sems.at[0])
    offsets_copy = pltpu.make_async_copy(offsets_hbm, offsets_ref, sems.at[1])
    for copy in [valid_copy] + copies + [offsets_copy]:
        copy.start()
    fill_table(table_ref, 16)
    owner = lax.broadcasted_iota(jnp.int32, (wins, wins * LANES), 0)
    column = lax.broadcasted_iota(jnp.int32, (wins, wins * LANES), 1) // LANES
    mine = (owner == column).astype(jnp.float32).astype(jnp.bfloat16)
    valid_copy.wait()
    keep_ref[...] = lax.dot_general(
        valid_ref[...].astype(jnp.float32).astype(jnp.bfloat16),
        mine,
        (((0,), (0,)), ((), ())),
        preferred_element_type=jnp.float32,
    )
    for i, copy in enumerate(copies):
        copy.wait()
        first = i * rows
        x = x_ref[first * wins : (first + rows) * wins, :]
        keep = keep_ref[first : first + rows]
        whiten_rows(first, rows, x, table_ref[...], keep, raw_ref, white_ref, short_ref)
    offsets_copy.wait()
    ahead = lax.broadcasted_iota(jnp.int32, (span, 2 * span), 1) - lax.broadcasted_iota(
        jnp.int32, (span, 2 * span), 0
    )
    for k in range(pairs):
        row = jnp.where(ahead == offsets_ref[k], jnp.float32(1.0), jnp.float32(0.0))
        pick_ref[k] = row.astype(jnp.bfloat16)


def stack_pairs(pick_ref, white_ref, near_ref, parts_refs, out_ref):
    wins, _, length = white_ref.shape
    pairs, rows, reach = pick_ref.shape
    bins = length // 2
    decay = [float(np.float32(DECAY) ** np.float32(wins - 1 - w)) for w in range(wins)]
    size = pairs // len(parts_refs)
    for group, parts_ref in enumerate(parts_refs):
        pick = pick_ref[group * size : (group + 1) * size].reshape(size * rows, reach)
        for w in range(wins):
            near = near_ref[:, w * length : (w + 1) * length]
            parts_ref[w] = jnp.dot(pick, near, preferred_element_type=jnp.float32)
    for group, parts_ref in enumerate(parts_refs):
        for c in range(0, rows, 16):
            for t in range(bins // LANES):
                re = slice(t * LANES, (t + 1) * LANES)
                im = slice(bins + t * LANES, bins + (t + 1) * LANES)
                head_re = [white_ref[w, c : c + 16, re] * decay[w] for w in range(wins)]
                head_im = [white_ref[w, c : c + 16, im] * decay[w] for w in range(wins)]
                for k in range(size):
                    here = slice(k * rows + c, k * rows + c + 16)
                    total_re = total_im = None
                    for w in range(wins):
                        part_re, part_im = parts_ref[w, here, re], parts_ref[w, here, im]
                        cross_re = head_re[w] * part_re + head_im[w] * part_im
                        cross_im = head_im[w] * part_re - head_re[w] * part_im
                        total_re = cross_re if w == 0 else total_re + cross_re
                        total_im = cross_im if w == 0 else total_im + cross_im
                    pair = group * size + k
                    out_ref[pair, c : c + 16, re] = total_re.astype(out_ref.dtype)
                    out_ref[pair, c : c + 16, im] = total_im.astype(out_ref.dtype)


def tail_kernel(
    x_ref, table_ref, keep_ref, pick_ref, head_ref, edge_ref, white_ref, short_ref, out_ref, raw_ref, near_ref, *parts_refs
):
    wins, span, length = white_ref.shape
    near_ref[:span] = edge_ref[...]
    rows = 16
    for first in range(0, span, rows):
        at = span + first
        x = x_ref[at * wins : (at + rows) * wins, :]
        keep = keep_ref[at : at + rows]
        whiten_rows(first, rows, x, table_ref[...], keep, raw_ref, white_ref, short_ref)
    near_ref[span:] = short_ref[...]
    stack_pairs(pick_ref, head_ref, near_ref, parts_refs, out_ref)


def cross_kernel(pick_ref, white_ref, short_ref, edge_ref, out_ref, near_ref, *parts_refs):
    span = short_ref.shape[0]
    near_ref[:span] = short_ref[...]
    near_ref[span:] = edge_ref[...]
    stack_pairs(pick_ref, white_ref, near_ref, parts_refs, out_ref)


def chosen(options, place):
    value = jnp.float32(options[0])
    for i, option in enumerate(options[1:]):
        value = jnp.where(place == i + 1, jnp.float32(option), value)
    return value


def weighted(terms, weights, place):
    total = None
    for term, options in zip(terms, weights):
        value = term[...].astype(jnp.float32)
        if set(options) != {1.0}:
            value = value * (options[0] if len(set(options)) == 1 else chosen(options, place))
        total = value if total is None else total + value
    return total


def whereabouts(groups):
    return lax.rem(lax.axis_index("chan"), 2) * groups + lax.axis_index("tm")


def mix_kernel(weights, *refs):
    place = whereabouts(len(weights[0]) // 2)
    total = weighted(refs[: len(weights)], weights, place)
    refs[-1][...] = total.astype(refs[-1].dtype)


def lag_kernel(scale, first, weights, table_ref, *rest):
    out_hbm, stage_ref, sems = rest[-3:]
    place = whereabouts(len(weights[0]) // 2)
    dims = (((1,), (1,)), ((), ()))
    pairs, rows, length = stage_ref.shape
    size = pairs // 2
    copies = []
    for piece in range(2):
        here = pl.ds(piece * size, size)
        refs = [ref.at[here] for ref in rest[: len(weights)]]
        stack = weighted(refs, weights, place).reshape(size * rows, length)
        high = stack.astype(jnp.bfloat16)
        low = (stack - high.astype(jnp.float32)).astype(jnp.bfloat16)
        table = table_ref[...]
        lagged = lax.dot_general(high, table, dims, preferred_element_type=jnp.float32)
        lagged = lagged + lax.dot_general(low, table, dims, preferred_element_type=jnp.float32)
        stage_ref[here] = (lagged * scale).astype(stage_ref.dtype).reshape(size, rows, length)
        there = out_hbm.at[here, pl.ds(first, rows)]
        copies.append(pltpu.make_async_copy(stage_ref.at[here], there, sems.at[piece]))
        copies[-1].start()
    for copy in copies:
        copy.wait()


def cost(flops, moved):
    return pl.CostEstimate(flops=flops, bytes_accessed=moved, transcendentals=0)


def whole(memory=pltpu.VMEM):
    return pl.BlockSpec(memory_space=memory)


def per_device(samples, valid, offsets):
    chans, wins, length = samples.shape
    bins = length // 2
    span = OFFSET_SPAN
    pairs = offsets.shape[0]
    tiles = bins // LANES
    groups = lax.axis_size("tm")
    factor = float(np.float32(DECAY) ** np.float32(wins))
    params = pltpu.CompilerParams(vmem_limit_bytes=VMEM)

    def in_hbm(value):
        return pltpu.with_memory_space_constraint(value, pltpu.HBM)

    half = chans - span
    flat = samples.reshape(chans * wins, length)
    white_type = jax.ShapeDtypeStruct((wins, span, length), jnp.float32)
    short_type = jax.ShapeDtypeStruct((span, wins * length), jnp.bfloat16)
    local_type = jax.ShapeDtypeStruct((pairs, span, length), jnp.bfloat16)
    raw_scratch = pltpu.VMEM((2 * tiles, span * wins, LANES), jnp.float32)
    near_scratch = pltpu.VMEM((2 * span, wins * length), jnp.bfloat16)
    parts_scratch = [pltpu.VMEM((wins, pairs // 2 * span, length), jnp.float32)] * 2

    white_a, short_a, table, pick, keep = pl.pallas_call(
        head_kernel,
        out_shape=(
            white_type,
            short_type,
            jax.ShapeDtypeStruct((length, length), jnp.bfloat16),
            jax.ShapeDtypeStruct((pairs, span, 2 * span), jnp.bfloat16),
            jax.ShapeDtypeStruct((chans, wins * LANES), jnp.float32),
        ),
        in_specs=[whole(pltpu.HBM)] * 3,
        out_specs=(whole(),) * 5,
        scratch_shapes=[
            pltpu.VMEM((span * wins, length), jnp.bfloat16),
            pltpu.VMEM((wins, chans), jnp.int32),
            pltpu.SMEM((pairs,), jnp.int32),
            raw_scratch,
            pltpu.SemaphoreType.DMA((2 + span // 16,)),
        ],
        compiler_params=params,
        cost_estimate=cost(span * wins * length * length * 2, 2 * 1024 * 1024),
        name="head",
    )(in_hbm(flat), in_hbm(valid.T), in_hbm(offsets))

    ring = lax.axis_size("chan")
    edge = lax.ppermute(short_a, "chan", [(i, i - 1) for i in range(1, ring)])

    white_b, short_b, local_a = pl.pallas_call(
        tail_kernel,
        out_shape=(white_type, short_type, local_type),
        in_specs=[whole()] * 6,
        out_specs=(whole(),) * 3,
        scratch_shapes=[raw_scratch, near_scratch] + parts_scratch,
        compiler_params=params,
        cost_estimate=cost(span * wins * length * length * 4, 4 * 1024 * 1024),
        name="tail",
    )(flat, table, keep, pick, white_a, short_a)

    local_b = pl.pallas_call(
        cross_kernel,
        out_shape=local_type,
        in_specs=[whole()] * 4,
        out_specs=whole(),
        scratch_shapes=[near_scratch] + parts_scratch,
        compiler_params=params,
        cost_estimate=cost(pairs * span * wins * bins * 8, 4 * 1024 * 1024),
        name="cross",
    )(pick, white_b, short_b, edge)

    power = [float(np.float32(factor) ** np.float32(d)) for d in range(groups)]
    columns = min(d for d in range(1, groups + 1) if groups % d == 0 and d * d >= groups)
    square = columns == 2 and groups == columns * columns

    def sent(value, even, odd):
        moves = [
            (c * groups + here, c * groups + there)
            for c in range(ring)
            for here, there in (odd if c % 2 else even)
        ]
        return lax.ppermute(value, ("chan", "tm"), moves)

    def mix(terms, weights, after):
        return pl.pallas_call(
            functools.partial(mix_kernel, weights),
            out_shape=local_type,
            in_specs=[whole()] * len(terms) + [whole(pl.ANY)],
            out_specs=whole(),
            compiler_params=params,
            cost_estimate=cost(len(terms) * terms[0].size * 4, 1024 * 1024),
            name="mix",
        )(*terms, after)

    def lags(first, terms, weights, *so_far):
        return pl.pallas_call(
            functools.partial(lag_kernel, bins**-0.5, first, weights),
            out_shape=jax.ShapeDtypeStruct((pairs, chans, length), jnp.bfloat16),
            in_specs=[whole()] * (1 + len(terms)) + [whole(pl.ANY)] * len(so_far),
            out_specs=whole(pl.ANY),
            scratch_shapes=[
                pltpu.VMEM((pairs, span, length), jnp.bfloat16),
                pltpu.SemaphoreType.DMA((2,)),
            ],
            input_output_aliases={1 + len(terms): 0} if so_far else {},
            compiler_params=params,
            cost_estimate=cost(pairs * span * length * length * 4, 1024 * 1024),
            name="lags",
        )(table, *terms, *so_far)

    unit = [1.0] * (2 * groups)

    def two_hops(local, after):
        f, ff = power[1], power[2]
        got = sent(local, [(0, 2), (1, 3)], [(0, 1), (1, 0), (2, 3)])
        total = mix(
            [local, got],
            [[1.0, 1.0, 1.0, 0.0, f, 1.0, 0.0, 0.0], [ff, ff, ff, 1.0, 1.0, f, 0.0, 0.0]],
            after,
        )
        more = sent(total, [(0, 1), (2, 3), (3, 2)], [(0, 2), (1, 3)])
        weights = [
            unit,
            [ff, ff, ff, ff, 0.0, f, 0.0, f],
            [f, f, f, f, 0.0, 0.0, f, ff],
        ]
        return [local, got, more], weights

    def one_hop(local, after):
        terms, weights = [local], [unit]
        for d in range(1, groups):
            moves = [(h, h + d) for h in range(groups - d)]
            terms.append(sent(local, moves, moves))
            weights.append([power[d]] * (2 * groups))
        return terms, weights

    spread = two_hops if square else one_hop
    result = lags(0, *spread(local_a, local_b))
    result = lags(half, *spread(local_b, local_b), result)
    return result.reshape(1, pairs, chans, length)


def solution(mesh):
    in_specs = (P("chan", "tm", None), P("chan", "tm"), P())
    out_specs = P("tm", None, "chan", None)
    return jax.shard_map(
        per_device, mesh=mesh, in_specs=in_specs, out_specs=out_specs, check_vma=False
    )
```

```python
import functools
import math

import jax
import jax.numpy as jnp
import numpy as np
from jax import lax
from jax.experimental import pallas as pl
from jax.experimental.pallas import tpu as pltpu
from jax.sharding import PartitionSpec as P

OFFSET_SPAN = 32
LANES = 128
DECAY = 0.99
VMEM = 24 * 1024 * 1024


def turns(number, length):
    part = (number - length * jnp.floor(number / length + 0.5)) * (1.0 / length)
    square = part * part
    cosine, sine = jnp.float32(0.0), jnp.float32(0.0)
    for k in range(10, -1, -1):
        cosine = cosine * square + (-1) ** k * (2 * math.pi) ** (2 * k) / math.factorial(2 * k)
        sine = sine * square + (-1) ** k * (2 * math.pi) ** (2 * k + 1) / math.factorial(2 * k + 1)
    return cosine, sine * part


def fill_table(table_ref, step):
    length = table_ref.shape[0]
    bins = length // 2

    def small(rows, by):
        row = lax.broadcasted_iota(jnp.int32, (rows, bins), 0)
        freq = lax.broadcasted_iota(jnp.int32, (rows, bins), 1) + 1
        return turns((row * (by * freq)).astype(jnp.float32), length)

    coarse_cos, coarse_sin = small(length // step, step)
    fine_cos, fine_sin = small(step, 1)
    for i in range(length // step):
        rows = slice(i * step, (i + 1) * step)
        cos_i, sin_i = coarse_cos[i : i + 1], coarse_sin[i : i + 1]
        table_ref[rows, :bins] = (cos_i * fine_cos - sin_i * fine_sin).astype(jnp.bfloat16)
        table_ref[rows, bins:] = -(sin_i * fine_cos + cos_i * fine_sin).astype(jnp.bfloat16)


def inverse_kernel(_, table_ref):
    length = table_ref.shape[0]
    bins = length // 2
    step = 16

    def small(rows, by, first):
        freq = (lax.broadcasted_iota(jnp.int32, (rows, length), 0) + first) * by
        lag = lax.broadcasted_iota(jnp.int32, (rows, length), 1)
        return turns((freq * lag).astype(jnp.float32), length)

    coarse_cos, coarse_sin = small(bins // step, step, 0)
    fine_cos, fine_sin = small(step, 1, 1)
    for i in range(bins // step):
        first = i * step
        cos_i, sin_i = coarse_cos[i : i + 1], coarse_sin[i : i + 1]
        cosine = cos_i * fine_cos - sin_i * fine_sin
        sine = sin_i * fine_cos + cos_i * fine_sin
        table_ref[first : first + step, :] = cosine.astype(jnp.bfloat16)
        table_ref[bins + first : bins + first + step, :] = (-sine).astype(jnp.bfloat16)


def whiten_block(x, table, keep, raw_ref, white_ref, short_ref):
    wins, span, length = white_ref.shape
    bins = length // 2
    tiles = bins // LANES
    raw = jnp.dot(x, table, preferred_element_type=jnp.float32)
    for t in range(2 * tiles):
        raw_ref[t] = raw[:, t * LANES : (t + 1) * LANES]
    for w in range(wins):
        part = [raw_ref[t, pl.ds(w, span, stride=wins), :] for t in range(2 * tiles)]
        power = [part[t] * part[t] + part[tiles + t] * part[tiles + t] for t in range(tiles)]
        total = power[0]
        for t in range(1, tiles):
            total = total + power[t]
        level = jnp.sum(total, axis=-1, keepdims=True) * (0.01 / bins) + 1e-06
        alive = keep[:, w * LANES : (w + 1) * LANES]
        for t in range(tiles):
            scale = alive * lax.rsqrt(power[t] + level)
            for s in (t, tiles + t):
                value = part[s] * scale
                here = pl.ds(w * length + s * LANES, LANES)
                white_ref[w, :, s * LANES : (s + 1) * LANES] = value
                short_ref[:, here] = value.astype(jnp.bfloat16)


def head_kernel(
    x_hbm,
    valid_hbm,
    offsets_hbm,
    white_ref,
    short_ref,
    table_ref,
    pick_ref,
    keep_ref,
    x_ref,
    valid_ref,
    offsets_ref,
    raw_ref,
    sems,
):
    wins, span, length = white_ref.shape
    pairs = offsets_ref.shape[0]
    valid_copy = pltpu.make_async_copy(valid_hbm, valid_ref, sems.at[0])
    x_copy = pltpu.make_async_copy(x_hbm.at[pl.ds(0, span * wins)], x_ref, sems.at[1])
    offsets_copy = pltpu.make_async_copy(offsets_hbm, offsets_ref, sems.at[2])
    for copy in (x_copy, valid_copy, offsets_copy):
        copy.start()
    fill_table(table_ref, 16)
    owner = lax.broadcasted_iota(jnp.int32, (wins, wins * LANES), 0)
    column = lax.broadcasted_iota(jnp.int32, (wins, wins * LANES), 1) // LANES
    mine = (owner == column).astype(jnp.float32).astype(jnp.bfloat16)
    valid_copy.wait()
    keep_ref[...] = lax.dot_general(
        valid_ref[...].astype(jnp.float32).astype(jnp.bfloat16),
        mine,
        (((0,), (0,)), ((), ())),
        preferred_element_type=jnp.float32,
    )
    x_copy.wait()
    whiten_block(x_ref[...], table_ref[...], keep_ref[:span], raw_ref, white_ref, short_ref)
    offsets_copy.wait()
    ahead = lax.broadcasted_iota(jnp.int32, (span, 2 * span), 1) - lax.broadcasted_iota(
        jnp.int32, (span, 2 * span), 0
    )
    for k in range(pairs):
        row = jnp.where(ahead == offsets_ref[k], jnp.float32(1.0), jnp.float32(0.0))
        pick_ref[k] = row.astype(jnp.bfloat16)


def stack_pairs(pick_ref, white_ref, near_ref, parts_ref, out_ref):
    wins, _, length = white_ref.shape
    pairs, rows, reach = pick_ref.shape
    bins = length // 2
    pick = pick_ref[...].reshape(pairs * rows, reach)
    decay = [float(np.float32(DECAY) ** np.float32(wins - 1 - w)) for w in range(wins)]
    for w in range(wins):
        parts_ref[w] = jnp.dot(
            pick, near_ref[:, w * length : (w + 1) * length], preferred_element_type=jnp.float32
        )
    for c in range(0, rows, 16):
        for t in range(bins // LANES):
            re = slice(t * LANES, (t + 1) * LANES)
            im = slice(bins + t * LANES, bins + (t + 1) * LANES)
            head_re = [white_ref[w, c : c + 16, re] * decay[w] for w in range(wins)]
            head_im = [white_ref[w, c : c + 16, im] * decay[w] for w in range(wins)]
            for k in range(pairs):
                here = slice(k * rows + c, k * rows + c + 16)
                total_re = total_im = None
                for w in range(wins):
                    part_re, part_im = parts_ref[w, here, re], parts_ref[w, here, im]
                    cross_re = head_re[w] * part_re + head_im[w] * part_im
                    cross_im = head_im[w] * part_re - head_re[w] * part_im
                    total_re = cross_re if w == 0 else total_re + cross_re
                    total_im = cross_im if w == 0 else total_im + cross_im
                out_ref[k, c : c + 16, re] = total_re.astype(out_ref.dtype)
                out_ref[k, c : c + 16, im] = total_im.astype(out_ref.dtype)


def tail_kernel(
    x_ref, table_ref, keep_ref, pick_ref, head_ref, edge_ref, white_ref, short_ref, out_ref, raw_ref, near_ref, parts_ref
):
    wins, span, length = white_ref.shape
    rows = slice(span * wins, 2 * span * wins)
    whiten_block(x_ref[rows, :], table_ref[...], keep_ref[span:], raw_ref, white_ref, short_ref)
    near_ref[:span] = edge_ref[...]
    near_ref[span:] = short_ref[...]
    stack_pairs(pick_ref, head_ref, near_ref, parts_ref, out_ref)


def cross_kernel(pick_ref, white_ref, short_ref, edge_ref, out_ref, near_ref, parts_ref):
    span = short_ref.shape[0]
    near_ref[:span] = short_ref[...]
    near_ref[span:] = edge_ref[...]
    stack_pairs(pick_ref, white_ref, near_ref, parts_ref, out_ref)


def chosen(options, place):
    value = jnp.float32(options[0])
    for i, option in enumerate(options[1:]):
        value = jnp.where(place == i + 1, jnp.float32(option), value)
    return value


def weighted(terms, weights, place):
    total = None
    for term, options in zip(terms, weights):
        value = term[...].astype(jnp.float32)
        if set(options) != {1.0}:
            value = value * (options[0] if len(set(options)) == 1 else chosen(options, place))
        total = value if total is None else total + value
    return total


def whereabouts(groups):
    return lax.rem(lax.axis_index("chan"), 2) * groups + lax.axis_index("tm")


def mix_kernel(weights, *refs):
    place = whereabouts(len(weights[0]) // 2)
    total = weighted(refs[: len(weights)], weights, place)
    refs[-1][...] = total.astype(refs[-1].dtype)


def lag_kernel(scale, first, weights, table_ref, *rest):
    out_hbm, stage_ref, sems = rest[-3:]
    place = whereabouts(len(weights[0]) // 2)
    pairs, rows, length = stage_ref.shape
    count = pairs * rows
    stack = weighted(rest[: len(weights)], weights, place).reshape(count, length)
    high = stack.astype(jnp.bfloat16)
    low = (stack - high.astype(jnp.float32)).astype(jnp.bfloat16)
    both = jnp.concatenate([high, low], axis=0)
    copies = []
    for half in range(2):
        lanes = pl.ds(half * length // 2, length // 2)
        lagged = jnp.dot(both, table_ref[:, lanes], preferred_element_type=jnp.float32)
        lagged = (lagged[:count] + lagged[count:]) * scale
        stage_ref[:, :, lanes] = lagged.astype(stage_ref.dtype).reshape(pairs, rows, length // 2)
        there = out_hbm.at[:, pl.ds(first, rows), lanes]
        copies.append(pltpu.make_async_copy(stage_ref.at[:, :, lanes], there, sems.at[half]))
        copies[-1].start()
    for copy in copies:
        copy.wait()


def cost(flops, moved):
    return pl.CostEstimate(flops=flops, bytes_accessed=moved, transcendentals=0)


def whole(memory=pltpu.VMEM):
    return pl.BlockSpec(memory_space=memory)


def per_device(samples, valid, offsets):
    chans, wins, length = samples.shape
    bins = length // 2
    span = OFFSET_SPAN
    pairs = offsets.shape[0]
    tiles = bins // LANES
    groups = lax.axis_size("tm")
    factor = float(np.float32(DECAY) ** np.float32(wins))
    params = pltpu.CompilerParams(vmem_limit_bytes=VMEM)

    def in_hbm(value):
        return pltpu.with_memory_space_constraint(value, pltpu.HBM)

    half = chans - span
    flat = samples.reshape(chans * wins, length)
    white_type = jax.ShapeDtypeStruct((wins, span, length), jnp.float32)
    short_type = jax.ShapeDtypeStruct((span, wins * length), jnp.bfloat16)
    local_type = jax.ShapeDtypeStruct((pairs, span, length), jnp.bfloat16)
    raw_scratch = pltpu.VMEM((2 * tiles, span * wins, LANES), jnp.float32)
    near_scratch = pltpu.VMEM((2 * span, wins * length), jnp.bfloat16)
    parts_scratch = pltpu.VMEM((wins, pairs * span, length), jnp.float32)

    white_a, short_a, table, pick, keep = pl.pallas_call(
        head_kernel,
        out_shape=(
            white_type,
            short_type,
            jax.ShapeDtypeStruct((length, length), jnp.bfloat16),
            jax.ShapeDtypeStruct((pairs, span, 2 * span), jnp.bfloat16),
            jax.ShapeDtypeStruct((chans, wins * LANES), jnp.float32),
        ),
        in_specs=[whole(pltpu.HBM)] * 3,
        out_specs=(whole(),) * 5,
        scratch_shapes=[
            pltpu.VMEM((span * wins, length), jnp.bfloat16),
            pltpu.VMEM((wins, chans), jnp.int32),
            pltpu.SMEM((pairs,), jnp.int32),
            raw_scratch,
            pltpu.SemaphoreType.DMA((3,)),
        ],
        compiler_params=params,
        cost_estimate=cost(span * wins * length * length * 2, 2 * 1024 * 1024),
        name="head",
    )(in_hbm(flat), in_hbm(valid.T), in_hbm(offsets))

    ring = lax.axis_size("chan")
    edge = lax.ppermute(short_a, "chan", [(i, i - 1) for i in range(1, ring)])

    white_b, short_b, local_a = pl.pallas_call(
        tail_kernel,
        out_shape=(white_type, short_type, local_type),
        in_specs=[whole()] * 6,
        out_specs=(whole(),) * 3,
        scratch_shapes=[raw_scratch, near_scratch, parts_scratch],
        compiler_params=params,
        cost_estimate=cost(span * wins * length * length * 4, 4 * 1024 * 1024),
        name="tail",
    )(flat, table, keep, pick, white_a, short_a)

    local_b = pl.pallas_call(
        cross_kernel,
        out_shape=local_type,
        in_specs=[whole()] * 4,
        out_specs=whole(),
        scratch_shapes=[near_scratch, parts_scratch],
        compiler_params=params,
        cost_estimate=cost(pairs * span * wins * bins * 8, 4 * 1024 * 1024),
        name="cross",
    )(pick, white_b, short_b, edge)

    power = [float(np.float32(factor) ** np.float32(d)) for d in range(groups)]
    columns = min(d for d in range(1, groups + 1) if groups % d == 0 and d * d >= groups)
    square = columns == 2 and groups == columns * columns

    def sent(value, even, odd):
        moves = [
            (c * groups + here, c * groups + there)
            for c in range(ring)
            for here, there in (odd if c % 2 else even)
        ]
        return lax.ppermute(value, ("chan", "tm"), moves)

    def mix(terms, weights, after):
        return pl.pallas_call(
            functools.partial(mix_kernel, weights),
            out_shape=local_type,
            in_specs=[whole()] * len(terms) + [whole(pl.ANY)],
            out_specs=whole(),
            compiler_params=params,
            cost_estimate=cost(len(terms) * terms[0].size * 4, 1024 * 1024),
            name="mix",
        )(*terms, after)

    inverse = pl.pallas_call(
        inverse_kernel,
        out_shape=jax.ShapeDtypeStruct((length, length), jnp.bfloat16),
        in_specs=[whole(pl.ANY)],
        out_specs=whole(),
        compiler_params=params,
        cost_estimate=cost(length * bins * 32, 512 * 1024),
        name="inverse",
    )(local_b)

    def lags(first, terms, weights, later, *so_far):
        so_far = list(so_far)
        return pl.pallas_call(
            functools.partial(lag_kernel, bins**-0.5, first, weights),
            out_shape=jax.ShapeDtypeStruct((pairs, chans, length), jnp.bfloat16),
            in_specs=[whole()] * (1 + len(terms)) + [whole(pl.ANY)] * len(later + so_far),
            out_specs=whole(pl.ANY),
            scratch_shapes=[
                pltpu.VMEM((pairs, span, length), jnp.bfloat16),
                pltpu.SemaphoreType.DMA((2,)),
            ],
            input_output_aliases={1 + len(terms + later): 0} if so_far else {},
            compiler_params=params,
            cost_estimate=cost(pairs * span * length * length * 4, 1024 * 1024),
            name="lags",
        )(inverse, *terms, *later, *so_far)

    unit = [1.0] * (2 * groups)

    def two_hops(local, after, apart):
        f, ff = power[1], power[2]
        last = [(2, 3)]
        got = sent(local, [(0, 2), (1, 3)], [(0, 1), (1, 0)] + ([] if apart else last))
        alone = [sent(local, [], last)] if apart else []
        total = mix(
            [local, got],
            [[1.0, 1.0, 1.0, 0.0, f, 1.0, 0.0, 0.0], [ff, ff, ff, 1.0, 1.0, f, 0.0, 0.0]],
            after,
        )
        more = sent(total, [(0, 1), (2, 3), (3, 2)], [(0, 2), (1, 3)])
        weights = [
            unit,
            [ff, ff, ff, ff, 0.0, f, 0.0, f],
            [f, f, f, f, 0.0, 0.0, f, ff],
        ] + [[f] * (2 * groups)] * len(alone)
        return [local, got, more] + alone, weights

    def one_hop(local, after, apart):
        terms, weights = [local], [unit]
        for d in range(1, groups):
            moves = [(h, h + d) for h in range(groups - d)]
            terms.append(sent(local, moves, moves))
            weights.append([power[d]] * (2 * groups))
        return terms, weights

    spread = two_hops if square else one_hop
    terms_a, weights_a = spread(local_a, local_b, False)
    terms_b, weights_b = spread(local_b, local_b, True)
    result = lags(0, terms_a, weights_a, terms_b[3:4])
    result = lags(half, terms_b, weights_b, [], result)
    return result.reshape(1, pairs, chans, length)


def solution(mesh):
    in_specs = (P("chan", "tm", None), P("chan", "tm"), P())
    out_specs = P("tm", None, "chan", None)
    return jax.shard_map(
        per_device, mesh=mesh, in_specs=in_specs, out_specs=out_specs, check_vma=False
    )
```

```python
import functools
import math

import jax
import jax.numpy as jnp
import numpy as np
from jax import lax
from jax.experimental import pallas as pl
from jax.experimental.pallas import tpu as pltpu
from jax.sharding import PartitionSpec as P

OFFSET_SPAN = 32
LANES = 128
DECAY = 0.99
VMEM = 24 * 1024 * 1024


def turns(number, length):
    part = (number - length * jnp.floor(number / length + 0.5)) * (1.0 / length)
    square = part * part
    cosine, sine = jnp.float32(0.0), jnp.float32(0.0)
    for k in range(10, -1, -1):
        cosine = cosine * square + (-1) ** k * (2 * math.pi) ** (2 * k) / math.factorial(2 * k)
        sine = sine * square + (-1) ** k * (2 * math.pi) ** (2 * k + 1) / math.factorial(2 * k + 1)
    return cosine, sine * part


def fill_table(table_ref, step):
    length = table_ref.shape[0]
    bins = length // 2

    def small(rows, by):
        row = lax.broadcasted_iota(jnp.int32, (rows, bins), 0)
        freq = lax.broadcasted_iota(jnp.int32, (rows, bins), 1) + 1
        return turns((row * (by * freq)).astype(jnp.float32), length)

    coarse_cos, coarse_sin = small(length // step, step)
    fine_cos, fine_sin = small(step, 1)
    for i in range(length // step):
        rows = slice(i * step, (i + 1) * step)
        cos_i, sin_i = coarse_cos[i : i + 1], coarse_sin[i : i + 1]
        table_ref[rows, :bins] = (cos_i * fine_cos - sin_i * fine_sin).astype(jnp.bfloat16)
        table_ref[rows, bins:] = -(sin_i * fine_cos + cos_i * fine_sin).astype(jnp.bfloat16)


def inverse_kernel(_, table_ref):
    length = table_ref.shape[0]
    bins = length // 2
    step = 16

    def small(rows, by, first):
        freq = (lax.broadcasted_iota(jnp.int32, (rows, length), 0) + first) * by
        lag = lax.broadcasted_iota(jnp.int32, (rows, length), 1)
        return turns((freq * lag).astype(jnp.float32), length)

    coarse_cos, coarse_sin = small(bins // step, step, 0)
    fine_cos, fine_sin = small(step, 1, 1)
    for i in range(bins // step):
        first = i * step
        cos_i, sin_i = coarse_cos[i : i + 1], coarse_sin[i : i + 1]
        cosine = cos_i * fine_cos - sin_i * fine_sin
        sine = sin_i * fine_cos + cos_i * fine_sin
        table_ref[first : first + step, :] = cosine.astype(jnp.bfloat16)
        table_ref[bins + first : bins + first + step, :] = (-sine).astype(jnp.bfloat16)


def whiten_block(x, table, keep, raw_ref, white_ref, short_ref):
    wins, span, length = white_ref.shape
    bins = length // 2
    tiles = bins // LANES
    raw = jnp.dot(x, table, preferred_element_type=jnp.float32)
    for t in range(2 * tiles):
        raw_ref[t] = raw[:, t * LANES : (t + 1) * LANES]
    for w in range(wins):
        part = [raw_ref[t, pl.ds(w, span, stride=wins), :] for t in range(2 * tiles)]
        power = [part[t] * part[t] + part[tiles + t] * part[tiles + t] for t in range(tiles)]
        total = power[0]
        for t in range(1, tiles):
            total = total + power[t]
        level = jnp.sum(total, axis=-1, keepdims=True) * (0.01 / bins) + 1e-06
        alive = keep[:, w * LANES : (w + 1) * LANES]
        for t in range(tiles):
            scale = alive * lax.rsqrt(power[t] + level)
            for s in (t, tiles + t):
                value = part[s] * scale
                here = pl.ds(w * length + s * LANES, LANES)
                white_ref[w, :, s * LANES : (s + 1) * LANES] = value
                short_ref[:, here] = value.astype(jnp.bfloat16)


def head_kernel(
    x_hbm,
    valid_hbm,
    offsets_hbm,
    white_ref,
    short_ref,
    table_ref,
    pick_ref,
    keep_ref,
    x_ref,
    valid_ref,
    offsets_ref,
    raw_ref,
    sems,
):
    wins, span, length = white_ref.shape
    pairs = offsets_ref.shape[0]
    copies = [
        pltpu.make_async_copy(valid_hbm, valid_ref, sems.at[0]),
        pltpu.make_async_copy(offsets_hbm, offsets_ref, sems.at[1]),
        pltpu.make_async_copy(x_hbm.at[pl.ds(0, span * wins)], x_ref, sems.at[2]),
    ]
    for copy in copies:
        copy.start()
    fill_table(table_ref, 16)
    copies[0].wait()
    copies[1].wait()
    ahead = lax.broadcasted_iota(jnp.int32, (span, 2 * span), 1) - lax.broadcasted_iota(
        jnp.int32, (span, 2 * span), 0
    )
    for k in range(pairs):
        chosen_row = jnp.where(ahead == offsets_ref[k], jnp.float32(1.0), jnp.float32(0.0))
        pick_ref[k] = chosen_row.astype(jnp.bfloat16)
    owner = lax.broadcasted_iota(jnp.int32, (wins, wins * LANES), 0)
    column = lax.broadcasted_iota(jnp.int32, (wins, wins * LANES), 1) // LANES
    keep_ref[...] = lax.dot_general(
        valid_ref[...].astype(jnp.float32).astype(jnp.bfloat16),
        (owner == column).astype(jnp.float32).astype(jnp.bfloat16),
        (((0,), (0,)), ((), ())),
        preferred_element_type=jnp.float32,
    )
    copies[2].wait()
    whiten_block(x_ref[...], table_ref[...], keep_ref[:span], raw_ref, white_ref, short_ref)


def stack_pairs(pick_ref, white_ref, near_ref, parts_refs, out_ref):
    wins, _, length = white_ref.shape
    pairs, rows, reach = pick_ref.shape
    bins = length // 2
    decay = [float(np.float32(DECAY) ** np.float32(wins - 1 - w)) for w in range(wins)]
    size = pairs // len(parts_refs)

    def select(group, w):
        pick = pick_ref[group * size : (group + 1) * size].reshape(size * rows, reach)
        near = near_ref[:, w * length : (w + 1) * length]
        parts_refs[group][w] = jnp.dot(pick, near, preferred_element_type=jnp.float32)

    def gather(group, c, t, k):
        parts_ref = parts_refs[group]
        re = slice(t * LANES, (t + 1) * LANES)
        im = slice(bins + t * LANES, bins + (t + 1) * LANES)
        here = slice(k * rows + c, k * rows + c + 16)
        total_re = total_im = None
        for w in range(wins):
            head_re = white_ref[w, c : c + 16, re] * decay[w]
            head_im = white_ref[w, c : c + 16, im] * decay[w]
            part_re, part_im = parts_ref[w, here, re], parts_ref[w, here, im]
            cross_re = head_re * part_re + head_im * part_im
            cross_im = head_im * part_re - head_re * part_im
            total_re = cross_re if w == 0 else total_re + cross_re
            total_im = cross_im if w == 0 else total_im + cross_im
        pair = group * size + k
        out_ref[pair, c : c + 16, re] = total_re.astype(out_ref.dtype)
        out_ref[pair, c : c + 16, im] = total_im.astype(out_ref.dtype)

    blocks = [(c, t, k) for c in range(0, rows, 16) for t in range(bins // LANES) for k in range(size)]
    for w in range(wins):
        select(0, w)
    for group in range(len(parts_refs)):
        ahead = list(range(wins)) if group + 1 < len(parts_refs) else []
        for i, block in enumerate(blocks):
            while ahead and len(blocks) * (wins - len(ahead)) <= i * wins:
                select(group + 1, ahead.pop(0))
            gather(group, *block)
        for w in ahead:
            select(group + 1, w)


def tail_kernel(
    x_ref, table_ref, keep_ref, pick_ref, head_ref, edge_ref, white_ref, short_ref, out_ref, raw_ref, near_ref, *parts_refs
):
    wins, span, length = white_ref.shape
    rows = slice(span * wins, 2 * span * wins)
    whiten_block(x_ref[rows, :], table_ref[...], keep_ref[span:], raw_ref, white_ref, short_ref)
    near_ref[:span] = edge_ref[...]
    near_ref[span:] = short_ref[...]
    stack_pairs(pick_ref, head_ref, near_ref, parts_refs, out_ref)


def cross_kernel(pick_ref, white_ref, short_ref, edge_ref, out_ref, near_ref, *parts_refs):
    span = short_ref.shape[0]
    near_ref[:span] = short_ref[...]
    near_ref[span:] = edge_ref[...]
    stack_pairs(pick_ref, white_ref, near_ref, parts_refs, out_ref)


def chosen(options, place):
    value = jnp.float32(options[0])
    for i, option in enumerate(options[1:]):
        value = jnp.where(place == i + 1, jnp.float32(option), value)
    return value


def weighted(terms, weights, place):
    total = None
    for term, options in zip(terms, weights):
        value = term[...].astype(jnp.float32)
        if set(options) != {1.0}:
            value = value * (options[0] if len(set(options)) == 1 else chosen(options, place))
        total = value if total is None else total + value
    return total


def whereabouts(groups):
    return lax.rem(lax.axis_index("chan"), 2) * groups + lax.axis_index("tm")


def mix_kernel(weights, *refs):
    place = whereabouts(len(weights[0]) // 2)
    total = weighted(refs[: len(weights)], weights, place)
    refs[-1][...] = total.astype(refs[-1].dtype)


def to_lags(stack, table):
    count = stack.shape[0]
    high = stack.astype(jnp.bfloat16)
    low = (stack - high.astype(jnp.float32)).astype(jnp.bfloat16)
    both = jnp.dot(jnp.concatenate([high, low]), table, preferred_element_type=jnp.float32)
    return both[:count] + both[count:]


def part_kernel(weights, table_ref, *refs):
    place = whereabouts(len(weights[0]) // 2)
    out_ref = refs[-1]
    stack = weighted(refs[: len(weights)], weights, place).reshape(out_ref.shape)
    out_ref[...] = to_lags(stack, table_ref[...])


def lag_kernel(scale, first, weights, table_ref, *rest):
    out_hbm, stage_ref, sem = rest[-3:]
    place = whereabouts(len(weights[0]) // 2)
    pairs, rows, length = stage_ref.shape
    stack = weighted(rest[: len(weights)], weights, place).reshape(pairs * rows, length)
    lagged = to_lags(stack, table_ref[...]) * scale
    stage_ref[...] = lagged.astype(stage_ref.dtype).reshape(pairs, rows, length)
    copy = pltpu.make_async_copy(stage_ref, out_hbm.at[:, pl.ds(first, rows)], sem)
    copy.start()
    copy.wait()


def last_kernel(scale, first, weights, table_ref, part_ref, more_ref, *rest):
    out_hbm, stage_ref, sem = rest[-3:]
    place = whereabouts(len(weights) // 2)
    pairs, rows, length = stage_ref.shape
    more = more_ref[...].reshape(pairs * rows, length)
    lagged = jnp.dot(more, table_ref[...], preferred_element_type=jnp.float32)
    lagged = (part_ref[...] + lagged * chosen(weights, place)) * scale
    stage_ref[...] = lagged.astype(stage_ref.dtype).reshape(pairs, rows, length)
    copy = pltpu.make_async_copy(stage_ref, out_hbm.at[:, pl.ds(first, rows)], sem)
    copy.start()
    copy.wait()


def cost(flops, moved):
    return pl.CostEstimate(flops=flops, bytes_accessed=moved, transcendentals=0)


def whole(memory=pltpu.VMEM):
    return pl.BlockSpec(memory_space=memory)


def per_device(samples, valid, offsets):
    chans, wins, length = samples.shape
    bins = length // 2
    span = OFFSET_SPAN
    pairs = offsets.shape[0]
    tiles = bins // LANES
    groups = lax.axis_size("tm")
    factor = float(np.float32(DECAY) ** np.float32(wins))
    params = pltpu.CompilerParams(vmem_limit_bytes=VMEM)

    def in_hbm(value):
        return pltpu.with_memory_space_constraint(value, pltpu.HBM)

    half = chans - span
    flat = samples.reshape(chans * wins, length)
    white_type = jax.ShapeDtypeStruct((wins, span, length), jnp.float32)
    short_type = jax.ShapeDtypeStruct((span, wins * length), jnp.bfloat16)
    local_type = jax.ShapeDtypeStruct((pairs, span, length), jnp.bfloat16)
    raw_scratch = pltpu.VMEM((2 * tiles, span * wins, LANES), jnp.float32)
    near_scratch = pltpu.VMEM((2 * span, wins * length), jnp.bfloat16)
    parts_scratch = [pltpu.VMEM((wins, pairs // 4 * span, length), jnp.float32)] * 4

    white_a, short_a, table, pick, keep = pl.pallas_call(
        head_kernel,
        out_shape=(
            white_type,
            short_type,
            jax.ShapeDtypeStruct((length, length), jnp.bfloat16),
            jax.ShapeDtypeStruct((pairs, span, 2 * span), jnp.bfloat16),
            jax.ShapeDtypeStruct((chans, wins * LANES), jnp.float32),
        ),
        in_specs=[whole(pltpu.HBM)] * 3,
        out_specs=(whole(),) * 5,
        scratch_shapes=[
            pltpu.VMEM((span * wins, length), jnp.bfloat16),
            pltpu.VMEM((wins, chans), jnp.int32),
            pltpu.SMEM((pairs,), jnp.int32),
            raw_scratch,
            pltpu.SemaphoreType.DMA((3,)),
        ],
        compiler_params=params,
        cost_estimate=cost(span * wins * length * length * 2, 2 * 1024 * 1024),
        name="head",
    )(in_hbm(flat), in_hbm(valid.T), in_hbm(offsets))

    ring = lax.axis_size("chan")
    edge = lax.ppermute(short_a, "chan", [(i, i - 1) for i in range(1, ring)])

    white_b, short_b, local_a = pl.pallas_call(
        tail_kernel,
        out_shape=(white_type, short_type, local_type),
        in_specs=[whole()] * 6,
        out_specs=(whole(),) * 3,
        scratch_shapes=[raw_scratch, near_scratch] + parts_scratch,
        compiler_params=params,
        cost_estimate=cost(span * wins * length * length * 4, 4 * 1024 * 1024),
        name="tail",
    )(flat, table, keep, pick, white_a, short_a)

    local_b = pl.pallas_call(
        cross_kernel,
        out_shape=local_type,
        in_specs=[whole()] * 4,
        out_specs=whole(),
        scratch_shapes=[near_scratch] + parts_scratch,
        compiler_params=params,
        cost_estimate=cost(pairs * span * wins * bins * 8, 4 * 1024 * 1024),
        name="cross",
    )(pick, white_b, short_b, edge)

    power = [float(np.float32(factor) ** np.float32(d)) for d in range(groups)]
    columns = min(d for d in range(1, groups + 1) if groups % d == 0 and d * d >= groups)
    square = columns == 2 and groups == columns * columns

    def sent(value, even, odd):
        moves = [
            (c * groups + here, c * groups + there)
            for c in range(ring)
            for here, there in (odd if c % 2 else even)
        ]
        return lax.ppermute(value, ("chan", "tm"), moves)

    def mix(terms, weights, after):
        return pl.pallas_call(
            functools.partial(mix_kernel, weights),
            out_shape=local_type,
            in_specs=[whole()] * len(terms) + [whole(pl.ANY)],
            out_specs=whole(),
            compiler_params=params,
            cost_estimate=cost(len(terms) * terms[0].size * 4, 1024 * 1024),
            name="mix",
        )(*terms, after)

    inverse = pl.pallas_call(
        inverse_kernel,
        out_shape=jax.ShapeDtypeStruct((length, length), jnp.bfloat16),
        in_specs=[whole(pl.ANY)],
        out_specs=whole(),
        compiler_params=params,
        cost_estimate=cost(length * bins * 32, 512 * 1024),
        name="inverse",
    )(local_b)

    def written(kernel, terms, *so_far):
        return pl.pallas_call(
            kernel,
            out_shape=jax.ShapeDtypeStruct((pairs, chans, length), jnp.bfloat16),
            in_specs=[whole()] * (1 + len(terms)) + [whole(pl.ANY)] * len(so_far),
            out_specs=whole(pl.ANY),
            scratch_shapes=[
                pltpu.VMEM((pairs, span, length), jnp.bfloat16),
                pltpu.SemaphoreType.DMA,
            ],
            input_output_aliases={1 + len(terms): 0} if so_far else {},
            compiler_params=params,
            cost_estimate=cost(pairs * span * length * length * 4, 1024 * 1024),
            name="lags",
        )(inverse, *terms, *so_far)

    def part(terms, weights):
        return pl.pallas_call(
            functools.partial(part_kernel, weights),
            out_shape=jax.ShapeDtypeStruct((pairs * span, length), jnp.float32),
            in_specs=[whole()] * (1 + len(terms)),
            out_specs=whole(),
            compiler_params=params,
            cost_estimate=cost(pairs * span * length * length * 4, 1024 * 1024),
            name="part",
        )(inverse, *terms)

    unit = [1.0] * (2 * groups)

    def two_hops(local, after):
        f, ff = power[1], power[2]
        got = sent(local, [(0, 2), (1, 3)], [(0, 1), (1, 0), (2, 3)])
        total = mix(
            [local, got],
            [[1.0, 1.0, 1.0, 0.0, f, 1.0, 0.0, 0.0], [ff, ff, ff, 1.0, 1.0, f, 0.0, 0.0]],
            after,
        )
        more = sent(total, [(0, 1), (2, 3), (3, 2)], [(0, 2), (1, 3)])
        weights = [
            unit,
            [ff, ff, ff, ff, 0.0, f, 0.0, f],
            [f, f, f, f, 0.0, 0.0, f, ff],
        ]
        return [local, got, more], weights

    def one_hop(local, after):
        terms, weights = [local], [unit]
        for d in range(1, groups):
            moves = [(h, h + d) for h in range(groups - d)]
            terms.append(sent(local, moves, moves))
            weights.append([power[d]] * (2 * groups))
        return terms, weights

    spread = two_hops if square else one_hop
    scale = bins**-0.5
    terms, weights = spread(local_a, local_b)
    result = written(functools.partial(lag_kernel, scale, 0, weights), terms)
    terms, weights = spread(local_b, local_b)
    before = part(terms[:-1], weights[:-1])
    last = functools.partial(last_kernel, scale, half, weights[-1])
    result = written(last, [before, terms[-1]], result)
    return result.reshape(1, pairs, chans, length)


def solution(mesh):
    in_specs = (P("chan", "tm", None), P("chan", "tm"), P())
    out_specs = P("tm", None, "chan", None)
    return jax.shard_map(
        per_device, mesh=mesh, in_specs=in_specs, out_specs=out_specs, check_vma=False
    )
```

```python
import functools
import math

import jax
import jax.numpy as jnp
import numpy as np
from jax import lax
from jax.experimental import pallas as pl
from jax.experimental.pallas import tpu as pltpu
from jax.sharding import PartitionSpec as P

OFFSET_SPAN = 32
LANES = 128
DECAY = 0.99
VMEM = 24 * 1024 * 1024


def turns(number, length):
    part = (number - length * jnp.floor(number / length + 0.5)) * (1.0 / length)
    square = part * part
    cosine, sine = jnp.float32(0.0), jnp.float32(0.0)
    for k in range(10, -1, -1):
        cosine = cosine * square + (-1) ** k * (2 * math.pi) ** (2 * k) / math.factorial(2 * k)
        sine = sine * square + (-1) ** k * (2 * math.pi) ** (2 * k + 1) / math.factorial(2 * k + 1)
    return cosine, sine * part


def fill_table(table_ref, step):
    length = table_ref.shape[0]
    bins = length // 2

    def small(rows, by):
        row = lax.broadcasted_iota(jnp.int32, (rows, bins), 0)
        freq = lax.broadcasted_iota(jnp.int32, (rows, bins), 1) + 1
        return turns((row * (by * freq)).astype(jnp.float32), length)

    coarse_cos, coarse_sin = small(length // step, step)
    fine_cos, fine_sin = small(step, 1)
    for i in range(length // step):
        rows = slice(i * step, (i + 1) * step)
        cos_i, sin_i = coarse_cos[i : i + 1], coarse_sin[i : i + 1]
        table_ref[rows, :bins] = (cos_i * fine_cos - sin_i * fine_sin).astype(jnp.bfloat16)
        table_ref[rows, bins:] = -(sin_i * fine_cos + cos_i * fine_sin).astype(jnp.bfloat16)


def inverse_kernel(_, table_ref):
    length = table_ref.shape[0]
    bins = length // 2
    step = 16

    def small(rows, by, first):
        freq = (lax.broadcasted_iota(jnp.int32, (rows, length), 0) + first) * by
        lag = lax.broadcasted_iota(jnp.int32, (rows, length), 1)
        return turns((freq * lag).astype(jnp.float32), length)

    coarse_cos, coarse_sin = small(bins // step, step, 0)
    fine_cos, fine_sin = small(step, 1, 1)
    for i in range(bins // step):
        first = i * step
        cos_i, sin_i = coarse_cos[i : i + 1], coarse_sin[i : i + 1]
        cosine = cos_i * fine_cos - sin_i * fine_sin
        sine = sin_i * fine_cos + cos_i * fine_sin
        table_ref[first : first + step, :] = cosine.astype(jnp.bfloat16)
        table_ref[bins + first : bins + first + step, :] = (-sine).astype(jnp.bfloat16)


def whiten_block(x, table, keep, raw_ref, white_ref, short_ref):
    wins, span, length = white_ref.shape
    bins = length // 2
    tiles = bins // LANES
    raw = jnp.dot(x, table, preferred_element_type=jnp.float32)
    for t in range(2 * tiles):
        raw_ref[t] = raw[:, t * LANES : (t + 1) * LANES]
    for w in range(wins):
        decay = float(np.float32(DECAY) ** np.float32(wins - 1 - w))
        part = [raw_ref[t, pl.ds(w, span, stride=wins), :] for t in range(2 * tiles)]
        power = [part[t] * part[t] + part[tiles + t] * part[tiles + t] for t in range(tiles)]
        total = power[0]
        for t in range(1, tiles):
            total = total + power[t]
        level = jnp.sum(total, axis=-1, keepdims=True) * (0.01 / bins) + 1e-06
        alive = keep[:, w * LANES : (w + 1) * LANES]
        for t in range(tiles):
            scale = alive * lax.rsqrt(power[t] + level)
            for s in (t, tiles + t):
                value = part[s] * scale
                here = pl.ds(w * length + s * LANES, LANES)
                white_ref[w, :, s * LANES : (s + 1) * LANES] = value * decay
                short_ref[:, here] = value.astype(jnp.bfloat16)


def head_kernel(
    x_hbm,
    valid_hbm,
    offsets_hbm,
    white_ref,
    short_ref,
    table_ref,
    pick_ref,
    keep_ref,
    x_ref,
    valid_ref,
    offsets_ref,
    raw_ref,
    sems,
):
    wins, span, length = white_ref.shape
    pairs = offsets_ref.shape[0]
    copies = [
        pltpu.make_async_copy(valid_hbm, valid_ref, sems.at[0]),
        pltpu.make_async_copy(offsets_hbm, offsets_ref, sems.at[1]),
        pltpu.make_async_copy(x_hbm.at[pl.ds(0, span * wins)], x_ref, sems.at[2]),
    ]
    for copy in copies:
        copy.start()
    fill_table(table_ref, 16)
    copies[0].wait()
    copies[1].wait()
    ahead = lax.broadcasted_iota(jnp.int32, (span, 2 * span), 1) - lax.broadcasted_iota(
        jnp.int32, (span, 2 * span), 0
    )
    for k in range(pairs):
        chosen_row = jnp.where(ahead == offsets_ref[k], jnp.float32(1.0), jnp.float32(0.0))
        pick_ref[k] = chosen_row.astype(jnp.bfloat16)
    owner = lax.broadcasted_iota(jnp.int32, (wins, wins * LANES), 0)
    column = lax.broadcasted_iota(jnp.int32, (wins, wins * LANES), 1) // LANES
    keep_ref[...] = lax.dot_general(
        valid_ref[...].astype(jnp.float32).astype(jnp.bfloat16),
        (owner == column).astype(jnp.float32).astype(jnp.bfloat16),
        (((0,), (0,)), ((), ())),
        preferred_element_type=jnp.float32,
    )
    copies[2].wait()
    whiten_block(x_ref[...], table_ref[...], keep_ref[:span], raw_ref, white_ref, short_ref)


def stack_pairs(pick_ref, white_ref, near_ref, parts_refs, out_ref):
    wins, _, length = white_ref.shape
    pairs, rows, reach = pick_ref.shape
    bins = length // 2
    size = pairs // len(parts_refs)

    def select(group, w):
        pick = pick_ref[group * size : (group + 1) * size].reshape(size * rows, reach)
        near = near_ref[:, w * length : (w + 1) * length]
        parts_refs[group][w] = jnp.dot(pick, near, preferred_element_type=jnp.float32)

    blocks = [(c, t) for c in range(0, rows, 16) for t in range(bins // LANES)]
    for w in range(wins):
        select(0, w)
    for group, parts_ref in enumerate(parts_refs):
        ahead = list(range(wins)) if group + 1 < len(parts_refs) else []
        for i, (c, t) in enumerate(blocks):
            for w in ahead[i :: len(blocks)]:
                select(group + 1, w)
            re = slice(t * LANES, (t + 1) * LANES)
            im = slice(bins + t * LANES, bins + (t + 1) * LANES)
            head_re = [white_ref[w, c : c + 16, re] for w in range(wins)]
            head_im = [white_ref[w, c : c + 16, im] for w in range(wins)]
            for k in range(size):
                here = slice(k * rows + c, k * rows + c + 16)
                total_re = total_im = None
                for w in range(wins):
                    part_re, part_im = parts_ref[w, here, re], parts_ref[w, here, im]
                    cross_re = head_re[w] * part_re + head_im[w] * part_im
                    cross_im = head_im[w] * part_re - head_re[w] * part_im
                    total_re = cross_re if w == 0 else total_re + cross_re
                    total_im = cross_im if w == 0 else total_im + cross_im
                pair = group * size + k
                out_ref[pair, c : c + 16, re] = total_re.astype(out_ref.dtype)
                out_ref[pair, c : c + 16, im] = total_im.astype(out_ref.dtype)


def sends_first(limits):
    return lax.axis_index("tm") < jnp.where(lax.rem(lax.axis_index("chan"), 2) == 0, *limits)


def tail_kernel(
    limits,
    now,
    x_ref,
    table_ref,
    keep_ref,
    pick_ref,
    head_ref,
    edge_ref,
    after_ref,
    white_ref,
    short_ref,
    out_ref,
    raw_ref,
    near_ref,
    *parts_refs,
):
    wins, span, length = white_ref.shape
    rows = slice(span * wins, 2 * span * wins)

    @pl.when(sends_first(limits) == now)
    def _():
        x = x_ref[rows, :]
        whiten_block(x, table_ref[...], keep_ref[span:], raw_ref, white_ref, short_ref)
        near_ref[:span] = edge_ref[...]
        near_ref[span:] = short_ref[...]
        stack_pairs(pick_ref, head_ref, near_ref, parts_refs, out_ref)


def cross_kernel(
    limits, now, pick_ref, white_ref, short_ref, edge_ref, after_ref, out_ref, near_ref, *parts_refs
):
    span = short_ref.shape[0]

    @pl.when(sends_first(limits) == now)
    def _():
        near_ref[:span] = short_ref[...]
        near_ref[span:] = edge_ref[...]
        stack_pairs(pick_ref, white_ref, near_ref, parts_refs, out_ref)


def chosen(options, place):
    value = jnp.float32(options[0])
    for i, option in enumerate(options[1:]):
        value = jnp.where(place == i + 1, jnp.float32(option), value)
    return value


def weighted(limits, terms, weights, place):
    total = None
    first = jnp.where(sends_first(limits), terms[0][...], terms[1][...])
    for term, options in zip([first] + list(terms[2:]), weights):
        value = term[...].astype(jnp.float32)
        if set(options) != {1.0}:
            value = value * (options[0] if len(set(options)) == 1 else chosen(options, place))
        total = value if total is None else total + value
    return total


def whereabouts(groups):
    return lax.rem(lax.axis_index("chan"), 2) * groups + lax.axis_index("tm")


def mix_kernel(limits, weights, *refs):
    place = whereabouts(len(weights[0]) // 2)
    total = weighted(limits, refs[: len(weights) + 1], weights, place)
    refs[-1][...] = total.astype(refs[-1].dtype)


def to_lags(stack, table):
    count = stack.shape[0]
    high = stack.astype(jnp.bfloat16)
    low = (stack - high.astype(jnp.float32)).astype(jnp.bfloat16)
    both = jnp.dot(jnp.concatenate([high, low]), table, preferred_element_type=jnp.float32)
    return both[:count] + both[count:]


def part_kernel(limits, weights, table_ref, *refs):
    place = whereabouts(len(weights[0]) // 2)
    out_ref = refs[-1]
    stack = weighted(limits, refs[: len(weights) + 1], weights, place).reshape(out_ref.shape)
    out_ref[...] = to_lags(stack, table_ref[...])


def lag_kernel(limits, scale, first, weights, table_ref, *rest):
    out_hbm, stage_ref, sem = rest[-3:]
    place = whereabouts(len(weights[0]) // 2)
    pairs, rows, length = stage_ref.shape
    stack = weighted(limits, rest[: len(weights) + 1], weights, place)
    stack = stack.reshape(pairs * rows, length)
    lagged = to_lags(stack, table_ref[...]) * scale
    stage_ref[...] = lagged.astype(stage_ref.dtype).reshape(pairs, rows, length)
    copy = pltpu.make_async_copy(stage_ref, out_hbm.at[:, pl.ds(first, rows)], sem)
    copy.start()
    copy.wait()


def last_kernel(scale, first, weights, table_ref, part_ref, more_ref, *rest):
    out_hbm, stage_ref, sem = rest[-3:]
    place = whereabouts(len(weights) // 2)
    pairs, rows, length = stage_ref.shape
    more = more_ref[...].reshape(pairs * rows, length)
    lagged = jnp.dot(more, table_ref[...], preferred_element_type=jnp.float32)
    lagged = (part_ref[...] + lagged * chosen(weights, place)) * scale
    stage_ref[...] = lagged.astype(stage_ref.dtype).reshape(pairs, rows, length)
    copy = pltpu.make_async_copy(stage_ref, out_hbm.at[:, pl.ds(first, rows)], sem)
    copy.start()
    copy.wait()


def cost(flops, moved):
    return pl.CostEstimate(flops=flops, bytes_accessed=moved, transcendentals=0)


def whole(memory=pltpu.VMEM):
    return pl.BlockSpec(memory_space=memory)


def per_device(samples, valid, offsets):
    chans, wins, length = samples.shape
    bins = length // 2
    span = OFFSET_SPAN
    pairs = offsets.shape[0]
    tiles = bins // LANES
    groups = lax.axis_size("tm")
    factor = float(np.float32(DECAY) ** np.float32(wins))
    params = pltpu.CompilerParams(vmem_limit_bytes=VMEM)

    def in_hbm(value):
        return pltpu.with_memory_space_constraint(value, pltpu.HBM)

    half = chans - span
    flat = samples.reshape(chans * wins, length)
    white_type = jax.ShapeDtypeStruct((wins, span, length), jnp.float32)
    short_type = jax.ShapeDtypeStruct((span, wins * length), jnp.bfloat16)
    local_type = jax.ShapeDtypeStruct((pairs, span, length), jnp.bfloat16)
    raw_scratch = pltpu.VMEM((2 * tiles, span * wins, LANES), jnp.float32)
    near_scratch = pltpu.VMEM((2 * span, wins * length), jnp.bfloat16)
    parts_scratch = [pltpu.VMEM((wins, pairs // 2 * span, length), jnp.float32)] * 2

    white_a, short_a, table, pick, keep = pl.pallas_call(
        head_kernel,
        out_shape=(
            white_type,
            short_type,
            jax.ShapeDtypeStruct((length, length), jnp.bfloat16),
            jax.ShapeDtypeStruct((pairs, span, 2 * span), jnp.bfloat16),
            jax.ShapeDtypeStruct((chans, wins * LANES), jnp.float32),
        ),
        in_specs=[whole(pltpu.HBM)] * 3,
        out_specs=(whole(),) * 5,
        scratch_shapes=[
            pltpu.VMEM((span * wins, length), jnp.bfloat16),
            pltpu.VMEM((wins, chans), jnp.int32),
            pltpu.SMEM((pairs,), jnp.int32),
            raw_scratch,
            pltpu.SemaphoreType.DMA((3,)),
        ],
        compiler_params=params,
        cost_estimate=cost(span * wins * length * length * 2, 2 * 1024 * 1024),
        name="head",
    )(in_hbm(flat), in_hbm(valid.T), in_hbm(offsets))

    ring = lax.axis_size("chan")
    edge = lax.ppermute(short_a, "chan", [(i, i - 1) for i in range(1, ring)])

    columns = min(d for d in range(1, groups + 1) if groups % d == 0 and d * d >= groups)
    square = columns == 2 and groups == columns * columns
    limits = (2, 3) if square else (groups, groups)

    def tail(now, after):
        return pl.pallas_call(
            functools.partial(tail_kernel, limits, now),
            out_shape=(white_type, short_type, local_type),
            in_specs=[whole()] * 6 + [whole(pl.ANY)],
            out_specs=(whole(),) * 3,
            scratch_shapes=[raw_scratch, near_scratch] + parts_scratch,
            compiler_params=params,
            cost_estimate=cost(span * wins * length * length * 4, 4 * 1024 * 1024),
            name="tail",
        )(flat, table, keep, pick, white_a, short_a, after)

    def cross(now, white, short, after):
        return pl.pallas_call(
            functools.partial(cross_kernel, limits, now),
            out_shape=local_type,
            in_specs=[whole()] * 4 + [whole(pl.ANY)],
            out_specs=whole(),
            scratch_shapes=[near_scratch] + parts_scratch,
            compiler_params=params,
            cost_estimate=cost(pairs * span * wins * bins * 8, 4 * 1024 * 1024),
            name="cross",
        )(pick, white, short, edge, after)

    white_b, short_b, local_a = tail(True, table)
    local_b = cross(True, white_b, short_b, table)
    white_late, short_late, late_a = tail(False, local_b)
    late_b = cross(False, white_late, short_late, local_b)

    power = [float(np.float32(factor) ** np.float32(d)) for d in range(groups)]
    def sent(value, even, odd):
        moves = [
            (c * groups + here, c * groups + there)
            for c in range(ring)
            for here, there in (odd if c % 2 else even)
        ]
        return lax.ppermute(value, ("chan", "tm"), moves)

    def mix(terms, weights, after):
        return pl.pallas_call(
            functools.partial(mix_kernel, limits, weights),
            out_shape=local_type,
            in_specs=[whole()] * len(terms) + [whole(pl.ANY)],
            out_specs=whole(),
            compiler_params=params,
            cost_estimate=cost(len(terms) * terms[0].size * 4, 1024 * 1024),
            name="mix",
        )(*terms, after)

    inverse = pl.pallas_call(
        inverse_kernel,
        out_shape=jax.ShapeDtypeStruct((length, length), jnp.bfloat16),
        in_specs=[whole(pl.ANY)],
        out_specs=whole(),
        compiler_params=params,
        cost_estimate=cost(length * bins * 32, 512 * 1024),
        name="inverse",
    )(local_b)

    def written(kernel, terms, *so_far):
        return pl.pallas_call(
            kernel,
            out_shape=jax.ShapeDtypeStruct((pairs, chans, length), jnp.bfloat16),
            in_specs=[whole()] * (1 + len(terms)) + [whole(pl.ANY)] * len(so_far),
            out_specs=whole(pl.ANY),
            scratch_shapes=[
                pltpu.VMEM((pairs, span, length), jnp.bfloat16),
                pltpu.SemaphoreType.DMA,
            ],
            input_output_aliases={1 + len(terms): 0} if so_far else {},
            compiler_params=params,
            cost_estimate=cost(pairs * span * length * length * 4, 1024 * 1024),
            name="lags",
        )(inverse, *terms, *so_far)

    def part(terms, weights):
        return pl.pallas_call(
            functools.partial(part_kernel, limits, weights),
            out_shape=jax.ShapeDtypeStruct((pairs * span, length), jnp.float32),
            in_specs=[whole()] * (1 + len(terms)),
            out_specs=whole(),
            compiler_params=params,
            cost_estimate=cost(pairs * span * length * length * 4, 1024 * 1024),
            name="part",
        )(inverse, *terms)

    unit = [1.0] * (2 * groups)

    def two_hops(local, late, after):
        f, ff = power[1], power[2]
        got = sent(local, [(0, 2), (1, 3)], [(0, 1), (1, 0), (2, 3)])
        total = mix(
            [local, late, got],
            [[1.0, 1.0, 1.0, 0.0, f, 1.0, 0.0, 0.0], [ff, ff, ff, 1.0, 1.0, f, 0.0, 0.0]],
            after,
        )
        more = sent(total, [(0, 1), (2, 3), (3, 2)], [(0, 2), (1, 3)])
        weights = [
            unit,
            [ff, ff, ff, ff, 0.0, f, 0.0, f],
            [f, f, f, f, 0.0, 0.0, f, ff],
        ]
        return [local, late, got, more], weights

    def one_hop(local, late, after):
        terms, weights = [local, late], [unit]
        for d in range(1, groups):
            moves = [(h, h + d) for h in range(groups - d)]
            terms.append(sent(local, moves, moves))
            weights.append([power[d]] * (2 * groups))
        return terms, weights

    spread = two_hops if square else one_hop
    scale = bins**-0.5
    terms, weights = spread(local_a, late_a, late_b)
    result = written(functools.partial(lag_kernel, limits, scale, 0, weights), terms)
    terms, weights = spread(local_b, late_b, local_b)
    before = part(terms[:-1], weights[:-1])
    last = functools.partial(last_kernel, scale, half, weights[-1])
    result = written(last, [before, terms[-1]], result)
    return result.reshape(1, pairs, chans, length)


def solution(mesh):
    in_specs = (P("chan", "tm", None), P("chan", "tm"), P())
    out_specs = P("tm", None, "chan", None)
    return jax.shard_map(
        per_device, mesh=mesh, in_specs=in_specs, out_specs=out_specs, check_vma=False
    )
```

```python
import functools
import math

import jax
import jax.numpy as jnp
import numpy as np
from jax import lax
from jax.experimental import pallas as pl
from jax.experimental.pallas import tpu as pltpu
from jax.sharding import PartitionSpec as P

OFFSET_SPAN = 32
LANES = 128
DECAY = 0.99
VMEM = 24 * 1024 * 1024


def turns(number, length):
    part = (number - length * jnp.floor(number / length + 0.5)) * (1.0 / length)
    square = part * part
    cosine, sine = jnp.float32(0.0), jnp.float32(0.0)
    for k in range(10, -1, -1):
        cosine = cosine * square + (-1) ** k * (2 * math.pi) ** (2 * k) / math.factorial(2 * k)
        sine = sine * square + (-1) ** k * (2 * math.pi) ** (2 * k + 1) / math.factorial(2 * k + 1)
    return cosine, sine * part


def fill_table(table_ref, step):
    length = table_ref.shape[0]
    bins = length // 2

    def small(rows, by):
        row = lax.broadcasted_iota(jnp.int32, (rows, bins), 0)
        freq = lax.broadcasted_iota(jnp.int32, (rows, bins), 1) + 1
        return turns((row * (by * freq)).astype(jnp.float32), length)

    coarse_cos, coarse_sin = small(length // step, step)
    fine_cos, fine_sin = small(step, 1)
    for i in range(length // step):
        rows = slice(i * step, (i + 1) * step)
        cos_i, sin_i = coarse_cos[i : i + 1], coarse_sin[i : i + 1]
        table_ref[rows, :bins] = (cos_i * fine_cos - sin_i * fine_sin).astype(jnp.bfloat16)
        table_ref[rows, bins:] = -(sin_i * fine_cos + cos_i * fine_sin).astype(jnp.bfloat16)


def inverse_kernel(_, table_ref):
    length = table_ref.shape[0]
    bins = length // 2
    step = 16

    def small(rows, by, first):
        freq = (lax.broadcasted_iota(jnp.int32, (rows, length), 0) + first) * by
        lag = lax.broadcasted_iota(jnp.int32, (rows, length), 1)
        return turns((freq * lag).astype(jnp.float32), length)

    coarse_cos, coarse_sin = small(bins // step, step, 0)
    fine_cos, fine_sin = small(step, 1, 1)
    for i in range(bins // step):
        first = i * step
        cos_i, sin_i = coarse_cos[i : i + 1], coarse_sin[i : i + 1]
        cosine = cos_i * fine_cos - sin_i * fine_sin
        sine = sin_i * fine_cos + cos_i * fine_sin
        table_ref[first : first + step, :] = cosine.astype(jnp.bfloat16)
        table_ref[bins + first : bins + first + step, :] = (-sine).astype(jnp.bfloat16)


def whiten_block(x, table, keep, raw_ref, white_ref, short_ref):
    wins, span, length = white_ref.shape
    bins = length // 2
    tiles = bins // LANES
    raw = jnp.dot(x, table, preferred_element_type=jnp.float32)
    for t in range(2 * tiles):
        raw_ref[t] = raw[:, t * LANES : (t + 1) * LANES]
    for w in range(wins):
        decay = float(np.float32(DECAY) ** np.float32(wins - 1 - w))
        part = [raw_ref[t, pl.ds(w, span, stride=wins), :] for t in range(2 * tiles)]
        power = [part[t] * part[t] + part[tiles + t] * part[tiles + t] for t in range(tiles)]
        total = power[0]
        for t in range(1, tiles):
            total = total + power[t]
        level = jnp.sum(total, axis=-1, keepdims=True) * (0.01 / bins) + 1e-06
        alive = keep[:, w * LANES : (w + 1) * LANES]
        for t in range(tiles):
            scale = alive * lax.rsqrt(power[t] + level)
            for s in (t, tiles + t):
                value = part[s] * scale
                here = pl.ds(w * length + s * LANES, LANES)
                white_ref[w, :, s * LANES : (s + 1) * LANES] = value * decay
                short_ref[:, here] = value.astype(jnp.bfloat16)


def head_kernel(
    x_hbm,
    valid_hbm,
    offsets_hbm,
    white_ref,
    short_ref,
    table_ref,
    pick_ref,
    keep_ref,
    x_ref,
    valid_ref,
    offsets_ref,
    raw_ref,
    sems,
):
    wins, span, length = white_ref.shape
    pairs = offsets_ref.shape[0]
    copies = [
        pltpu.make_async_copy(valid_hbm, valid_ref, sems.at[0]),
        pltpu.make_async_copy(offsets_hbm, offsets_ref, sems.at[1]),
        pltpu.make_async_copy(x_hbm.at[pl.ds(0, span * wins)], x_ref, sems.at[2]),
    ]
    for copy in copies:
        copy.start()
    fill_table(table_ref, 16)
    copies[0].wait()
    copies[1].wait()
    ahead = lax.broadcasted_iota(jnp.int32, (span, 2 * span), 1) - lax.broadcasted_iota(
        jnp.int32, (span, 2 * span), 0
    )
    for k in range(pairs):
        chosen_row = jnp.where(ahead == offsets_ref[k], jnp.float32(1.0), jnp.float32(0.0))
        pick_ref[k] = chosen_row.astype(jnp.bfloat16)
    owner = lax.broadcasted_iota(jnp.int32, (wins, wins * LANES), 0)
    column = lax.broadcasted_iota(jnp.int32, (wins, wins * LANES), 1) // LANES
    keep_ref[...] = lax.dot_general(
        valid_ref[...].astype(jnp.float32).astype(jnp.bfloat16),
        (owner == column).astype(jnp.float32).astype(jnp.bfloat16),
        (((0,), (0,)), ((), ())),
        preferred_element_type=jnp.float32,
    )
    copies[2].wait()
    whiten_block(x_ref[...], table_ref[...], keep_ref[:span], raw_ref, white_ref, short_ref)


def stack_pairs(pick_ref, white_ref, near_ref, parts_refs, out_ref):
    wins, _, length = white_ref.shape
    pairs, rows, reach = pick_ref.shape
    bins = length // 2
    size = pairs // len(parts_refs)

    def select(group, w):
        pick = pick_ref[group * size : (group + 1) * size].reshape(size * rows, reach)
        near = near_ref[:, w * length : (w + 1) * length]
        parts_refs[group][w] = jnp.dot(pick, near, preferred_element_type=jnp.float32)

    blocks = [(c, t) for c in range(0, rows, 16) for t in range(bins // LANES)]
    for w in range(wins):
        select(0, w)
    for group, parts_ref in enumerate(parts_refs):
        ahead = list(range(wins)) if group + 1 < len(parts_refs) else []
        for i, (c, t) in enumerate(blocks):
            for w in ahead[i :: len(blocks)]:
                select(group + 1, w)
            re = slice(t * LANES, (t + 1) * LANES)
            im = slice(bins + t * LANES, bins + (t + 1) * LANES)
            head_re = [white_ref[w, c : c + 16, re] for w in range(wins)]
            head_im = [white_ref[w, c : c + 16, im] for w in range(wins)]
            for k in range(size):
                here = slice(k * rows + c, k * rows + c + 16)
                total_re = total_im = None
                for w in range(wins):
                    part_re, part_im = parts_ref[w, here, re], parts_ref[w, here, im]
                    cross_re = head_re[w] * part_re + head_im[w] * part_im
                    cross_im = head_im[w] * part_re - head_re[w] * part_im
                    total_re = cross_re if w == 0 else total_re + cross_re
                    total_im = cross_im if w == 0 else total_im + cross_im
                pair = group * size + k
                out_ref[pair, c : c + 16, re] = total_re.astype(out_ref.dtype)
                out_ref[pair, c : c + 16, im] = total_im.astype(out_ref.dtype)


def sends_first(limits):
    return lax.axis_index("tm") < jnp.where(lax.rem(lax.axis_index("chan"), 2) == 0, *limits)


def tail_kernel(
    limits,
    now,
    x_ref,
    table_ref,
    keep_ref,
    pick_ref,
    head_ref,
    edge_ref,
    after_ref,
    white_ref,
    short_ref,
    out_ref,
    raw_ref,
    near_ref,
    *parts_refs,
):
    wins, span, length = white_ref.shape
    rows = slice(span * wins, 2 * span * wins)

    @pl.when(sends_first(limits) == now)
    def _():
        x = x_ref[rows, :]
        whiten_block(x, table_ref[...], keep_ref[span:], raw_ref, white_ref, short_ref)
        near_ref[:span] = edge_ref[...]
        near_ref[span:] = short_ref[...]
        stack_pairs(pick_ref, head_ref, near_ref, parts_refs, out_ref)


def cross_kernel(
    limits, now, pick_ref, white_ref, short_ref, edge_ref, after_ref, out_ref, near_ref, *parts_refs
):
    span = short_ref.shape[0]

    @pl.when(sends_first(limits) == now)
    def _():
        near_ref[:span] = short_ref[...]
        near_ref[span:] = edge_ref[...]
        stack_pairs(pick_ref, white_ref, near_ref, parts_refs, out_ref)


def chosen(options, place):
    value = jnp.float32(options[0])
    for i, option in enumerate(options[1:]):
        value = jnp.where(place == i + 1, jnp.float32(option), value)
    return value


def weighted(limits, terms, weights, place):
    total = None
    first = jnp.where(sends_first(limits), terms[0][...], terms[1][...])
    for term, options in zip([first] + list(terms[2:]), weights):
        value = term[...].astype(jnp.float32)
        if set(options) != {1.0}:
            value = value * (options[0] if len(set(options)) == 1 else chosen(options, place))
        total = value if total is None else total + value
    return total


def whereabouts(groups):
    return lax.rem(lax.axis_index("chan"), 2) * groups + lax.axis_index("tm")


def mix_kernel(limits, weights, *refs):
    place = whereabouts(len(weights[0]) // 2)
    total = weighted(limits, refs[: len(weights) + 1], weights, place)
    refs[-1][...] = total.astype(refs[-1].dtype)


def to_lags(stack, table):
    count = stack.shape[0]
    high = stack.astype(jnp.bfloat16)
    low = (stack - high.astype(jnp.float32)).astype(jnp.bfloat16)
    both = jnp.dot(jnp.concatenate([high, low]), table, preferred_element_type=jnp.float32)
    return both[:count] + both[count:]


def part_kernel(limits, weights, table_ref, *refs):
    place = whereabouts(len(weights[0]) // 2)
    out_ref = refs[-1]
    stack = weighted(limits, refs[: len(weights) + 1], weights, place).reshape(out_ref.shape)
    out_ref[...] = to_lags(stack, table_ref[...])


def lag_kernel(limits, scale, first, weights, table_ref, *rest):
    out_hbm, stage_ref, sem = rest[-3:]
    place = whereabouts(len(weights[0]) // 2)
    pairs, rows, length = stage_ref.shape
    stack = weighted(limits, rest[: len(weights) + 1], weights, place)
    stack = stack.reshape(pairs * rows, length)
    lagged = to_lags(stack, table_ref[...]) * scale
    stage_ref[...] = lagged.astype(stage_ref.dtype).reshape(pairs, rows, length)
    copy = pltpu.make_async_copy(stage_ref, out_hbm.at[:, pl.ds(first, rows)], sem)
    copy.start()
    copy.wait()


def last_kernel(scale, first, weights, table_ref, part_ref, more_ref, *rest):
    out_hbm, stage_ref, sem = rest[-3:]
    place = whereabouts(len(weights) // 2)
    pairs, rows, length = stage_ref.shape
    more = more_ref[...].reshape(pairs * rows, length)
    lagged = jnp.dot(more, table_ref[...], preferred_element_type=jnp.float32)
    lagged = (part_ref[...] + lagged * chosen(weights, place)) * scale
    stage_ref[...] = lagged.astype(stage_ref.dtype).reshape(pairs, rows, length)
    copy = pltpu.make_async_copy(stage_ref, out_hbm.at[:, pl.ds(first, rows)], sem)
    copy.start()
    copy.wait()


def cost(flops, moved):
    return pl.CostEstimate(flops=flops, bytes_accessed=moved, transcendentals=0)


def whole(memory=pltpu.VMEM):
    return pl.BlockSpec(memory_space=memory)


def per_device(samples, valid, offsets):
    chans, wins, length = samples.shape
    bins = length // 2
    span = OFFSET_SPAN
    pairs = offsets.shape[0]
    tiles = bins // LANES
    groups = lax.axis_size("tm")
    factor = float(np.float32(DECAY) ** np.float32(wins))
    params = pltpu.CompilerParams(vmem_limit_bytes=VMEM)

    def in_hbm(value):
        return pltpu.with_memory_space_constraint(value, pltpu.HBM)

    half = chans - span
    flat = samples.reshape(chans * wins, length)
    white_type = jax.ShapeDtypeStruct((wins, span, length), jnp.float32)
    short_type = jax.ShapeDtypeStruct((span, wins * length), jnp.bfloat16)
    local_type = jax.ShapeDtypeStruct((pairs, span, length), jnp.bfloat16)
    raw_scratch = pltpu.VMEM((2 * tiles, span * wins, LANES), jnp.float32)
    near_scratch = pltpu.VMEM((2 * span, wins * length), jnp.bfloat16)
    parts_scratch = [pltpu.VMEM((wins, pairs // 2 * span, length), jnp.float32)] * 2

    white_a, short_a, table, pick, keep = pl.pallas_call(
        head_kernel,
        out_shape=(
            white_type,
            short_type,
            jax.ShapeDtypeStruct((length, length), jnp.bfloat16),
            jax.ShapeDtypeStruct((pairs, span, 2 * span), jnp.bfloat16),
            jax.ShapeDtypeStruct((chans, wins * LANES), jnp.float32),
        ),
        in_specs=[whole(pltpu.HBM)] * 3,
        out_specs=(whole(),) * 5,
        scratch_shapes=[
            pltpu.VMEM((span * wins, length), jnp.bfloat16),
            pltpu.VMEM((wins, chans), jnp.int32),
            pltpu.SMEM((pairs,), jnp.int32),
            raw_scratch,
            pltpu.SemaphoreType.DMA((3,)),
        ],
        compiler_params=params,
        cost_estimate=cost(span * wins * length * length * 2, 2 * 1024 * 1024),
        name="head",
    )(in_hbm(flat), in_hbm(valid.T), in_hbm(offsets))

    ring = lax.axis_size("chan")
    edge = lax.ppermute(short_a, "chan", [(i, i - 1) for i in range(1, ring)])

    columns = min(d for d in range(1, groups + 1) if groups % d == 0 and d * d >= groups)
    square = columns == 2 and groups == columns * columns
    limits = (2, 3) if square else (groups, groups)

    def tail(now, after):
        return pl.pallas_call(
            functools.partial(tail_kernel, limits, now),
            out_shape=(white_type, short_type, local_type),
            in_specs=[whole()] * 6 + [whole(pl.ANY)],
            out_specs=(whole(),) * 3,
            scratch_shapes=[raw_scratch, near_scratch] + parts_scratch,
            compiler_params=params,
            cost_estimate=cost(span * wins * length * length * 4, 4 * 1024 * 1024),
            name="tail",
        )(flat, table, keep, pick, white_a, short_a, after)

    def cross(now, white, short, after):
        return pl.pallas_call(
            functools.partial(cross_kernel, limits, now),
            out_shape=local_type,
            in_specs=[whole()] * 4 + [whole(pl.ANY)],
            out_specs=whole(),
            scratch_shapes=[near_scratch] + parts_scratch,
            compiler_params=params,
            cost_estimate=cost(pairs * span * wins * bins * 8, 4 * 1024 * 1024),
            name="cross",
        )(pick, white, short, edge, after)

    white_b, short_b, local_a = tail(True, table)
    local_b = cross(True, white_b, short_b, table)
    white_late, short_late, late_a = tail(False, local_b)
    late_b = cross(False, white_late, short_late, local_b)

    power = [float(np.float32(factor) ** np.float32(d)) for d in range(groups)]
    def sent(value, even, odd):
        moves = [
            (c * groups + here, c * groups + there)
            for c in range(ring)
            for here, there in (odd if c % 2 else even)
        ]
        return lax.ppermute(value, ("chan", "tm"), moves)

    def mix(terms, weights, after):
        return pl.pallas_call(
            functools.partial(mix_kernel, limits, weights),
            out_shape=local_type,
            in_specs=[whole()] * len(terms) + [whole(pl.ANY)],
            out_specs=whole(),
            compiler_params=params,
            cost_estimate=cost(len(terms) * terms[0].size * 4, 1024 * 1024),
            name="mix",
        )(*terms, after)

    inverse = pl.pallas_call(
        inverse_kernel,
        out_shape=jax.ShapeDtypeStruct((length, length), jnp.bfloat16),
        in_specs=[whole(pl.ANY)],
        out_specs=whole(),
        compiler_params=params,
        cost_estimate=cost(length * bins * 32, 512 * 1024),
        name="inverse",
    )(local_b)

    def written(kernel, terms, later, *so_far):
        return pl.pallas_call(
            kernel,
            out_shape=jax.ShapeDtypeStruct((pairs, chans, length), jnp.bfloat16),
            in_specs=[whole()] * (1 + len(terms)) + [whole(pl.ANY)] * (len(later) + len(so_far)),
            out_specs=whole(pl.ANY),
            scratch_shapes=[
                pltpu.VMEM((pairs, span, length), jnp.bfloat16),
                pltpu.SemaphoreType.DMA,
            ],
            input_output_aliases={1 + len(terms) + len(later): 0} if so_far else {},
            compiler_params=params,
            cost_estimate=cost(pairs * span * length * length * 4, 1024 * 1024),
            name="lags",
        )(inverse, *terms, *later, *so_far)

    def part(terms, weights):
        return pl.pallas_call(
            functools.partial(part_kernel, limits, weights),
            out_shape=jax.ShapeDtypeStruct((pairs * span, length), jnp.float32),
            in_specs=[whole()] * (1 + len(terms)),
            out_specs=whole(),
            compiler_params=params,
            cost_estimate=cost(pairs * span * length * length * 4, 1024 * 1024),
            name="part",
        )(inverse, *terms)

    unit = [1.0] * (2 * groups)

    def two_hops(local, late, after, apart):
        f, ff = power[1], power[2]
        last = [(2, 3)]
        got = sent(local, [(0, 2), (1, 3)], [(0, 1), (1, 0)] + ([] if apart else last))
        alone = [sent(local, [], last)] if apart else []
        total = mix(
            [local, late, got],
            [[1.0, 1.0, 1.0, 0.0, f, 1.0, 0.0, 0.0], [ff, ff, ff, 1.0, 1.0, f, 0.0, 0.0]],
            after,
        )
        more = sent(total, [(0, 1), (2, 3), (3, 2)], [(0, 2), (1, 3)])
        weights = [
            unit,
            [ff, ff, ff, ff, 0.0, f, 0.0, f],
        ]
        weights += [[f] * (2 * groups)] * len(alone) + [[f, f, f, f, 0.0, 0.0, f, ff]]
        return [local, late, got] + alone + [more], weights

    def one_hop(local, late, after, apart):
        terms, weights = [local, late], [unit]
        for d in range(1, groups):
            moves = [(h, h + d) for h in range(groups - d)]
            terms.append(sent(local, moves, moves))
            weights.append([power[d]] * (2 * groups))
        return terms, weights

    spread = two_hops if square else one_hop
    scale = bins**-0.5
    terms_a, weights_a = spread(local_a, late_a, late_b, False)
    terms_b, weights_b = spread(local_b, late_b, local_b, True)
    before = part(terms_b[:-1], weights_b[:-1])
    first = functools.partial(lag_kernel, limits, scale, 0, weights_a)
    result = written(first, terms_a, [before])
    last = functools.partial(last_kernel, scale, half, weights_b[-1])
    result = written(last, [before, terms_b[-1]], [], result)
    return result.reshape(1, pairs, chans, length)


def solution(mesh):
    in_specs = (P("chan", "tm", None), P("chan", "tm"), P())
    out_specs = P("tm", None, "chan", None)
    return jax.shard_map(
        per_device, mesh=mesh, in_specs=in_specs, out_specs=out_specs, check_vma=False
    )
```

```python
import functools
import math

import jax
import jax.numpy as jnp
import numpy as np
from jax import lax
from jax.experimental import pallas as pl
from jax.experimental.pallas import tpu as pltpu
from jax.sharding import PartitionSpec as P

OFFSET_SPAN = 32
LANES = 128
DECAY = 0.99
VMEM = 24 * 1024 * 1024


def turns(number, length):
    part = (number - length * jnp.floor(number / length + 0.5)) * (1.0 / length)
    square = part * part
    cosine, sine = jnp.float32(0.0), jnp.float32(0.0)
    for k in range(10, -1, -1):
        cosine = cosine * square + (-1) ** k * (2 * math.pi) ** (2 * k) / math.factorial(2 * k)
        sine = sine * square + (-1) ** k * (2 * math.pi) ** (2 * k + 1) / math.factorial(2 * k + 1)
    return cosine, sine * part


def fill_table(table_ref, step):
    length = table_ref.shape[0]
    bins = length // 2

    def small(rows, by):
        row = lax.broadcasted_iota(jnp.int32, (rows, bins), 0)
        freq = lax.broadcasted_iota(jnp.int32, (rows, bins), 1) + 1
        return turns((row * (by * freq)).astype(jnp.float32), length)

    coarse_cos, coarse_sin = small(length // step, step)
    fine_cos, fine_sin = small(step, 1)
    for i in range(length // step):
        rows = slice(i * step, (i + 1) * step)
        cos_i, sin_i = coarse_cos[i : i + 1], coarse_sin[i : i + 1]
        cosine = (cos_i * fine_cos - sin_i * fine_sin).astype(jnp.bfloat16)
        sine = (sin_i * fine_cos + cos_i * fine_sin).astype(jnp.bfloat16)
        for t in range(bins // LANES):
            here = slice(t * LANES, (t + 1) * LANES)
            table_ref[rows, 2 * t * LANES : (2 * t + 1) * LANES] = cosine[:, here]
            table_ref[rows, (2 * t + 1) * LANES : (2 * t + 2) * LANES] = -sine[:, here]


def inverse_kernel(_, table_ref):
    length = table_ref.shape[0]
    bins = length // 2
    step = 16

    def small(rows, by, first):
        freq = (lax.broadcasted_iota(jnp.int32, (rows, length), 0) + first) * by
        lag = lax.broadcasted_iota(jnp.int32, (rows, length), 1)
        return turns((freq * lag).astype(jnp.float32), length)

    coarse_cos, coarse_sin = small(bins // step, step, 0)
    fine_cos, fine_sin = small(step, 1, 1)
    for i in range(bins // step):
        first = i * step
        cos_i, sin_i = coarse_cos[i : i + 1], coarse_sin[i : i + 1]
        cosine = cos_i * fine_cos - sin_i * fine_sin
        sine = sin_i * fine_cos + cos_i * fine_sin
        table_ref[first : first + step, :] = cosine.astype(jnp.bfloat16)
        table_ref[bins + first : bins + first + step, :] = (-sine).astype(jnp.bfloat16)


def whiten_block(x, table_ref, keep, raw_ref, white_ref, short_ref):
    wins, span, length = white_ref.shape
    bins = length // 2
    tiles = bins // LANES

    def strided(t, w):
        return raw_ref[t, pl.ds(w, span, stride=wins), :]

    total = [None] * wins
    for t in range(tiles):
        lanes = slice(2 * t * LANES, (2 * t + 2) * LANES)
        raw = jnp.dot(x, table_ref[:, lanes], preferred_element_type=jnp.float32)
        raw_ref[2 * t] = raw[:, :LANES]
        raw_ref[2 * t + 1] = raw[:, LANES:]
    for t in range(tiles):
        for w in range(wins):
            real_part, imag_part = strided(2 * t, w), strided(2 * t + 1, w)
            power = real_part * real_part + imag_part * imag_part
            total[w] = power if t == 0 else total[w] + power
    for w in range(wins):
        decay = float(np.float32(DECAY) ** np.float32(wins - 1 - w))
        level = jnp.sum(total[w], axis=-1, keepdims=True) * (0.01 / bins) + 1e-06
        alive = keep[:, w * LANES : (w + 1) * LANES]
        for t in range(tiles):
            part = [strided(2 * t, w), strided(2 * t + 1, w)]
            power = part[0] * part[0] + part[1] * part[1]
            scale = alive * lax.rsqrt(power + level)
            for i, s in enumerate((t, tiles + t)):
                value = part[i] * scale
                here = pl.ds(w * length + s * LANES, LANES)
                white_ref[w, :, s * LANES : (s + 1) * LANES] = value * decay
                short_ref[:, here] = value.astype(jnp.bfloat16)


def head_kernel(
    x_hbm,
    valid_hbm,
    offsets_hbm,
    white_ref,
    short_ref,
    table_ref,
    pick_ref,
    keep_ref,
    x_ref,
    valid_ref,
    offsets_ref,
    raw_ref,
    sems,
):
    wins, span, length = white_ref.shape
    pairs = offsets_ref.shape[0]
    copies = [
        pltpu.make_async_copy(valid_hbm, valid_ref, sems.at[0]),
        pltpu.make_async_copy(offsets_hbm, offsets_ref, sems.at[1]),
        pltpu.make_async_copy(x_hbm.at[pl.ds(0, span * wins)], x_ref, sems.at[2]),
    ]
    for copy in copies:
        copy.start()
    fill_table(table_ref, 16)
    copies[0].wait()
    copies[1].wait()
    ahead = lax.broadcasted_iota(jnp.int32, (span, 2 * span), 1) - lax.broadcasted_iota(
        jnp.int32, (span, 2 * span), 0
    )
    for k in range(pairs):
        chosen_row = jnp.where(ahead == offsets_ref[k], jnp.float32(1.0), jnp.float32(0.0))
        pick_ref[k] = chosen_row.astype(jnp.bfloat16)
    owner = lax.broadcasted_iota(jnp.int32, (wins, wins * LANES), 0)
    column = lax.broadcasted_iota(jnp.int32, (wins, wins * LANES), 1) // LANES
    keep_ref[...] = lax.dot_general(
        valid_ref[...].astype(jnp.float32).astype(jnp.bfloat16),
        (owner == column).astype(jnp.float32).astype(jnp.bfloat16),
        (((0,), (0,)), ((), ())),
        preferred_element_type=jnp.float32,
    )
    copies[2].wait()
    whiten_block(x_ref[...], table_ref, keep_ref[:span], raw_ref, white_ref, short_ref)


def stack_pairs(pick_ref, white_ref, near_ref, parts_refs, out_ref):
    wins, _, length = white_ref.shape
    pairs, rows, reach = pick_ref.shape
    bins = length // 2
    size = pairs // len(parts_refs)

    def select(group, w):
        pick = pick_ref[group * size : (group + 1) * size].reshape(size * rows, reach)
        near = near_ref[:, w * length : (w + 1) * length]
        parts_refs[group][w] = jnp.dot(pick, near, preferred_element_type=jnp.float32)

    blocks = [(c, t) for c in range(0, rows, 16) for t in range(bins // LANES)]
    for w in range(wins):
        select(0, w)
    for group, parts_ref in enumerate(parts_refs):
        ahead = list(range(wins)) if group + 1 < len(parts_refs) else []
        for i, (c, t) in enumerate(blocks):
            for w in ahead[i :: len(blocks)]:
                select(group + 1, w)
            re = slice(t * LANES, (t + 1) * LANES)
            im = slice(bins + t * LANES, bins + (t + 1) * LANES)
            head_re = [white_ref[w, c : c + 16, re] for w in range(wins)]
            head_im = [white_ref[w, c : c + 16, im] for w in range(wins)]
            for k in range(size):
                here = slice(k * rows + c, k * rows + c + 16)
                total_re = total_im = None
                for w in range(wins):
                    part_re, part_im = parts_ref[w, here, re], parts_ref[w, here, im]
                    cross_re = head_re[w] * part_re + head_im[w] * part_im
                    cross_im = head_im[w] * part_re - head_re[w] * part_im
                    total_re = cross_re if w == 0 else total_re + cross_re
                    total_im = cross_im if w == 0 else total_im + cross_im
                pair = group * size + k
                out_ref[pair, c : c + 16, re] = total_re.astype(out_ref.dtype)
                out_ref[pair, c : c + 16, im] = total_im.astype(out_ref.dtype)


def role(limits):
    odd = lax.rem(lax.axis_index("chan"), 2)
    first = lax.axis_index("tm") < jnp.where(odd == 0, *limits)
    return jnp.where(first, 0, 1 + odd)


def tail_kernel(
    limits,
    now,
    x_ref,
    table_ref,
    keep_ref,
    pick_ref,
    head_ref,
    edge_ref,
    after_ref,
    white_ref,
    short_ref,
    out_ref,
    raw_ref,
    near_ref,
    *parts_refs,
):
    wins, span, length = white_ref.shape
    rows = slice(span * wins, 2 * span * wins)

    @pl.when(role(limits) == now)
    def _():
        x = x_ref[rows, :]
        whiten_block(x, table_ref, keep_ref[span:], raw_ref, white_ref, short_ref)
        near_ref[:span] = edge_ref[...]
        near_ref[span:] = short_ref[...]
        stack_pairs(pick_ref, head_ref, near_ref, parts_refs, out_ref)


def cross_kernel(
    limits, now, pick_ref, white_ref, short_ref, edge_ref, after_ref, out_ref, near_ref, *parts_refs
):
    span = short_ref.shape[0]

    @pl.when(role(limits) == now)
    def _():
        near_ref[:span] = short_ref[...]
        near_ref[span:] = edge_ref[...]
        stack_pairs(pick_ref, white_ref, near_ref, parts_refs, out_ref)


def chosen(options, place):
    value = jnp.float32(options[0])
    for i, option in enumerate(options[1:]):
        value = jnp.where(place == i + 1, jnp.float32(option), value)
    return value


def weighted(limits, terms, weights, place):
    total = None
    mine = role(limits)
    late = len(terms) - len(weights)
    first = terms[late][...]
    for i in range(late - 1, -1, -1):
        first = jnp.where(mine == i, terms[i][...], first)
    for term, options in zip([first] + list(terms[late + 1 :]), weights):
        value = term[...].astype(jnp.float32)
        if set(options) != {1.0}:
            value = value * (options[0] if len(set(options)) == 1 else chosen(options, place))
        total = value if total is None else total + value
    return total


def whereabouts(groups):
    return lax.rem(lax.axis_index("chan"), 2) * groups + lax.axis_index("tm")


def mix_kernel(limits, weights, *refs):
    count = len(weights) + 1
    place = whereabouts(len(weights[0]) // 2)
    total = weighted(limits, refs[:count], weights, place)
    refs[-1][...] = total.astype(refs[-1].dtype)


def to_lags(stack, table):
    count = stack.shape[0]
    high = stack.astype(jnp.bfloat16)
    low = (stack - high.astype(jnp.float32)).astype(jnp.bfloat16)
    both = jnp.dot(jnp.concatenate([high, low]), table, preferred_element_type=jnp.float32)
    return both[:count] + both[count:]


def part_kernel(limits, weights, table_ref, *refs):
    place = whereabouts(len(weights[0]) // 2)
    out_ref = refs[-1]
    stack = weighted(limits, refs[: len(weights) + 2], weights, place).reshape(out_ref.shape)
    out_ref[...] = to_lags(stack, table_ref[...])


def lag_kernel(limits, scale, first, weights, table_ref, *rest):
    out_hbm, stage_ref, sem = rest[-3:]
    place = whereabouts(len(weights[0]) // 2)
    pairs, rows, length = stage_ref.shape
    stack = weighted(limits, rest[: len(weights) + 2], weights, place)
    stack = stack.reshape(pairs * rows, length)
    lagged = to_lags(stack, table_ref[...]) * scale
    stage_ref[...] = lagged.astype(stage_ref.dtype).reshape(pairs, rows, length)
    copy = pltpu.make_async_copy(stage_ref, out_hbm.at[:, pl.ds(first, rows)], sem)
    copy.start()
    copy.wait()


def last_kernel(scale, first, weights, table_ref, part_ref, more_ref, *rest):
    out_hbm, stage_ref, sem = rest[-3:]
    place = whereabouts(len(weights) // 2)
    pairs, rows, length = stage_ref.shape
    more = more_ref[...].reshape(pairs * rows, length)
    lagged = jnp.dot(more, table_ref[...], preferred_element_type=jnp.float32)
    lagged = (part_ref[...] + lagged * chosen(weights, place)) * scale
    stage_ref[...] = lagged.astype(stage_ref.dtype).reshape(pairs, rows, length)
    copy = pltpu.make_async_copy(stage_ref, out_hbm.at[:, pl.ds(first, rows)], sem)
    copy.start()
    copy.wait()


def cost(flops, moved):
    return pl.CostEstimate(flops=flops, bytes_accessed=moved, transcendentals=0)


def whole(memory=pltpu.VMEM):
    return pl.BlockSpec(memory_space=memory)


def per_device(samples, valid, offsets):
    chans, wins, length = samples.shape
    bins = length // 2
    span = OFFSET_SPAN
    pairs = offsets.shape[0]
    tiles = bins // LANES
    groups = lax.axis_size("tm")
    factor = float(np.float32(DECAY) ** np.float32(wins))
    params = pltpu.CompilerParams(vmem_limit_bytes=VMEM)

    def in_hbm(value):
        return pltpu.with_memory_space_constraint(value, pltpu.HBM)

    half = chans - span
    flat = samples.reshape(chans * wins, length)
    white_type = jax.ShapeDtypeStruct((wins, span, length), jnp.float32)
    short_type = jax.ShapeDtypeStruct((span, wins * length), jnp.bfloat16)
    local_type = jax.ShapeDtypeStruct((pairs, span, length), jnp.bfloat16)
    raw_scratch = pltpu.VMEM((2 * tiles, span * wins, LANES), jnp.float32)
    near_scratch = pltpu.VMEM((2 * span, wins * length), jnp.bfloat16)
    parts_scratch = [pltpu.VMEM((wins, pairs // 4 * span, length), jnp.float32)] * 4

    white_a, short_a, table, pick, keep = pl.pallas_call(
        head_kernel,
        out_shape=(
            white_type,
            short_type,
            jax.ShapeDtypeStruct((length, length), jnp.bfloat16),
            jax.ShapeDtypeStruct((pairs, span, 2 * span), jnp.bfloat16),
            jax.ShapeDtypeStruct((chans, wins * LANES), jnp.float32),
        ),
        in_specs=[whole(pltpu.HBM)] * 3,
        out_specs=(whole(),) * 5,
        scratch_shapes=[
            pltpu.VMEM((span * wins, length), jnp.bfloat16),
            pltpu.VMEM((wins, chans), jnp.int32),
            pltpu.SMEM((pairs,), jnp.int32),
            raw_scratch,
            pltpu.SemaphoreType.DMA((3,)),
        ],
        compiler_params=params,
        cost_estimate=cost(span * wins * length * length * 2, 2 * 1024 * 1024),
        name="head",
    )(in_hbm(flat), in_hbm(valid.T), in_hbm(offsets))

    ring = lax.axis_size("chan")
    edge = lax.ppermute(short_a, "chan", [(i, i - 1) for i in range(1, ring)])

    columns = min(d for d in range(1, groups + 1) if groups % d == 0 and d * d >= groups)
    square = columns == 2 and groups == columns * columns
    limits = (2, 3) if square else (groups, groups)

    def tail(now, after):
        return pl.pallas_call(
            functools.partial(tail_kernel, limits, now),
            out_shape=(white_type, short_type, local_type),
            in_specs=[whole()] * 6 + [whole(pl.ANY)],
            out_specs=(whole(),) * 3,
            scratch_shapes=[raw_scratch, near_scratch] + parts_scratch,
            compiler_params=params,
            cost_estimate=cost(span * wins * length * length * 4, 4 * 1024 * 1024),
            name="tail",
        )(flat, table, keep, pick, white_a, short_a, after)

    def cross(now, white, short, after):
        return pl.pallas_call(
            functools.partial(cross_kernel, limits, now),
            out_shape=local_type,
            in_specs=[whole()] * 4 + [whole(pl.ANY)],
            out_specs=whole(),
            scratch_shapes=[near_scratch] + parts_scratch,
            compiler_params=params,
            cost_estimate=cost(pairs * span * wins * bins * 8, 4 * 1024 * 1024),
            name="cross",
        )(pick, white, short, edge, after)

    white_b, short_b, local_a = tail(0, table)
    local_b = cross(0, white_b, short_b, table)
    white_late, short_late, late_a = tail(1, local_b)
    late_b = cross(1, white_late, short_late, local_b)

    power = [float(np.float32(factor) ** np.float32(d)) for d in range(groups)]
    def sent(value, even, odd):
        moves = [
            (c * groups + here, c * groups + there)
            for c in range(ring)
            for here, there in (odd if c % 2 else even)
        ]
        return lax.ppermute(value, ("chan", "tm"), moves)

    def mix(terms, weights, after):
        return pl.pallas_call(
            functools.partial(mix_kernel, limits, weights),
            out_shape=local_type,
            in_specs=[whole()] * len(terms) + [whole(pl.ANY)],
            out_specs=whole(),
            compiler_params=params,
            cost_estimate=cost(len(terms) * terms[0].size * 4, 1024 * 1024),
            name="mix",
        )(*terms, after)

    inverse = pl.pallas_call(
        inverse_kernel,
        out_shape=jax.ShapeDtypeStruct((length, length), jnp.bfloat16),
        in_specs=[whole(pl.ANY)],
        out_specs=whole(),
        compiler_params=params,
        cost_estimate=cost(length * bins * 32, 512 * 1024),
        name="inverse",
    )(local_b)

    def written(kernel, terms, later, *so_far):
        return pl.pallas_call(
            kernel,
            out_shape=jax.ShapeDtypeStruct((pairs, chans, length), jnp.bfloat16),
            in_specs=[whole()] * (1 + len(terms)) + [whole(pl.ANY)] * (len(later) + len(so_far)),
            out_specs=whole(pl.ANY),
            scratch_shapes=[
                pltpu.VMEM((pairs, span, length), jnp.bfloat16),
                pltpu.SemaphoreType.DMA,
            ],
            input_output_aliases={1 + len(terms) + len(later): 0} if so_far else {},
            compiler_params=params,
            cost_estimate=cost(pairs * span * length * length * 4, 1024 * 1024),
            name="lags",
        )(inverse, *terms, *later, *so_far)

    def part(terms, weights):
        return pl.pallas_call(
            functools.partial(part_kernel, limits, weights),
            out_shape=jax.ShapeDtypeStruct((pairs * span, length), jnp.float32),
            in_specs=[whole()] * (1 + len(terms)),
            out_specs=whole(),
            compiler_params=params,
            cost_estimate=cost(pairs * span * length * length * 4, 1024 * 1024),
            name="part",
        )(inverse, *terms)

    unit = [1.0] * (2 * groups)

    def two_hops(local, late, after, apart):
        f, ff = power[1], power[2]
        last = [(2, 3)]
        got = sent(local, [(0, 2), (1, 3)], [(0, 1), (1, 0)] + ([] if apart else last))
        alone = [sent(local, [], last)] if apart else []
        total = mix(
            [local, late, got],
            [[1.0, 1.0, 1.0, 0.0, f, 1.0, 0.0, 0.0], [ff, ff, ff, 1.0, 1.0, f, 0.0, 0.0]],
            after,
        )
        more = sent(total, [(0, 1), (2, 3), (3, 2)], [(0, 2), (1, 3)])
        weights = [
            unit,
            [ff, ff, ff, ff, 0.0, f, 0.0, f],
        ]
        weights += [[f] * (2 * groups)] * len(alone) + [[f, f, f, f, 0.0, 0.0, f, ff]]
        return total, [got] + alone + [more], weights

    def one_hop(local, late, after, apart):
        terms, weights = [], [unit]
        for d in range(1, groups):
            moves = [(h, h + d) for h in range(groups - d)]
            terms.append(sent(local, moves, moves))
            weights.append([power[d]] * (2 * groups))
        return local, terms, weights

    spread = two_hops if square else one_hop
    scale = bins**-0.5
    _, terms_a, weights_a = spread(local_a, late_a, late_b, False)
    ahead, terms_b, weights_b = spread(local_b, late_b, local_b, True)
    white_last, short_last, last_a = tail(2, ahead)
    last_b = cross(2, white_last, short_last, ahead)
    terms_a = [local_a, late_a, last_a] + terms_a
    terms_b = [local_b, late_b, last_b] + terms_b
    before = part(terms_b[:-1], weights_b[:-1])
    first = functools.partial(lag_kernel, limits, scale, 0, weights_a)
    result = written(first, terms_a, [before])
    last = functools.partial(last_kernel, scale, half, weights_b[-1])
    result = written(last, [before, terms_b[-1]], [], result)
    return result.reshape(1, pairs, chans, length)


def solution(mesh):
    in_specs = (P("chan", "tm", None), P("chan", "tm"), P())
    out_specs = P("tm", None, "chan", None)
    return jax.shard_map(
        per_device, mesh=mesh, in_specs=in_specs, out_specs=out_specs, check_vma=False
    )
```

```python
import functools
import math

import jax
import jax.numpy as jnp
import numpy as np
from jax import lax
from jax.experimental import pallas as pl
from jax.experimental.pallas import tpu as pltpu
from jax.sharding import PartitionSpec as P

OFFSET_SPAN = 32
LANES = 128
DECAY = 0.99
VMEM = 24 * 1024 * 1024


def turns(number, length):
    part = (number - length * jnp.floor(number / length + 0.5)) * (1.0 / length)
    square = part * part
    cosine, sine = jnp.float32(0.0), jnp.float32(0.0)
    for k in range(10, -1, -1):
        cosine = cosine * square + (-1) ** k * (2 * math.pi) ** (2 * k) / math.factorial(2 * k)
        sine = sine * square + (-1) ** k * (2 * math.pi) ** (2 * k + 1) / math.factorial(2 * k + 1)
    return cosine, sine * part


def fill_table(table_ref, step):
    length = table_ref.shape[0]
    bins = length // 2

    def small(rows, by):
        row = lax.broadcasted_iota(jnp.int32, (rows, bins), 0)
        freq = lax.broadcasted_iota(jnp.int32, (rows, bins), 1) + 1
        return turns((row * (by * freq)).astype(jnp.float32), length)

    coarse_cos, coarse_sin = small(length // step, step)
    fine_cos, fine_sin = small(step, 1)
    for i in range(length // step):
        rows = slice(i * step, (i + 1) * step)
        cos_i, sin_i = coarse_cos[i : i + 1], coarse_sin[i : i + 1]
        cosine = (cos_i * fine_cos - sin_i * fine_sin).astype(jnp.bfloat16)
        sine = (sin_i * fine_cos + cos_i * fine_sin).astype(jnp.bfloat16)
        for t in range(bins // LANES):
            here = slice(t * LANES, (t + 1) * LANES)
            table_ref[rows, 2 * t * LANES : (2 * t + 1) * LANES] = cosine[:, here]
            table_ref[rows, (2 * t + 1) * LANES : (2 * t + 2) * LANES] = -sine[:, here]


def inverse_kernel(_, table_ref):
    length = table_ref.shape[0]
    bins = length // 2
    step = 16

    def small(rows, by, first):
        freq = (lax.broadcasted_iota(jnp.int32, (rows, length), 0) + first) * by
        lag = lax.broadcasted_iota(jnp.int32, (rows, length), 1)
        return turns((freq * lag).astype(jnp.float32), length)

    coarse_cos, coarse_sin = small(bins // step, step, 0)
    fine_cos, fine_sin = small(step, 1, 1)
    for i in range(bins // step):
        first = i * step
        cos_i, sin_i = coarse_cos[i : i + 1], coarse_sin[i : i + 1]
        cosine = cos_i * fine_cos - sin_i * fine_sin
        sine = sin_i * fine_cos + cos_i * fine_sin
        table_ref[first : first + step, :] = cosine.astype(jnp.bfloat16)
        table_ref[bins + first : bins + first + step, :] = (-sine).astype(jnp.bfloat16)


def whiten_block(x, table_ref, keep, raw_ref, white_ref, short_ref):
    wins, span, length = white_ref.shape
    bins = length // 2
    tiles = bins // LANES

    def strided(t, w):
        return raw_ref[t, pl.ds(w, span, stride=wins), :]

    total = [None] * wins
    for t in range(tiles):
        lanes = slice(2 * t * LANES, (2 * t + 2) * LANES)
        raw = jnp.dot(x, table_ref[:, lanes], preferred_element_type=jnp.float32)
        raw_ref[2 * t] = raw[:, :LANES]
        raw_ref[2 * t + 1] = raw[:, LANES:]
    for t in range(tiles):
        for w in range(wins):
            real_part, imag_part = strided(2 * t, w), strided(2 * t + 1, w)
            power = real_part * real_part + imag_part * imag_part
            total[w] = power if t == 0 else total[w] + power
    for w in range(wins):
        decay = float(np.float32(DECAY) ** np.float32(wins - 1 - w))
        level = jnp.sum(total[w], axis=-1, keepdims=True) * (0.01 / bins) + 1e-06
        alive = keep[:, w * LANES : (w + 1) * LANES]
        for t in range(tiles):
            part = [strided(2 * t, w), strided(2 * t + 1, w)]
            power = part[0] * part[0] + part[1] * part[1]
            scale = alive * lax.rsqrt(power + level)
            for i, s in enumerate((t, tiles + t)):
                value = part[i] * scale
                here = pl.ds(w * length + s * LANES, LANES)
                white_ref[w, :, s * LANES : (s + 1) * LANES] = value * decay
                short_ref[:, here] = value.astype(jnp.bfloat16)


def head_kernel(
    x_hbm,
    valid_hbm,
    offsets_hbm,
    white_ref,
    short_ref,
    table_ref,
    pick_ref,
    keep_ref,
    x_ref,
    valid_ref,
    offsets_ref,
    raw_ref,
    sems,
):
    wins, span, length = white_ref.shape
    pairs = offsets_ref.shape[0]
    copies = [
        pltpu.make_async_copy(valid_hbm, valid_ref, sems.at[0]),
        pltpu.make_async_copy(offsets_hbm, offsets_ref, sems.at[1]),
        pltpu.make_async_copy(x_hbm.at[pl.ds(0, span * wins)], x_ref, sems.at[2]),
    ]
    for copy in copies:
        copy.start()
    fill_table(table_ref, 16)
    copies[0].wait()
    copies[1].wait()
    ahead = lax.broadcasted_iota(jnp.int32, (span, 2 * span), 1) - lax.broadcasted_iota(
        jnp.int32, (span, 2 * span), 0
    )
    for k in range(pairs):
        chosen_row = jnp.where(ahead == offsets_ref[k], jnp.float32(1.0), jnp.float32(0.0))
        pick_ref[k] = chosen_row.astype(jnp.bfloat16)
    owner = lax.broadcasted_iota(jnp.int32, (wins, wins * LANES), 0)
    column = lax.broadcasted_iota(jnp.int32, (wins, wins * LANES), 1) // LANES
    keep_ref[...] = lax.dot_general(
        valid_ref[...].astype(jnp.float32).astype(jnp.bfloat16),
        (owner == column).astype(jnp.float32).astype(jnp.bfloat16),
        (((0,), (0,)), ((), ())),
        preferred_element_type=jnp.float32,
    )
    copies[2].wait()
    whiten_block(x_ref[...], table_ref, keep_ref[:span], raw_ref, white_ref, short_ref)


def stack_pairs(pick_ref, white_ref, near_ref, parts_refs, out_ref):
    wins, _, length = white_ref.shape
    pairs, rows, reach = pick_ref.shape
    bins = length // 2
    size = pairs // len(parts_refs)

    def select(group, w):
        pick = pick_ref[group * size : (group + 1) * size].reshape(size * rows, reach)
        near = near_ref[:, w * length : (w + 1) * length]
        parts_refs[group][w] = jnp.dot(pick, near, preferred_element_type=jnp.float32)

    blocks = [(c, t) for c in range(0, rows, 16) for t in range(bins // LANES)]
    for w in range(wins):
        select(0, w)
    for group, parts_ref in enumerate(parts_refs):
        ahead = list(range(wins)) if group + 1 < len(parts_refs) else []
        for i, (c, t) in enumerate(blocks):
            for w in ahead[i :: len(blocks)]:
                select(group + 1, w)
            re = slice(t * LANES, (t + 1) * LANES)
            im = slice(bins + t * LANES, bins + (t + 1) * LANES)
            head_re = [white_ref[w, c : c + 16, re] for w in range(wins)]
            head_im = [white_ref[w, c : c + 16, im] for w in range(wins)]
            for k in range(size):
                here = slice(k * rows + c, k * rows + c + 16)
                total_re = total_im = None
                for w in range(wins):
                    part_re, part_im = parts_ref[w, here, re], parts_ref[w, here, im]
                    cross_re = head_re[w] * part_re + head_im[w] * part_im
                    cross_im = head_im[w] * part_re - head_re[w] * part_im
                    total_re = cross_re if w == 0 else total_re + cross_re
                    total_im = cross_im if w == 0 else total_im + cross_im
                pair = group * size + k
                out_ref[pair, c : c + 16, re] = total_re.astype(out_ref.dtype)
                out_ref[pair, c : c + 16, im] = total_im.astype(out_ref.dtype)


def role(limits):
    odd = lax.rem(lax.axis_index("chan"), 2)
    first = lax.axis_index("tm") < jnp.where(odd == 0, *limits)
    return jnp.where(first, 0, 1 + odd)


def tail_kernel(
    limits,
    now,
    x_ref,
    table_ref,
    keep_ref,
    pick_ref,
    head_ref,
    edge_ref,
    after_ref,
    white_ref,
    short_ref,
    out_ref,
    raw_ref,
    near_ref,
    *parts_refs,
):
    wins, span, length = white_ref.shape
    rows = slice(span * wins, 2 * span * wins)

    @pl.when(role(limits) == now)
    def _():
        x = x_ref[rows, :]
        whiten_block(x, table_ref, keep_ref[span:], raw_ref, white_ref, short_ref)
        near_ref[:span] = edge_ref[...]
        near_ref[span:] = short_ref[...]
        stack_pairs(pick_ref, head_ref, near_ref, parts_refs, out_ref)


def cross_kernel(
    limits, now, pick_ref, white_ref, short_ref, edge_ref, after_ref, out_ref, near_ref, *parts_refs
):
    span = short_ref.shape[0]

    @pl.when(role(limits) == now)
    def _():
        near_ref[:span] = short_ref[...]
        near_ref[span:] = edge_ref[...]
        stack_pairs(pick_ref, white_ref, near_ref, parts_refs, out_ref)


def last_cross_kernel(
    limits,
    limits_b,
    pick_ref,
    early_white_ref,
    early_short_ref,
    white_ref,
    short_ref,
    edge_ref,
    after_ref,
    out_ref,
    near_ref,
    *parts_refs,
):
    span = short_ref.shape[0]
    for late, heads, shorts in ((0, early_white_ref, early_short_ref), (2, white_ref, short_ref)):

        @pl.when((role(limits_b) == 2) & (role(limits) == late))
        def _(heads=heads, shorts=shorts):
            near_ref[:span] = shorts[...]
            near_ref[span:] = edge_ref[...]
            stack_pairs(pick_ref, heads, near_ref, parts_refs, out_ref)


def chosen(options, place):
    value = jnp.float32(options[0])
    for i, option in enumerate(options[1:]):
        value = jnp.where(place == i + 1, jnp.float32(option), value)
    return value


def weighted(limits, terms, weights, place):
    total = None
    mine = role(limits)
    late = len(terms) - len(weights)
    first = terms[late][...]
    for i in range(late - 1, -1, -1):
        first = jnp.where(mine == i, terms[i][...], first)
    for term, options in zip([first] + list(terms[late + 1 :]), weights):
        value = term[...].astype(jnp.float32)
        if set(options) != {1.0}:
            value = value * (options[0] if len(set(options)) == 1 else chosen(options, place))
        total = value if total is None else total + value
    return total


def whereabouts(groups):
    return lax.rem(lax.axis_index("chan"), 2) * groups + lax.axis_index("tm")


def mix_kernel(limits, weights, *refs):
    count = len(weights) + 1
    place = whereabouts(len(weights[0]) // 2)
    total = weighted(limits, refs[:count], weights, place)
    refs[-1][...] = total.astype(refs[-1].dtype)


def to_lags(stack, table):
    count = stack.shape[0]
    high = stack.astype(jnp.bfloat16)
    low = (stack - high.astype(jnp.float32)).astype(jnp.bfloat16)
    both = jnp.dot(jnp.concatenate([high, low]), table, preferred_element_type=jnp.float32)
    return both[:count] + both[count:]


def part_kernel(limits, weights, table_ref, *refs):
    place = whereabouts(len(weights[0]) // 2)
    out_ref = refs[-1]
    stack = weighted(limits, refs[: len(weights) + 2], weights, place).reshape(out_ref.shape)
    out_ref[...] = to_lags(stack, table_ref[...])


def lag_kernel(limits, scale, first, weights, table_ref, *rest):
    out_hbm, stage_ref, sem = rest[-3:]
    place = whereabouts(len(weights[0]) // 2)
    pairs, rows, length = stage_ref.shape
    stack = weighted(limits, rest[: len(weights) + 2], weights, place)
    stack = stack.reshape(pairs * rows, length)
    lagged = to_lags(stack, table_ref[...]) * scale
    stage_ref[...] = lagged.astype(stage_ref.dtype).reshape(pairs, rows, length)
    copy = pltpu.make_async_copy(stage_ref, out_hbm.at[:, pl.ds(first, rows)], sem)
    copy.start()
    copy.wait()


def last_kernel(scale, first, weights, table_ref, part_ref, more_ref, *rest):
    out_hbm, stage_ref, sem = rest[-3:]
    place = whereabouts(len(weights) // 2)
    pairs, rows, length = stage_ref.shape
    more = more_ref[...].reshape(pairs * rows, length)
    lagged = jnp.dot(more, table_ref[...], preferred_element_type=jnp.float32)
    lagged = (part_ref[...] + lagged * chosen(weights, place)) * scale
    stage_ref[...] = lagged.astype(stage_ref.dtype).reshape(pairs, rows, length)
    copy = pltpu.make_async_copy(stage_ref, out_hbm.at[:, pl.ds(first, rows)], sem)
    copy.start()
    copy.wait()


def cost(flops, moved):
    return pl.CostEstimate(flops=flops, bytes_accessed=moved, transcendentals=0)


def whole(memory=pltpu.VMEM):
    return pl.BlockSpec(memory_space=memory)


def per_device(samples, valid, offsets):
    chans, wins, length = samples.shape
    bins = length // 2
    span = OFFSET_SPAN
    pairs = offsets.shape[0]
    tiles = bins // LANES
    groups = lax.axis_size("tm")
    factor = float(np.float32(DECAY) ** np.float32(wins))
    params = pltpu.CompilerParams(vmem_limit_bytes=VMEM)

    def in_hbm(value):
        return pltpu.with_memory_space_constraint(value, pltpu.HBM)

    half = chans - span
    flat = samples.reshape(chans * wins, length)
    white_type = jax.ShapeDtypeStruct((wins, span, length), jnp.float32)
    short_type = jax.ShapeDtypeStruct((span, wins * length), jnp.bfloat16)
    local_type = jax.ShapeDtypeStruct((pairs, span, length), jnp.bfloat16)
    raw_scratch = pltpu.VMEM((2 * tiles, span * wins, LANES), jnp.float32)
    near_scratch = pltpu.VMEM((2 * span, wins * length), jnp.bfloat16)
    parts_scratch = [pltpu.VMEM((wins, pairs // 4 * span, length), jnp.float32)] * 4

    white_a, short_a, table, pick, keep = pl.pallas_call(
        head_kernel,
        out_shape=(
            white_type,
            short_type,
            jax.ShapeDtypeStruct((length, length), jnp.bfloat16),
            jax.ShapeDtypeStruct((pairs, span, 2 * span), jnp.bfloat16),
            jax.ShapeDtypeStruct((chans, wins * LANES), jnp.float32),
        ),
        in_specs=[whole(pltpu.HBM)] * 3,
        out_specs=(whole(),) * 5,
        scratch_shapes=[
            pltpu.VMEM((span * wins, length), jnp.bfloat16),
            pltpu.VMEM((wins, chans), jnp.int32),
            pltpu.SMEM((pairs,), jnp.int32),
            raw_scratch,
            pltpu.SemaphoreType.DMA((3,)),
        ],
        compiler_params=params,
        cost_estimate=cost(span * wins * length * length * 2, 2 * 1024 * 1024),
        name="head",
    )(in_hbm(flat), in_hbm(valid.T), in_hbm(offsets))

    columns = min(d for d in range(1, groups + 1) if groups % d == 0 and d * d >= groups)
    square = columns == 2 and groups == columns * columns
    limits, limits_b = ((2, 3), (2, 2)) if square else ((groups, groups), (groups, groups))
    ring = lax.axis_size("chan")

    def to_previous(odd, even):
        moves = [
            (c * groups + h, (c - 1) * groups + h)
            for c in range(1, ring)
            for h in (odd if c % 2 else even)
        ]
        return lax.ppermute(short_a, ("chan", "tm"), moves)

    edge = to_previous(range(groups), range(limits_b[0]))
    edge_last = to_previous([], range(limits_b[0], groups)) if square else edge

    def tail(now, after):
        return pl.pallas_call(
            functools.partial(tail_kernel, limits, now),
            out_shape=(white_type, short_type, local_type),
            in_specs=[whole()] * 6 + [whole(pl.ANY)],
            out_specs=(whole(),) * 3,
            scratch_shapes=[raw_scratch, near_scratch] + parts_scratch,
            compiler_params=params,
            cost_estimate=cost(span * wins * length * length * 4, 4 * 1024 * 1024),
            name="tail",
        )(flat, table, keep, pick, white_a, short_a, after)

    def cross(kernel, halves, edge, after):
        return pl.pallas_call(
            kernel,
            out_shape=local_type,
            in_specs=[whole()] * (2 + len(halves)) + [whole(pl.ANY)],
            out_specs=whole(),
            scratch_shapes=[near_scratch] + parts_scratch,
            compiler_params=params,
            cost_estimate=cost(pairs * span * wins * bins * 8, 4 * 1024 * 1024),
            name="cross",
        )(pick, *halves, edge, after)

    white_b, short_b, local_a = tail(0, table)
    local_b = cross(functools.partial(cross_kernel, limits_b, 0), [white_b, short_b], edge, table)
    white_late, short_late, late_a = tail(1, local_b)
    late_b = cross(
        functools.partial(cross_kernel, limits_b, 1), [white_late, short_late], edge, local_b
    )

    power = [float(np.float32(factor) ** np.float32(d)) for d in range(groups)]
    def sent(value, even, odd):
        moves = [
            (c * groups + here, c * groups + there)
            for c in range(ring)
            for here, there in (odd if c % 2 else even)
        ]
        return lax.ppermute(value, ("chan", "tm"), moves)

    def mix(terms, weights, limits_of, after):
        return pl.pallas_call(
            functools.partial(mix_kernel, limits_of, weights),
            out_shape=local_type,
            in_specs=[whole()] * len(terms) + [whole(pl.ANY)] * len(after),
            out_specs=whole(),
            compiler_params=params,
            cost_estimate=cost(len(terms) * terms[0].size * 4, 1024 * 1024),
            name="mix",
        )(*terms, *after)

    inverse = pl.pallas_call(
        inverse_kernel,
        out_shape=jax.ShapeDtypeStruct((length, length), jnp.bfloat16),
        in_specs=[whole(pl.ANY)],
        out_specs=whole(),
        compiler_params=params,
        cost_estimate=cost(length * bins * 32, 512 * 1024),
        name="inverse",
    )(local_b)

    def written(kernel, terms, later, *so_far):
        return pl.pallas_call(
            kernel,
            out_shape=jax.ShapeDtypeStruct((pairs, chans, length), jnp.bfloat16),
            in_specs=[whole()] * (1 + len(terms)) + [whole(pl.ANY)] * (len(later) + len(so_far)),
            out_specs=whole(pl.ANY),
            scratch_shapes=[
                pltpu.VMEM((pairs, span, length), jnp.bfloat16),
                pltpu.SemaphoreType.DMA,
            ],
            input_output_aliases={1 + len(terms) + len(later): 0} if so_far else {},
            compiler_params=params,
            cost_estimate=cost(pairs * span * length * length * 4, 1024 * 1024),
            name="lags",
        )(inverse, *terms, *later, *so_far)

    def part(terms, weights, after):
        return pl.pallas_call(
            functools.partial(part_kernel, limits_b, weights),
            out_shape=jax.ShapeDtypeStruct((pairs * span, length), jnp.float32),
            in_specs=[whole()] * (1 + len(terms)) + [whole(pl.ANY)],
            out_specs=whole(),
            compiler_params=params,
            cost_estimate=cost(pairs * span * length * length * 4, 1024 * 1024),
            name="part",
        )(inverse, *terms, after)

    unit = [1.0] * (2 * groups)

    def two_hops(local, late, limits_of, after, alone):
        f, ff = power[1], power[2]
        last = [(2, 3)]
        got = sent(local, [(0, 2), (1, 3)], [(0, 1), (1, 0)] + ([] if alone else last))
        total = mix(
            [local, late, got],
            [[1.0, 1.0, 1.0, 0.0, f, 1.0, 0.0, 0.0], [ff, ff, ff, 1.0, 1.0, f, 0.0, 0.0]],
            limits_of,
            after,
        )
        more = sent(total, [(0, 1), (2, 3), (3, 2)], [(0, 2), (1, 3)])
        weights = [
            unit,
            [ff, ff, ff, ff, 0.0, f, 0.0, f],
        ]
        weights.append([f, f, f, f, 0.0, 0.0, f, ff])
        return total, [got, more], weights

    def one_hop(local, late, limits_of, after, alone):
        terms, weights = [], [unit]
        for d in range(1, groups):
            moves = [(h, h + d) for h in range(groups - d)]
            terms.append(sent(local, moves, moves))
            weights.append([power[d]] * (2 * groups))
        return local, terms, weights

    spread = two_hops if square else one_hop
    scale = bins**-0.5
    white_last, short_last, last_a = tail(2, local_b)
    ahead, terms_a, weights_a = spread(local_a, late_a, limits, [late_b, last_a], False)
    _, terms_b, weights_b = spread(local_b, late_b, limits_b, [], True)
    last_b = cross(
        functools.partial(last_cross_kernel, limits, limits_b),
        [white_b, short_b, white_last, short_last],
        edge_last,
        ahead,
    )
    if square:
        terms_b[1:1] = [sent(last_b, [], [(2, 3)])]
        weights_b[2:2] = [[power[1]] * (2 * groups)]
    first = functools.partial(lag_kernel, limits, scale, 0, weights_a)
    result = written(first, [local_a, late_a, last_a] + terms_a, [])
    before = part([local_b, late_b, last_b] + terms_b[:-1], weights_b[:-1], result)
    last = functools.partial(last_kernel, scale, half, weights_b[-1])
    result = written(last, [before, terms_b[-1]], [], result)
    return result.reshape(1, pairs, chans, length)


def solution(mesh):
    in_specs = (P("chan", "tm", None), P("chan", "tm"), P())
    out_specs = P("tm", None, "chan", None)
    return jax.shard_map(
        per_device, mesh=mesh, in_specs=in_specs, out_specs=out_specs, check_vma=False
    )
```

```python
import functools
import math

import jax
import jax.numpy as jnp
import numpy as np
from jax import lax
from jax.experimental import pallas as pl
from jax.experimental.pallas import tpu as pltpu
from jax.sharding import PartitionSpec as P

OFFSET_SPAN = 32
LANES = 128
DECAY = 0.99
X_PIECES = 4
VMEM = 24 * 1024 * 1024


def turns(number, length):
    part = (number - length * jnp.floor(number / length + 0.5)) * (1.0 / length)
    square = part * part
    cosine, sine = jnp.float32(0.0), jnp.float32(0.0)
    for k in range(10, -1, -1):
        cosine = cosine * square + (-1) ** k * (2 * math.pi) ** (2 * k) / math.factorial(2 * k)
        sine = sine * square + (-1) ** k * (2 * math.pi) ** (2 * k + 1) / math.factorial(2 * k + 1)
    return cosine, sine * part


def fill_table(table_ref, step):
    length = table_ref.shape[0]
    bins = length // 2

    def small(rows, by):
        row = lax.broadcasted_iota(jnp.int32, (rows, bins), 0)
        freq = lax.broadcasted_iota(jnp.int32, (rows, bins), 1) + 1
        return turns((row * (by * freq)).astype(jnp.float32), length)

    coarse_cos, coarse_sin = small(length // step, step)
    fine_cos, fine_sin = small(step, 1)
    for i in range(length // step):
        rows = slice(i * step, (i + 1) * step)
        cos_i, sin_i = coarse_cos[i : i + 1], coarse_sin[i : i + 1]
        cosine = (cos_i * fine_cos - sin_i * fine_sin).astype(jnp.bfloat16)
        sine = (sin_i * fine_cos + cos_i * fine_sin).astype(jnp.bfloat16)
        for t in range(bins // LANES):
            here = slice(t * LANES, (t + 1) * LANES)
            table_ref[rows, 2 * t * LANES : (2 * t + 1) * LANES] = cosine[:, here]
            table_ref[rows, (2 * t + 1) * LANES : (2 * t + 2) * LANES] = -sine[:, here]


def inverse_kernel(_, table_ref):
    length = table_ref.shape[0]
    bins = length // 2
    step = 16

    def small(rows, by, first):
        freq = (lax.broadcasted_iota(jnp.int32, (rows, length), 0) + first) * by
        lag = lax.broadcasted_iota(jnp.int32, (rows, length), 1)
        return turns((freq * lag).astype(jnp.float32), length)

    coarse_cos, coarse_sin = small(bins // step, step, 0)
    fine_cos, fine_sin = small(step, 1, 1)
    for i in range(bins // step):
        first = i * step
        cos_i, sin_i = coarse_cos[i : i + 1], coarse_sin[i : i + 1]
        cosine = cos_i * fine_cos - sin_i * fine_sin
        sine = sin_i * fine_cos + cos_i * fine_sin
        table_ref[first : first + step, :] = cosine.astype(jnp.bfloat16)
        table_ref[bins + first : bins + first + step, :] = (-sine).astype(jnp.bfloat16)


def whiten_block(x, table_ref, keep, raw_ref, white_ref, short_ref):
    wins, span, length = white_ref.shape
    bins = length // 2
    tiles = bins // LANES

    def strided(t, w):
        return raw_ref[t, pl.ds(w, span, stride=wins), :]

    total = [None] * wins
    for t in range(tiles):
        lanes = slice(2 * t * LANES, (2 * t + 2) * LANES)
        raw = jnp.dot(x, table_ref[:, lanes], preferred_element_type=jnp.float32)
        raw_ref[2 * t] = raw[:, :LANES]
        raw_ref[2 * t + 1] = raw[:, LANES:]
    for t in range(tiles):
        for w in range(wins):
            real_part, imag_part = strided(2 * t, w), strided(2 * t + 1, w)
            power = real_part * real_part + imag_part * imag_part
            total[w] = power if t == 0 else total[w] + power
    for w in range(wins):
        decay = float(np.float32(DECAY) ** np.float32(wins - 1 - w))
        level = jnp.sum(total[w], axis=-1, keepdims=True) * (0.01 / bins) + 1e-06
        alive = keep[:, w * LANES : (w + 1) * LANES]
        for t in range(tiles):
            part = [strided(2 * t, w), strided(2 * t + 1, w)]
            power = part[0] * part[0] + part[1] * part[1]
            scale = alive * lax.rsqrt(power + level)
            for i, s in enumerate((t, tiles + t)):
                value = part[i] * scale
                here = pl.ds(w * length + s * LANES, LANES)
                white_ref[w, :, s * LANES : (s + 1) * LANES] = value * decay
                short_ref[:, here] = value.astype(jnp.bfloat16)


def head_kernel(
    x_hbm,
    valid_hbm,
    offsets_hbm,
    white_ref,
    short_ref,
    table_ref,
    pick_ref,
    keep_ref,
    x_ref,
    valid_ref,
    offsets_ref,
    raw_ref,
    sems,
):
    wins, span, length = white_ref.shape
    pairs = offsets_ref.shape[0]
    valid_copy = pltpu.make_async_copy(valid_hbm, valid_ref, sems.at[0])
    offsets_copy = pltpu.make_async_copy(offsets_hbm, offsets_ref, sems.at[1])
    size = span * wins // X_PIECES
    pieces = [pl.ds(i * size, size) for i in range(X_PIECES)]
    x_copies = [
        pltpu.make_async_copy(x_hbm.at[piece], x_ref.at[piece], sems.at[2 + i])
        for i, piece in enumerate(pieces)
    ]
    for copy in x_copies + [valid_copy, offsets_copy]:
        copy.start()
    fill_table(table_ref, 16)
    valid_copy.wait()
    offsets_copy.wait()
    ahead = lax.broadcasted_iota(jnp.int32, (span, 2 * span), 1) - lax.broadcasted_iota(
        jnp.int32, (span, 2 * span), 0
    )
    for k in range(pairs):
        chosen_row = jnp.where(ahead == offsets_ref[k], jnp.float32(1.0), jnp.float32(0.0))
        pick_ref[k] = chosen_row.astype(jnp.bfloat16)
    owner = lax.broadcasted_iota(jnp.int32, (wins, wins * LANES), 0)
    column = lax.broadcasted_iota(jnp.int32, (wins, wins * LANES), 1) // LANES
    keep_ref[...] = lax.dot_general(
        valid_ref[...].astype(jnp.float32).astype(jnp.bfloat16),
        (owner == column).astype(jnp.float32).astype(jnp.bfloat16),
        (((0,), (0,)), ((), ())),
        preferred_element_type=jnp.float32,
    )
    for copy in x_copies:
        copy.wait()
    whiten_block(x_ref[...], table_ref, keep_ref[:span], raw_ref, white_ref, short_ref)


def stack_pairs(pick_ref, white_ref, near_ref, parts_refs, out_ref):
    wins, _, length = white_ref.shape
    pairs, rows, reach = pick_ref.shape
    bins = length // 2
    size = pairs // len(parts_refs)

    def select(group, w):
        pick = pick_ref[group * size : (group + 1) * size].reshape(size * rows, reach)
        near = near_ref[:, w * length : (w + 1) * length]
        parts_refs[group][w] = jnp.dot(pick, near, preferred_element_type=jnp.float32)

    blocks = [(c, t) for c in range(0, rows, 16) for t in range(bins // LANES)]
    for w in range(wins):
        select(0, w)
    for group, parts_ref in enumerate(parts_refs):
        ahead = list(range(wins)) if group + 1 < len(parts_refs) else []
        for i, (c, t) in enumerate(blocks):
            for w in ahead[i :: len(blocks)]:
                select(group + 1, w)
            re = slice(t * LANES, (t + 1) * LANES)
            im = slice(bins + t * LANES, bins + (t + 1) * LANES)
            head_re = [white_ref[w, c : c + 16, re] for w in range(wins)]
            head_im = [white_ref[w, c : c + 16, im] for w in range(wins)]
            for k in range(size):
                here = slice(k * rows + c, k * rows + c + 16)
                total_re = total_im = None
                for w in range(wins):
                    part_re, part_im = parts_ref[w, here, re], parts_ref[w, here, im]
                    cross_re = head_re[w] * part_re + head_im[w] * part_im
                    cross_im = head_im[w] * part_re - head_re[w] * part_im
                    total_re = cross_re if w == 0 else total_re + cross_re
                    total_im = cross_im if w == 0 else total_im + cross_im
                pair = group * size + k
                out_ref[pair, c : c + 16, re] = total_re.astype(out_ref.dtype)
                out_ref[pair, c : c + 16, im] = total_im.astype(out_ref.dtype)


def role(limits):
    odd = lax.rem(lax.axis_index("chan"), 2)
    first = lax.axis_index("tm") < jnp.where(odd == 0, *limits)
    return jnp.where(first, 0, 1 + odd)


def tail_kernel(
    limits,
    now,
    x_ref,
    table_ref,
    keep_ref,
    pick_ref,
    head_ref,
    edge_ref,
    after_ref,
    white_ref,
    short_ref,
    out_ref,
    raw_ref,
    near_ref,
    *parts_refs,
):
    wins, span, length = white_ref.shape
    rows = slice(span * wins, 2 * span * wins)

    @pl.when(role(limits) == now)
    def _():
        x = x_ref[rows, :]
        whiten_block(x, table_ref, keep_ref[span:], raw_ref, white_ref, short_ref)
        near_ref[:span] = edge_ref[...]
        near_ref[span:] = short_ref[...]
        stack_pairs(pick_ref, head_ref, near_ref, parts_refs, out_ref)


def cross_kernel(
    limits, now, pick_ref, white_ref, short_ref, edge_ref, after_ref, out_ref, near_ref, *parts_refs
):
    span = short_ref.shape[0]

    @pl.when(role(limits) == now)
    def _():
        near_ref[:span] = short_ref[...]
        near_ref[span:] = edge_ref[...]
        stack_pairs(pick_ref, white_ref, near_ref, parts_refs, out_ref)


def chosen(options, place):
    value = jnp.float32(options[0])
    for i, option in enumerate(options[1:]):
        value = jnp.where(place == i + 1, jnp.float32(option), value)
    return value


def weighted(limits, terms, weights, place):
    total = None
    mine = role(limits)
    late = len(terms) - len(weights)
    first = terms[late][...]
    for i in range(late - 1, -1, -1):
        first = jnp.where(mine == i, terms[i][...], first)
    for term, options in zip([first] + list(terms[late + 1 :]), weights):
        value = term[...].astype(jnp.float32)
        if set(options) != {1.0}:
            value = value * (options[0] if len(set(options)) == 1 else chosen(options, place))
        total = value if total is None else total + value
    return total


def whereabouts(groups):
    return lax.rem(lax.axis_index("chan"), 2) * groups + lax.axis_index("tm")


def mix_kernel(limits, weights, *refs):
    count = len(weights) + 1
    place = whereabouts(len(weights[0]) // 2)
    total = weighted(limits, refs[:count], weights, place)
    refs[-1][...] = total.astype(refs[-1].dtype)


def to_lags(stack, table):
    count = stack.shape[0]
    high = stack.astype(jnp.bfloat16)
    low = (stack - high.astype(jnp.float32)).astype(jnp.bfloat16)
    both = jnp.dot(jnp.concatenate([high, low]), table, preferred_element_type=jnp.float32)
    return both[:count] + both[count:]


def part_kernel(limits, weights, table_ref, *refs):
    place = whereabouts(len(weights[0]) // 2)
    out_ref = refs[-1]
    stack = weighted(limits, refs[: len(weights) + 2], weights, place).reshape(out_ref.shape)
    out_ref[...] = to_lags(stack, table_ref[...])


def lag_kernel(limits, scale, first, weights, table_ref, *rest):
    out_hbm, stage_ref, sems = rest[-3:]
    place = whereabouts(len(weights[0]) // 2)
    pairs, rows, length = stage_ref.shape
    stack = weighted(limits, rest[: len(weights) + 2], weights, place)
    stack = stack.reshape(pairs * rows, length)
    lagged = to_lags(stack, table_ref[...]) * scale
    stage_ref[...] = lagged.astype(stage_ref.dtype).reshape(pairs, rows, length)
    copy = pltpu.make_async_copy(stage_ref, out_hbm.at[:, pl.ds(first, rows)], sems.at[0])
    copy.start()
    copy.wait()


def last_kernel(scale, first, weights, table_ref, part_ref, more_ref, *rest):
    out_hbm, stage_ref, sems = rest[-3:]
    place = whereabouts(len(weights) // 2)
    pairs, rows, length = stage_ref.shape
    more = more_ref[...].reshape(pairs * rows, length)
    lagged = jnp.dot(more, table_ref[...], preferred_element_type=jnp.float32)
    weight = chosen(weights, place)
    size = pairs // 2
    copies = []
    for piece in range(2):
        here = slice(piece * size * rows, (piece + 1) * size * rows)
        value = (part_ref[here] + lagged[here] * weight) * scale
        there = pl.ds(piece * size, size)
        stage_ref[there] = value.astype(stage_ref.dtype).reshape(size, rows, length)
        target = out_hbm.at[there, pl.ds(first, rows)]
        copies.append(pltpu.make_async_copy(stage_ref.at[there], target, sems.at[piece]))
        copies[-1].start()
    for copy in copies:
        copy.wait()


def cost(flops, moved):
    return pl.CostEstimate(flops=flops, bytes_accessed=moved, transcendentals=0)


def whole(memory=pltpu.VMEM):
    return pl.BlockSpec(memory_space=memory)


def per_device(samples, valid, offsets):
    chans, wins, length = samples.shape
    bins = length // 2
    span = OFFSET_SPAN
    pairs = offsets.shape[0]
    tiles = bins // LANES
    groups = lax.axis_size("tm")
    factor = float(np.float32(DECAY) ** np.float32(wins))
    params = pltpu.CompilerParams(vmem_limit_bytes=VMEM)

    def in_hbm(value):
        return pltpu.with_memory_space_constraint(value, pltpu.HBM)

    half = chans - span
    flat = samples.reshape(chans * wins, length)
    white_type = jax.ShapeDtypeStruct((wins, span, length), jnp.float32)
    short_type = jax.ShapeDtypeStruct((span, wins * length), jnp.bfloat16)
    local_type = jax.ShapeDtypeStruct((pairs, span, length), jnp.bfloat16)
    raw_scratch = pltpu.VMEM((2 * tiles, span * wins, LANES), jnp.float32)
    near_scratch = pltpu.VMEM((2 * span, wins * length), jnp.bfloat16)
    parts_scratch = [pltpu.VMEM((wins, pairs // 4 * span, length), jnp.float32)] * 4

    white_a, short_a, table, pick, keep = pl.pallas_call(
        head_kernel,
        out_shape=(
            white_type,
            short_type,
            jax.ShapeDtypeStruct((length, length), jnp.bfloat16),
            jax.ShapeDtypeStruct((pairs, span, 2 * span), jnp.bfloat16),
            jax.ShapeDtypeStruct((chans, wins * LANES), jnp.float32),
        ),
        in_specs=[whole(pltpu.HBM)] * 3,
        out_specs=(whole(),) * 5,
        scratch_shapes=[
            pltpu.VMEM((span * wins, length), jnp.bfloat16),
            pltpu.VMEM((wins, chans), jnp.int32),
            pltpu.SMEM((pairs,), jnp.int32),
            raw_scratch,
            pltpu.SemaphoreType.DMA((2 + X_PIECES,)),
        ],
        compiler_params=params,
        cost_estimate=cost(span * wins * length * length * 2, 2 * 1024 * 1024),
        name="head",
    )(in_hbm(flat), in_hbm(valid.T), in_hbm(offsets))

    ring = lax.axis_size("chan")
    edge = lax.ppermute(short_a, "chan", [(i, i - 1) for i in range(1, ring)])

    columns = min(d for d in range(1, groups + 1) if groups % d == 0 and d * d >= groups)
    square = columns == 2 and groups == columns * columns
    limits = (2, 3) if square else (groups, groups)

    def tail(now, after):
        return pl.pallas_call(
            functools.partial(tail_kernel, limits, now),
            out_shape=(white_type, short_type, local_type),
            in_specs=[whole()] * 6 + [whole(pl.ANY)],
            out_specs=(whole(),) * 3,
            scratch_shapes=[raw_scratch, near_scratch] + parts_scratch,
            compiler_params=params,
            cost_estimate=cost(span * wins * length * length * 4, 4 * 1024 * 1024),
            name="tail",
        )(flat, table, keep, pick, white_a, short_a, after)

    def cross(now, white, short, after):
        return pl.pallas_call(
            functools.partial(cross_kernel, limits, now),
            out_shape=local_type,
            in_specs=[whole()] * 4 + [whole(pl.ANY)],
            out_specs=whole(),
            scratch_shapes=[near_scratch] + parts_scratch,
            compiler_params=params,
            cost_estimate=cost(pairs * span * wins * bins * 8, 4 * 1024 * 1024),
            name="cross",
        )(pick, white, short, edge, after)

    white_b, short_b, local_a = tail(0, table)
    local_b = cross(0, white_b, short_b, table)
    white_late, short_late, late_a = tail(1, local_b)
    late_b = cross(1, white_late, short_late, local_b)

    power = [float(np.float32(factor) ** np.float32(d)) for d in range(groups)]
    def sent(value, even, odd):
        moves = [
            (c * groups + here, c * groups + there)
            for c in range(ring)
            for here, there in (odd if c % 2 else even)
        ]
        return lax.ppermute(value, ("chan", "tm"), moves)

    def mix(terms, weights, after):
        return pl.pallas_call(
            functools.partial(mix_kernel, limits, weights),
            out_shape=local_type,
            in_specs=[whole()] * len(terms) + [whole(pl.ANY)],
            out_specs=whole(),
            compiler_params=params,
            cost_estimate=cost(len(terms) * terms[0].size * 4, 1024 * 1024),
            name="mix",
        )(*terms, after)

    inverse = pl.pallas_call(
        inverse_kernel,
        out_shape=jax.ShapeDtypeStruct((length, length), jnp.bfloat16),
        in_specs=[whole(pl.ANY)],
        out_specs=whole(),
        compiler_params=params,
        cost_estimate=cost(length * bins * 32, 512 * 1024),
        name="inverse",
    )(local_b)

    def written(kernel, terms, later, *so_far):
        return pl.pallas_call(
            kernel,
            out_shape=jax.ShapeDtypeStruct((pairs, chans, length), jnp.bfloat16),
            in_specs=[whole()] * (1 + len(terms)) + [whole(pl.ANY)] * (len(later) + len(so_far)),
            out_specs=whole(pl.ANY),
            scratch_shapes=[
                pltpu.VMEM((pairs, span, length), jnp.bfloat16),
                pltpu.SemaphoreType.DMA((2,)),
            ],
            input_output_aliases={1 + len(terms) + len(later): 0} if so_far else {},
            compiler_params=params,
            cost_estimate=cost(pairs * span * length * length * 4, 1024 * 1024),
            name="lags",
        )(inverse, *terms, *later, *so_far)

    def part(terms, weights):
        return pl.pallas_call(
            functools.partial(part_kernel, limits, weights),
            out_shape=jax.ShapeDtypeStruct((pairs * span, length), jnp.float32),
            in_specs=[whole()] * (1 + len(terms)),
            out_specs=whole(),
            compiler_params=params,
            cost_estimate=cost(pairs * span * length * length * 4, 1024 * 1024),
            name="part",
        )(inverse, *terms)

    unit = [1.0] * (2 * groups)

    def two_hops(local, late, after, apart):
        f, ff = power[1], power[2]
        last = [(2, 3)]
        got = sent(local, [(0, 2), (1, 3)], [(0, 1), (1, 0)] + ([] if apart else last))
        alone = [sent(local, [], last)] if apart else []
        total = mix(
            [local, late, got],
            [[1.0, 1.0, 1.0, 0.0, f, 1.0, 0.0, 0.0], [ff, ff, ff, 1.0, 1.0, f, 0.0, 0.0]],
            after,
        )
        more = sent(total, [(0, 1), (2, 3), (3, 2)], [(0, 2), (1, 3)])
        weights = [
            unit,
            [ff, ff, ff, ff, 0.0, f, 0.0, f],
        ]
        weights += [[f] * (2 * groups)] * len(alone) + [[f, f, f, f, 0.0, 0.0, f, ff]]
        return total, [got] + alone + [more], weights

    def one_hop(local, late, after, apart):
        terms, weights = [], [unit]
        for d in range(1, groups):
            moves = [(h, h + d) for h in range(groups - d)]
            terms.append(sent(local, moves, moves))
            weights.append([power[d]] * (2 * groups))
        return local, terms, weights

    spread = two_hops if square else one_hop
    scale = bins**-0.5
    _, terms_a, weights_a = spread(local_a, late_a, late_b, False)
    ahead, terms_b, weights_b = spread(local_b, late_b, local_b, True)
    white_last, short_last, last_a = tail(2, ahead)
    last_b = cross(2, white_last, short_last, ahead)
    terms_a = [local_a, late_a, last_a] + terms_a
    terms_b = [local_b, late_b, last_b] + terms_b
    before = part(terms_b[:-1], weights_b[:-1])
    first = functools.partial(lag_kernel, limits, scale, 0, weights_a)
    result = written(first, terms_a, [before])
    last = functools.partial(last_kernel, scale, half, weights_b[-1])
    result = written(last, [before, terms_b[-1]], [], result)
    return result.reshape(1, pairs, chans, length)


def solution(mesh):
    in_specs = (P("chan", "tm", None), P("chan", "tm"), P())
    out_specs = P("tm", None, "chan", None)
    return jax.shard_map(
        per_device, mesh=mesh, in_specs=in_specs, out_specs=out_specs, check_vma=False
    )
```

```python
import functools
import math

import jax
import jax.numpy as jnp
import numpy as np
from jax import lax
from jax.experimental import pallas as pl
from jax.experimental.pallas import tpu as pltpu
from jax.sharding import PartitionSpec as P

OFFSET_SPAN = 32
LANES = 128
DECAY = 0.99
VMEM = 24 * 1024 * 1024


def turns(number, length):
    part = (number - length * jnp.floor(number / length + 0.5)) * (1.0 / length)
    square = part * part
    cosine, sine = jnp.float32(0.0), jnp.float32(0.0)
    for k in range(10, -1, -1):
        cosine = cosine * square + (-1) ** k * (2 * math.pi) ** (2 * k) / math.factorial(2 * k)
        sine = sine * square + (-1) ** k * (2 * math.pi) ** (2 * k + 1) / math.factorial(2 * k + 1)
    return cosine, sine * part


def fill_table(table_ref, step):
    length = table_ref.shape[0]
    bins = length // 2

    def small(rows, by):
        row = lax.broadcasted_iota(jnp.int32, (rows, bins), 0)
        freq = lax.broadcasted_iota(jnp.int32, (rows, bins), 1) + 1
        return turns((row * (by * freq)).astype(jnp.float32), length)

    coarse_cos, coarse_sin = small(length // step, step)
    fine_cos, fine_sin = small(step, 1)
    for i in range(length // step):
        rows = slice(i * step, (i + 1) * step)
        cos_i, sin_i = coarse_cos[i : i + 1], coarse_sin[i : i + 1]
        cosine = (cos_i * fine_cos - sin_i * fine_sin).astype(jnp.bfloat16)
        sine = (sin_i * fine_cos + cos_i * fine_sin).astype(jnp.bfloat16)
        for t in range(bins // LANES):
            here = slice(t * LANES, (t + 1) * LANES)
            table_ref[rows, 2 * t * LANES : (2 * t + 1) * LANES] = cosine[:, here]
            table_ref[rows, (2 * t + 1) * LANES : (2 * t + 2) * LANES] = -sine[:, here]


def inverse_kernel(_, table_ref):
    length = table_ref.shape[0]
    bins = length // 2
    step = 16

    def small(rows, by, first):
        freq = (lax.broadcasted_iota(jnp.int32, (rows, length), 0) + first) * by
        lag = lax.broadcasted_iota(jnp.int32, (rows, length), 1)
        return turns((freq * lag).astype(jnp.float32), length)

    coarse_cos, coarse_sin = small(bins // step, step, 0)
    fine_cos, fine_sin = small(step, 1, 1)
    for i in range(bins // step):
        first = i * step
        cos_i, sin_i = coarse_cos[i : i + 1], coarse_sin[i : i + 1]
        cosine = cos_i * fine_cos - sin_i * fine_sin
        sine = sin_i * fine_cos + cos_i * fine_sin
        table_ref[first : first + step, :] = cosine.astype(jnp.bfloat16)
        table_ref[bins + first : bins + first + step, :] = (-sine).astype(jnp.bfloat16)


def whiten_block(x, table_ref, keep, raw_ref, white_ref, short_ref, send_ref=None):
    span = short_ref.shape[0]
    wins, length = x.shape[0] // span, x.shape[1]
    bins = length // 2
    tiles = bins // LANES

    def strided(t, w):
        return raw_ref[t, pl.ds(w, span, stride=wins), :]

    total = [None] * wins
    for t in range(tiles):
        lanes = slice(2 * t * LANES, (2 * t + 2) * LANES)
        raw = jnp.dot(x, table_ref[:, lanes], preferred_element_type=jnp.float32)
        raw_ref[2 * t] = raw[:, :LANES]
        raw_ref[2 * t + 1] = raw[:, LANES:]
    for t in range(tiles):
        for w in range(wins):
            real_part, imag_part = strided(2 * t, w), strided(2 * t + 1, w)
            power = real_part * real_part + imag_part * imag_part
            total[w] = power if t == 0 else total[w] + power
    for w in range(wins):
        decay = float(np.float32(DECAY) ** np.float32(wins - 1 - w))
        level = jnp.sum(total[w], axis=-1, keepdims=True) * (0.01 / bins) + 1e-06
        for t in range(tiles):
            part = [strided(2 * t, w), strided(2 * t + 1, w)]
            power = part[0] * part[0] + part[1] * part[1]
            scale = lax.rsqrt(power + level)
            if keep is not None:
                scale = scale * keep[:, w * LANES : (w + 1) * LANES]
            for i, s in enumerate((t, tiles + t)):
                value = part[i] * scale
                here = pl.ds(w * length + s * LANES, LANES)
                short_ref[:, here] = value.astype(jnp.bfloat16)
                if white_ref is not None:
                    white_ref[w, :, s * LANES : (s + 1) * LANES] = value * decay
                if send_ref is not None:
                    rows = slice(w * span, (w + 1) * span)
                    send_ref[rows, s * LANES : (s + 1) * LANES] = value.astype(jnp.bfloat16)


def on_odd():
    return lax.rem(lax.axis_index("chan"), 2) == 1


def head_kernel(
    x_hbm,
    valid_hbm,
    offsets_hbm,
    white_ref,
    short_ref,
    send_ref,
    table_ref,
    pick_ref,
    keep_ref,
    x_ref,
    valid_ref,
    offsets_ref,
    raw_ref,
    sems,
):
    wins, span, length = white_ref.shape
    pairs = offsets_ref.shape[0]
    copies = [
        pltpu.make_async_copy(valid_hbm, valid_ref, sems.at[0]),
        pltpu.make_async_copy(offsets_hbm, offsets_ref, sems.at[1]),
        pltpu.make_async_copy(x_hbm.at[pl.ds(0, span * wins)], x_ref, sems.at[2]),
    ]
    for copy in copies:
        copy.start()
    fill_table(table_ref, 16)
    copies[0].wait()
    copies[1].wait()
    ahead = lax.broadcasted_iota(jnp.int32, (span, 2 * span), 1) - lax.broadcasted_iota(
        jnp.int32, (span, 2 * span), 0
    )
    for k in range(pairs):
        chosen_row = jnp.where(ahead == offsets_ref[k], jnp.float32(1.0), jnp.float32(0.0))
        pick_ref[k] = chosen_row.astype(jnp.bfloat16)
    owner = lax.broadcasted_iota(jnp.int32, (wins, wins * LANES), 0)
    column = lax.broadcasted_iota(jnp.int32, (wins, wins * LANES), 1) // LANES
    keep_ref[...] = lax.dot_general(
        valid_ref[...].astype(jnp.float32).astype(jnp.bfloat16),
        (owner == column).astype(jnp.float32).astype(jnp.bfloat16),
        (((0,), (0,)), ((), ())),
        preferred_element_type=jnp.float32,
    )
    copies[2].wait()

    @pl.when(jnp.logical_not(on_odd()))
    def _():
        keep = keep_ref[:span]
        whiten_block(x_ref[...], table_ref, keep, raw_ref, white_ref, short_ref, send_ref)

    @pl.when(on_odd())
    def _():
        count = span * wins
        row = lax.broadcasted_iota(jnp.int32, (count, valid_ref.shape[1]), 0) // wins
        chan = lax.broadcasted_iota(jnp.int32, (count, valid_ref.shape[1]), 1)
        per_window = lax.dot_general(
            (row == chan).astype(jnp.float32).astype(jnp.bfloat16),
            valid_ref[...].astype(jnp.float32).astype(jnp.bfloat16),
            (((1,), (1,)), ((), ())),
            preferred_element_type=jnp.float32,
        )
        window = lax.rem(lax.broadcasted_iota(jnp.int32, (count, wins), 0), wins)
        mine = window == lax.broadcasted_iota(jnp.int32, (count, wins), 1)
        chosen_one = jnp.where(mine, per_window, 0.0).astype(jnp.bfloat16)
        ones = jnp.ones((wins, LANES), jnp.bfloat16)
        mask = jnp.dot(chosen_one, ones, preferred_element_type=jnp.float32)
        for t in range(length // LANES):
            lanes = slice(t * LANES, (t + 1) * LANES)
            send_ref[:, lanes] = (x_ref[:, lanes].astype(jnp.float32) * mask).astype(jnp.bfloat16)


def odd_head_kernel(x_ref, table_ref, keep_ref, _, __, white_ref, short_ref, raw_ref):
    wins, span, _ = white_ref.shape

    @pl.when(on_odd())
    def _():
        x = x_ref[: span * wins, :]
        whiten_block(x, table_ref, keep_ref[:span], raw_ref, white_ref, short_ref)


def stack_pairs(pick_ref, white_ref, near_ref, parts_refs, out_ref):
    wins, _, length = white_ref.shape
    pairs, rows, reach = pick_ref.shape
    bins = length // 2
    size = pairs // len(parts_refs)

    def select(group, w):
        pick = pick_ref[group * size : (group + 1) * size].reshape(size * rows, reach)
        near = near_ref[:, w * length : (w + 1) * length]
        parts_refs[group][w] = jnp.dot(pick, near, preferred_element_type=jnp.float32)

    blocks = [(c, t) for c in range(0, rows, 16) for t in range(bins // LANES)]
    for w in range(wins):
        select(0, w)
    for group, parts_ref in enumerate(parts_refs):
        ahead = list(range(wins)) if group + 1 < len(parts_refs) else []
        for i, (c, t) in enumerate(blocks):
            for w in ahead[i :: len(blocks)]:
                select(group + 1, w)
            re = slice(t * LANES, (t + 1) * LANES)
            im = slice(bins + t * LANES, bins + (t + 1) * LANES)
            head_re = [white_ref[w, c : c + 16, re] for w in range(wins)]
            head_im = [white_ref[w, c : c + 16, im] for w in range(wins)]
            for k in range(size):
                here = slice(k * rows + c, k * rows + c + 16)
                total_re = total_im = None
                for w in range(wins):
                    part_re, part_im = parts_ref[w, here, re], parts_ref[w, here, im]
                    cross_re = head_re[w] * part_re + head_im[w] * part_im
                    cross_im = head_im[w] * part_re - head_re[w] * part_im
                    total_re = cross_re if w == 0 else total_re + cross_re
                    total_im = cross_im if w == 0 else total_im + cross_im
                pair = group * size + k
                out_ref[pair, c : c + 16, re] = total_re.astype(out_ref.dtype)
                out_ref[pair, c : c + 16, im] = total_im.astype(out_ref.dtype)


def role(limits):
    odd = lax.rem(lax.axis_index("chan"), 2)
    first = lax.axis_index("tm") < jnp.where(odd == 0, *limits)
    return jnp.where(first, 0, 1 + odd)


def tail_kernel(
    limits,
    now,
    x_ref,
    table_ref,
    keep_ref,
    pick_ref,
    head_ref,
    edge_ref,
    after_ref,
    white_ref,
    short_ref,
    out_ref,
    raw_ref,
    near_ref,
    *parts_refs,
):
    wins, span, length = white_ref.shape
    rows = slice(span * wins, 2 * span * wins)

    @pl.when(role(limits) == now)
    def _():
        x = x_ref[rows, :]
        whiten_block(x, table_ref, keep_ref[span:], raw_ref, white_ref, short_ref)
        near_ref[:span] = edge_ref[...]
        near_ref[span:] = short_ref[...]
        stack_pairs(pick_ref, head_ref, near_ref, parts_refs, out_ref)


def cross_kernel(
    limits,
    now,
    pick_ref,
    white_ref,
    short_ref,
    edge_ref,
    table_ref,
    after_ref,
    out_ref,
    raw_ref,
    near_ref,
    *parts_refs,
):
    span = short_ref.shape[0]
    wins, _, length = white_ref.shape
    far_ref = near_ref.at[pl.ds(span, span)]

    @pl.when((role(limits) == now) & jnp.logical_not(on_odd()))
    def _():
        whiten_block(edge_ref[...], table_ref, None, raw_ref, None, far_ref)

    @pl.when((role(limits) == now) & on_odd())
    def _():
        for w in range(wins):
            far_ref[:, w * length : (w + 1) * length] = edge_ref[w * span : (w + 1) * span, :]

    @pl.when(role(limits) == now)
    def _():
        near_ref[:span] = short_ref[...]
        stack_pairs(pick_ref, white_ref, near_ref, parts_refs, out_ref)


def chosen(options, place):
    value = jnp.float32(options[0])
    for i, option in enumerate(options[1:]):
        value = jnp.where(place == i + 1, jnp.float32(option), value)
    return value


def weighted(limits, terms, weights, place):
    total = None
    mine = role(limits)
    late = len(terms) - len(weights)
    first = terms[late][...]
    for i in range(late - 1, -1, -1):
        first = jnp.where(mine == i, terms[i][...], first)
    for term, options in zip([first] + list(terms[late + 1 :]), weights):
        value = term[...].astype(jnp.float32)
        if set(options) != {1.0}:
            value = value * (options[0] if len(set(options)) == 1 else chosen(options, place))
        total = value if total is None else total + value
    return total


def whereabouts(groups):
    return lax.rem(lax.axis_index("chan"), 2) * groups + lax.axis_index("tm")


def mix_kernel(limits, weights, *refs):
    count = len(weights) + 1
    place = whereabouts(len(weights[0]) // 2)
    total = weighted(limits, refs[:count], weights, place)
    refs[-1][...] = total.astype(refs[-1].dtype)


def to_lags(stack, table):
    count = stack.shape[0]
    high = stack.astype(jnp.bfloat16)
    low = (stack - high.astype(jnp.float32)).astype(jnp.bfloat16)
    both = jnp.dot(jnp.concatenate([high, low]), table, preferred_element_type=jnp.float32)
    return both[:count] + both[count:]


def part_kernel(limits, weights, table_ref, *refs):
    place = whereabouts(len(weights[0]) // 2)
    out_ref = refs[-1]
    stack = weighted(limits, refs[: len(weights) + 2], weights, place).reshape(out_ref.shape)
    out_ref[...] = to_lags(stack, table_ref[...])


def lag_kernel(limits, scale, first, weights, table_ref, *rest):
    out_hbm, stage_ref, sem = rest[-3:]
    place = whereabouts(len(weights[0]) // 2)
    pairs, rows, length = stage_ref.shape
    stack = weighted(limits, rest[: len(weights) + 2], weights, place)
    stack = stack.reshape(pairs * rows, length)
    lagged = to_lags(stack, table_ref[...]) * scale
    stage_ref[...] = lagged.astype(stage_ref.dtype).reshape(pairs, rows, length)
    copy = pltpu.make_async_copy(stage_ref, out_hbm.at[:, pl.ds(first, rows)], sem)
    copy.start()
    copy.wait()


def last_kernel(scale, first, weights, table_ref, part_ref, more_ref, *rest):
    out_hbm, stage_ref, sem = rest[-3:]
    place = whereabouts(len(weights) // 2)
    pairs, rows, length = stage_ref.shape
    more = more_ref[...].reshape(pairs * rows, length)
    lagged = jnp.dot(more, table_ref[...], preferred_element_type=jnp.float32)
    lagged = (part_ref[...] + lagged * chosen(weights, place)) * scale
    stage_ref[...] = lagged.astype(stage_ref.dtype).reshape(pairs, rows, length)
    copy = pltpu.make_async_copy(stage_ref, out_hbm.at[:, pl.ds(first, rows)], sem)
    copy.start()
    copy.wait()


def cost(flops, moved):
    return pl.CostEstimate(flops=flops, bytes_accessed=moved, transcendentals=0)


def whole(memory=pltpu.VMEM):
    return pl.BlockSpec(memory_space=memory)


def per_device(samples, valid, offsets):
    chans, wins, length = samples.shape
    bins = length // 2
    span = OFFSET_SPAN
    pairs = offsets.shape[0]
    tiles = bins // LANES
    groups = lax.axis_size("tm")
    factor = float(np.float32(DECAY) ** np.float32(wins))
    params = pltpu.CompilerParams(vmem_limit_bytes=VMEM)

    def in_hbm(value):
        return pltpu.with_memory_space_constraint(value, pltpu.HBM)

    half = chans - span
    flat = samples.reshape(chans * wins, length)
    white_type = jax.ShapeDtypeStruct((wins, span, length), jnp.float32)
    short_type = jax.ShapeDtypeStruct((span, wins * length), jnp.bfloat16)
    local_type = jax.ShapeDtypeStruct((pairs, span, length), jnp.bfloat16)
    raw_scratch = pltpu.VMEM((2 * tiles, span * wins, LANES), jnp.float32)
    near_scratch = pltpu.VMEM((2 * span, wins * length), jnp.bfloat16)
    parts_scratch = [pltpu.VMEM((wins, pairs // 4 * span, length), jnp.float32)] * 4

    white_a, short_a, edge, table, pick, keep = pl.pallas_call(
        head_kernel,
        out_shape=(
            white_type,
            short_type,
            jax.ShapeDtypeStruct((wins * span, length), jnp.bfloat16),
            jax.ShapeDtypeStruct((length, length), jnp.bfloat16),
            jax.ShapeDtypeStruct((pairs, span, 2 * span), jnp.bfloat16),
            jax.ShapeDtypeStruct((chans, wins * LANES), jnp.float32),
        ),
        in_specs=[whole(pltpu.HBM)] * 3,
        out_specs=(whole(),) * 6,
        scratch_shapes=[
            pltpu.VMEM((span * wins, length), jnp.bfloat16),
            pltpu.VMEM((wins, chans), jnp.int32),
            pltpu.SMEM((pairs,), jnp.int32),
            raw_scratch,
            pltpu.SemaphoreType.DMA((3,)),
        ],
        compiler_params=params,
        cost_estimate=cost(span * wins * length * length * 2, 2 * 1024 * 1024),
        name="head",
    )(in_hbm(flat), in_hbm(valid.T), in_hbm(offsets))

    ring = lax.axis_size("chan")
    edge = lax.ppermute(edge, "chan", [(i, i - 1) for i in range(1, ring)])

    white_a, short_a = pl.pallas_call(
        odd_head_kernel,
        out_shape=(white_type, short_type),
        in_specs=[whole()] * 5,
        out_specs=(whole(),) * 2,
        scratch_shapes=[raw_scratch],
        input_output_aliases={3: 0, 4: 1},
        compiler_params=params,
        cost_estimate=cost(span * wins * length * length * 2, 2 * 1024 * 1024),
        name="odd_head",
    )(flat, table, keep, white_a, short_a)

    columns = min(d for d in range(1, groups + 1) if groups % d == 0 and d * d >= groups)
    square = columns == 2 and groups == columns * columns
    limits = (2, 3) if square else (groups, groups)

    def tail(now, after):
        return pl.pallas_call(
            functools.partial(tail_kernel, limits, now),
            out_shape=(white_type, short_type, local_type),
            in_specs=[whole()] * 6 + [whole(pl.ANY)],
            out_specs=(whole(),) * 3,
            scratch_shapes=[raw_scratch, near_scratch] + parts_scratch,
            compiler_params=params,
            cost_estimate=cost(span * wins * length * length * 4, 4 * 1024 * 1024),
            name="tail",
        )(flat, table, keep, pick, white_a, short_a, after)

    def cross(now, white, short, after):
        return pl.pallas_call(
            functools.partial(cross_kernel, limits, now),
            out_shape=local_type,
            in_specs=[whole()] * 5 + [whole(pl.ANY)],
            out_specs=whole(),
            scratch_shapes=[raw_scratch, near_scratch] + parts_scratch,
            compiler_params=params,
            cost_estimate=cost(pairs * span * wins * bins * 8, 4 * 1024 * 1024),
            name="cross",
        )(pick, white, short, edge, table, after)

    white_b, short_b, local_a = tail(0, table)
    white_late, short_late, late_a = tail(1, local_a)
    local_b = cross(0, white_b, short_b, late_a)
    late_b = cross(1, white_late, short_late, local_b)

    power = [float(np.float32(factor) ** np.float32(d)) for d in range(groups)]
    def sent(value, even, odd):
        moves = [
            (c * groups + here, c * groups + there)
            for c in range(ring)
            for here, there in (odd if c % 2 else even)
        ]
        return lax.ppermute(value, ("chan", "tm"), moves)

    def mix(terms, weights, after):
        return pl.pallas_call(
            functools.partial(mix_kernel, limits, weights),
            out_shape=local_type,
            in_specs=[whole()] * len(terms) + [whole(pl.ANY)],
            out_specs=whole(),
            compiler_params=params,
            cost_estimate=cost(len(terms) * terms[0].size * 4, 1024 * 1024),
            name="mix",
        )(*terms, after)

    inverse = pl.pallas_call(
        inverse_kernel,
        out_shape=jax.ShapeDtypeStruct((length, length), jnp.bfloat16),
        in_specs=[whole(pl.ANY)],
        out_specs=whole(),
        compiler_params=params,
        cost_estimate=cost(length * bins * 32, 512 * 1024),
        name="inverse",
    )(local_b)

    def written(kernel, terms, later, *so_far):
        return pl.pallas_call(
            kernel,
            out_shape=jax.ShapeDtypeStruct((pairs, chans, length), jnp.bfloat16),
            in_specs=[whole()] * (1 + len(terms)) + [whole(pl.ANY)] * (len(later) + len(so_far)),
            out_specs=whole(pl.ANY),
            scratch_shapes=[
                pltpu.VMEM((pairs, span, length), jnp.bfloat16),
                pltpu.SemaphoreType.DMA,
            ],
            input_output_aliases={1 + len(terms) + len(later): 0} if so_far else {},
            compiler_params=params,
            cost_estimate=cost(pairs * span * length * length * 4, 1024 * 1024),
            name="lags",
        )(inverse, *terms, *later, *so_far)

    def part(terms, weights):
        return pl.pallas_call(
            functools.partial(part_kernel, limits, weights),
            out_shape=jax.ShapeDtypeStruct((pairs * span, length), jnp.float32),
            in_specs=[whole()] * (1 + len(terms)),
            out_specs=whole(),
            compiler_params=params,
            cost_estimate=cost(pairs * span * length * length * 4, 1024 * 1024),
            name="part",
        )(inverse, *terms)

    unit = [1.0] * (2 * groups)

    def two_hops(local, late, after, apart):
        f, ff = power[1], power[2]
        last = [(2, 3)]
        got = sent(local, [(0, 2), (1, 3)], [(0, 1), (1, 0)] + ([] if apart else last))
        alone = [sent(local, [], last)] if apart else []
        total = mix(
            [local, late, got],
            [[1.0, 1.0, 1.0, 0.0, f, 1.0, 0.0, 0.0], [ff, ff, ff, 1.0, 1.0, f, 0.0, 0.0]],
            after,
        )
        more = sent(total, [(0, 1), (2, 3), (3, 2)], [(0, 2), (1, 3)])
        weights = [
            unit,
            [ff, ff, ff, ff, 0.0, f, 0.0, f],
        ]
        weights += [[f] * (2 * groups)] * len(alone) + [[f, f, f, f, 0.0, 0.0, f, ff]]
        return total, [got] + alone + [more], weights

    def one_hop(local, late, after, apart):
        terms, weights = [], [unit]
        for d in range(1, groups):
            moves = [(h, h + d) for h in range(groups - d)]
            terms.append(sent(local, moves, moves))
            weights.append([power[d]] * (2 * groups))
        return local, terms, weights

    spread = two_hops if square else one_hop
    scale = bins**-0.5
    _, terms_a, weights_a = spread(local_a, late_a, late_b, False)
    ahead, terms_b, weights_b = spread(local_b, late_b, local_b, True)
    white_last, short_last, last_a = tail(2, ahead)
    last_b = cross(2, white_last, short_last, ahead)
    terms_a = [local_a, late_a, last_a] + terms_a
    terms_b = [local_b, late_b, last_b] + terms_b
    before = part(terms_b[:-1], weights_b[:-1])
    first = functools.partial(lag_kernel, limits, scale, 0, weights_a)
    result = written(first, terms_a, [before])
    last = functools.partial(last_kernel, scale, half, weights_b[-1])
    result = written(last, [before, terms_b[-1]], [], result)
    return result.reshape(1, pairs, chans, length)


def solution(mesh):
    in_specs = (P("chan", "tm", None), P("chan", "tm"), P())
    out_specs = P("tm", None, "chan", None)
    return jax.shard_map(
        per_device, mesh=mesh, in_specs=in_specs, out_specs=out_specs, check_vma=False
    )
```

```python
import functools
import math

import jax
import jax.numpy as jnp
import numpy as np
from jax import lax
from jax.experimental import pallas as pl
from jax.experimental.pallas import tpu as pltpu
from jax.sharding import PartitionSpec as P

OFFSET_SPAN = 32
LANES = 128
DECAY = 0.99
VMEM = 24 * 1024 * 1024


def turns(number, length):
    part = (number - length * jnp.floor(number / length + 0.5)) * (1.0 / length)
    square = part * part
    cosine, sine = jnp.float32(0.0), jnp.float32(0.0)
    for k in range(10, -1, -1):
        cosine = cosine * square + (-1) ** k * (2 * math.pi) ** (2 * k) / math.factorial(2 * k)
        sine = sine * square + (-1) ** k * (2 * math.pi) ** (2 * k + 1) / math.factorial(2 * k + 1)
    return cosine, sine * part


def fill_table(table_ref, step):
    length = table_ref.shape[0]
    bins = length // 2

    def small(rows, by):
        row = lax.broadcasted_iota(jnp.int32, (rows, bins), 0)
        freq = lax.broadcasted_iota(jnp.int32, (rows, bins), 1) + 1
        return turns((row * (by * freq)).astype(jnp.float32), length)

    coarse_cos, coarse_sin = small(length // step, step)
    fine_cos, fine_sin = small(step, 1)
    for i in range(length // step):
        rows = slice(i * step, (i + 1) * step)
        cos_i, sin_i = coarse_cos[i : i + 1], coarse_sin[i : i + 1]
        cosine = (cos_i * fine_cos - sin_i * fine_sin).astype(jnp.bfloat16)
        sine = (sin_i * fine_cos + cos_i * fine_sin).astype(jnp.bfloat16)
        for t in range(bins // LANES):
            here = slice(t * LANES, (t + 1) * LANES)
            table_ref[rows, 2 * t * LANES : (2 * t + 1) * LANES] = cosine[:, here]
            table_ref[rows, (2 * t + 1) * LANES : (2 * t + 2) * LANES] = -sine[:, here]


def inverse_kernel(_, table_ref):
    length = table_ref.shape[0]
    bins = length // 2
    step = 16

    def small(rows, by, first):
        freq = (lax.broadcasted_iota(jnp.int32, (rows, length), 0) + first) * by
        lag = lax.broadcasted_iota(jnp.int32, (rows, length), 1)
        return turns((freq * lag).astype(jnp.float32), length)

    coarse_cos, coarse_sin = small(bins // step, step, 0)
    fine_cos, fine_sin = small(step, 1, 1)
    for i in range(bins // step):
        first = i * step
        cos_i, sin_i = coarse_cos[i : i + 1], coarse_sin[i : i + 1]
        cosine = cos_i * fine_cos - sin_i * fine_sin
        sine = sin_i * fine_cos + cos_i * fine_sin
        table_ref[first : first + step, :] = cosine.astype(jnp.bfloat16)
        table_ref[bins + first : bins + first + step, :] = (-sine).astype(jnp.bfloat16)


def whiten_block(x, table_ref, keep, raw_ref, white_ref, short_ref):
    wins, span, length = white_ref.shape
    bins = length // 2
    tiles = bins // LANES

    def strided(t, w):
        return raw_ref[t, pl.ds(w, span, stride=wins), :]

    total = [None] * wins
    for t in range(tiles):
        lanes = slice(2 * t * LANES, (2 * t + 2) * LANES)
        raw = jnp.dot(x, table_ref[:, lanes], preferred_element_type=jnp.float32)
        raw_ref[2 * t] = raw[:, :LANES]
        raw_ref[2 * t + 1] = raw[:, LANES:]
    for t in range(tiles):
        for w in range(wins):
            real_part, imag_part = strided(2 * t, w), strided(2 * t + 1, w)
            power = real_part * real_part + imag_part * imag_part
            total[w] = power if t == 0 else total[w] + power
    for w in range(wins):
        decay = float(np.float32(DECAY) ** np.float32(wins - 1 - w))
        level = jnp.sum(total[w], axis=-1, keepdims=True) * (0.01 / bins) + 1e-06
        alive = keep[:, w * LANES : (w + 1) * LANES]
        for t in range(tiles):
            part = [strided(2 * t, w), strided(2 * t + 1, w)]
            power = part[0] * part[0] + part[1] * part[1]
            scale = alive * lax.rsqrt(power + level)
            for i, s in enumerate((t, tiles + t)):
                value = part[i] * scale
                here = pl.ds(w * length + s * LANES, LANES)
                white_ref[w, :, s * LANES : (s + 1) * LANES] = value * decay
                short_ref[:, here] = value.astype(jnp.bfloat16)


def head_kernel(
    x_hbm,
    valid_hbm,
    offsets_hbm,
    white_ref,
    short_ref,
    table_ref,
    pick_ref,
    keep_ref,
    x_ref,
    valid_ref,
    offsets_ref,
    raw_ref,
    sems,
):
    wins, span, length = white_ref.shape
    pairs = offsets_ref.shape[0]
    copies = [
        pltpu.make_async_copy(valid_hbm, valid_ref, sems.at[0]),
        pltpu.make_async_copy(offsets_hbm, offsets_ref, sems.at[1]),
        pltpu.make_async_copy(x_hbm.at[pl.ds(0, span * wins)], x_ref, sems.at[2]),
    ]
    for copy in copies:
        copy.start()
    fill_table(table_ref, 16)
    copies[0].wait()
    copies[1].wait()
    ahead = lax.broadcasted_iota(jnp.int32, (span, 2 * span), 1) - lax.broadcasted_iota(
        jnp.int32, (span, 2 * span), 0
    )
    for k in range(pairs):
        chosen_row = jnp.where(ahead == offsets_ref[k], jnp.float32(1.0), jnp.float32(0.0))
        pick_ref[k] = chosen_row.astype(jnp.bfloat16)
    owner = lax.broadcasted_iota(jnp.int32, (wins, wins * LANES), 0)
    column = lax.broadcasted_iota(jnp.int32, (wins, wins * LANES), 1) // LANES
    keep_ref[...] = lax.dot_general(
        valid_ref[...].astype(jnp.float32).astype(jnp.bfloat16),
        (owner == column).astype(jnp.float32).astype(jnp.bfloat16),
        (((0,), (0,)), ((), ())),
        preferred_element_type=jnp.float32,
    )
    copies[2].wait()
    whiten_block(x_ref[...], table_ref, keep_ref[:span], raw_ref, white_ref, short_ref)


def stack_pairs(pick_ref, white_ref, near_ref, parts_refs, out_ref):
    wins, _, length = white_ref.shape
    pairs, rows, reach = pick_ref.shape
    bins = length // 2
    size = pairs // len(parts_refs)

    def select(group, w):
        pick = pick_ref[group * size : (group + 1) * size].reshape(size * rows, reach)
        near = near_ref[:, w * length : (w + 1) * length]
        parts_refs[group][w] = jnp.dot(pick, near, preferred_element_type=jnp.float32)

    blocks = [(c, t) for c in range(0, rows, 16) for t in range(bins // LANES)]
    for w in range(wins):
        select(0, w)
    for group, parts_ref in enumerate(parts_refs):
        ahead = list(range(wins)) if group + 1 < len(parts_refs) else []
        for i, (c, t) in enumerate(blocks):
            for w in ahead[i :: len(blocks)]:
                select(group + 1, w)
            re = slice(t * LANES, (t + 1) * LANES)
            im = slice(bins + t * LANES, bins + (t + 1) * LANES)
            head_re = [white_ref[w, c : c + 16, re] for w in range(wins)]
            head_im = [white_ref[w, c : c + 16, im] for w in range(wins)]
            for k in range(size):
                here = slice(k * rows + c, k * rows + c + 16)
                total_re = total_im = None
                for w in range(wins):
                    part_re, part_im = parts_ref[w, here, re], parts_ref[w, here, im]
                    cross_re = head_re[w] * part_re + head_im[w] * part_im
                    cross_im = head_im[w] * part_re - head_re[w] * part_im
                    total_re = cross_re if w == 0 else total_re + cross_re
                    total_im = cross_im if w == 0 else total_im + cross_im
                pair = group * size + k
                out_ref[pair, c : c + 16, re] = total_re.astype(out_ref.dtype)
                out_ref[pair, c : c + 16, im] = total_im.astype(out_ref.dtype)


def role(limits):
    odd = lax.rem(lax.axis_index("chan"), 2)
    first = lax.axis_index("tm") < jnp.where(odd == 0, *limits)
    return jnp.where(first, 0, 1 + odd)


def tail_kernel(
    limits,
    now,
    x_ref,
    table_ref,
    keep_ref,
    pick_ref,
    head_ref,
    edge_ref,
    after_ref,
    white_ref,
    short_ref,
    out_ref,
    raw_ref,
    near_ref,
    *parts_refs,
):
    wins, span, length = white_ref.shape
    rows = slice(span * wins, 2 * span * wins)

    @pl.when(role(limits) == now)
    def _():
        x = x_ref[rows, :]
        whiten_block(x, table_ref, keep_ref[span:], raw_ref, white_ref, short_ref)
        near_ref[:span] = edge_ref[...]
        near_ref[span:] = short_ref[...]
        stack_pairs(pick_ref, head_ref, near_ref, parts_refs, out_ref)


def cross_kernel(
    limits, now, pick_ref, white_ref, short_ref, edge_ref, after_ref, out_ref, near_ref, *parts_refs
):
    span = short_ref.shape[0]

    @pl.when(role(limits) == now)
    def _():
        near_ref[:span] = short_ref[...]
        near_ref[span:] = edge_ref[...]
        stack_pairs(pick_ref, white_ref, near_ref, parts_refs, out_ref)


def chosen(options, place):
    value = jnp.float32(options[0])
    for i, option in enumerate(options[1:]):
        value = jnp.where(place == i + 1, jnp.float32(option), value)
    return value


def weighted(limits, terms, weights, place):
    total = None
    mine = role(limits)
    late = len(terms) - len(weights)
    first = terms[late][...]
    for i in range(late - 1, -1, -1):
        first = jnp.where(mine == i, terms[i][...], first)
    for term, options in zip([first] + list(terms[late + 1 :]), weights):
        value = term[...].astype(jnp.float32)
        if set(options) != {1.0}:
            value = value * (options[0] if len(set(options)) == 1 else chosen(options, place))
        total = value if total is None else total + value
    return total


def whereabouts(groups):
    return lax.rem(lax.axis_index("chan"), 2) * groups + lax.axis_index("tm")


def mix_kernel(limits, weights, *refs):
    count = len(weights) + 1
    place = whereabouts(len(weights[0]) // 2)
    total = weighted(limits, refs[:count], weights, place)
    refs[-1][...] = total.astype(refs[-1].dtype)


def to_lags(stack, table):
    count = stack.shape[0]
    high = stack.astype(jnp.bfloat16)
    low = (stack - high.astype(jnp.float32)).astype(jnp.bfloat16)
    both = jnp.dot(jnp.concatenate([high, low]), table, preferred_element_type=jnp.float32)
    return both[:count] + both[count:]


def part_kernel(limits, weights, table_ref, *refs):
    place = whereabouts(len(weights[0]) // 2)
    out_ref = refs[-1]
    stack = weighted(limits, refs[: len(weights) + 2], weights, place).reshape(out_ref.shape)
    out_ref[...] = to_lags(stack, table_ref[...])


def lag_kernel(limits, scale, first, weights, table_ref, *rest):
    out_hbm, stage_ref, sems = rest[-3:]
    place = whereabouts(len(weights[0]) // 2)
    pairs, rows, length = stage_ref.shape
    stack = weighted(limits, rest[: len(weights) + 2], weights, place)
    stack = stack.reshape(pairs * rows, length)
    lagged = to_lags(stack, table_ref[...]) * scale
    stage_ref[...] = lagged.astype(stage_ref.dtype).reshape(pairs, rows, length)
    copy = pltpu.make_async_copy(stage_ref, out_hbm.at[:, pl.ds(first, rows)], sems.at[0])
    copy.start()
    copy.wait()


def last_kernel(scale, first, weights, table_ref, part_ref, more_ref, *rest):
    out_hbm, stage_ref, sems = rest[-3:]
    place = whereabouts(len(weights) // 2)
    pairs, rows, length = stage_ref.shape
    more = more_ref[...].reshape(pairs * rows, length)
    lagged = jnp.dot(more, table_ref[...], preferred_element_type=jnp.float32)
    weight = chosen(weights, place)
    size = pairs // 2
    copies = []
    for piece in range(2):
        here = slice(piece * size * rows, (piece + 1) * size * rows)
        value = (part_ref[here] + lagged[here] * weight) * scale
        there = pl.ds(piece * size, size)
        stage_ref[there] = value.astype(stage_ref.dtype).reshape(size, rows, length)
        target = out_hbm.at[there, pl.ds(first, rows)]
        copies.append(pltpu.make_async_copy(stage_ref.at[there], target, sems.at[piece]))
        copies[-1].start()
    for copy in copies:
        copy.wait()


def cost(flops, moved):
    return pl.CostEstimate(flops=flops, bytes_accessed=moved, transcendentals=0)


def whole(memory=pltpu.VMEM):
    return pl.BlockSpec(memory_space=memory)


def per_device(samples, valid, offsets):
    chans, wins, length = samples.shape
    bins = length // 2
    span = OFFSET_SPAN
    pairs = offsets.shape[0]
    tiles = bins // LANES
    groups = lax.axis_size("tm")
    factor = float(np.float32(DECAY) ** np.float32(wins))
    params = pltpu.CompilerParams(vmem_limit_bytes=VMEM)

    def in_hbm(value):
        return pltpu.with_memory_space_constraint(value, pltpu.HBM)

    half = chans - span
    flat = samples.reshape(chans * wins, length)
    white_type = jax.ShapeDtypeStruct((wins, span, length), jnp.float32)
    short_type = jax.ShapeDtypeStruct((span, wins * length), jnp.bfloat16)
    local_type = jax.ShapeDtypeStruct((pairs, span, length), jnp.bfloat16)
    raw_scratch = pltpu.VMEM((2 * tiles, span * wins, LANES), jnp.float32)
    near_scratch = pltpu.VMEM((2 * span, wins * length), jnp.bfloat16)
    parts_scratch = [pltpu.VMEM((wins, pairs // 4 * span, length), jnp.float32)] * 4

    white_a, short_a, table, pick, keep = pl.pallas_call(
        head_kernel,
        out_shape=(
            white_type,
            short_type,
            jax.ShapeDtypeStruct((length, length), jnp.bfloat16),
            jax.ShapeDtypeStruct((pairs, span, 2 * span), jnp.bfloat16),
            jax.ShapeDtypeStruct((chans, wins * LANES), jnp.float32),
        ),
        in_specs=[whole(pltpu.HBM)] * 3,
        out_specs=(whole(),) * 5,
        scratch_shapes=[
            pltpu.VMEM((span * wins, length), jnp.bfloat16),
            pltpu.VMEM((wins, chans), jnp.int32),
            pltpu.SMEM((pairs,), jnp.int32),
            raw_scratch,
            pltpu.SemaphoreType.DMA((3,)),
        ],
        compiler_params=params,
        cost_estimate=cost(span * wins * length * length * 2, 2 * 1024 * 1024),
        name="head",
    )(in_hbm(flat), in_hbm(valid.T), in_hbm(offsets))

    ring = lax.axis_size("chan")
    edge = lax.ppermute(short_a, "chan", [(i, i - 1) for i in range(1, ring)])

    columns = min(d for d in range(1, groups + 1) if groups % d == 0 and d * d >= groups)
    square = columns == 2 and groups == columns * columns
    limits = (2, 3) if square else (groups, groups)

    def tail(now, after):
        return pl.pallas_call(
            functools.partial(tail_kernel, limits, now),
            out_shape=(white_type, short_type, local_type),
            in_specs=[whole()] * 6 + [whole(pl.ANY)],
            out_specs=(whole(),) * 3,
            scratch_shapes=[raw_scratch, near_scratch] + parts_scratch,
            compiler_params=params,
            cost_estimate=cost(span * wins * length * length * 4, 4 * 1024 * 1024),
            name="tail",
        )(flat, table, keep, pick, white_a, short_a, after)

    def cross(now, white, short, after):
        return pl.pallas_call(
            functools.partial(cross_kernel, limits, now),
            out_shape=local_type,
            in_specs=[whole()] * 4 + [whole(pl.ANY)],
            out_specs=whole(),
            scratch_shapes=[near_scratch] + parts_scratch,
            compiler_params=params,
            cost_estimate=cost(pairs * span * wins * bins * 8, 4 * 1024 * 1024),
            name="cross",
        )(pick, white, short, edge, after)

    white_b, short_b, local_a = tail(0, table)
    local_b = cross(0, white_b, short_b, table)
    white_late, short_late, late_a = tail(1, local_b)
    late_b = cross(1, white_late, short_late, local_b)

    power = [float(np.float32(factor) ** np.float32(d)) for d in range(groups)]
    def sent(value, even, odd):
        moves = [
            (c * groups + here, c * groups + there)
            for c in range(ring)
            for here, there in (odd if c % 2 else even)
        ]
        return lax.ppermute(value, ("chan", "tm"), moves)

    def mix(terms, weights, after):
        return pl.pallas_call(
            functools.partial(mix_kernel, limits, weights),
            out_shape=local_type,
            in_specs=[whole()] * len(terms) + [whole(pl.ANY)],
            out_specs=whole(),
            compiler_params=params,
            cost_estimate=cost(len(terms) * terms[0].size * 4, 1024 * 1024),
            name="mix",
        )(*terms, after)

    inverse = pl.pallas_call(
        inverse_kernel,
        out_shape=jax.ShapeDtypeStruct((length, length), jnp.bfloat16),
        in_specs=[whole(pl.ANY)],
        out_specs=whole(),
        compiler_params=params,
        cost_estimate=cost(length * bins * 32, 512 * 1024),
        name="inverse",
    )(local_b)

    def written(kernel, terms, later, *so_far):
        return pl.pallas_call(
            kernel,
            out_shape=jax.ShapeDtypeStruct((pairs, chans, length), jnp.bfloat16),
            in_specs=[whole()] * (1 + len(terms)) + [whole(pl.ANY)] * (len(later) + len(so_far)),
            out_specs=whole(pl.ANY),
            scratch_shapes=[
                pltpu.VMEM((pairs, span, length), jnp.bfloat16),
                pltpu.SemaphoreType.DMA((2,)),
            ],
            input_output_aliases={1 + len(terms) + len(later): 0} if so_far else {},
            compiler_params=params,
            cost_estimate=cost(pairs * span * length * length * 4, 1024 * 1024),
            name="lags",
        )(inverse, *terms, *later, *so_far)

    def part(terms, weights):
        return pl.pallas_call(
            functools.partial(part_kernel, limits, weights),
            out_shape=jax.ShapeDtypeStruct((pairs * span, length), jnp.float32),
            in_specs=[whole()] * (1 + len(terms)),
            out_specs=whole(),
            compiler_params=params,
            cost_estimate=cost(pairs * span * length * length * 4, 1024 * 1024),
            name="part",
        )(inverse, *terms)

    unit = [1.0] * (2 * groups)

    def two_hops(local, late, after, apart):
        f, ff = power[1], power[2]
        last = [(2, 3)]
        got = sent(local, [(0, 2), (1, 3)], [(0, 1), (1, 0)] + ([] if apart else last))
        alone = [sent(local, [], last)] if apart else []
        total = mix(
            [local, late, got],
            [[1.0, 1.0, 1.0, 0.0, f, 1.0, 0.0, 0.0], [ff, ff, ff, 1.0, 1.0, f, 0.0, 0.0]],
            after,
        )
        more = sent(total, [(0, 1), (2, 3), (3, 2)], [(0, 2), (1, 3)])
        weights = [
            unit,
            [ff, ff, ff, ff, 0.0, f, 0.0, f],
        ]
        weights += [[f] * (2 * groups)] * len(alone) + [[f, f, f, f, 0.0, 0.0, f, ff]]
        return total, [got] + alone + [more], weights

    def one_hop(local, late, after, apart):
        terms, weights = [], [unit]
        for d in range(1, groups):
            moves = [(h, h + d) for h in range(groups - d)]
            terms.append(sent(local, moves, moves))
            weights.append([power[d]] * (2 * groups))
        return local, terms, weights

    spread = two_hops if square else one_hop
    scale = bins**-0.5
    _, terms_a, weights_a = spread(local_a, late_a, late_b, False)
    ahead, terms_b, weights_b = spread(local_b, late_b, local_b, True)
    white_last, short_last, last_a = tail(2, ahead)
    last_b = cross(2, white_last, short_last, ahead)
    terms_a = [local_a, late_a, last_a] + terms_a
    terms_b = [local_b, late_b, last_b] + terms_b
    before = part(terms_b[:-1], weights_b[:-1])
    first = functools.partial(lag_kernel, limits, scale, 0, weights_a)
    result = written(first, terms_a, [before])
    last = functools.partial(last_kernel, scale, half, weights_b[-1])
    result = written(last, [before, terms_b[-1]], [], result)
    return result.reshape(1, pairs, chans, length)


def solution(mesh):
    in_specs = (P("chan", "tm", None), P("chan", "tm"), P())
    out_specs = P("tm", None, "chan", None)
    return jax.shard_map(
        per_device, mesh=mesh, in_specs=in_specs, out_specs=out_specs, check_vma=False
    )
```

```python
import functools
import math

import jax
import jax.numpy as jnp
import numpy as np
from jax import lax
from jax.experimental import pallas as pl
from jax.experimental.pallas import tpu as pltpu
from jax.sharding import PartitionSpec as P

OFFSET_SPAN = 32
LANES = 128
DECAY = 0.99
VMEM = 24 * 1024 * 1024


def turns(number, length):
    part = (number - length * jnp.floor(number / length + 0.5)) * (1.0 / length)
    square = part * part
    cosine, sine = jnp.float32(0.0), jnp.float32(0.0)
    for k in range(10, -1, -1):
        cosine = cosine * square + (-1) ** k * (2 * math.pi) ** (2 * k) / math.factorial(2 * k)
        sine = sine * square + (-1) ** k * (2 * math.pi) ** (2 * k + 1) / math.factorial(2 * k + 1)
    return cosine, sine * part


def fill_table(table_ref, step):
    length = table_ref.shape[0]
    bins = length // 2

    def small(rows, by):
        row = lax.broadcasted_iota(jnp.int32, (rows, bins), 0)
        freq = lax.broadcasted_iota(jnp.int32, (rows, bins), 1) + 1
        return turns((row * (by * freq)).astype(jnp.float32), length)

    coarse_cos, coarse_sin = small(length // step, step)
    fine_cos, fine_sin = small(step, 1)
    for i in range(length // step):
        rows = slice(i * step, (i + 1) * step)
        cos_i, sin_i = coarse_cos[i : i + 1], coarse_sin[i : i + 1]
        cosine = (cos_i * fine_cos - sin_i * fine_sin).astype(jnp.bfloat16)
        sine = (sin_i * fine_cos + cos_i * fine_sin).astype(jnp.bfloat16)
        for t in range(bins // LANES):
            here = slice(t * LANES, (t + 1) * LANES)
            table_ref[rows, 2 * t * LANES : (2 * t + 1) * LANES] = cosine[:, here]
            table_ref[rows, (2 * t + 1) * LANES : (2 * t + 2) * LANES] = -sine[:, here]


def inverse_kernel(_, table_ref):
    length = table_ref.shape[0]
    bins = length // 2
    step = 16

    def small(rows, by, first):
        freq = (lax.broadcasted_iota(jnp.int32, (rows, length), 0) + first) * by
        lag = lax.broadcasted_iota(jnp.int32, (rows, length), 1)
        return turns((freq * lag).astype(jnp.float32), length)

    coarse_cos, coarse_sin = small(bins // step, step, 0)
    fine_cos, fine_sin = small(step, 1, 1)
    for i in range(bins // step):
        first = i * step
        cos_i, sin_i = coarse_cos[i : i + 1], coarse_sin[i : i + 1]
        cosine = cos_i * fine_cos - sin_i * fine_sin
        sine = sin_i * fine_cos + cos_i * fine_sin
        table_ref[first : first + step, :] = cosine.astype(jnp.bfloat16)
        table_ref[bins + first : bins + first + step, :] = (-sine).astype(jnp.bfloat16)


def whiten_block(x, table_ref, keep, raw_ref, short_ref):
    span = short_ref.shape[0]
    wins, length = x.shape[0] // span, x.shape[1]
    bins = length // 2
    tiles = bins // LANES

    def strided(t, w):
        return raw_ref[t, pl.ds(w, span, stride=wins), :]

    total = [None] * wins
    for t in range(tiles):
        lanes = slice(2 * t * LANES, (2 * t + 2) * LANES)
        raw = jnp.dot(x, table_ref[:, lanes], preferred_element_type=jnp.float32)
        raw_ref[2 * t] = raw[:, :LANES]
        raw_ref[2 * t + 1] = raw[:, LANES:]
    for t in range(tiles):
        for w in range(wins):
            real_part, imag_part = strided(2 * t, w), strided(2 * t + 1, w)
            power = real_part * real_part + imag_part * imag_part
            total[w] = power if t == 0 else total[w] + power
    for w in range(wins):
        level = jnp.sum(total[w], axis=-1, keepdims=True) * (0.01 / bins) + 1e-06
        alive = keep[:, w * LANES : (w + 1) * LANES]
        for t in range(tiles):
            part = [strided(2 * t, w), strided(2 * t + 1, w)]
            power = part[0] * part[0] + part[1] * part[1]
            scale = alive * lax.rsqrt(power + level)
            for i, s in enumerate((t, tiles + t)):
                value = part[i] * scale
                here = pl.ds(w * length + s * LANES, LANES)
                short_ref[:, here] = value.astype(jnp.bfloat16)


def head_kernel(
    x_hbm,
    valid_hbm,
    offsets_hbm,
    short_ref,
    table_ref,
    pick_ref,
    keep_ref,
    x_ref,
    valid_ref,
    offsets_ref,
    raw_ref,
    sems,
):
    span = short_ref.shape[0]
    wins = valid_ref.shape[0]
    pairs = offsets_ref.shape[0]
    copies = [
        pltpu.make_async_copy(valid_hbm, valid_ref, sems.at[0]),
        pltpu.make_async_copy(offsets_hbm, offsets_ref, sems.at[1]),
        pltpu.make_async_copy(x_hbm.at[pl.ds(0, span * wins)], x_ref, sems.at[2]),
    ]
    for copy in copies:
        copy.start()
    fill_table(table_ref, 16)
    copies[0].wait()
    copies[1].wait()
    ahead = lax.broadcasted_iota(jnp.int32, (span, 2 * span), 1) - lax.broadcasted_iota(
        jnp.int32, (span, 2 * span), 0
    )
    for k in range(pairs):
        chosen_row = jnp.where(ahead == offsets_ref[k], jnp.float32(1.0), jnp.float32(0.0))
        pick_ref[k] = chosen_row.astype(jnp.bfloat16)
    owner = lax.broadcasted_iota(jnp.int32, (wins, wins * LANES), 0)
    column = lax.broadcasted_iota(jnp.int32, (wins, wins * LANES), 1) // LANES
    keep_ref[...] = lax.dot_general(
        valid_ref[...].astype(jnp.float32).astype(jnp.bfloat16),
        (owner == column).astype(jnp.float32).astype(jnp.bfloat16),
        (((0,), (0,)), ((), ())),
        preferred_element_type=jnp.float32,
    )
    copies[2].wait()
    whiten_block(x_ref[...], table_ref, keep_ref[:span], raw_ref, short_ref)


def stack_pairs(pick_ref, near_ref, parts_refs, out_ref):
    pairs, rows, reach = pick_ref.shape
    length = out_ref.shape[2]
    wins = near_ref.shape[1] // length
    bins = length // 2
    size = pairs // len(parts_refs)

    def select(group, w):
        pick = pick_ref[group * size : (group + 1) * size].reshape(size * rows, reach)
        near = near_ref[:, w * length : (w + 1) * length]
        parts_refs[group][w] = jnp.dot(pick, near, preferred_element_type=jnp.float32)

    def head(w, c, lane):
        lanes = slice(w * length + lane, w * length + lane + LANES)
        decay = float(np.float32(DECAY) ** np.float32(wins - 1 - w))
        return near_ref[c : c + 16, lanes].astype(jnp.float32) * decay

    blocks = [(c, t) for c in range(0, rows, 16) for t in range(bins // LANES)]
    for w in range(wins):
        select(0, w)
    for group, parts_ref in enumerate(parts_refs):
        ahead = list(range(wins)) if group + 1 < len(parts_refs) else []
        for i, (c, t) in enumerate(blocks):
            for w in ahead[i :: len(blocks)]:
                select(group + 1, w)
            re = slice(t * LANES, (t + 1) * LANES)
            im = slice(bins + t * LANES, bins + (t + 1) * LANES)
            head_re = [head(w, c, t * LANES) for w in range(wins)]
            head_im = [head(w, c, bins + t * LANES) for w in range(wins)]
            for k in range(size):
                here = slice(k * rows + c, k * rows + c + 16)
                total_re = total_im = None
                for w in range(wins):
                    part_re, part_im = parts_ref[w, here, re], parts_ref[w, here, im]
                    cross_re = head_re[w] * part_re + head_im[w] * part_im
                    cross_im = head_im[w] * part_re - head_re[w] * part_im
                    total_re = cross_re if w == 0 else total_re + cross_re
                    total_im = cross_im if w == 0 else total_im + cross_im
                pair = group * size + k
                out_ref[pair, c : c + 16, re] = total_re.astype(out_ref.dtype)
                out_ref[pair, c : c + 16, im] = total_im.astype(out_ref.dtype)


def role(limits):
    odd = lax.rem(lax.axis_index("chan"), 2)
    first = lax.axis_index("tm") < jnp.where(odd == 0, *limits)
    return jnp.where(first, 0, 1 + odd)


def tail_kernel(
    limits,
    now,
    x_ref,
    table_ref,
    keep_ref,
    pick_ref,
    edge_ref,
    after_ref,
    short_ref,
    out_ref,
    raw_ref,
    near_ref,
    *parts_refs,
):
    span = short_ref.shape[0]
    wins = x_ref.shape[0] // (2 * span)
    rows = slice(span * wins, 2 * span * wins)

    @pl.when(role(limits) == now)
    def _():
        x = x_ref[rows, :]
        whiten_block(x, table_ref, keep_ref[span:], raw_ref, short_ref)
        near_ref[:span] = edge_ref[...]
        near_ref[span:] = short_ref[...]
        stack_pairs(pick_ref, near_ref, parts_refs, out_ref)


def cross_kernel(
    limits, now, pick_ref, short_ref, edge_ref, after_ref, out_ref, near_ref, *parts_refs
):
    span = short_ref.shape[0]

    @pl.when(role(limits) == now)
    def _():
        near_ref[:span] = short_ref[...]
        near_ref[span:] = edge_ref[...]
        stack_pairs(pick_ref, near_ref, parts_refs, out_ref)


def chosen(options, place):
    value = jnp.float32(options[0])
    for i, option in enumerate(options[1:]):
        value = jnp.where(place == i + 1, jnp.float32(option), value)
    return value


def weighted(limits, terms, weights, place):
    total = None
    mine = role(limits)
    late = len(terms) - len(weights)
    first = terms[late][...]
    for i in range(late - 1, -1, -1):
        first = jnp.where(mine == i, terms[i][...], first)
    for term, options in zip([first] + list(terms[late + 1 :]), weights):
        value = term[...].astype(jnp.float32)
        if set(options) != {1.0}:
            value = value * (options[0] if len(set(options)) == 1 else chosen(options, place))
        total = value if total is None else total + value
    return total


def whereabouts(groups):
    return lax.rem(lax.axis_index("chan"), 2) * groups + lax.axis_index("tm")


def mix_kernel(limits, weights, *refs):
    count = len(weights) + 1
    place = whereabouts(len(weights[0]) // 2)
    total = weighted(limits, refs[:count], weights, place)
    refs[-1][...] = total.astype(refs[-1].dtype)


def to_lags(stack, table):
    count = stack.shape[0]
    high = stack.astype(jnp.bfloat16)
    low = (stack - high.astype(jnp.float32)).astype(jnp.bfloat16)
    both = jnp.dot(jnp.concatenate([high, low]), table, preferred_element_type=jnp.float32)
    return both[:count] + both[count:]


def part_kernel(limits, weights, table_ref, *refs):
    place = whereabouts(len(weights[0]) // 2)
    out_ref = refs[-1]
    stack = weighted(limits, refs[: len(weights) + 2], weights, place).reshape(out_ref.shape)
    out_ref[...] = to_lags(stack, table_ref[...])


def lag_kernel(limits, scale, first, weights, table_ref, *rest):
    out_hbm, stage_ref, sems = rest[-3:]
    place = whereabouts(len(weights[0]) // 2)
    pairs, rows, length = stage_ref.shape
    stack = weighted(limits, rest[: len(weights) + 2], weights, place)
    stack = stack.reshape(pairs * rows, length)
    lagged = to_lags(stack, table_ref[...]) * scale
    stage_ref[...] = lagged.astype(stage_ref.dtype).reshape(pairs, rows, length)
    copy = pltpu.make_async_copy(stage_ref, out_hbm.at[:, pl.ds(first, rows)], sems.at[0])
    copy.start()
    copy.wait()


def last_kernel(scale, first, weights, table_ref, part_ref, more_ref, *rest):
    out_hbm, stage_ref, sems = rest[-3:]
    place = whereabouts(len(weights) // 2)
    pairs, rows, length = stage_ref.shape
    more = more_ref[...].reshape(pairs * rows, length)
    lagged = jnp.dot(more, table_ref[...], preferred_element_type=jnp.float32)
    weight = chosen(weights, place)
    size = pairs // 2
    copies = []
    for piece in range(2):
        here = slice(piece * size * rows, (piece + 1) * size * rows)
        value = (part_ref[here] + lagged[here] * weight) * scale
        there = pl.ds(piece * size, size)
        stage_ref[there] = value.astype(stage_ref.dtype).reshape(size, rows, length)
        target = out_hbm.at[there, pl.ds(first, rows)]
        copies.append(pltpu.make_async_copy(stage_ref.at[there], target, sems.at[piece]))
        copies[-1].start()
    for copy in copies:
        copy.wait()


def cost(flops, moved):
    return pl.CostEstimate(flops=flops, bytes_accessed=moved, transcendentals=0)


def whole(memory=pltpu.VMEM):
    return pl.BlockSpec(memory_space=memory)


def per_device(samples, valid, offsets):
    chans, wins, length = samples.shape
    bins = length // 2
    span = OFFSET_SPAN
    pairs = offsets.shape[0]
    tiles = bins // LANES
    groups = lax.axis_size("tm")
    factor = float(np.float32(DECAY) ** np.float32(wins))
    params = pltpu.CompilerParams(vmem_limit_bytes=VMEM)

    def in_hbm(value):
        return pltpu.with_memory_space_constraint(value, pltpu.HBM)

    half = chans - span
    flat = samples.reshape(chans * wins, length)
    short_type = jax.ShapeDtypeStruct((span, wins * length), jnp.bfloat16)
    local_type = jax.ShapeDtypeStruct((pairs, span, length), jnp.bfloat16)
    raw_scratch = pltpu.VMEM((2 * tiles, span * wins, LANES), jnp.float32)
    near_scratch = pltpu.VMEM((2 * span, wins * length), jnp.bfloat16)
    parts_scratch = [pltpu.VMEM((wins, pairs // 4 * span, length), jnp.float32)] * 4

    short_a, table, pick, keep = pl.pallas_call(
        head_kernel,
        out_shape=(
            short_type,
            jax.ShapeDtypeStruct((length, length), jnp.bfloat16),
            jax.ShapeDtypeStruct((pairs, span, 2 * span), jnp.bfloat16),
            jax.ShapeDtypeStruct((chans, wins * LANES), jnp.float32),
        ),
        in_specs=[whole(pltpu.HBM)] * 3,
        out_specs=(whole(),) * 4,
        scratch_shapes=[
            pltpu.VMEM((span * wins, length), jnp.bfloat16),
            pltpu.VMEM((wins, chans), jnp.int32),
            pltpu.SMEM((pairs,), jnp.int32),
            raw_scratch,
            pltpu.SemaphoreType.DMA((3,)),
        ],
        compiler_params=params,
        cost_estimate=cost(span * wins * length * length * 2, 2 * 1024 * 1024),
        name="head",
    )(in_hbm(flat), in_hbm(valid.T), in_hbm(offsets))

    ring = lax.axis_size("chan")
    edge = lax.ppermute(short_a, "chan", [(i, i - 1) for i in range(1, ring)])

    columns = min(d for d in range(1, groups + 1) if groups % d == 0 and d * d >= groups)
    square = columns == 2 and groups == columns * columns
    limits = (2, 3) if square else (groups, groups)

    def tail(now, after):
        return pl.pallas_call(
            functools.partial(tail_kernel, limits, now),
            out_shape=(short_type, local_type),
            in_specs=[whole()] * 5 + [whole(pl.ANY)],
            out_specs=(whole(),) * 2,
            scratch_shapes=[raw_scratch, near_scratch] + parts_scratch,
            compiler_params=params,
            cost_estimate=cost(span * wins * length * length * 4, 4 * 1024 * 1024),
            name="tail",
        )(flat, table, keep, pick, short_a, after)

    def cross(now, short, after):
        return pl.pallas_call(
            functools.partial(cross_kernel, limits, now),
            out_shape=local_type,
            in_specs=[whole()] * 3 + [whole(pl.ANY)],
            out_specs=whole(),
            scratch_shapes=[near_scratch] + parts_scratch,
            compiler_params=params,
            cost_estimate=cost(pairs * span * wins * bins * 8, 4 * 1024 * 1024),
            name="cross",
        )(pick, short, edge, after)

    short_b, local_a = tail(0, table)
    local_b = cross(0, short_b, table)
    short_late, late_a = tail(1, local_b)
    late_b = cross(1, short_late, local_b)

    power = [float(np.float32(factor) ** np.float32(d)) for d in range(groups)]
    def sent(value, even, odd):
        moves = [
            (c * groups + here, c * groups + there)
            for c in range(ring)
            for here, there in (odd if c % 2 else even)
        ]
        return lax.ppermute(value, ("chan", "tm"), moves)

    def mix(terms, weights, after):
        return pl.pallas_call(
            functools.partial(mix_kernel, limits, weights),
            out_shape=local_type,
            in_specs=[whole()] * len(terms) + [whole(pl.ANY)],
            out_specs=whole(),
            compiler_params=params,
            cost_estimate=cost(len(terms) * terms[0].size * 4, 1024 * 1024),
            name="mix",
        )(*terms, after)

    inverse = pl.pallas_call(
        inverse_kernel,
        out_shape=jax.ShapeDtypeStruct((length, length), jnp.bfloat16),
        in_specs=[whole(pl.ANY)],
        out_specs=whole(),
        compiler_params=params,
        cost_estimate=cost(length * bins * 32, 512 * 1024),
        name="inverse",
    )(local_b)

    def written(kernel, terms, later, *so_far):
        return pl.pallas_call(
            kernel,
            out_shape=jax.ShapeDtypeStruct((pairs, chans, length), jnp.bfloat16),
            in_specs=[whole()] * (1 + len(terms)) + [whole(pl.ANY)] * (len(later) + len(so_far)),
            out_specs=whole(pl.ANY),
            scratch_shapes=[
                pltpu.VMEM((pairs, span, length), jnp.bfloat16),
                pltpu.SemaphoreType.DMA((2,)),
            ],
            input_output_aliases={1 + len(terms) + len(later): 0} if so_far else {},
            compiler_params=params,
            cost_estimate=cost(pairs * span * length * length * 4, 1024 * 1024),
            name="lags",
        )(inverse, *terms, *later, *so_far)

    def part(terms, weights):
        return pl.pallas_call(
            functools.partial(part_kernel, limits, weights),
            out_shape=jax.ShapeDtypeStruct((pairs * span, length), jnp.float32),
            in_specs=[whole()] * (1 + len(terms)),
            out_specs=whole(),
            compiler_params=params,
            cost_estimate=cost(pairs * span * length * length * 4, 1024 * 1024),
            name="part",
        )(inverse, *terms)

    unit = [1.0] * (2 * groups)

    def two_hops(local, late, after, apart):
        f, ff = power[1], power[2]
        last = [(2, 3)]
        got = sent(local, [(0, 2), (1, 3)], [(0, 1), (1, 0)] + ([] if apart else last))
        alone = [sent(local, [], last)] if apart else []
        total = mix(
            [local, late, got],
            [[1.0, 1.0, 1.0, 0.0, f, 1.0, 0.0, 0.0], [ff, ff, ff, 1.0, 1.0, f, 0.0, 0.0]],
            after,
        )
        more = sent(total, [(0, 1), (2, 3), (3, 2)], [(0, 2), (1, 3)])
        weights = [
            unit,
            [ff, ff, ff, ff, 0.0, f, 0.0, f],
        ]
        weights += [[f] * (2 * groups)] * len(alone) + [[f, f, f, f, 0.0, 0.0, f, ff]]
        return total, [got] + alone + [more], weights

    def one_hop(local, late, after, apart):
        terms, weights = [], [unit]
        for d in range(1, groups):
            moves = [(h, h + d) for h in range(groups - d)]
            terms.append(sent(local, moves, moves))
            weights.append([power[d]] * (2 * groups))
        return local, terms, weights

    spread = two_hops if square else one_hop
    scale = bins**-0.5
    _, terms_a, weights_a = spread(local_a, late_a, late_b, False)
    ahead, terms_b, weights_b = spread(local_b, late_b, local_b, True)
    short_last, last_a = tail(2, ahead)
    last_b = cross(2, short_last, ahead)
    terms_a = [local_a, late_a, last_a] + terms_a
    terms_b = [local_b, late_b, last_b] + terms_b
    before = part(terms_b[:-1], weights_b[:-1])
    first = functools.partial(lag_kernel, limits, scale, 0, weights_a)
    result = written(first, terms_a, [before])
    last = functools.partial(last_kernel, scale, half, weights_b[-1])
    result = written(last, [before, terms_b[-1]], [], result)
    return result.reshape(1, pairs, chans, length)


def solution(mesh):
    in_specs = (P("chan", "tm", None), P("chan", "tm"), P())
    out_specs = P("tm", None, "chan", None)
    return jax.shard_map(
        per_device, mesh=mesh, in_specs=in_specs, out_specs=out_specs, check_vma=False
    )
```

```python
import functools
import math

import jax
import jax.numpy as jnp
import numpy as np
from jax import lax
from jax.experimental import pallas as pl
from jax.experimental.pallas import tpu as pltpu
from jax.sharding import PartitionSpec as P

OFFSET_SPAN = 32
LANES = 128
DECAY = 0.99
VMEM = 24 * 1024 * 1024


def turns(number, length):
    part = (number - length * jnp.floor(number / length + 0.5)) * (1.0 / length)
    square = part * part
    cosine, sine = jnp.float32(0.0), jnp.float32(0.0)
    for k in range(10, -1, -1):
        cosine = cosine * square + (-1) ** k * (2 * math.pi) ** (2 * k) / math.factorial(2 * k)
        sine = sine * square + (-1) ** k * (2 * math.pi) ** (2 * k + 1) / math.factorial(2 * k + 1)
    return cosine, sine * part


def fill_table(table_ref, step):
    length = table_ref.shape[0]
    bins = length // 2

    def small(rows, by):
        row = lax.broadcasted_iota(jnp.int32, (rows, bins), 0)
        freq = lax.broadcasted_iota(jnp.int32, (rows, bins), 1) + 1
        return turns((row * (by * freq)).astype(jnp.float32), length)

    coarse_cos, coarse_sin = small(length // step, step)
    fine_cos, fine_sin = small(step, 1)
    for i in range(length // step):
        rows = slice(i * step, (i + 1) * step)
        cos_i, sin_i = coarse_cos[i : i + 1], coarse_sin[i : i + 1]
        cosine = (cos_i * fine_cos - sin_i * fine_sin).astype(jnp.bfloat16)
        sine = (sin_i * fine_cos + cos_i * fine_sin).astype(jnp.bfloat16)
        for t in range(bins // LANES):
            here = slice(t * LANES, (t + 1) * LANES)
            table_ref[rows, 2 * t * LANES : (2 * t + 1) * LANES] = cosine[:, here]
            table_ref[rows, (2 * t + 1) * LANES : (2 * t + 2) * LANES] = -sine[:, here]


def inverse_kernel(_, table_ref):
    length = table_ref.shape[0]
    bins = length // 2
    step = 16

    def small(rows, by, first):
        freq = (lax.broadcasted_iota(jnp.int32, (rows, length), 0) + first) * by
        lag = lax.broadcasted_iota(jnp.int32, (rows, length), 1)
        return turns((freq * lag).astype(jnp.float32), length)

    coarse_cos, coarse_sin = small(bins // step, step, 0)
    fine_cos, fine_sin = small(step, 1, 1)
    for i in range(bins // step):
        first = i * step
        cos_i, sin_i = coarse_cos[i : i + 1], coarse_sin[i : i + 1]
        cosine = cos_i * fine_cos - sin_i * fine_sin
        sine = sin_i * fine_cos + cos_i * fine_sin
        table_ref[first : first + step, :] = cosine.astype(jnp.bfloat16)
        table_ref[bins + first : bins + first + step, :] = (-sine).astype(jnp.bfloat16)


def whiten_block(x, table_ref, keep, raw_ref, white_ref, short_ref):
    wins, span, length = white_ref.shape
    bins = length // 2
    tiles = bins // LANES

    def strided(t, w):
        return raw_ref[t, pl.ds(w, span, stride=wins), :]

    total = [None] * wins
    for t in range(tiles):
        lanes = slice(2 * t * LANES, (2 * t + 2) * LANES)
        raw = jnp.dot(x, table_ref[:, lanes], preferred_element_type=jnp.float32)
        raw_ref[2 * t] = raw[:, :LANES]
        raw_ref[2 * t + 1] = raw[:, LANES:]
    for t in range(tiles):
        for w in range(wins):
            real_part, imag_part = strided(2 * t, w), strided(2 * t + 1, w)
            power = real_part * real_part + imag_part * imag_part
            total[w] = power if t == 0 else total[w] + power
    for w in range(wins):
        decay = float(np.float32(DECAY) ** np.float32(wins - 1 - w))
        level = jnp.sum(total[w], axis=-1, keepdims=True) * (0.01 / bins) + 1e-06
        alive = keep[:, w * LANES : (w + 1) * LANES]
        for t in range(tiles):
            part = [strided(2 * t, w), strided(2 * t + 1, w)]
            power = part[0] * part[0] + part[1] * part[1]
            scale = alive * lax.rsqrt(power + level)
            for i, s in enumerate((t, tiles + t)):
                value = part[i] * scale
                here = pl.ds(w * length + s * LANES, LANES)
                white_ref[w, :, s * LANES : (s + 1) * LANES] = value * decay
                short_ref[:, here] = value.astype(jnp.bfloat16)


def head_kernel(
    x_hbm,
    valid_hbm,
    offsets_hbm,
    white_ref,
    short_ref,
    table_ref,
    pick_ref,
    keep_ref,
    rest_ref,
    x_ref,
    valid_ref,
    offsets_ref,
    raw_ref,
    sems,
):
    wins, span, length = white_ref.shape
    pairs = offsets_ref.shape[0]
    copies = [
        pltpu.make_async_copy(valid_hbm, valid_ref, sems.at[0]),
        pltpu.make_async_copy(offsets_hbm, offsets_ref, sems.at[1]),
        pltpu.make_async_copy(x_hbm.at[pl.ds(0, span * wins)], x_ref, sems.at[2]),
        pltpu.make_async_copy(x_hbm.at[pl.ds(span * wins, span * wins)], rest_ref, sems.at[3]),
    ]
    for copy in copies:
        copy.start()
    fill_table(table_ref, 16)
    copies[0].wait()
    copies[1].wait()
    ahead = lax.broadcasted_iota(jnp.int32, (span, 2 * span), 1) - lax.broadcasted_iota(
        jnp.int32, (span, 2 * span), 0
    )
    for k in range(pairs):
        chosen_row = jnp.where(ahead == offsets_ref[k], jnp.float32(1.0), jnp.float32(0.0))
        pick_ref[k] = chosen_row.astype(jnp.bfloat16)
    owner = lax.broadcasted_iota(jnp.int32, (wins, wins * LANES), 0)
    column = lax.broadcasted_iota(jnp.int32, (wins, wins * LANES), 1) // LANES
    keep_ref[...] = lax.dot_general(
        valid_ref[...].astype(jnp.float32).astype(jnp.bfloat16),
        (owner == column).astype(jnp.float32).astype(jnp.bfloat16),
        (((0,), (0,)), ((), ())),
        preferred_element_type=jnp.float32,
    )
    copies[2].wait()
    whiten_block(x_ref[...], table_ref, keep_ref[:span], raw_ref, white_ref, short_ref)
    copies[3].wait()


def stack_pairs(pick_ref, white_ref, near_ref, parts_refs, out_ref):
    wins, _, length = white_ref.shape
    pairs, rows, reach = pick_ref.shape
    bins = length // 2
    size = pairs // len(parts_refs)

    def select(group, w):
        pick = pick_ref[group * size : (group + 1) * size].reshape(size * rows, reach)
        near = near_ref[:, w * length : (w + 1) * length]
        parts_refs[group][w] = jnp.dot(pick, near, preferred_element_type=jnp.float32)

    blocks = [(c, t) for c in range(0, rows, 16) for t in range(bins // LANES)]
    for w in range(wins):
        select(0, w)
    for group, parts_ref in enumerate(parts_refs):
        ahead = list(range(wins)) if group + 1 < len(parts_refs) else []
        for i, (c, t) in enumerate(blocks):
            for w in ahead[i :: len(blocks)]:
                select(group + 1, w)
            re = slice(t * LANES, (t + 1) * LANES)
            im = slice(bins + t * LANES, bins + (t + 1) * LANES)
            head_re = [white_ref[w, c : c + 16, re] for w in range(wins)]
            head_im = [white_ref[w, c : c + 16, im] for w in range(wins)]
            for k in range(size):
                here = slice(k * rows + c, k * rows + c + 16)
                total_re = total_im = None
                for w in range(wins):
                    part_re, part_im = parts_ref[w, here, re], parts_ref[w, here, im]
                    cross_re = head_re[w] * part_re + head_im[w] * part_im
                    cross_im = head_im[w] * part_re - head_re[w] * part_im
                    total_re = cross_re if w == 0 else total_re + cross_re
                    total_im = cross_im if w == 0 else total_im + cross_im
                pair = group * size + k
                out_ref[pair, c : c + 16, re] = total_re.astype(out_ref.dtype)
                out_ref[pair, c : c + 16, im] = total_im.astype(out_ref.dtype)


def role(limits):
    odd = lax.rem(lax.axis_index("chan"), 2)
    first = lax.axis_index("tm") < jnp.where(odd == 0, *limits)
    return jnp.where(first, 0, 1 + odd)


def tail_kernel(
    limits,
    now,
    x_ref,
    table_ref,
    keep_ref,
    pick_ref,
    head_ref,
    edge_ref,
    after_ref,
    white_ref,
    short_ref,
    out_ref,
    raw_ref,
    near_ref,
    *parts_refs,
):
    wins, span, length = white_ref.shape

    @pl.when(role(limits) == now)
    def _():
        whiten_block(x_ref[...], table_ref, keep_ref[span:], raw_ref, white_ref, short_ref)
        near_ref[:span] = edge_ref[...]
        near_ref[span:] = short_ref[...]
        stack_pairs(pick_ref, head_ref, near_ref, parts_refs, out_ref)


def cross_kernel(
    limits, now, pick_ref, white_ref, short_ref, edge_ref, after_ref, out_ref, near_ref, *parts_refs
):
    span = short_ref.shape[0]

    @pl.when(role(limits) == now)
    def _():
        near_ref[:span] = short_ref[...]
        near_ref[span:] = edge_ref[...]
        stack_pairs(pick_ref, white_ref, near_ref, parts_refs, out_ref)


def chosen(options, place):
    value = jnp.float32(options[0])
    for i, option in enumerate(options[1:]):
        value = jnp.where(place == i + 1, jnp.float32(option), value)
    return value


def weighted(limits, terms, weights, place):
    total = None
    mine = role(limits)
    late = len(terms) - len(weights)
    first = terms[late][...]
    for i in range(late - 1, -1, -1):
        first = jnp.where(mine == i, terms[i][...], first)
    for term, options in zip([first] + list(terms[late + 1 :]), weights):
        value = term[...].astype(jnp.float32)
        if set(options) != {1.0}:
            value = value * (options[0] if len(set(options)) == 1 else chosen(options, place))
        total = value if total is None else total + value
    return total


def whereabouts(groups):
    return lax.rem(lax.axis_index("chan"), 2) * groups + lax.axis_index("tm")


def mix_kernel(limits, weights, *refs):
    count = len(weights) + 1
    place = whereabouts(len(weights[0]) // 2)
    total = weighted(limits, refs[:count], weights, place)
    refs[-1][...] = total.astype(refs[-1].dtype)


def to_lags(stack, table):
    count = stack.shape[0]
    high = stack.astype(jnp.bfloat16)
    low = (stack - high.astype(jnp.float32)).astype(jnp.bfloat16)
    both = jnp.dot(jnp.concatenate([high, low]), table, preferred_element_type=jnp.float32)
    return both[:count] + both[count:]


def part_kernel(limits, weights, table_ref, *refs):
    place = whereabouts(len(weights[0]) // 2)
    out_ref = refs[-1]
    stack = weighted(limits, refs[: len(weights) + 2], weights, place).reshape(out_ref.shape)
    out_ref[...] = to_lags(stack, table_ref[...])


def lag_kernel(limits, scale, first, weights, table_ref, *rest):
    out_hbm, stage_ref, sem = rest[-3:]
    place = whereabouts(len(weights[0]) // 2)
    pairs, rows, length = stage_ref.shape
    stack = weighted(limits, rest[: len(weights) + 2], weights, place)
    stack = stack.reshape(pairs * rows, length)
    lagged = to_lags(stack, table_ref[...]) * scale
    stage_ref[...] = lagged.astype(stage_ref.dtype).reshape(pairs, rows, length)
    copy = pltpu.make_async_copy(stage_ref, out_hbm.at[:, pl.ds(first, rows)], sem)
    copy.start()
    copy.wait()


def last_kernel(scale, first, weights, table_ref, part_ref, more_ref, *rest):
    out_hbm, stage_ref, sem = rest[-3:]
    place = whereabouts(len(weights) // 2)
    pairs, rows, length = stage_ref.shape
    more = more_ref[...].reshape(pairs * rows, length)
    lagged = jnp.dot(more, table_ref[...], preferred_element_type=jnp.float32)
    lagged = (part_ref[...] + lagged * chosen(weights, place)) * scale
    stage_ref[...] = lagged.astype(stage_ref.dtype).reshape(pairs, rows, length)
    copy = pltpu.make_async_copy(stage_ref, out_hbm.at[:, pl.ds(first, rows)], sem)
    copy.start()
    copy.wait()


def cost(flops, moved):
    return pl.CostEstimate(flops=flops, bytes_accessed=moved, transcendentals=0)


def whole(memory=pltpu.VMEM):
    return pl.BlockSpec(memory_space=memory)


def per_device(samples, valid, offsets):
    chans, wins, length = samples.shape
    bins = length // 2
    span = OFFSET_SPAN
    pairs = offsets.shape[0]
    tiles = bins // LANES
    groups = lax.axis_size("tm")
    factor = float(np.float32(DECAY) ** np.float32(wins))
    params = pltpu.CompilerParams(vmem_limit_bytes=VMEM)

    def in_hbm(value):
        return pltpu.with_memory_space_constraint(value, pltpu.HBM)

    half = chans - span
    flat = samples.reshape(chans * wins, length)
    white_type = jax.ShapeDtypeStruct((wins, span, length), jnp.float32)
    short_type = jax.ShapeDtypeStruct((span, wins * length), jnp.bfloat16)
    local_type = jax.ShapeDtypeStruct((pairs, span, length), jnp.bfloat16)
    raw_scratch = pltpu.VMEM((2 * tiles, span * wins, LANES), jnp.float32)
    near_scratch = pltpu.VMEM((2 * span, wins * length), jnp.bfloat16)
    parts_scratch = [pltpu.VMEM((wins, pairs // 4 * span, length), jnp.float32)] * 4

    white_a, short_a, table, pick, keep, rest = pl.pallas_call(
        head_kernel,
        out_shape=(
            white_type,
            short_type,
            jax.ShapeDtypeStruct((length, length), jnp.bfloat16),
            jax.ShapeDtypeStruct((pairs, span, 2 * span), jnp.bfloat16),
            jax.ShapeDtypeStruct((chans, wins * LANES), jnp.float32),
            jax.ShapeDtypeStruct((span * wins, length), jnp.bfloat16),
        ),
        in_specs=[whole(pltpu.HBM)] * 3,
        out_specs=(whole(),) * 6,
        scratch_shapes=[
            pltpu.VMEM((span * wins, length), jnp.bfloat16),
            pltpu.VMEM((wins, chans), jnp.int32),
            pltpu.SMEM((pairs,), jnp.int32),
            raw_scratch,
            pltpu.SemaphoreType.DMA((4,)),
        ],
        compiler_params=params,
        cost_estimate=cost(span * wins * length * length * 2, 2 * 1024 * 1024),
        name="head",
    )(in_hbm(flat), in_hbm(valid.T), in_hbm(offsets))

    ring = lax.axis_size("chan")
    edge = lax.ppermute(short_a, "chan", [(i, i - 1) for i in range(1, ring)])

    columns = min(d for d in range(1, groups + 1) if groups % d == 0 and d * d >= groups)
    square = columns == 2 and groups == columns * columns
    limits = (2, 3) if square else (groups, groups)

    def tail(now, after):
        return pl.pallas_call(
            functools.partial(tail_kernel, limits, now),
            out_shape=(white_type, short_type, local_type),
            in_specs=[whole()] * 6 + [whole(pl.ANY)],
            out_specs=(whole(),) * 3,
            scratch_shapes=[raw_scratch, near_scratch] + parts_scratch,
            compiler_params=params,
            cost_estimate=cost(span * wins * length * length * 4, 4 * 1024 * 1024),
            name="tail",
        )(rest, table, keep, pick, white_a, short_a, after)

    def cross(now, white, short, after):
        return pl.pallas_call(
            functools.partial(cross_kernel, limits, now),
            out_shape=local_type,
            in_specs=[whole()] * 4 + [whole(pl.ANY)],
            out_specs=whole(),
            scratch_shapes=[near_scratch] + parts_scratch,
            compiler_params=params,
            cost_estimate=cost(pairs * span * wins * bins * 8, 4 * 1024 * 1024),
            name="cross",
        )(pick, white, short, edge, after)

    white_b, short_b, local_a = tail(0, table)
    local_b = cross(0, white_b, short_b, table)
    white_late, short_late, late_a = tail(1, local_b)
    late_b = cross(1, white_late, short_late, local_b)

    power = [float(np.float32(factor) ** np.float32(d)) for d in range(groups)]
    def sent(value, even, odd):
        moves = [
            (c * groups + here, c * groups + there)
            for c in range(ring)
            for here, there in (odd if c % 2 else even)
        ]
        return lax.ppermute(value, ("chan", "tm"), moves)

    def mix(terms, weights, after):
        return pl.pallas_call(
            functools.partial(mix_kernel, limits, weights),
            out_shape=local_type,
            in_specs=[whole()] * len(terms) + [whole(pl.ANY)],
            out_specs=whole(),
            compiler_params=params,
            cost_estimate=cost(len(terms) * terms[0].size * 4, 1024 * 1024),
            name="mix",
        )(*terms, after)

    inverse = pl.pallas_call(
        inverse_kernel,
        out_shape=jax.ShapeDtypeStruct((length, length), jnp.bfloat16),
        in_specs=[whole(pl.ANY)],
        out_specs=whole(),
        compiler_params=params,
        cost_estimate=cost(length * bins * 32, 512 * 1024),
        name="inverse",
    )(local_b)

    def written(kernel, terms, later, *so_far):
        return pl.pallas_call(
            kernel,
            out_shape=jax.ShapeDtypeStruct((pairs, chans, length), jnp.bfloat16),
            in_specs=[whole()] * (1 + len(terms)) + [whole(pl.ANY)] * (len(later) + len(so_far)),
            out_specs=whole(pl.ANY),
            scratch_shapes=[
                pltpu.VMEM((pairs, span, length), jnp.bfloat16),
                pltpu.SemaphoreType.DMA,
            ],
            input_output_aliases={1 + len(terms) + len(later): 0} if so_far else {},
            compiler_params=params,
            cost_estimate=cost(pairs * span * length * length * 4, 1024 * 1024),
            name="lags",
        )(inverse, *terms, *later, *so_far)

    def part(terms, weights):
        return pl.pallas_call(
            functools.partial(part_kernel, limits, weights),
            out_shape=jax.ShapeDtypeStruct((pairs * span, length), jnp.float32),
            in_specs=[whole()] * (1 + len(terms)),
            out_specs=whole(),
            compiler_params=params,
            cost_estimate=cost(pairs * span * length * length * 4, 1024 * 1024),
            name="part",
        )(inverse, *terms)

    unit = [1.0] * (2 * groups)

    def two_hops(local, late, after, apart):
        f, ff = power[1], power[2]
        last = [(2, 3)]
        got = sent(local, [(0, 2), (1, 3)], [(0, 1), (1, 0)] + ([] if apart else last))
        alone = [sent(local, [], last)] if apart else []
        total = mix(
            [local, late, got],
            [[1.0, 1.0, 1.0, 0.0, f, 1.0, 0.0, 0.0], [ff, ff, ff, 1.0, 1.0, f, 0.0, 0.0]],
            after,
        )
        more = sent(total, [(0, 1), (2, 3), (3, 2)], [(0, 2), (1, 3)])
        weights = [
            unit,
            [ff, ff, ff, ff, 0.0, f, 0.0, f],
        ]
        weights += [[f] * (2 * groups)] * len(alone) + [[f, f, f, f, 0.0, 0.0, f, ff]]
        return total, [got] + alone + [more], weights

    def one_hop(local, late, after, apart):
        terms, weights = [], [unit]
        for d in range(1, groups):
            moves = [(h, h + d) for h in range(groups - d)]
            terms.append(sent(local, moves, moves))
            weights.append([power[d]] * (2 * groups))
        return local, terms, weights

    spread = two_hops if square else one_hop
    scale = bins**-0.5
    _, terms_a, weights_a = spread(local_a, late_a, late_b, False)
    ahead, terms_b, weights_b = spread(local_b, late_b, local_b, True)
    white_last, short_last, last_a = tail(2, ahead)
    last_b = cross(2, white_last, short_last, ahead)
    terms_a = [local_a, late_a, last_a] + terms_a
    terms_b = [local_b, late_b, last_b] + terms_b
    before = part(terms_b[:-1], weights_b[:-1])
    first = functools.partial(lag_kernel, limits, scale, 0, weights_a)
    result = written(first, terms_a, [before])
    last = functools.partial(last_kernel, scale, half, weights_b[-1])
    result = written(last, [before, terms_b[-1]], [], result)
    return result.reshape(1, pairs, chans, length)


def solution(mesh):
    in_specs = (P("chan", "tm", None), P("chan", "tm"), P())
    out_specs = P("tm", None, "chan", None)
    return jax.shard_map(
        per_device, mesh=mesh, in_specs=in_specs, out_specs=out_specs, check_vma=False
    )
```

```python
import functools
import math

import jax
import jax.numpy as jnp
import numpy as np
from jax import lax
from jax.experimental import pallas as pl
from jax.experimental.pallas import tpu as pltpu
from jax.sharding import PartitionSpec as P

OFFSET_SPAN = 32
LANES = 128
DECAY = 0.99
VMEM = 24 * 1024 * 1024


def turns(number, length):
    part = (number - length * jnp.floor(number / length + 0.5)) * (1.0 / length)
    square = part * part
    cosine, sine = jnp.float32(0.0), jnp.float32(0.0)
    for k in range(10, -1, -1):
        cosine = cosine * square + (-1) ** k * (2 * math.pi) ** (2 * k) / math.factorial(2 * k)
        sine = sine * square + (-1) ** k * (2 * math.pi) ** (2 * k + 1) / math.factorial(2 * k + 1)
    return cosine, sine * part


def fill_table(table_ref, step):
    length = table_ref.shape[0]
    bins = length // 2

    def small(rows, by):
        row = lax.broadcasted_iota(jnp.int32, (rows, bins), 0)
        freq = lax.broadcasted_iota(jnp.int32, (rows, bins), 1) + 1
        return turns((row * (by * freq)).astype(jnp.float32), length)

    coarse_cos, coarse_sin = small(length // step, step)
    fine_cos, fine_sin = small(step, 1)
    for i in range(length // step):
        rows = slice(i * step, (i + 1) * step)
        cos_i, sin_i = coarse_cos[i : i + 1], coarse_sin[i : i + 1]
        cosine = (cos_i * fine_cos - sin_i * fine_sin).astype(jnp.bfloat16)
        sine = (sin_i * fine_cos + cos_i * fine_sin).astype(jnp.bfloat16)
        for t in range(bins // LANES):
            here = slice(t * LANES, (t + 1) * LANES)
            table_ref[rows, 2 * t * LANES : (2 * t + 1) * LANES] = cosine[:, here]
            table_ref[rows, (2 * t + 1) * LANES : (2 * t + 2) * LANES] = -sine[:, here]


def inverse_kernel(_, table_ref):
    length = table_ref.shape[0]
    bins = length // 2
    step = 16

    def small(rows, by, first):
        freq = (lax.broadcasted_iota(jnp.int32, (rows, length), 0) + first) * by
        lag = lax.broadcasted_iota(jnp.int32, (rows, length), 1)
        return turns((freq * lag).astype(jnp.float32), length)

    coarse_cos, coarse_sin = small(bins // step, step, 0)
    fine_cos, fine_sin = small(step, 1, 1)
    for i in range(bins // step):
        first = i * step
        cos_i, sin_i = coarse_cos[i : i + 1], coarse_sin[i : i + 1]
        cosine = cos_i * fine_cos - sin_i * fine_sin
        sine = sin_i * fine_cos + cos_i * fine_sin
        table_ref[first : first + step, :] = cosine.astype(jnp.bfloat16)
        table_ref[bins + first : bins + first + step, :] = (-sine).astype(jnp.bfloat16)


def whiten_block(x, table_ref, keep, raw_ref, white_ref, short_ref):
    wins, span, length = white_ref.shape
    bins = length // 2
    tiles = bins // LANES

    def strided(t, w):
        return raw_ref[t, pl.ds(w, span, stride=wins), :]

    total = [None] * wins
    for t in range(tiles):
        lanes = slice(2 * t * LANES, (2 * t + 2) * LANES)
        raw = jnp.dot(x, table_ref[:, lanes], preferred_element_type=jnp.float32)
        raw_ref[2 * t] = raw[:, :LANES]
        raw_ref[2 * t + 1] = raw[:, LANES:]
    for t in range(tiles):
        for w in range(wins):
            real_part, imag_part = strided(2 * t, w), strided(2 * t + 1, w)
            power = real_part * real_part + imag_part * imag_part
            total[w] = power if t == 0 else total[w] + power
    for w in range(wins):
        decay = float(np.float32(DECAY) ** np.float32(wins - 1 - w))
        level = jnp.sum(total[w], axis=-1, keepdims=True) * (0.01 / bins) + 1e-06
        alive = keep[:, w * LANES : (w + 1) * LANES]
        for t in range(tiles):
            part = [strided(2 * t, w), strided(2 * t + 1, w)]
            power = part[0] * part[0] + part[1] * part[1]
            scale = alive * lax.rsqrt(power + level)
            for i, s in enumerate((t, tiles + t)):
                value = part[i] * scale
                here = pl.ds(w * length + s * LANES, LANES)
                white_ref[w, :, s * LANES : (s + 1) * LANES] = value * decay
                short_ref[:, here] = value.astype(jnp.bfloat16)


def head_kernel(
    x_hbm,
    valid_hbm,
    offsets_hbm,
    white_ref,
    short_ref,
    table_ref,
    pick_ref,
    keep_ref,
    x_ref,
    valid_ref,
    offsets_ref,
    raw_ref,
    sems,
):
    wins, span, length = white_ref.shape
    pairs = offsets_ref.shape[0]
    copies = [
        pltpu.make_async_copy(valid_hbm, valid_ref, sems.at[0]),
        pltpu.make_async_copy(offsets_hbm, offsets_ref, sems.at[1]),
        pltpu.make_async_copy(x_hbm.at[pl.ds(0, span * wins)], x_ref, sems.at[2]),
    ]
    for copy in copies:
        copy.start()
    fill_table(table_ref, 16)
    copies[0].wait()
    copies[1].wait()
    ahead = lax.broadcasted_iota(jnp.int32, (span, 2 * span), 1) - lax.broadcasted_iota(
        jnp.int32, (span, 2 * span), 0
    )
    for k in range(pairs):
        chosen_row = jnp.where(ahead == offsets_ref[k], jnp.float32(1.0), jnp.float32(0.0))
        pick_ref[k] = chosen_row.astype(jnp.bfloat16)
    owner = lax.broadcasted_iota(jnp.int32, (wins, wins * LANES), 0)
    column = lax.broadcasted_iota(jnp.int32, (wins, wins * LANES), 1) // LANES
    keep_ref[...] = lax.dot_general(
        valid_ref[...].astype(jnp.float32).astype(jnp.bfloat16),
        (owner == column).astype(jnp.float32).astype(jnp.bfloat16),
        (((0,), (0,)), ((), ())),
        preferred_element_type=jnp.float32,
    )
    copies[2].wait()
    whiten_block(x_ref[...], table_ref, keep_ref[:span], raw_ref, white_ref, short_ref)


def stack_pairs(pick_ref, white_ref, near_ref, parts_refs, out_ref):
    wins, _, length = white_ref.shape
    pairs, rows, reach = pick_ref.shape
    bins = length // 2
    size = pairs // len(parts_refs)

    def select(group, w):
        pick = pick_ref[group * size : (group + 1) * size].reshape(size * rows, reach)
        near = near_ref[:, w * length : (w + 1) * length]
        parts_refs[group][w] = jnp.dot(pick, near, preferred_element_type=jnp.float32)

    blocks = [(c, t) for c in range(0, rows, 16) for t in range(bins // LANES)]
    for w in range(wins):
        select(0, w)
    for group, parts_ref in enumerate(parts_refs):
        ahead = list(range(wins)) if group + 1 < len(parts_refs) else []
        for i, (c, t) in enumerate(blocks):
            for w in ahead[i :: len(blocks)]:
                select(group + 1, w)
            re = slice(t * LANES, (t + 1) * LANES)
            im = slice(bins + t * LANES, bins + (t + 1) * LANES)
            head_re = [white_ref[w, c : c + 16, re] for w in range(wins)]
            head_im = [white_ref[w, c : c + 16, im] for w in range(wins)]
            for k in range(size):
                here = slice(k * rows + c, k * rows + c + 16)
                total_re = total_im = None
                for w in range(wins):
                    part_re, part_im = parts_ref[w, here, re], parts_ref[w, here, im]
                    cross_re = head_re[w] * part_re + head_im[w] * part_im
                    cross_im = head_im[w] * part_re - head_re[w] * part_im
                    total_re = cross_re if w == 0 else total_re + cross_re
                    total_im = cross_im if w == 0 else total_im + cross_im
                pair = group * size + k
                out_ref[pair, c : c + 16, re] = total_re.astype(out_ref.dtype)
                out_ref[pair, c : c + 16, im] = total_im.astype(out_ref.dtype)


def role(limits):
    odd = lax.rem(lax.axis_index("chan") + 1, 2)
    first = lax.axis_index("tm") < jnp.where(odd == 0, *limits)
    return jnp.where(first, 0, 1 + odd)


def tail_kernel(
    limits,
    now,
    x_ref,
    table_ref,
    keep_ref,
    pick_ref,
    head_ref,
    edge_ref,
    after_ref,
    white_ref,
    short_ref,
    out_ref,
    raw_ref,
    near_ref,
    *parts_refs,
):
    wins, span, length = white_ref.shape
    rows = slice(span * wins, 2 * span * wins)

    @pl.when(role(limits) == now)
    def _():
        x = x_ref[rows, :]
        whiten_block(x, table_ref, keep_ref[span:], raw_ref, white_ref, short_ref)
        near_ref[:span] = edge_ref[...]
        near_ref[span:] = short_ref[...]
        stack_pairs(pick_ref, head_ref, near_ref, parts_refs, out_ref)


def cross_kernel(
    limits, now, pick_ref, white_ref, short_ref, edge_ref, after_ref, out_ref, near_ref, *parts_refs
):
    span = short_ref.shape[0]

    @pl.when(role(limits) == now)
    def _():
        near_ref[:span] = short_ref[...]
        near_ref[span:] = edge_ref[...]
        stack_pairs(pick_ref, white_ref, near_ref, parts_refs, out_ref)


def chosen(options, place):
    value = jnp.float32(options[0])
    for i, option in enumerate(options[1:]):
        value = jnp.where(place == i + 1, jnp.float32(option), value)
    return value


def weighted(limits, terms, weights, place):
    total = None
    mine = role(limits)
    late = len(terms) - len(weights)
    first = terms[late][...]
    for i in range(late - 1, -1, -1):
        first = jnp.where(mine == i, terms[i][...], first)
    for term, options in zip([first] + list(terms[late + 1 :]), weights):
        value = term[...].astype(jnp.float32)
        if set(options) != {1.0}:
            value = value * (options[0] if len(set(options)) == 1 else chosen(options, place))
        total = value if total is None else total + value
    return total


def whereabouts(groups):
    return lax.rem(lax.axis_index("chan") + 1, 2) * groups + lax.axis_index("tm")


def mix_kernel(limits, weights, *refs):
    count = len(weights) + 1
    place = whereabouts(len(weights[0]) // 2)
    total = weighted(limits, refs[:count], weights, place)
    refs[-1][...] = total.astype(refs[-1].dtype)


def to_lags(stack, table):
    count = stack.shape[0]
    high = stack.astype(jnp.bfloat16)
    low = (stack - high.astype(jnp.float32)).astype(jnp.bfloat16)
    both = jnp.dot(jnp.concatenate([high, low]), table, preferred_element_type=jnp.float32)
    return both[:count] + both[count:]


def part_kernel(limits, weights, table_ref, *refs):
    place = whereabouts(len(weights[0]) // 2)
    out_ref = refs[-1]
    stack = weighted(limits, refs[: len(weights) + 2], weights, place).reshape(out_ref.shape)
    out_ref[...] = to_lags(stack, table_ref[...])


def lag_kernel(limits, scale, first, weights, table_ref, *rest):
    out_hbm, stage_ref, sem = rest[-3:]
    place = whereabouts(len(weights[0]) // 2)
    pairs, rows, length = stage_ref.shape
    stack = weighted(limits, rest[: len(weights) + 2], weights, place)
    stack = stack.reshape(pairs * rows, length)
    lagged = to_lags(stack, table_ref[...]) * scale
    stage_ref[...] = lagged.astype(stage_ref.dtype).reshape(pairs, rows, length)
    copy = pltpu.make_async_copy(stage_ref, out_hbm.at[:, pl.ds(first, rows)], sem)
    copy.start()
    copy.wait()


def last_kernel(scale, first, weights, table_ref, part_ref, more_ref, *rest):
    out_hbm, stage_ref, sem = rest[-3:]
    place = whereabouts(len(weights) // 2)
    pairs, rows, length = stage_ref.shape
    more = more_ref[...].reshape(pairs * rows, length)
    lagged = jnp.dot(more, table_ref[...], preferred_element_type=jnp.float32)
    lagged = (part_ref[...] + lagged * chosen(weights, place)) * scale
    stage_ref[...] = lagged.astype(stage_ref.dtype).reshape(pairs, rows, length)
    copy = pltpu.make_async_copy(stage_ref, out_hbm.at[:, pl.ds(first, rows)], sem)
    copy.start()
    copy.wait()


def cost(flops, moved):
    return pl.CostEstimate(flops=flops, bytes_accessed=moved, transcendentals=0)


def whole(memory=pltpu.VMEM):
    return pl.BlockSpec(memory_space=memory)


def per_device(samples, valid, offsets):
    chans, wins, length = samples.shape
    bins = length // 2
    span = OFFSET_SPAN
    pairs = offsets.shape[0]
    tiles = bins // LANES
    groups = lax.axis_size("tm")
    factor = float(np.float32(DECAY) ** np.float32(wins))
    params = pltpu.CompilerParams(vmem_limit_bytes=VMEM)

    def in_hbm(value):
        return pltpu.with_memory_space_constraint(value, pltpu.HBM)

    half = chans - span
    flat = samples.reshape(chans * wins, length)
    white_type = jax.ShapeDtypeStruct((wins, span, length), jnp.float32)
    short_type = jax.ShapeDtypeStruct((span, wins * length), jnp.bfloat16)
    local_type = jax.ShapeDtypeStruct((pairs, span, length), jnp.bfloat16)
    raw_scratch = pltpu.VMEM((2 * tiles, span * wins, LANES), jnp.float32)
    near_scratch = pltpu.VMEM((2 * span, wins * length), jnp.bfloat16)
    parts_scratch = [pltpu.VMEM((wins, pairs // 4 * span, length), jnp.float32)] * 4

    white_a, short_a, table, pick, keep = pl.pallas_call(
        head_kernel,
        out_shape=(
            white_type,
            short_type,
            jax.ShapeDtypeStruct((length, length), jnp.bfloat16),
            jax.ShapeDtypeStruct((pairs, span, 2 * span), jnp.bfloat16),
            jax.ShapeDtypeStruct((chans, wins * LANES), jnp.float32),
        ),
        in_specs=[whole(pltpu.HBM)] * 3,
        out_specs=(whole(),) * 5,
        scratch_shapes=[
            pltpu.VMEM((span * wins, length), jnp.bfloat16),
            pltpu.VMEM((wins, chans), jnp.int32),
            pltpu.SMEM((pairs,), jnp.int32),
            raw_scratch,
            pltpu.SemaphoreType.DMA((3,)),
        ],
        compiler_params=params,
        cost_estimate=cost(span * wins * length * length * 2, 2 * 1024 * 1024),
        name="head",
    )(in_hbm(flat), in_hbm(valid.T), in_hbm(offsets))

    ring = lax.axis_size("chan")
    edge = lax.ppermute(short_a, "chan", [(i, i - 1) for i in range(1, ring)])

    columns = min(d for d in range(1, groups + 1) if groups % d == 0 and d * d >= groups)
    square = columns == 2 and groups == columns * columns
    limits = (2, 3) if square else (groups, groups)

    def tail(now, after):
        return pl.pallas_call(
            functools.partial(tail_kernel, limits, now),
            out_shape=(white_type, short_type, local_type),
            in_specs=[whole()] * 6 + [whole(pl.ANY)],
            out_specs=(whole(),) * 3,
            scratch_shapes=[raw_scratch, near_scratch] + parts_scratch,
            compiler_params=params,
            cost_estimate=cost(span * wins * length * length * 4, 4 * 1024 * 1024),
            name="tail",
        )(flat, table, keep, pick, white_a, short_a, after)

    def cross(now, white, short, after):
        return pl.pallas_call(
            functools.partial(cross_kernel, limits, now),
            out_shape=local_type,
            in_specs=[whole()] * 4 + [whole(pl.ANY)],
            out_specs=whole(),
            scratch_shapes=[near_scratch] + parts_scratch,
            compiler_params=params,
            cost_estimate=cost(pairs * span * wins * bins * 8, 4 * 1024 * 1024),
            name="cross",
        )(pick, white, short, edge, after)

    white_b, short_b, local_a = tail(0, table)
    local_b = cross(0, white_b, short_b, table)
    white_late, short_late, late_a = tail(1, local_b)
    late_b = cross(1, white_late, short_late, local_b)

    power = [float(np.float32(factor) ** np.float32(d)) for d in range(groups)]
    def sent(value, even, odd):
        moves = [
            (c * groups + here, c * groups + there)
            for c in range(ring)
            for here, there in (even if c % 2 else odd)
        ]
        return lax.ppermute(value, ("chan", "tm"), moves)

    def mix(terms, weights, after):
        return pl.pallas_call(
            functools.partial(mix_kernel, limits, weights),
            out_shape=local_type,
            in_specs=[whole()] * len(terms) + [whole(pl.ANY)],
            out_specs=whole(),
            compiler_params=params,
            cost_estimate=cost(len(terms) * terms[0].size * 4, 1024 * 1024),
            name="mix",
        )(*terms, after)

    inverse = pl.pallas_call(
        inverse_kernel,
        out_shape=jax.ShapeDtypeStruct((length, length), jnp.bfloat16),
        in_specs=[whole(pl.ANY)],
        out_specs=whole(),
        compiler_params=params,
        cost_estimate=cost(length * bins * 32, 512 * 1024),
        name="inverse",
    )(local_b)

    def written(kernel, terms, later, *so_far):
        return pl.pallas_call(
            kernel,
            out_shape=jax.ShapeDtypeStruct((pairs, chans, length), jnp.bfloat16),
            in_specs=[whole()] * (1 + len(terms)) + [whole(pl.ANY)] * (len(later) + len(so_far)),
            out_specs=whole(pl.ANY),
            scratch_shapes=[
                pltpu.VMEM((pairs, span, length), jnp.bfloat16),
                pltpu.SemaphoreType.DMA,
            ],
            input_output_aliases={1 + len(terms) + len(later): 0} if so_far else {},
            compiler_params=params,
            cost_estimate=cost(pairs * span * length * length * 4, 1024 * 1024),
            name="lags",
        )(inverse, *terms, *later, *so_far)

    def part(terms, weights):
        return pl.pallas_call(
            functools.partial(part_kernel, limits, weights),
            out_shape=jax.ShapeDtypeStruct((pairs * span, length), jnp.float32),
            in_specs=[whole()] * (1 + len(terms)),
            out_specs=whole(),
            compiler_params=params,
            cost_estimate=cost(pairs * span * length * length * 4, 1024 * 1024),
            name="part",
        )(inverse, *terms)

    unit = [1.0] * (2 * groups)

    def two_hops(local, late, after, apart):
        f, ff = power[1], power[2]
        last = [(2, 3)]
        got = sent(local, [(0, 2), (1, 3)], [(0, 1), (1, 0)] + ([] if apart else last))
        alone = [sent(local, [], last)] if apart else []
        total = mix(
            [local, late, got],
            [[1.0, 1.0, 1.0, 0.0, f, 1.0, 0.0, 0.0], [ff, ff, ff, 1.0, 1.0, f, 0.0, 0.0]],
            after,
        )
        more = sent(total, [(0, 1), (2, 3), (3, 2)], [(0, 2), (1, 3)])
        weights = [
            unit,
            [ff, ff, ff, ff, 0.0, f, 0.0, f],
        ]
        weights += [[f] * (2 * groups)] * len(alone) + [[f, f, f, f, 0.0, 0.0, f, ff]]
        return total, [got] + alone + [more], weights

    def one_hop(local, late, after, apart):
        terms, weights = [], [unit]
        for d in range(1, groups):
            moves = [(h, h + d) for h in range(groups - d)]
            terms.append(sent(local, moves, moves))
            weights.append([power[d]] * (2 * groups))
        return local, terms, weights

    spread = two_hops if square else one_hop
    scale = bins**-0.5
    _, terms_a, weights_a = spread(local_a, late_a, late_b, False)
    ahead, terms_b, weights_b = spread(local_b, late_b, local_b, True)
    white_last, short_last, last_a = tail(2, ahead)
    last_b = cross(2, white_last, short_last, ahead)
    terms_a = [local_a, late_a, last_a] + terms_a
    terms_b = [local_b, late_b, last_b] + terms_b
    before = part(terms_b[:-1], weights_b[:-1])
    first = functools.partial(lag_kernel, limits, scale, 0, weights_a)
    result = written(first, terms_a, [before])
    last = functools.partial(last_kernel, scale, half, weights_b[-1])
    result = written(last, [before, terms_b[-1]], [], result)
    return result.reshape(1, pairs, chans, length)


def solution(mesh):
    in_specs = (P("chan", "tm", None), P("chan", "tm"), P())
    out_specs = P("tm", None, "chan", None)
    return jax.shard_map(
        per_device, mesh=mesh, in_specs=in_specs, out_specs=out_specs, check_vma=False
    )
```

```python
import functools
import math

import jax
import jax.numpy as jnp
import numpy as np
from jax import lax
from jax.experimental import pallas as pl
from jax.experimental.pallas import tpu as pltpu
from jax.sharding import PartitionSpec as P

OFFSET_SPAN = 32
LANES = 128
DECAY = 0.99
VMEM = 24 * 1024 * 1024


def turns(number, length):
    part = (number - length * jnp.floor(number / length + 0.5)) * (1.0 / length)
    square = part * part
    cosine, sine = jnp.float32(0.0), jnp.float32(0.0)
    for k in range(10, -1, -1):
        cosine = cosine * square + (-1) ** k * (2 * math.pi) ** (2 * k) / math.factorial(2 * k)
        sine = sine * square + (-1) ** k * (2 * math.pi) ** (2 * k + 1) / math.factorial(2 * k + 1)
    return cosine, sine * part


def fill_table(table_ref, step):
    length = table_ref.shape[0]
    bins = length // 2

    def small(rows, by):
        row = lax.broadcasted_iota(jnp.int32, (rows, bins), 0)
        freq = lax.broadcasted_iota(jnp.int32, (rows, bins), 1) + 1
        return turns((row * (by * freq)).astype(jnp.float32), length)

    coarse_cos, coarse_sin = small(length // step, step)
    fine_cos, fine_sin = small(step, 1)
    for i in range(length // step):
        rows = slice(i * step, (i + 1) * step)
        cos_i, sin_i = coarse_cos[i : i + 1], coarse_sin[i : i + 1]
        cosine = (cos_i * fine_cos - sin_i * fine_sin).astype(jnp.bfloat16)
        sine = (sin_i * fine_cos + cos_i * fine_sin).astype(jnp.bfloat16)
        for t in range(bins // LANES):
            here = slice(t * LANES, (t + 1) * LANES)
            table_ref[rows, 2 * t * LANES : (2 * t + 1) * LANES] = cosine[:, here]
            table_ref[rows, (2 * t + 1) * LANES : (2 * t + 2) * LANES] = -sine[:, here]


def inverse_kernel(_, table_ref):
    length = table_ref.shape[0]
    bins = length // 2
    step = 16

    def small(rows, by, first):
        freq = (lax.broadcasted_iota(jnp.int32, (rows, length), 0) + first) * by
        lag = lax.broadcasted_iota(jnp.int32, (rows, length), 1)
        return turns((freq * lag).astype(jnp.float32), length)

    coarse_cos, coarse_sin = small(bins // step, step, 0)
    fine_cos, fine_sin = small(step, 1, 1)
    for i in range(bins // step):
        first = i * step
        cos_i, sin_i = coarse_cos[i : i + 1], coarse_sin[i : i + 1]
        cosine = cos_i * fine_cos - sin_i * fine_sin
        sine = sin_i * fine_cos + cos_i * fine_sin
        table_ref[first : first + step, :] = cosine.astype(jnp.bfloat16)
        table_ref[bins + first : bins + first + step, :] = (-sine).astype(jnp.bfloat16)


def whiten_block(x, table_ref, keep, raw_ref, white_ref, short_ref):
    wins, span, length = white_ref.shape
    bins = length // 2
    tiles = bins // LANES

    def strided(t, w):
        return raw_ref[t, pl.ds(w, span, stride=wins), :]

    total = [None] * wins
    for t in range(tiles):
        lanes = slice(2 * t * LANES, (2 * t + 2) * LANES)
        raw = jnp.dot(x, table_ref[:, lanes], preferred_element_type=jnp.float32)
        raw_ref[2 * t] = raw[:, :LANES]
        raw_ref[2 * t + 1] = raw[:, LANES:]
    for t in range(tiles):
        for w in range(wins):
            real_part, imag_part = strided(2 * t, w), strided(2 * t + 1, w)
            power = real_part * real_part + imag_part * imag_part
            total[w] = power if t == 0 else total[w] + power
    for w in range(wins):
        decay = float(np.float32(DECAY) ** np.float32(wins - 1 - w))
        level = jnp.sum(total[w], axis=-1, keepdims=True) * (0.01 / bins) + 1e-06
        alive = keep[:, w * LANES : (w + 1) * LANES]
        for t in range(tiles):
            part = [strided(2 * t, w), strided(2 * t + 1, w)]
            power = part[0] * part[0] + part[1] * part[1]
            scale = alive * lax.rsqrt(power + level)
            for i, s in enumerate((t, tiles + t)):
                value = part[i] * scale
                here = pl.ds(w * length + s * LANES, LANES)
                white_ref[w, :, s * LANES : (s + 1) * LANES] = value * decay
                short_ref[:, here] = value.astype(jnp.bfloat16)


def head_kernel(
    x_hbm,
    valid_hbm,
    offsets_hbm,
    white_ref,
    short_ref,
    table_ref,
    pick_ref,
    keep_ref,
    x_ref,
    valid_ref,
    offsets_ref,
    raw_ref,
    sems,
):
    wins, span, length = white_ref.shape
    pairs = offsets_ref.shape[0]
    copies = [
        pltpu.make_async_copy(valid_hbm, valid_ref, sems.at[0]),
        pltpu.make_async_copy(offsets_hbm, offsets_ref, sems.at[1]),
        pltpu.make_async_copy(x_hbm.at[pl.ds(0, span * wins)], x_ref, sems.at[2]),
    ]
    for copy in copies:
        copy.start()
    fill_table(table_ref, 16)
    copies[0].wait()
    copies[1].wait()
    ahead = lax.broadcasted_iota(jnp.int32, (span, 2 * span), 1) - lax.broadcasted_iota(
        jnp.int32, (span, 2 * span), 0
    )
    for k in range(pairs):
        chosen_row = jnp.where(ahead == offsets_ref[k], jnp.float32(1.0), jnp.float32(0.0))
        pick_ref[k] = chosen_row.astype(jnp.bfloat16)
    owner = lax.broadcasted_iota(jnp.int32, (wins, wins * LANES), 0)
    column = lax.broadcasted_iota(jnp.int32, (wins, wins * LANES), 1) // LANES
    keep_ref[...] = lax.dot_general(
        valid_ref[...].astype(jnp.float32).astype(jnp.bfloat16),
        (owner == column).astype(jnp.float32).astype(jnp.bfloat16),
        (((0,), (0,)), ((), ())),
        preferred_element_type=jnp.float32,
    )
    copies[2].wait()
    whiten_block(x_ref[...], table_ref, keep_ref[:span], raw_ref, white_ref, short_ref)


def stack_pairs(pick_ref, white_ref, near_ref, parts_refs, out_ref):
    wins, _, length = white_ref.shape
    pairs, rows, reach = pick_ref.shape
    bins = length // 2
    size = pairs // len(parts_refs)

    def select(group, w):
        pick = pick_ref[group * size : (group + 1) * size].reshape(size * rows, reach)
        near = near_ref[:, w * length : (w + 1) * length]
        parts_refs[group][w] = jnp.dot(pick, near, preferred_element_type=jnp.float32)

    blocks = [(c, t) for c in range(0, rows, 16) for t in range(bins // LANES)]
    for w in range(wins):
        select(0, w)
    for group, parts_ref in enumerate(parts_refs):
        ahead = list(range(wins)) if group + 1 < len(parts_refs) else []
        for i, (c, t) in enumerate(blocks):
            for w in ahead[i :: len(blocks)]:
                select(group + 1, w)
            re = slice(t * LANES, (t + 1) * LANES)
            im = slice(bins + t * LANES, bins + (t + 1) * LANES)
            head_re = [white_ref[w, c : c + 16, re] for w in range(wins)]
            head_im = [white_ref[w, c : c + 16, im] for w in range(wins)]
            for k in range(size):
                here = slice(k * rows + c, k * rows + c + 16)
                total_re = total_im = None
                for w in range(wins):
                    part_re, part_im = parts_ref[w, here, re], parts_ref[w, here, im]
                    cross_re = head_re[w] * part_re + head_im[w] * part_im
                    cross_im = head_im[w] * part_re - head_re[w] * part_im
                    total_re = cross_re if w == 0 else total_re + cross_re
                    total_im = cross_im if w == 0 else total_im + cross_im
                pair = group * size + k
                out_ref[pair, c : c + 16, re] = total_re.astype(out_ref.dtype)
                out_ref[pair, c : c + 16, im] = total_im.astype(out_ref.dtype)


def role(limits):
    odd = lax.rem(lax.axis_index("chan") + 1, 2)
    first = lax.axis_index("tm") < jnp.where(odd == 0, *limits)
    return jnp.where(first, 0, 1 + odd)


def tail_kernel(
    limits,
    now,
    x_ref,
    table_ref,
    keep_ref,
    pick_ref,
    head_ref,
    edge_ref,
    after_ref,
    white_ref,
    short_ref,
    out_ref,
    raw_ref,
    near_ref,
    *parts_refs,
):
    wins, span, length = white_ref.shape
    rows = slice(span * wins, 2 * span * wins)

    @pl.when(role(limits) == now)
    def _():
        x = x_ref[rows, :]
        whiten_block(x, table_ref, keep_ref[span:], raw_ref, white_ref, short_ref)
        near_ref[:span] = edge_ref[...]
        near_ref[span:] = short_ref[...]
        stack_pairs(pick_ref, head_ref, near_ref, parts_refs, out_ref)


def cross_kernel(
    limits, now, pick_ref, white_ref, short_ref, edge_ref, after_ref, out_ref, near_ref, *parts_refs
):
    span = short_ref.shape[0]

    @pl.when(role(limits) == now)
    def _():
        near_ref[:span] = short_ref[...]
        near_ref[span:] = edge_ref[...]
        stack_pairs(pick_ref, white_ref, near_ref, parts_refs, out_ref)


def chosen(options, place):
    value = jnp.float32(options[0])
    for i, option in enumerate(options[1:]):
        value = jnp.where(place == i + 1, jnp.float32(option), value)
    return value


def weighted(limits, terms, weights, place):
    total = None
    mine = role(limits)
    late = len(terms) - len(weights)
    first = terms[late][...]
    for i in range(late - 1, -1, -1):
        first = jnp.where(mine == i, terms[i][...], first)
    for term, options in zip([first] + list(terms[late + 1 :]), weights):
        value = term[...].astype(jnp.float32)
        if set(options) != {1.0}:
            value = value * (options[0] if len(set(options)) == 1 else chosen(options, place))
        total = value if total is None else total + value
    return total


def whereabouts(groups):
    return lax.rem(lax.axis_index("chan") + 1, 2) * groups + lax.axis_index("tm")


def mix_kernel(limits, weights, *refs):
    count = len(weights) + 1
    place = whereabouts(len(weights[0]) // 2)
    total = weighted(limits, refs[:count], weights, place)
    refs[-1][...] = total.astype(refs[-1].dtype)


def to_lags(stack, table):
    count = stack.shape[0]
    high = stack.astype(jnp.bfloat16)
    low = (stack - high.astype(jnp.float32)).astype(jnp.bfloat16)
    both = jnp.dot(jnp.concatenate([high, low]), table, preferred_element_type=jnp.float32)
    return both[:count] + both[count:]


def part_kernel(limits, weights, table_ref, *refs):
    place = whereabouts(len(weights[0]) // 2)
    out_ref = refs[-1]
    stack = weighted(limits, refs[: len(weights) + 2], weights, place).reshape(out_ref.shape)
    out_ref[...] = to_lags(stack, table_ref[...])


def lag_kernel(limits, scale, first, weights, table_ref, *rest):
    out_hbm, stage_ref, sem = rest[-3:]
    place = whereabouts(len(weights[0]) // 2)
    pairs, rows, length = stage_ref.shape
    stack = weighted(limits, rest[: len(weights) + 2], weights, place)
    stack = stack.reshape(pairs * rows, length)
    lagged = to_lags(stack, table_ref[...]) * scale
    stage_ref[...] = lagged.astype(stage_ref.dtype).reshape(pairs, rows, length)
    copy = pltpu.make_async_copy(stage_ref, out_hbm.at[:, pl.ds(first, rows)], sem)
    copy.start()
    copy.wait()


def last_kernel(scale, first, weights, table_ref, part_ref, more_ref, *rest):
    out_hbm, stage_ref, sem = rest[-3:]
    place = whereabouts(len(weights) // 2)
    pairs, rows, length = stage_ref.shape
    more = more_ref[...].reshape(pairs * rows, length)
    lagged = jnp.dot(more, table_ref[...], preferred_element_type=jnp.float32)
    lagged = (part_ref[...] + lagged * chosen(weights, place)) * scale
    stage_ref[...] = lagged.astype(stage_ref.dtype).reshape(pairs, rows, length)
    copy = pltpu.make_async_copy(stage_ref, out_hbm.at[:, pl.ds(first, rows)], sem)
    copy.start()
    copy.wait()


def cost(flops, moved):
    return pl.CostEstimate(flops=flops, bytes_accessed=moved, transcendentals=0)


def whole(memory=pltpu.VMEM):
    return pl.BlockSpec(memory_space=memory)


def per_device(samples, valid, offsets):
    chans, wins, length = samples.shape
    bins = length // 2
    span = OFFSET_SPAN
    pairs = offsets.shape[0]
    tiles = bins // LANES
    groups = lax.axis_size("tm")
    factor = float(np.float32(DECAY) ** np.float32(wins))
    params = pltpu.CompilerParams(vmem_limit_bytes=VMEM)

    def in_hbm(value):
        return pltpu.with_memory_space_constraint(value, pltpu.HBM)

    half = chans - span
    flat = samples.reshape(chans * wins, length)
    white_type = jax.ShapeDtypeStruct((wins, span, length), jnp.float32)
    short_type = jax.ShapeDtypeStruct((span, wins * length), jnp.bfloat16)
    local_type = jax.ShapeDtypeStruct((pairs, span, length), jnp.bfloat16)
    raw_scratch = pltpu.VMEM((2 * tiles, span * wins, LANES), jnp.float32)
    near_scratch = pltpu.VMEM((2 * span, wins * length), jnp.bfloat16)
    parts_scratch = [pltpu.VMEM((wins, pairs // 4 * span, length), jnp.float32)] * 4

    white_a, short_a, table, pick, keep = pl.pallas_call(
        head_kernel,
        out_shape=(
            white_type,
            short_type,
            jax.ShapeDtypeStruct((length, length), jnp.bfloat16),
            jax.ShapeDtypeStruct((pairs, span, 2 * span), jnp.bfloat16),
            jax.ShapeDtypeStruct((chans, wins * LANES), jnp.float32),
        ),
        in_specs=[whole(pltpu.HBM)] * 3,
        out_specs=(whole(),) * 5,
        scratch_shapes=[
            pltpu.VMEM((span * wins, length), jnp.bfloat16),
            pltpu.VMEM((wins, chans), jnp.int32),
            pltpu.SMEM((pairs,), jnp.int32),
            raw_scratch,
            pltpu.SemaphoreType.DMA((3,)),
        ],
        compiler_params=params,
        cost_estimate=cost(span * wins * length * length * 2, 2 * 1024 * 1024),
        name="head",
    )(in_hbm(flat), in_hbm(valid.T), in_hbm(offsets))

    ring = lax.axis_size("chan")

    def to_previous(odd, even):
        moves = [
            (c * groups + h, (c - 1) * groups + h)
            for c in range(1, ring)
            for h in (odd if c % 2 else even)
        ]
        return lax.ppermute(short_a, ("chan", "tm"), moves)


    columns = min(d for d in range(1, groups + 1) if groups % d == 0 and d * d >= groups)
    square = columns == 2 and groups == columns * columns
    limits = (2, 3) if square else (groups, groups)

    ahead = 2 if square else groups
    edge = to_previous(range(groups), range(ahead))
    edge_late = to_previous([], range(ahead, groups)) if square else edge

    def tail(now, after):
        return pl.pallas_call(
            functools.partial(tail_kernel, limits, now),
            out_shape=(white_type, short_type, local_type),
            in_specs=[whole()] * 6 + [whole(pl.ANY)],
            out_specs=(whole(),) * 3,
            scratch_shapes=[raw_scratch, near_scratch] + parts_scratch,
            compiler_params=params,
            cost_estimate=cost(span * wins * length * length * 4, 4 * 1024 * 1024),
            name="tail",
        )(flat, table, keep, pick, white_a, short_a, after)

    def cross(now, white, short, edge, after):
        return pl.pallas_call(
            functools.partial(cross_kernel, limits, now),
            out_shape=local_type,
            in_specs=[whole()] * 4 + [whole(pl.ANY)],
            out_specs=whole(),
            scratch_shapes=[near_scratch] + parts_scratch,
            compiler_params=params,
            cost_estimate=cost(pairs * span * wins * bins * 8, 4 * 1024 * 1024),
            name="cross",
        )(pick, white, short, edge, after)

    white_b, short_b, local_a = tail(0, table)
    white_late, short_late, late_a = tail(1, local_a)
    local_b = cross(0, white_b, short_b, edge, late_a)
    late_b = cross(1, white_late, short_late, edge_late, local_b)

    power = [float(np.float32(factor) ** np.float32(d)) for d in range(groups)]
    def sent(value, even, odd):
        moves = [
            (c * groups + here, c * groups + there)
            for c in range(ring)
            for here, there in (even if c % 2 else odd)
        ]
        return lax.ppermute(value, ("chan", "tm"), moves)

    def mix(terms, weights, after):
        return pl.pallas_call(
            functools.partial(mix_kernel, limits, weights),
            out_shape=local_type,
            in_specs=[whole()] * len(terms) + [whole(pl.ANY)],
            out_specs=whole(),
            compiler_params=params,
            cost_estimate=cost(len(terms) * terms[0].size * 4, 1024 * 1024),
            name="mix",
        )(*terms, after)

    inverse = pl.pallas_call(
        inverse_kernel,
        out_shape=jax.ShapeDtypeStruct((length, length), jnp.bfloat16),
        in_specs=[whole(pl.ANY)],
        out_specs=whole(),
        compiler_params=params,
        cost_estimate=cost(length * bins * 32, 512 * 1024),
        name="inverse",
    )(local_b)

    def written(kernel, terms, later, *so_far):
        return pl.pallas_call(
            kernel,
            out_shape=jax.ShapeDtypeStruct((pairs, chans, length), jnp.bfloat16),
            in_specs=[whole()] * (1 + len(terms)) + [whole(pl.ANY)] * (len(later) + len(so_far)),
            out_specs=whole(pl.ANY),
            scratch_shapes=[
                pltpu.VMEM((pairs, span, length), jnp.bfloat16),
                pltpu.SemaphoreType.DMA,
            ],
            input_output_aliases={1 + len(terms) + len(later): 0} if so_far else {},
            compiler_params=params,
            cost_estimate=cost(pairs * span * length * length * 4, 1024 * 1024),
            name="lags",
        )(inverse, *terms, *later, *so_far)

    def part(terms, weights):
        return pl.pallas_call(
            functools.partial(part_kernel, limits, weights),
            out_shape=jax.ShapeDtypeStruct((pairs * span, length), jnp.float32),
            in_specs=[whole()] * (1 + len(terms)),
            out_specs=whole(),
            compiler_params=params,
            cost_estimate=cost(pairs * span * length * length * 4, 1024 * 1024),
            name="part",
        )(inverse, *terms)

    unit = [1.0] * (2 * groups)

    def two_hops(local, late, after, apart):
        f, ff = power[1], power[2]
        last = [(2, 3)]
        got = sent(local, [(0, 2), (1, 3)], [(0, 1), (1, 0)] + ([] if apart else last))
        alone = [sent(local, [], last)] if apart else []
        total = mix(
            [local, late, got],
            [[1.0, 1.0, 1.0, 0.0, f, 1.0, 0.0, 0.0], [ff, ff, ff, 1.0, 1.0, f, 0.0, 0.0]],
            after,
        )
        more = sent(total, [(0, 1), (2, 3), (3, 2)], [(0, 2), (1, 3)])
        weights = [
            unit,
            [ff, ff, ff, ff, 0.0, f, 0.0, f],
        ]
        weights += [[f] * (2 * groups)] * len(alone) + [[f, f, f, f, 0.0, 0.0, f, ff]]
        return total, [got] + alone + [more], weights

    def one_hop(local, late, after, apart):
        terms, weights = [], [unit]
        for d in range(1, groups):
            moves = [(h, h + d) for h in range(groups - d)]
            terms.append(sent(local, moves, moves))
            weights.append([power[d]] * (2 * groups))
        return local, terms, weights

    spread = two_hops if square else one_hop
    scale = bins**-0.5
    _, terms_a, weights_a = spread(local_a, late_a, local_b, False)
    ahead, terms_b, weights_b = spread(local_b, late_b, local_b, True)
    white_last, short_last, last_a = tail(2, ahead)
    last_b = cross(2, white_last, short_last, edge, ahead)
    terms_a = [local_a, late_a, last_a] + terms_a
    terms_b = [local_b, late_b, last_b] + terms_b
    before = part(terms_b[:-1], weights_b[:-1])
    first = functools.partial(lag_kernel, limits, scale, 0, weights_a)
    result = written(first, terms_a, [before])
    last = functools.partial(last_kernel, scale, half, weights_b[-1])
    result = written(last, [before, terms_b[-1]], [], result)
    return result.reshape(1, pairs, chans, length)


def solution(mesh):
    in_specs = (P("chan", "tm", None), P("chan", "tm"), P())
    out_specs = P("tm", None, "chan", None)
    return jax.shard_map(
        per_device, mesh=mesh, in_specs=in_specs, out_specs=out_specs, check_vma=False
    )
```

```python
import functools
import math

import jax
import jax.numpy as jnp
import numpy as np
from jax import lax
from jax.experimental import pallas as pl
from jax.experimental.pallas import tpu as pltpu
from jax.sharding import PartitionSpec as P

OFFSET_SPAN = 32
LANES = 128
DECAY = 0.99
VMEM = 24 * 1024 * 1024


def turns(number, length):
    part = (number - length * jnp.floor(number / length + 0.5)) * (1.0 / length)
    square = part * part
    cosine, sine = jnp.float32(0.0), jnp.float32(0.0)
    for k in range(10, -1, -1):
        cosine = cosine * square + (-1) ** k * (2 * math.pi) ** (2 * k) / math.factorial(2 * k)
        sine = sine * square + (-1) ** k * (2 * math.pi) ** (2 * k + 1) / math.factorial(2 * k + 1)
    return cosine, sine * part


def fill_table(table_ref, step):
    length = table_ref.shape[0]
    bins = length // 2

    def small(rows, by):
        row = lax.broadcasted_iota(jnp.int32, (rows, bins), 0)
        freq = lax.broadcasted_iota(jnp.int32, (rows, bins), 1) + 1
        return turns((row * (by * freq)).astype(jnp.float32), length)

    coarse_cos, coarse_sin = small(length // step, step)
    fine_cos, fine_sin = small(step, 1)
    for i in range(length // step):
        rows = slice(i * step, (i + 1) * step)
        cos_i, sin_i = coarse_cos[i : i + 1], coarse_sin[i : i + 1]
        cosine = (cos_i * fine_cos - sin_i * fine_sin).astype(jnp.bfloat16)
        sine = (sin_i * fine_cos + cos_i * fine_sin).astype(jnp.bfloat16)
        for t in range(bins // LANES):
            here = slice(t * LANES, (t + 1) * LANES)
            table_ref[rows, 2 * t * LANES : (2 * t + 1) * LANES] = cosine[:, here]
            table_ref[rows, (2 * t + 1) * LANES : (2 * t + 2) * LANES] = -sine[:, here]


def inverse_kernel(_, table_ref):
    length = table_ref.shape[0]
    bins = length // 2
    step = 16

    def small(rows, by, first):
        freq = (lax.broadcasted_iota(jnp.int32, (rows, length), 0) + first) * by
        lag = lax.broadcasted_iota(jnp.int32, (rows, length), 1)
        return turns((freq * lag).astype(jnp.float32), length)

    coarse_cos, coarse_sin = small(bins // step, step, 0)
    fine_cos, fine_sin = small(step, 1, 1)
    for i in range(bins // step):
        first = i * step
        cos_i, sin_i = coarse_cos[i : i + 1], coarse_sin[i : i + 1]
        cosine = cos_i * fine_cos - sin_i * fine_sin
        sine = sin_i * fine_cos + cos_i * fine_sin
        table_ref[first : first + step, :] = cosine.astype(jnp.bfloat16)
        table_ref[bins + first : bins + first + step, :] = (-sine).astype(jnp.bfloat16)


def whiten_block(x, table_ref, keep, raw_ref, white_ref, short_ref):
    wins, span, length = white_ref.shape
    bins = length // 2
    tiles = bins // LANES

    def strided(t, w):
        return raw_ref[t, pl.ds(w, span, stride=wins), :]

    total = [None] * wins
    for t in range(tiles):
        lanes = slice(2 * t * LANES, (2 * t + 2) * LANES)
        raw = jnp.dot(x, table_ref[:, lanes], preferred_element_type=jnp.float32)
        raw_ref[2 * t] = raw[:, :LANES]
        raw_ref[2 * t + 1] = raw[:, LANES:]
    for t in range(tiles):
        for w in range(wins):
            real_part, imag_part = strided(2 * t, w), strided(2 * t + 1, w)
            power = real_part * real_part + imag_part * imag_part
            total[w] = power if t == 0 else total[w] + power
    for w in range(wins):
        decay = float(np.float32(DECAY) ** np.float32(wins - 1 - w))
        level = jnp.sum(total[w], axis=-1, keepdims=True) * (0.01 / bins) + 1e-06
        alive = keep[:, w * LANES : (w + 1) * LANES]
        for t in range(tiles):
            part = [strided(2 * t, w), strided(2 * t + 1, w)]
            power = part[0] * part[0] + part[1] * part[1]
            scale = alive * lax.rsqrt(power + level)
            for i, s in enumerate((t, tiles + t)):
                value = part[i] * scale
                here = pl.ds(w * length + s * LANES, LANES)
                white_ref[w, :, s * LANES : (s + 1) * LANES] = value * decay
                short_ref[:, here] = value.astype(jnp.bfloat16)


def head_kernel(
    x_hbm,
    valid_hbm,
    offsets_hbm,
    white_ref,
    short_ref,
    table_ref,
    pick_ref,
    keep_ref,
    x_ref,
    valid_ref,
    offsets_ref,
    raw_ref,
    sems,
):
    wins, span, length = white_ref.shape
    pairs = offsets_ref.shape[0]
    copies = [
        pltpu.make_async_copy(valid_hbm, valid_ref, sems.at[0]),
        pltpu.make_async_copy(offsets_hbm, offsets_ref, sems.at[1]),
        pltpu.make_async_copy(x_hbm.at[pl.ds(0, span * wins)], x_ref, sems.at[2]),
    ]
    for copy in copies:
        copy.start()
    fill_table(table_ref, 16)
    copies[0].wait()
    copies[1].wait()
    ahead = lax.broadcasted_iota(jnp.int32, (span, 2 * span), 1) - lax.broadcasted_iota(
        jnp.int32, (span, 2 * span), 0
    )
    for k in range(pairs):
        chosen_row = jnp.where(ahead == offsets_ref[k], jnp.float32(1.0), jnp.float32(0.0))
        pick_ref[k] = chosen_row.astype(jnp.bfloat16)
    owner = lax.broadcasted_iota(jnp.int32, (wins, wins * LANES), 0)
    column = lax.broadcasted_iota(jnp.int32, (wins, wins * LANES), 1) // LANES
    keep_ref[...] = lax.dot_general(
        valid_ref[...].astype(jnp.float32).astype(jnp.bfloat16),
        (owner == column).astype(jnp.float32).astype(jnp.bfloat16),
        (((0,), (0,)), ((), ())),
        preferred_element_type=jnp.float32,
    )
    copies[2].wait()
    whiten_block(x_ref[...], table_ref, keep_ref[:span], raw_ref, white_ref, short_ref)


def stack_pairs(pick_ref, white_ref, near_ref, parts_refs, out_ref):
    wins, _, length = white_ref.shape
    pairs, rows, reach = pick_ref.shape
    bins = length // 2
    size = pairs // len(parts_refs)

    def select(group, w):
        pick = pick_ref[group * size : (group + 1) * size].reshape(size * rows, reach)
        near = near_ref[:, w * length : (w + 1) * length]
        parts_refs[group][w] = jnp.dot(pick, near, preferred_element_type=jnp.float32)

    blocks = [(c, t) for c in range(0, rows, 16) for t in range(bins // LANES)]
    for w in range(wins):
        select(0, w)
    for group, parts_ref in enumerate(parts_refs):
        ahead = list(range(wins)) if group + 1 < len(parts_refs) else []
        for i, (c, t) in enumerate(blocks):
            for w in ahead[i :: len(blocks)]:
                select(group + 1, w)
            re = slice(t * LANES, (t + 1) * LANES)
            im = slice(bins + t * LANES, bins + (t + 1) * LANES)
            head_re = [white_ref[w, c : c + 16, re] for w in range(wins)]
            head_im = [white_ref[w, c : c + 16, im] for w in range(wins)]
            for k in range(size):
                here = slice(k * rows + c, k * rows + c + 16)
                total_re = total_im = None
                for w in range(wins):
                    part_re, part_im = parts_ref[w, here, re], parts_ref[w, here, im]
                    cross_re = head_re[w] * part_re + head_im[w] * part_im
                    cross_im = head_im[w] * part_re - head_re[w] * part_im
                    total_re = cross_re if w == 0 else total_re + cross_re
                    total_im = cross_im if w == 0 else total_im + cross_im
                pair = group * size + k
                out_ref[pair, c : c + 16, re] = total_re.astype(out_ref.dtype)
                out_ref[pair, c : c + 16, im] = total_im.astype(out_ref.dtype)


def role(limits):
    odd = lax.rem(lax.axis_index("chan") + 1, 2)
    first = lax.axis_index("tm") < jnp.where(odd == 0, *limits)
    return jnp.where(first, 0, 1 + odd)


def tail_kernel(
    limits,
    now,
    x_ref,
    table_ref,
    keep_ref,
    pick_ref,
    head_ref,
    edge_ref,
    after_ref,
    white_ref,
    short_ref,
    out_ref,
    again_ref,
    raw_ref,
    near_ref,
    *parts_refs,
):
    wins, span, length = white_ref.shape
    rows = slice(span * wins, 2 * span * wins)

    if now == 0:
        again_ref[...] = edge_ref[...]

    @pl.when(role(limits) == now)
    def _():
        x = x_ref[rows, :]
        whiten_block(x, table_ref, keep_ref[span:], raw_ref, white_ref, short_ref)
        near_ref[:span] = edge_ref[...]
        near_ref[span:] = short_ref[...]
        stack_pairs(pick_ref, head_ref, near_ref, parts_refs, out_ref)


def cross_kernel(
    limits, now, pick_ref, white_ref, short_ref, edge_ref, after_ref, out_ref, near_ref, *parts_refs
):
    span = short_ref.shape[0]

    @pl.when(role(limits) == now)
    def _():
        near_ref[:span] = short_ref[...]
        near_ref[span:] = edge_ref[...]
        stack_pairs(pick_ref, white_ref, near_ref, parts_refs, out_ref)


def chosen(options, place):
    value = jnp.float32(options[0])
    for i, option in enumerate(options[1:]):
        value = jnp.where(place == i + 1, jnp.float32(option), value)
    return value


def weighted(limits, terms, weights, place):
    total = None
    mine = role(limits)
    late = len(terms) - len(weights)
    first = terms[late][...]
    for i in range(late - 1, -1, -1):
        first = jnp.where(mine == i, terms[i][...], first)
    for term, options in zip([first] + list(terms[late + 1 :]), weights):
        value = term[...].astype(jnp.float32)
        if set(options) != {1.0}:
            value = value * (options[0] if len(set(options)) == 1 else chosen(options, place))
        total = value if total is None else total + value
    return total


def whereabouts(groups):
    return lax.rem(lax.axis_index("chan") + 1, 2) * groups + lax.axis_index("tm")


def mix_kernel(limits, weights, *refs):
    count = len(weights) + 1
    place = whereabouts(len(weights[0]) // 2)
    total = weighted(limits, refs[:count], weights, place)
    refs[-1][...] = total.astype(refs[-1].dtype)


def to_lags(stack, table):
    count = stack.shape[0]
    high = stack.astype(jnp.bfloat16)
    low = (stack - high.astype(jnp.float32)).astype(jnp.bfloat16)
    both = jnp.dot(jnp.concatenate([high, low]), table, preferred_element_type=jnp.float32)
    return both[:count] + both[count:]


def part_kernel(limits, weights, table_ref, *refs):
    place = whereabouts(len(weights[0]) // 2)
    out_ref = refs[-1]
    stack = weighted(limits, refs[: len(weights) + 2], weights, place).reshape(out_ref.shape)
    out_ref[...] = to_lags(stack, table_ref[...])


def lag_kernel(limits, scale, first, weights, table_ref, *rest):
    out_hbm, stage_ref, sem = rest[-3:]
    place = whereabouts(len(weights[0]) // 2)
    pairs, rows, length = stage_ref.shape
    stack = weighted(limits, rest[: len(weights) + 2], weights, place)
    stack = stack.reshape(pairs * rows, length)
    lagged = to_lags(stack, table_ref[...]) * scale
    stage_ref[...] = lagged.astype(stage_ref.dtype).reshape(pairs, rows, length)
    copy = pltpu.make_async_copy(stage_ref, out_hbm.at[:, pl.ds(first, rows)], sem)
    copy.start()
    copy.wait()


def last_kernel(scale, first, weights, table_ref, part_ref, more_ref, *rest):
    out_hbm, stage_ref, sem = rest[-3:]
    place = whereabouts(len(weights) // 2)
    pairs, rows, length = stage_ref.shape
    more = more_ref[...].reshape(pairs * rows, length)
    lagged = jnp.dot(more, table_ref[...], preferred_element_type=jnp.float32)
    lagged = (part_ref[...] + lagged * chosen(weights, place)) * scale
    stage_ref[...] = lagged.astype(stage_ref.dtype).reshape(pairs, rows, length)
    copy = pltpu.make_async_copy(stage_ref, out_hbm.at[:, pl.ds(first, rows)], sem)
    copy.start()
    copy.wait()


def cost(flops, moved):
    return pl.CostEstimate(flops=flops, bytes_accessed=moved, transcendentals=0)


def whole(memory=pltpu.VMEM):
    return pl.BlockSpec(memory_space=memory)


def per_device(samples, valid, offsets):
    chans, wins, length = samples.shape
    bins = length // 2
    span = OFFSET_SPAN
    pairs = offsets.shape[0]
    tiles = bins // LANES
    groups = lax.axis_size("tm")
    factor = float(np.float32(DECAY) ** np.float32(wins))
    params = pltpu.CompilerParams(vmem_limit_bytes=VMEM)

    def in_hbm(value):
        return pltpu.with_memory_space_constraint(value, pltpu.HBM)

    half = chans - span
    flat = samples.reshape(chans * wins, length)
    white_type = jax.ShapeDtypeStruct((wins, span, length), jnp.float32)
    short_type = jax.ShapeDtypeStruct((span, wins * length), jnp.bfloat16)
    local_type = jax.ShapeDtypeStruct((pairs, span, length), jnp.bfloat16)
    raw_scratch = pltpu.VMEM((2 * tiles, span * wins, LANES), jnp.float32)
    near_scratch = pltpu.VMEM((2 * span, wins * length), jnp.bfloat16)
    parts_scratch = [pltpu.VMEM((wins, pairs // 4 * span, length), jnp.float32)] * 4

    white_a, short_a, table, pick, keep = pl.pallas_call(
        head_kernel,
        out_shape=(
            white_type,
            short_type,
            jax.ShapeDtypeStruct((length, length), jnp.bfloat16),
            jax.ShapeDtypeStruct((pairs, span, 2 * span), jnp.bfloat16),
            jax.ShapeDtypeStruct((chans, wins * LANES), jnp.float32),
        ),
        in_specs=[whole(pltpu.HBM)] * 3,
        out_specs=(whole(),) * 5,
        scratch_shapes=[
            pltpu.VMEM((span * wins, length), jnp.bfloat16),
            pltpu.VMEM((wins, chans), jnp.int32),
            pltpu.SMEM((pairs,), jnp.int32),
            raw_scratch,
            pltpu.SemaphoreType.DMA((3,)),
        ],
        compiler_params=params,
        cost_estimate=cost(span * wins * length * length * 2, 2 * 1024 * 1024),
        name="head",
    )(in_hbm(flat), in_hbm(valid.T), in_hbm(offsets))

    ring = lax.axis_size("chan")

    def to_previous(value, odd, even):
        moves = [
            (c * groups + h, (c - 1) * groups + h)
            for c in range(1, ring)
            for h in (odd if c % 2 else even)
        ]
        return lax.ppermute(value, ("chan", "tm"), moves)


    columns = min(d for d in range(1, groups + 1) if groups % d == 0 and d * d >= groups)
    square = columns == 2 and groups == columns * columns
    limits = (2, 3) if square else (groups, groups)

    ahead = 2 if square else groups
    edge = to_previous(short_a, range(groups), range(ahead))

    def tail(now, after):
        return pl.pallas_call(
            functools.partial(tail_kernel, limits, now),
            out_shape=(white_type, short_type, local_type, short_type),
            in_specs=[whole()] * 6 + [whole(pl.ANY)],
            out_specs=(whole(),) * 4,
            scratch_shapes=[raw_scratch, near_scratch] + parts_scratch,
            compiler_params=params,
            cost_estimate=cost(span * wins * length * length * 4, 4 * 1024 * 1024),
            name="tail",
        )(flat, table, keep, pick, white_a, short_a, after)

    def cross(now, white, short, edge, after):
        return pl.pallas_call(
            functools.partial(cross_kernel, limits, now),
            out_shape=local_type,
            in_specs=[whole()] * 4 + [whole(pl.ANY)],
            out_specs=whole(),
            scratch_shapes=[near_scratch] + parts_scratch,
            compiler_params=params,
            cost_estimate=cost(pairs * span * wins * bins * 8, 4 * 1024 * 1024),
            name="cross",
        )(pick, white, short, edge, after)

    white_b, short_b, local_a, again = tail(0, table)
    edge_late = to_previous(again, [], range(ahead, groups)) if square else edge
    white_late, short_late, late_a, _ = tail(1, local_a)
    local_b = cross(0, white_b, short_b, edge, late_a)
    late_b = cross(1, white_late, short_late, edge_late, local_b)

    power = [float(np.float32(factor) ** np.float32(d)) for d in range(groups)]
    def sent(value, even, odd):
        moves = [
            (c * groups + here, c * groups + there)
            for c in range(ring)
            for here, there in (even if c % 2 else odd)
        ]
        return lax.ppermute(value, ("chan", "tm"), moves)

    def mix(terms, weights, after):
        return pl.pallas_call(
            functools.partial(mix_kernel, limits, weights),
            out_shape=local_type,
            in_specs=[whole()] * len(terms) + [whole(pl.ANY)],
            out_specs=whole(),
            compiler_params=params,
            cost_estimate=cost(len(terms) * terms[0].size * 4, 1024 * 1024),
            name="mix",
        )(*terms, after)

    inverse = pl.pallas_call(
        inverse_kernel,
        out_shape=jax.ShapeDtypeStruct((length, length), jnp.bfloat16),
        in_specs=[whole(pl.ANY)],
        out_specs=whole(),
        compiler_params=params,
        cost_estimate=cost(length * bins * 32, 512 * 1024),
        name="inverse",
    )(local_b)

    def written(kernel, terms, later, *so_far):
        return pl.pallas_call(
            kernel,
            out_shape=jax.ShapeDtypeStruct((pairs, chans, length), jnp.bfloat16),
            in_specs=[whole()] * (1 + len(terms)) + [whole(pl.ANY)] * (len(later) + len(so_far)),
            out_specs=whole(pl.ANY),
            scratch_shapes=[
                pltpu.VMEM((pairs, span, length), jnp.bfloat16),
                pltpu.SemaphoreType.DMA,
            ],
            input_output_aliases={1 + len(terms) + len(later): 0} if so_far else {},
            compiler_params=params,
            cost_estimate=cost(pairs * span * length * length * 4, 1024 * 1024),
            name="lags",
        )(inverse, *terms, *later, *so_far)

    def part(terms, weights):
        return pl.pallas_call(
            functools.partial(part_kernel, limits, weights),
            out_shape=jax.ShapeDtypeStruct((pairs * span, length), jnp.float32),
            in_specs=[whole()] * (1 + len(terms)),
            out_specs=whole(),
            compiler_params=params,
            cost_estimate=cost(pairs * span * length * length * 4, 1024 * 1024),
            name="part",
        )(inverse, *terms)

    unit = [1.0] * (2 * groups)

    def two_hops(local, late, after, apart):
        f, ff = power[1], power[2]
        last = [(2, 3)]
        got = sent(local, [(0, 2), (1, 3)], [(0, 1), (1, 0)] + ([] if apart else last))
        alone = [sent(local, [], last)] if apart else []
        total = mix(
            [local, late, got],
            [[1.0, 1.0, 1.0, 0.0, f, 1.0, 0.0, 0.0], [ff, ff, ff, 1.0, 1.0, f, 0.0, 0.0]],
            after,
        )
        more = sent(total, [(0, 1), (2, 3), (3, 2)], [(0, 2), (1, 3)])
        weights = [
            unit,
            [ff, ff, ff, ff, 0.0, f, 0.0, f],
        ]
        weights += [[f] * (2 * groups)] * len(alone) + [[f, f, f, f, 0.0, 0.0, f, ff]]
        return total, [got] + alone + [more], weights

    def one_hop(local, late, after, apart):
        terms, weights = [], [unit]
        for d in range(1, groups):
            moves = [(h, h + d) for h in range(groups - d)]
            terms.append(sent(local, moves, moves))
            weights.append([power[d]] * (2 * groups))
        return local, terms, weights

    spread = two_hops if square else one_hop
    scale = bins**-0.5
    _, terms_a, weights_a = spread(local_a, late_a, local_b, False)
    ahead, terms_b, weights_b = spread(local_b, late_b, local_b, True)
    white_last, short_last, last_a, _ = tail(2, ahead)
    last_b = cross(2, white_last, short_last, edge, ahead)
    terms_a = [local_a, late_a, last_a] + terms_a
    terms_b = [local_b, late_b, last_b] + terms_b
    before = part(terms_b[:-1], weights_b[:-1])
    first = functools.partial(lag_kernel, limits, scale, 0, weights_a)
    result = written(first, terms_a, [before])
    last = functools.partial(last_kernel, scale, half, weights_b[-1])
    result = written(last, [before, terms_b[-1]], [], result)
    return result.reshape(1, pairs, chans, length)


def solution(mesh):
    in_specs = (P("chan", "tm", None), P("chan", "tm"), P())
    out_specs = P("tm", None, "chan", None)
    return jax.shard_map(
        per_device, mesh=mesh, in_specs=in_specs, out_specs=out_specs, check_vma=False
    )
```

```python
import functools
import math

import jax
import jax.numpy as jnp
import numpy as np
from jax import lax
from jax.experimental import pallas as pl
from jax.experimental.pallas import tpu as pltpu
from jax.sharding import PartitionSpec as P

OFFSET_SPAN = 32
LANES = 128
DECAY = 0.99
VMEM = 24 * 1024 * 1024


def turns(number, length):
    part = (number - length * jnp.floor(number / length + 0.5)) * (1.0 / length)
    square = part * part
    cosine, sine = jnp.float32(0.0), jnp.float32(0.0)
    for k in range(10, -1, -1):
        cosine = cosine * square + (-1) ** k * (2 * math.pi) ** (2 * k) / math.factorial(2 * k)
        sine = sine * square + (-1) ** k * (2 * math.pi) ** (2 * k + 1) / math.factorial(2 * k + 1)
    return cosine, sine * part


def fill_table(table_ref, step):
    length = table_ref.shape[0]
    bins = length // 2

    def small(rows, by):
        row = lax.broadcasted_iota(jnp.int32, (rows, bins), 0)
        freq = lax.broadcasted_iota(jnp.int32, (rows, bins), 1) + 1
        return turns((row * (by * freq)).astype(jnp.float32), length)

    coarse_cos, coarse_sin = small(length // step, step)
    fine_cos, fine_sin = small(step, 1)
    for i in range(length // step):
        rows = slice(i * step, (i + 1) * step)
        cos_i, sin_i = coarse_cos[i : i + 1], coarse_sin[i : i + 1]
        cosine = (cos_i * fine_cos - sin_i * fine_sin).astype(jnp.bfloat16)
        sine = (sin_i * fine_cos + cos_i * fine_sin).astype(jnp.bfloat16)
        for t in range(bins // LANES):
            here = slice(t * LANES, (t + 1) * LANES)
            table_ref[rows, 2 * t * LANES : (2 * t + 1) * LANES] = cosine[:, here]
            table_ref[rows, (2 * t + 1) * LANES : (2 * t + 2) * LANES] = -sine[:, here]


def inverse_kernel(_, table_ref):
    length = table_ref.shape[0]
    bins = length // 2
    step = 16

    def small(rows, by, first):
        freq = (lax.broadcasted_iota(jnp.int32, (rows, length), 0) + first) * by
        lag = lax.broadcasted_iota(jnp.int32, (rows, length), 1)
        return turns((freq * lag).astype(jnp.float32), length)

    coarse_cos, coarse_sin = small(bins // step, step, 0)
    fine_cos, fine_sin = small(step, 1, 1)
    for i in range(bins // step):
        first = i * step
        cos_i, sin_i = coarse_cos[i : i + 1], coarse_sin[i : i + 1]
        cosine = cos_i * fine_cos - sin_i * fine_sin
        sine = sin_i * fine_cos + cos_i * fine_sin
        table_ref[first : first + step, :] = cosine.astype(jnp.bfloat16)
        table_ref[bins + first : bins + first + step, :] = (-sine).astype(jnp.bfloat16)


def whiten_block(x, table_ref, keep, raw_ref, white_ref, short_ref):
    wins, span, length = white_ref.shape
    bins = length // 2
    tiles = bins // LANES

    def strided(t, w):
        return raw_ref[t, pl.ds(w, span, stride=wins), :]

    total = [None] * wins
    for t in range(tiles):
        lanes = slice(2 * t * LANES, (2 * t + 2) * LANES)
        raw = jnp.dot(x, table_ref[:, lanes], preferred_element_type=jnp.float32)
        raw_ref[2 * t] = raw[:, :LANES]
        raw_ref[2 * t + 1] = raw[:, LANES:]
    for t in range(tiles):
        for w in range(wins):
            real_part, imag_part = strided(2 * t, w), strided(2 * t + 1, w)
            power = real_part * real_part + imag_part * imag_part
            total[w] = power if t == 0 else total[w] + power
    for w in range(wins):
        decay = float(np.float32(DECAY) ** np.float32(wins - 1 - w))
        level = jnp.sum(total[w], axis=-1, keepdims=True) * (0.01 / bins) + 1e-06
        alive = keep[:, w * LANES : (w + 1) * LANES]
        for t in range(tiles):
            part = [strided(2 * t, w), strided(2 * t + 1, w)]
            power = part[0] * part[0] + part[1] * part[1]
            scale = alive * lax.rsqrt(power + level)
            for i, s in enumerate((t, tiles + t)):
                value = part[i] * scale
                here = pl.ds(w * length + s * LANES, LANES)
                white_ref[w, :, s * LANES : (s + 1) * LANES] = value * decay
                short_ref[:, here] = value.astype(jnp.bfloat16)


def head_kernel(
    x_hbm,
    valid_hbm,
    offsets_hbm,
    white_ref,
    short_ref,
    table_ref,
    pick_ref,
    keep_ref,
    x_ref,
    valid_ref,
    offsets_ref,
    raw_ref,
    sems,
):
    wins, span, length = white_ref.shape
    pairs = offsets_ref.shape[0]
    copies = [
        pltpu.make_async_copy(valid_hbm, valid_ref, sems.at[0]),
        pltpu.make_async_copy(offsets_hbm, offsets_ref, sems.at[1]),
        pltpu.make_async_copy(x_hbm.at[pl.ds(0, span * wins)], x_ref, sems.at[2]),
    ]
    for copy in copies:
        copy.start()
    fill_table(table_ref, 16)
    copies[0].wait()
    copies[1].wait()
    ahead = lax.broadcasted_iota(jnp.int32, (span, 2 * span), 1) - lax.broadcasted_iota(
        jnp.int32, (span, 2 * span), 0
    )
    for k in range(pairs):
        chosen_row = jnp.where(ahead == offsets_ref[k], jnp.float32(1.0), jnp.float32(0.0))
        pick_ref[k] = chosen_row.astype(jnp.bfloat16)
    owner = lax.broadcasted_iota(jnp.int32, (wins, wins * LANES), 0)
    column = lax.broadcasted_iota(jnp.int32, (wins, wins * LANES), 1) // LANES
    keep_ref[...] = lax.dot_general(
        valid_ref[...].astype(jnp.float32).astype(jnp.bfloat16),
        (owner == column).astype(jnp.float32).astype(jnp.bfloat16),
        (((0,), (0,)), ((), ())),
        preferred_element_type=jnp.float32,
    )
    copies[2].wait()
    whiten_block(x_ref[...], table_ref, keep_ref[:span], raw_ref, white_ref, short_ref)


def stack_pairs(pick_ref, white_ref, near_ref, parts_refs, out_ref):
    wins, _, length = white_ref.shape
    pairs, rows, reach = pick_ref.shape
    bins = length // 2
    size = pairs // len(parts_refs)

    def select(group, w):
        pick = pick_ref[group * size : (group + 1) * size].reshape(size * rows, reach)
        near = near_ref[:, w * length : (w + 1) * length]
        parts_refs[group][w] = jnp.dot(pick, near, preferred_element_type=jnp.float32)

    blocks = [(c, t) for c in range(0, rows, 16) for t in range(bins // LANES)]
    for w in range(wins):
        select(0, w)
    for group, parts_ref in enumerate(parts_refs):
        ahead = list(range(wins)) if group + 1 < len(parts_refs) else []
        for i, (c, t) in enumerate(blocks):
            for w in ahead[i :: len(blocks)]:
                select(group + 1, w)
            re = slice(t * LANES, (t + 1) * LANES)
            im = slice(bins + t * LANES, bins + (t + 1) * LANES)
            head_re = [white_ref[w, c : c + 16, re] for w in range(wins)]
            head_im = [white_ref[w, c : c + 16, im] for w in range(wins)]
            for k in range(size):
                here = slice(k * rows + c, k * rows + c + 16)
                total_re = total_im = None
                for w in range(wins):
                    part_re, part_im = parts_ref[w, here, re], parts_ref[w, here, im]
                    cross_re = head_re[w] * part_re + head_im[w] * part_im
                    cross_im = head_im[w] * part_re - head_re[w] * part_im
                    total_re = cross_re if w == 0 else total_re + cross_re
                    total_im = cross_im if w == 0 else total_im + cross_im
                pair = group * size + k
                out_ref[pair, c : c + 16, re] = total_re.astype(out_ref.dtype)
                out_ref[pair, c : c + 16, im] = total_im.astype(out_ref.dtype)


def role(limits):
    odd = lax.rem(lax.axis_index("chan") + 1, 2)
    first = lax.axis_index("tm") < jnp.where(odd == 0, *limits)
    return jnp.where(first, 0, 1 + odd)


def tail_kernel(
    limits,
    now,
    x_ref,
    table_ref,
    keep_ref,
    pick_ref,
    head_ref,
    edge_ref,
    after_ref,
    white_ref,
    short_ref,
    out_ref,
    *rest,
):
    wins, span, length = white_ref.shape
    rows = slice(span * wins, 2 * span * wins)

    if now == 0:
        rest[0][...] = edge_ref[...]
        rest = rest[1:]
    raw_ref, near_ref, *parts_refs = rest

    @pl.when(role(limits) == now)
    def _():
        x = x_ref[rows, :]
        whiten_block(x, table_ref, keep_ref[span:], raw_ref, white_ref, short_ref)
        near_ref[:span] = edge_ref[...]
        near_ref[span:] = short_ref[...]
        stack_pairs(pick_ref, head_ref, near_ref, parts_refs, out_ref)


def cross_kernel(
    limits, now, pick_ref, white_ref, short_ref, edge_ref, after_ref, out_ref, near_ref, *parts_refs
):
    span = short_ref.shape[0]

    @pl.when(role(limits) == now)
    def _():
        near_ref[:span] = short_ref[...]
        near_ref[span:] = edge_ref[...]
        stack_pairs(pick_ref, white_ref, near_ref, parts_refs, out_ref)


def chosen(options, place):
    value = jnp.float32(options[0])
    for i, option in enumerate(options[1:]):
        value = jnp.where(place == i + 1, jnp.float32(option), value)
    return value


def weighted(limits, terms, weights, place):
    total = None
    mine = role(limits)
    late = len(terms) - len(weights)
    first = terms[late][...]
    for i in range(late - 1, -1, -1):
        first = jnp.where(mine == i, terms[i][...], first)
    for term, options in zip([first] + list(terms[late + 1 :]), weights):
        value = term[...].astype(jnp.float32)
        if set(options) != {1.0}:
            value = value * (options[0] if len(set(options)) == 1 else chosen(options, place))
        total = value if total is None else total + value
    return total


def whereabouts(groups):
    return lax.rem(lax.axis_index("chan") + 1, 2) * groups + lax.axis_index("tm")


def mix_kernel(limits, weights, *refs):
    count = len(weights) + 1
    place = whereabouts(len(weights[0]) // 2)
    total = weighted(limits, refs[:count], weights, place)
    refs[-1][...] = total.astype(refs[-1].dtype)


def to_lags(stack, table):
    count = stack.shape[0]
    high = stack.astype(jnp.bfloat16)
    low = (stack - high.astype(jnp.float32)).astype(jnp.bfloat16)
    both = jnp.dot(jnp.concatenate([high, low]), table, preferred_element_type=jnp.float32)
    return both[:count] + both[count:]


def part_kernel(limits, weights, table_ref, *refs):
    place = whereabouts(len(weights[0]) // 2)
    out_ref = refs[-1]
    stack = weighted(limits, refs[: len(weights) + 2], weights, place).reshape(out_ref.shape)
    out_ref[...] = to_lags(stack, table_ref[...])


def lag_kernel(limits, scale, first, weights, table_ref, *rest):
    out_hbm, stage_ref, sem = rest[-3:]
    place = whereabouts(len(weights[0]) // 2)
    pairs, rows, length = stage_ref.shape
    stack = weighted(limits, rest[: len(weights) + 2], weights, place)
    stack = stack.reshape(pairs * rows, length)
    lagged = to_lags(stack, table_ref[...]) * scale
    stage_ref[...] = lagged.astype(stage_ref.dtype).reshape(pairs, rows, length)
    copy = pltpu.make_async_copy(stage_ref, out_hbm.at[:, pl.ds(first, rows)], sem)
    copy.start()
    copy.wait()


def last_kernel(scale, first, weights, table_ref, part_ref, more_ref, *rest):
    out_hbm, stage_ref, sem = rest[-3:]
    place = whereabouts(len(weights) // 2)
    pairs, rows, length = stage_ref.shape
    more = more_ref[...].reshape(pairs * rows, length)
    lagged = jnp.dot(more, table_ref[...], preferred_element_type=jnp.float32)
    lagged = (part_ref[...] + lagged * chosen(weights, place)) * scale
    stage_ref[...] = lagged.astype(stage_ref.dtype).reshape(pairs, rows, length)
    copy = pltpu.make_async_copy(stage_ref, out_hbm.at[:, pl.ds(first, rows)], sem)
    copy.start()
    copy.wait()


def cost(flops, moved):
    return pl.CostEstimate(flops=flops, bytes_accessed=moved, transcendentals=0)


def whole(memory=pltpu.VMEM):
    return pl.BlockSpec(memory_space=memory)


def per_device(samples, valid, offsets):
    chans, wins, length = samples.shape
    bins = length // 2
    span = OFFSET_SPAN
    pairs = offsets.shape[0]
    tiles = bins // LANES
    groups = lax.axis_size("tm")
    factor = float(np.float32(DECAY) ** np.float32(wins))
    params = pltpu.CompilerParams(vmem_limit_bytes=VMEM)

    def in_hbm(value):
        return pltpu.with_memory_space_constraint(value, pltpu.HBM)

    half = chans - span
    flat = samples.reshape(chans * wins, length)
    white_type = jax.ShapeDtypeStruct((wins, span, length), jnp.float32)
    short_type = jax.ShapeDtypeStruct((span, wins * length), jnp.bfloat16)
    local_type = jax.ShapeDtypeStruct((pairs, span, length), jnp.bfloat16)
    raw_scratch = pltpu.VMEM((2 * tiles, span * wins, LANES), jnp.float32)
    near_scratch = pltpu.VMEM((2 * span, wins * length), jnp.bfloat16)
    parts_scratch = [pltpu.VMEM((wins, pairs // 4 * span, length), jnp.float32)] * 4

    white_a, short_a, table, pick, keep = pl.pallas_call(
        head_kernel,
        out_shape=(
            white_type,
            short_type,
            jax.ShapeDtypeStruct((length, length), jnp.bfloat16),
            jax.ShapeDtypeStruct((pairs, span, 2 * span), jnp.bfloat16),
            jax.ShapeDtypeStruct((chans, wins * LANES), jnp.float32),
        ),
        in_specs=[whole(pltpu.HBM)] * 3,
        out_specs=(whole(),) * 5,
        scratch_shapes=[
            pltpu.VMEM((span * wins, length), jnp.bfloat16),
            pltpu.VMEM((wins, chans), jnp.int32),
            pltpu.SMEM((pairs,), jnp.int32),
            raw_scratch,
            pltpu.SemaphoreType.DMA((3,)),
        ],
        compiler_params=params,
        cost_estimate=cost(span * wins * length * length * 2, 2 * 1024 * 1024),
        name="head",
    )(in_hbm(flat), in_hbm(valid.T), in_hbm(offsets))

    ring = lax.axis_size("chan")

    def to_previous(value, odd, even):
        moves = [
            (c * groups + h, (c - 1) * groups + h)
            for c in range(1, ring)
            for h in (odd if c % 2 else even)
        ]
        return lax.ppermute(value, ("chan", "tm"), moves)


    columns = min(d for d in range(1, groups + 1) if groups % d == 0 and d * d >= groups)
    square = columns == 2 and groups == columns * columns
    limits = (2, 3) if square else (groups, groups)

    ahead = 2 if square else groups
    edge = to_previous(short_a, range(groups), range(ahead))

    def tail(now, after):
        return pl.pallas_call(
            functools.partial(tail_kernel, limits, now),
            out_shape=(white_type, short_type, local_type) + (short_type,) * (now == 0),
            in_specs=[whole()] * 6 + [whole(pl.ANY)],
            out_specs=(whole(),) * (3 + (now == 0)),
            scratch_shapes=[raw_scratch, near_scratch] + parts_scratch,
            compiler_params=params,
            cost_estimate=cost(span * wins * length * length * 4, 4 * 1024 * 1024),
            name="tail",
        )(flat, table, keep, pick, white_a, short_a, after)

    def cross(now, white, short, edge, after):
        return pl.pallas_call(
            functools.partial(cross_kernel, limits, now),
            out_shape=local_type,
            in_specs=[whole()] * 4 + [whole(pl.ANY)],
            out_specs=whole(),
            scratch_shapes=[near_scratch] + parts_scratch,
            compiler_params=params,
            cost_estimate=cost(pairs * span * wins * bins * 8, 4 * 1024 * 1024),
            name="cross",
        )(pick, white, short, edge, after)

    white_b, short_b, local_a, again = tail(0, table)
    edge_late = to_previous(again, [], range(ahead, groups)) if square else edge
    white_late, short_late, late_a = tail(1, local_a)
    local_b = cross(0, white_b, short_b, edge, late_a)
    late_b = cross(1, white_late, short_late, edge_late, local_b)

    power = [float(np.float32(factor) ** np.float32(d)) for d in range(groups)]
    def sent(value, even, odd):
        moves = [
            (c * groups + here, c * groups + there)
            for c in range(ring)
            for here, there in (even if c % 2 else odd)
        ]
        return lax.ppermute(value, ("chan", "tm"), moves)

    def mix(terms, weights, after):
        return pl.pallas_call(
            functools.partial(mix_kernel, limits, weights),
            out_shape=local_type,
            in_specs=[whole()] * len(terms) + [whole(pl.ANY)],
            out_specs=whole(),
            compiler_params=params,
            cost_estimate=cost(len(terms) * terms[0].size * 4, 1024 * 1024),
            name="mix",
        )(*terms, after)

    inverse = pl.pallas_call(
        inverse_kernel,
        out_shape=jax.ShapeDtypeStruct((length, length), jnp.bfloat16),
        in_specs=[whole(pl.ANY)],
        out_specs=whole(),
        compiler_params=params,
        cost_estimate=cost(length * bins * 32, 512 * 1024),
        name="inverse",
    )(local_b)

    def written(kernel, terms, later, *so_far):
        return pl.pallas_call(
            kernel,
            out_shape=jax.ShapeDtypeStruct((pairs, chans, length), jnp.bfloat16),
            in_specs=[whole()] * (1 + len(terms)) + [whole(pl.ANY)] * (len(later) + len(so_far)),
            out_specs=whole(pl.ANY),
            scratch_shapes=[
                pltpu.VMEM((pairs, span, length), jnp.bfloat16),
                pltpu.SemaphoreType.DMA,
            ],
            input_output_aliases={1 + len(terms) + len(later): 0} if so_far else {},
            compiler_params=params,
            cost_estimate=cost(pairs * span * length * length * 4, 1024 * 1024),
            name="lags",
        )(inverse, *terms, *later, *so_far)

    def part(terms, weights):
        return pl.pallas_call(
            functools.partial(part_kernel, limits, weights),
            out_shape=jax.ShapeDtypeStruct((pairs * span, length), jnp.float32),
            in_specs=[whole()] * (1 + len(terms)),
            out_specs=whole(),
            compiler_params=params,
            cost_estimate=cost(pairs * span * length * length * 4, 1024 * 1024),
            name="part",
        )(inverse, *terms)

    unit = [1.0] * (2 * groups)

    def two_hops(local, late, after, apart):
        f, ff = power[1], power[2]
        last = [(2, 3)]
        got = sent(local, [(0, 2), (1, 3)], [(0, 1), (1, 0)] + ([] if apart else last))
        alone = [sent(local, [], last)] if apart else []
        total = mix(
            [local, late, got],
            [[1.0, 1.0, 1.0, 0.0, f, 1.0, 0.0, 0.0], [ff, ff, ff, 1.0, 1.0, f, 0.0, 0.0]],
            after,
        )
        more = sent(total, [(0, 1), (2, 3), (3, 2)], [(0, 2), (1, 3)])
        weights = [
            unit,
            [ff, ff, ff, ff, 0.0, f, 0.0, f],
        ]
        weights += [[f] * (2 * groups)] * len(alone) + [[f, f, f, f, 0.0, 0.0, f, ff]]
        return total, [got] + alone + [more], weights

    def one_hop(local, late, after, apart):
        terms, weights = [], [unit]
        for d in range(1, groups):
            moves = [(h, h + d) for h in range(groups - d)]
            terms.append(sent(local, moves, moves))
            weights.append([power[d]] * (2 * groups))
        return local, terms, weights

    spread = two_hops if square else one_hop
    scale = bins**-0.5
    _, terms_a, weights_a = spread(local_a, late_a, local_b, False)
    ahead, terms_b, weights_b = spread(local_b, late_b, local_b, True)
    white_last, short_last, last_a = tail(2, ahead)
    last_b = cross(2, white_last, short_last, edge, ahead)
    terms_a = [local_a, late_a, last_a] + terms_a
    terms_b = [local_b, late_b, last_b] + terms_b
    before = part(terms_b[:-1], weights_b[:-1])
    first = functools.partial(lag_kernel, limits, scale, 0, weights_a)
    result = written(first, terms_a, [before])
    last = functools.partial(last_kernel, scale, half, weights_b[-1])
    result = written(last, [before, terms_b[-1]], [], result)
    return result.reshape(1, pairs, chans, length)


def solution(mesh):
    in_specs = (P("chan", "tm", None), P("chan", "tm"), P())
    out_specs = P("tm", None, "chan", None)
    return jax.shard_map(
        per_device, mesh=mesh, in_specs=in_specs, out_specs=out_specs, check_vma=False
    )
```

```python
import functools
import math

import jax
import jax.numpy as jnp
import numpy as np
from jax import lax
from jax.experimental import pallas as pl
from jax.experimental.pallas import tpu as pltpu
from jax.sharding import PartitionSpec as P

OFFSET_SPAN = 32
LANES = 128
DECAY = 0.99
VMEM = 24 * 1024 * 1024


def turns(number, length):
    part = (number - length * jnp.floor(number / length + 0.5)) * (1.0 / length)
    square = part * part
    cosine, sine = jnp.float32(0.0), jnp.float32(0.0)
    for k in range(10, -1, -1):
        cosine = cosine * square + (-1) ** k * (2 * math.pi) ** (2 * k) / math.factorial(2 * k)
        sine = sine * square + (-1) ** k * (2 * math.pi) ** (2 * k + 1) / math.factorial(2 * k + 1)
    return cosine, sine * part


def fill_table(table_ref, step):
    length = table_ref.shape[0]
    bins = length // 2

    def small(rows, by):
        row = lax.broadcasted_iota(jnp.int32, (rows, bins), 0)
        freq = lax.broadcasted_iota(jnp.int32, (rows, bins), 1) + 1
        return turns((row * (by * freq)).astype(jnp.float32), length)

    coarse_cos, coarse_sin = small(length // step, step)
    fine_cos, fine_sin = small(step, 1)
    for i in range(length // step):
        rows = slice(i * step, (i + 1) * step)
        cos_i, sin_i = coarse_cos[i : i + 1], coarse_sin[i : i + 1]
        cosine = (cos_i * fine_cos - sin_i * fine_sin).astype(jnp.bfloat16)
        sine = (sin_i * fine_cos + cos_i * fine_sin).astype(jnp.bfloat16)
        for t in range(bins // LANES):
            here = slice(t * LANES, (t + 1) * LANES)
            table_ref[rows, 2 * t * LANES : (2 * t + 1) * LANES] = cosine[:, here]
            table_ref[rows, (2 * t + 1) * LANES : (2 * t + 2) * LANES] = -sine[:, here]


def inverse_kernel(_, table_ref):
    length = table_ref.shape[0]
    bins = length // 2
    step = 16

    def small(rows, by, first):
        freq = (lax.broadcasted_iota(jnp.int32, (rows, length), 0) + first) * by
        lag = lax.broadcasted_iota(jnp.int32, (rows, length), 1)
        return turns((freq * lag).astype(jnp.float32), length)

    coarse_cos, coarse_sin = small(bins // step, step, 0)
    fine_cos, fine_sin = small(step, 1, 1)
    for i in range(bins // step):
        first = i * step
        cos_i, sin_i = coarse_cos[i : i + 1], coarse_sin[i : i + 1]
        cosine = cos_i * fine_cos - sin_i * fine_sin
        sine = sin_i * fine_cos + cos_i * fine_sin
        table_ref[first : first + step, :] = cosine.astype(jnp.bfloat16)
        table_ref[bins + first : bins + first + step, :] = (-sine).astype(jnp.bfloat16)


def whiten_block(x, table_ref, keep, raw_ref, white_ref, short_ref):
    wins, span, length = white_ref.shape
    bins = length // 2
    tiles = bins // LANES

    def strided(t, w):
        return raw_ref[t, pl.ds(w, span, stride=wins), :]

    total = [None] * wins
    for t in range(tiles):
        lanes = slice(2 * t * LANES, (2 * t + 2) * LANES)
        raw = jnp.dot(x, table_ref[:, lanes], preferred_element_type=jnp.float32)
        raw_ref[2 * t] = raw[:, :LANES]
        raw_ref[2 * t + 1] = raw[:, LANES:]
    for t in range(tiles):
        for w in range(wins):
            real_part, imag_part = strided(2 * t, w), strided(2 * t + 1, w)
            power = real_part * real_part + imag_part * imag_part
            total[w] = power if t == 0 else total[w] + power
    for w in range(wins):
        decay = float(np.float32(DECAY) ** np.float32(wins - 1 - w))
        level = jnp.sum(total[w], axis=-1, keepdims=True) * (0.01 / bins) + 1e-06
        alive = keep[:, w * LANES : (w + 1) * LANES]
        for t in range(tiles):
            part = [strided(2 * t, w), strided(2 * t + 1, w)]
            power = part[0] * part[0] + part[1] * part[1]
            scale = alive * lax.rsqrt(power + level)
            for i, s in enumerate((t, tiles + t)):
                value = part[i] * scale
                here = pl.ds(w * length + s * LANES, LANES)
                white_ref[w, :, s * LANES : (s + 1) * LANES] = value * decay
                short_ref[:, here] = value.astype(jnp.bfloat16)


def head_kernel(
    x_hbm,
    valid_hbm,
    offsets_hbm,
    white_ref,
    short_ref,
    table_ref,
    pick_ref,
    keep_ref,
    x_ref,
    valid_ref,
    offsets_ref,
    raw_ref,
    sems,
):
    wins, span, length = white_ref.shape
    pairs = offsets_ref.shape[0]
    copies = [
        pltpu.make_async_copy(valid_hbm, valid_ref, sems.at[0]),
        pltpu.make_async_copy(offsets_hbm, offsets_ref, sems.at[1]),
        pltpu.make_async_copy(x_hbm.at[pl.ds(0, span * wins)], x_ref, sems.at[2]),
    ]
    for copy in copies:
        copy.start()
    fill_table(table_ref, 16)
    copies[0].wait()
    copies[1].wait()
    ahead = lax.broadcasted_iota(jnp.int32, (span, 2 * span), 1) - lax.broadcasted_iota(
        jnp.int32, (span, 2 * span), 0
    )
    for k in range(pairs):
        chosen_row = jnp.where(ahead == offsets_ref[k], jnp.float32(1.0), jnp.float32(0.0))
        pick_ref[k] = chosen_row.astype(jnp.bfloat16)
    owner = lax.broadcasted_iota(jnp.int32, (wins, wins * LANES), 0)
    column = lax.broadcasted_iota(jnp.int32, (wins, wins * LANES), 1) // LANES
    keep_ref[...] = lax.dot_general(
        valid_ref[...].astype(jnp.float32).astype(jnp.bfloat16),
        (owner == column).astype(jnp.float32).astype(jnp.bfloat16),
        (((0,), (0,)), ((), ())),
        preferred_element_type=jnp.float32,
    )
    copies[2].wait()
    whiten_block(x_ref[...], table_ref, keep_ref[:span], raw_ref, white_ref, short_ref)


def stack_pairs(pick_ref, white_ref, near_ref, parts_refs, out_ref):
    wins, _, length = white_ref.shape
    pairs, rows, reach = pick_ref.shape
    bins = length // 2
    size = pairs // len(parts_refs)

    def select(group, w):
        pick = pick_ref[group * size : (group + 1) * size].reshape(size * rows, reach)
        near = near_ref[:, w * length : (w + 1) * length]
        parts_refs[group][w] = jnp.dot(pick, near, preferred_element_type=jnp.float32)

    blocks = [(c, t) for c in range(0, rows, 16) for t in range(bins // LANES)]
    for w in range(wins):
        select(0, w)
    for group, parts_ref in enumerate(parts_refs):
        ahead = list(range(wins)) if group + 1 < len(parts_refs) else []
        for i, (c, t) in enumerate(blocks):
            for w in ahead[i :: len(blocks)]:
                select(group + 1, w)
            re = slice(t * LANES, (t + 1) * LANES)
            im = slice(bins + t * LANES, bins + (t + 1) * LANES)
            head_re = [white_ref[w, c : c + 16, re] for w in range(wins)]
            head_im = [white_ref[w, c : c + 16, im] for w in range(wins)]
            for k in range(size):
                here = slice(k * rows + c, k * rows + c + 16)
                total_re = total_im = None
                for w in range(wins):
                    part_re, part_im = parts_ref[w, here, re], parts_ref[w, here, im]
                    cross_re = head_re[w] * part_re + head_im[w] * part_im
                    cross_im = head_im[w] * part_re - head_re[w] * part_im
                    total_re = cross_re if w == 0 else total_re + cross_re
                    total_im = cross_im if w == 0 else total_im + cross_im
                pair = group * size + k
                out_ref[pair, c : c + 16, re] = total_re.astype(out_ref.dtype)
                out_ref[pair, c : c + 16, im] = total_im.astype(out_ref.dtype)


def role(limits):
    odd = lax.rem(lax.axis_index("chan") + 1, 2)
    first = lax.axis_index("tm") < jnp.where(odd == 0, *limits)
    return jnp.where(first, 0, 1 + odd)


def tail_kernel(
    limits,
    now,
    x_ref,
    table_ref,
    keep_ref,
    pick_ref,
    head_ref,
    edge_ref,
    after_ref,
    white_ref,
    short_ref,
    out_ref,
    *rest,
):
    wins, span, length = white_ref.shape
    rows = slice(span * wins, 2 * span * wins)

    if now == 0:
        again_ref, *rest = rest

        @pl.when(lax.axis_index("tm") >= min(limits))
        def _():
            again_ref[...] = edge_ref[...]

    raw_ref, near_ref, *parts_refs = rest

    @pl.when(role(limits) == now)
    def _():
        x = x_ref[rows, :]
        whiten_block(x, table_ref, keep_ref[span:], raw_ref, white_ref, short_ref)
        near_ref[:span] = edge_ref[...]
        near_ref[span:] = short_ref[...]
        stack_pairs(pick_ref, head_ref, near_ref, parts_refs, out_ref)


def cross_kernel(
    limits, now, pick_ref, white_ref, short_ref, edge_ref, after_ref, out_ref, near_ref, *parts_refs
):
    span = short_ref.shape[0]

    @pl.when(role(limits) == now)
    def _():
        near_ref[:span] = short_ref[...]
        near_ref[span:] = edge_ref[...]
        stack_pairs(pick_ref, white_ref, near_ref, parts_refs, out_ref)


def chosen(options, place):
    value = jnp.float32(options[0])
    for i, option in enumerate(options[1:]):
        value = jnp.where(place == i + 1, jnp.float32(option), value)
    return value


def weighted(limits, terms, weights, place):
    total = None
    mine = role(limits)
    late = len(terms) - len(weights)
    first = terms[late][...]
    for i in range(late - 1, -1, -1):
        first = jnp.where(mine == i, terms[i][...], first)
    for term, options in zip([first] + list(terms[late + 1 :]), weights):
        value = term[...].astype(jnp.float32)
        if set(options) != {1.0}:
            value = value * (options[0] if len(set(options)) == 1 else chosen(options, place))
        total = value if total is None else total + value
    return total


def whereabouts(groups):
    return lax.rem(lax.axis_index("chan") + 1, 2) * groups + lax.axis_index("tm")


def mix_kernel(limits, weights, *refs):
    count = len(weights) + 1
    place = whereabouts(len(weights[0]) // 2)
    total = weighted(limits, refs[:count], weights, place)
    refs[-1][...] = total.astype(refs[-1].dtype)


def to_lags(stack, table):
    count = stack.shape[0]
    high = stack.astype(jnp.bfloat16)
    low = (stack - high.astype(jnp.float32)).astype(jnp.bfloat16)
    both = jnp.dot(jnp.concatenate([high, low]), table, preferred_element_type=jnp.float32)
    return both[:count] + both[count:]


def part_kernel(limits, weights, table_ref, *refs):
    place = whereabouts(len(weights[0]) // 2)
    out_ref = refs[-1]
    stack = weighted(limits, refs[: len(weights) + 2], weights, place).reshape(out_ref.shape)
    out_ref[...] = to_lags(stack, table_ref[...])


def lag_kernel(limits, scale, first, weights, table_ref, *rest):
    out_hbm, stage_ref, sems = rest[-3:]
    place = whereabouts(len(weights[0]) // 2)
    pairs, rows, length = stage_ref.shape
    stack = weighted(limits, rest[: len(weights) + 2], weights, place)
    stack = stack.reshape(pairs * rows, length)
    lagged = to_lags(stack, table_ref[...]) * scale
    stage_ref[...] = lagged.astype(stage_ref.dtype).reshape(pairs, rows, length)
    copy = pltpu.make_async_copy(stage_ref, out_hbm.at[:, pl.ds(first, rows)], sems.at[0])
    copy.start()
    copy.wait()


def last_kernel(scale, first, weights, table_ref, part_ref, more_ref, *rest):
    out_hbm, stage_ref, sems = rest[-3:]
    place = whereabouts(len(weights) // 2)
    pairs, rows, length = stage_ref.shape
    more = more_ref[...].reshape(pairs * rows, length)
    lagged = jnp.dot(more, table_ref[...], preferred_element_type=jnp.float32)
    weight = chosen(weights, place)
    size = pairs // 2
    copies = []
    for piece in range(2):
        here = slice(piece * size * rows, (piece + 1) * size * rows)
        value = (part_ref[here] + lagged[here] * weight) * scale
        there = pl.ds(piece * size, size)
        stage_ref[there] = value.astype(stage_ref.dtype).reshape(size, rows, length)
        target = out_hbm.at[there, pl.ds(first, rows)]
        copies.append(pltpu.make_async_copy(stage_ref.at[there], target, sems.at[piece]))
        copies[-1].start()
    for copy in copies:
        copy.wait()


def cost(flops, moved):
    return pl.CostEstimate(flops=flops, bytes_accessed=moved, transcendentals=0)


def whole(memory=pltpu.VMEM):
    return pl.BlockSpec(memory_space=memory)


def per_device(samples, valid, offsets):
    chans, wins, length = samples.shape
    bins = length // 2
    span = OFFSET_SPAN
    pairs = offsets.shape[0]
    tiles = bins // LANES
    groups = lax.axis_size("tm")
    factor = float(np.float32(DECAY) ** np.float32(wins))
    params = pltpu.CompilerParams(vmem_limit_bytes=VMEM)

    def in_hbm(value):
        return pltpu.with_memory_space_constraint(value, pltpu.HBM)

    half = chans - span
    flat = samples.reshape(chans * wins, length)
    white_type = jax.ShapeDtypeStruct((wins, span, length), jnp.float32)
    short_type = jax.ShapeDtypeStruct((span, wins * length), jnp.bfloat16)
    local_type = jax.ShapeDtypeStruct((pairs, span, length), jnp.bfloat16)
    raw_scratch = pltpu.VMEM((2 * tiles, span * wins, LANES), jnp.float32)
    near_scratch = pltpu.VMEM((2 * span, wins * length), jnp.bfloat16)
    parts_scratch = [pltpu.VMEM((wins, pairs // 4 * span, length), jnp.float32)] * 4

    white_a, short_a, table, pick, keep = pl.pallas_call(
        head_kernel,
        out_shape=(
            white_type,
            short_type,
            jax.ShapeDtypeStruct((length, length), jnp.bfloat16),
            jax.ShapeDtypeStruct((pairs, span, 2 * span), jnp.bfloat16),
            jax.ShapeDtypeStruct((chans, wins * LANES), jnp.float32),
        ),
        in_specs=[whole(pltpu.HBM)] * 3,
        out_specs=(whole(),) * 5,
        scratch_shapes=[
            pltpu.VMEM((span * wins, length), jnp.bfloat16),
            pltpu.VMEM((wins, chans), jnp.int32),
            pltpu.SMEM((pairs,), jnp.int32),
            raw_scratch,
            pltpu.SemaphoreType.DMA((3,)),
        ],
        compiler_params=params,
        cost_estimate=cost(span * wins * length * length * 2, 2 * 1024 * 1024),
        name="head",
    )(in_hbm(flat), in_hbm(valid.T), in_hbm(offsets))

    ring = lax.axis_size("chan")

    def to_previous(value, odd, even):
        moves = [
            (c * groups + h, (c - 1) * groups + h)
            for c in range(1, ring)
            for h in (odd if c % 2 else even)
        ]
        return lax.ppermute(value, ("chan", "tm"), moves)


    columns = min(d for d in range(1, groups + 1) if groups % d == 0 and d * d >= groups)
    square = columns == 2 and groups == columns * columns
    limits = (2, 3) if square else (groups, groups)

    ahead = 2 if square else groups
    edge = to_previous(short_a, range(groups), range(ahead))

    def tail(now, after):
        return pl.pallas_call(
            functools.partial(tail_kernel, limits, now),
            out_shape=(white_type, short_type, local_type) + (short_type,) * (now == 0),
            in_specs=[whole()] * 6 + [whole(pl.ANY)],
            out_specs=(whole(),) * (3 + (now == 0)),
            scratch_shapes=[raw_scratch, near_scratch] + parts_scratch,
            compiler_params=params,
            cost_estimate=cost(span * wins * length * length * 4, 4 * 1024 * 1024),
            name="tail",
        )(flat, table, keep, pick, white_a, short_a, after)

    def cross(now, white, short, edge, after):
        return pl.pallas_call(
            functools.partial(cross_kernel, limits, now),
            out_shape=local_type,
            in_specs=[whole()] * 4 + [whole(pl.ANY)],
            out_specs=whole(),
            scratch_shapes=[near_scratch] + parts_scratch,
            compiler_params=params,
            cost_estimate=cost(pairs * span * wins * bins * 8, 4 * 1024 * 1024),
            name="cross",
        )(pick, white, short, edge, after)

    white_b, short_b, local_a, again = tail(0, table)
    edge_late = to_previous(again, [], range(ahead, groups)) if square else edge
    white_late, short_late, late_a = tail(1, local_a)
    local_b = cross(0, white_b, short_b, edge, late_a)
    late_b = cross(1, white_late, short_late, edge_late, local_b)

    power = [float(np.float32(factor) ** np.float32(d)) for d in range(groups)]
    def sent(value, even, odd):
        moves = [
            (c * groups + here, c * groups + there)
            for c in range(ring)
            for here, there in (even if c % 2 else odd)
        ]
        return lax.ppermute(value, ("chan", "tm"), moves)

    def mix(terms, weights, after):
        return pl.pallas_call(
            functools.partial(mix_kernel, limits, weights),
            out_shape=local_type,
            in_specs=[whole()] * len(terms) + [whole(pl.ANY)],
            out_specs=whole(),
            compiler_params=params,
            cost_estimate=cost(len(terms) * terms[0].size * 4, 1024 * 1024),
            name="mix",
        )(*terms, after)

    inverse = pl.pallas_call(
        inverse_kernel,
        out_shape=jax.ShapeDtypeStruct((length, length), jnp.bfloat16),
        in_specs=[whole(pl.ANY)],
        out_specs=whole(),
        compiler_params=params,
        cost_estimate=cost(length * bins * 32, 512 * 1024),
        name="inverse",
    )(local_b)

    def written(kernel, terms, later, *so_far):
        return pl.pallas_call(
            kernel,
            out_shape=jax.ShapeDtypeStruct((pairs, chans, length), jnp.bfloat16),
            in_specs=[whole()] * (1 + len(terms)) + [whole(pl.ANY)] * (len(later) + len(so_far)),
            out_specs=whole(pl.ANY),
            scratch_shapes=[
                pltpu.VMEM((pairs, span, length), jnp.bfloat16),
                pltpu.SemaphoreType.DMA((2,)),
            ],
            input_output_aliases={1 + len(terms) + len(later): 0} if so_far else {},
            compiler_params=params,
            cost_estimate=cost(pairs * span * length * length * 4, 1024 * 1024),
            name="lags",
        )(inverse, *terms, *later, *so_far)

    def part(terms, weights):
        return pl.pallas_call(
            functools.partial(part_kernel, limits, weights),
            out_shape=jax.ShapeDtypeStruct((pairs * span, length), jnp.float32),
            in_specs=[whole()] * (1 + len(terms)),
            out_specs=whole(),
            compiler_params=params,
            cost_estimate=cost(pairs * span * length * length * 4, 1024 * 1024),
            name="part",
        )(inverse, *terms)

    unit = [1.0] * (2 * groups)

    def two_hops(local, late, after, apart):
        f, ff = power[1], power[2]
        last = [(2, 3)]
        got = sent(local, [(0, 2), (1, 3)], [(0, 1), (1, 0)] + ([] if apart else last))
        alone = [sent(local, [], last)] if apart else []
        total = mix(
            [local, late, got],
            [[1.0, 1.0, 1.0, 0.0, f, 1.0, 0.0, 0.0], [ff, ff, ff, 1.0, 1.0, f, 0.0, 0.0]],
            after,
        )
        more = sent(total, [(0, 1), (2, 3), (3, 2)], [(0, 2), (1, 3)])
        weights = [
            unit,
            [ff, ff, ff, ff, 0.0, f, 0.0, f],
        ]
        weights += [[f] * (2 * groups)] * len(alone) + [[f, f, f, f, 0.0, 0.0, f, ff]]
        return total, [got] + alone + [more], weights

    def one_hop(local, late, after, apart):
        terms, weights = [], [unit]
        for d in range(1, groups):
            moves = [(h, h + d) for h in range(groups - d)]
            terms.append(sent(local, moves, moves))
            weights.append([power[d]] * (2 * groups))
        return local, terms, weights

    spread = two_hops if square else one_hop
    scale = bins**-0.5
    _, terms_a, weights_a = spread(local_a, late_a, local_b, False)
    ahead, terms_b, weights_b = spread(local_b, late_b, local_b, True)
    white_last, short_last, last_a = tail(2, ahead)
    last_b = cross(2, white_last, short_last, edge, ahead)
    terms_a = [local_a, late_a, last_a] + terms_a
    terms_b = [local_b, late_b, last_b] + terms_b
    before = part(terms_b[:-1], weights_b[:-1])
    first = functools.partial(lag_kernel, limits, scale, 0, weights_a)
    result = written(first, terms_a, [before])
    last = functools.partial(last_kernel, scale, half, weights_b[-1])
    result = written(last, [before, terms_b[-1]], [], result)
    return result.reshape(1, pairs, chans, length)


def solution(mesh):
    in_specs = (P("chan", "tm", None), P("chan", "tm"), P())
    out_specs = P("tm", None, "chan", None)
    return jax.shard_map(
        per_device, mesh=mesh, in_specs=in_specs, out_specs=out_specs, check_vma=False
    )
```
